32 devices in a mesh: dp: 4 (over y, x), row: 4 (over z), col: 2 (over core).
Axes of the slice: x: 2, y: 2, z: 4, core: 2. Of those that a mesh axis runs over, the one named last changes fastest.
Arguments:
- tokens: bfloat16 [1088, 8192], P('col', ('dp', 'row')), may hold values from -6 to 6
- ln1_gain: float32 [1088], P('col'), may hold values from 0.1 to 1.9
- ln1_bias: float32 [1088], P('col'), may hold values from -3 to 3
- qkv_weight: bfloat16 [1088, 3, 1088], P('col', None, 'row'), may hold values from -0.1875 to 0.1875
- qv_bias: bfloat16 [2, 1088], P(None, 'row'), may hold values from -3 to 3
- out_weight: bfloat16 [1088, 1088], P('row', 'col'), may hold values from -1.5 to 1.5
- out_bias: bfloat16 [1088], P('col'), may hold values from -3 to 3
- ln2_gain: float32 [1088], P('col'), may hold values from 0.1 to 1.9
- ln2_bias: float32 [1088], P('col'), may hold values from -3 to 3
- fc_weight: bfloat16 [1088, 4352], P('col', 'row'), may hold values from -0.1875 to 0.1875
- fc_bias: bfloat16 [4352], P('row'), may hold values from -3 to 3
- proj_weight: bfloat16 [1088, 4352], P('col', 'row'), may hold values from -0.09375 to 0.09375
- proj_bias: bfloat16 [1088], P('col'), may hold values from -3 to 3
- doc_lengths: int32 [8, 20], P(('dp', 'col')), may hold values from 0 to 1024, as said below
- cotangent: bfloat16 [1088, 8192], P('col', ('dp', 'row')), may hold values from -6 to 6
Outputs:
- output: bfloat16 [1088, 8192], P('col', ('dp', 'row'))
- input_grad: bfloat16 [1088, 8192], P('col', ('dp', 'row'))
- ln1_gain_grad: float32 [1088], P('col')
- ln1_bias_grad: float32 [1088], P('col')
- qkv_weight_grad: float32 [1088, 3, 1088], P('col', None, 'row')
- qv_bias_grad: float32 [2, 1088], P(None, 'row')
- out_weight_grad: float32 [1088, 1088], P('row', 'col')
- out_bias_grad: float32 [1088], P('col')
- ln2_gain_grad: float32 [1088], P('col')
- ln2_bias_grad: float32 [1088], P('col')
- fc_weight_grad: float32 [1088, 4352], P('col', 'row')
- fc_bias_grad: float32 [4352], P('row')
- proj_weight_grad: float32 [1088, 4352], P('col', 'row')
- proj_bias_grad: float32 [1088], P('col')
The draws below stay inside these ranges and needn't reach their ends.
Inputs may be any that keep to these rules, and one draw needn't show every extreme that they name: `doc_lengths`: each row lists the lengths of one sequence's documents in order, zeros after the last; the positions after their sum (fewer than 64) are padding. In each run of 2 sequences starting at a multiple of 2, one holds a single document of all 1024 positions; in the others every document but the last has 64 to 512 tokens and the last at most 512.
All inputs are finite; a program needn't handle non-finite values.
Results may differ from the reference program's by a relative error of at most 0.012.
The reference program's roundings to bfloat16 on the way count: a program that leaves them out, or rounds other values in their place, can miss the bound.
Values may be sent and summed in bfloat16 or wider, within the bound.
A program may use at most 256 MiB of HBM per device.

```python
import math
from functools import partial
import jax
import jax.numpy as jnp
from jax import lax

HEADS = 17
HEAD_DIM = 64
D = 1088
FF = 4352
NDOC = 20
SEQ = 1024
SEQS = 8
TOKENS = 8192
DOC_MIN = 64
DOC_MAX = 512
N_COL = 2


def draw_doc_lengths(key, part):
    first_key, second_key, third_key = jax.random.split(jax.random.fold_in(key, 11), 3)
    raw_lengths = jax.random.randint(first_key, (SEQS, NDOC), DOC_MIN, DOC_MAX + 1, dtype=jnp.int32)
    padding = jax.random.randint(second_key, (SEQS, 1), 0, DOC_MIN, dtype=jnp.int32)
    doc_ends = jnp.minimum(jnp.cumsum(raw_lengths, axis=1).astype(jnp.int32), SEQ - padding)
    lengths = doc_ends - jnp.concatenate([jnp.zeros((SEQS, 1), jnp.int32), doc_ends[:, :-1]], axis=1)
    chosen = jax.random.randint(third_key, (SEQS // N_COL, 1), 0, N_COL, dtype=jnp.int32)
    single = (jnp.arange(N_COL, dtype=jnp.int32)[None, :] == chosen).reshape(SEQS)
    whole_doc = jnp.zeros((SEQS, NDOC), jnp.int32).at[:, 0].set(SEQ)
    return jnp.where(single[:, None], whole_doc, lengths).astype(jnp.int32)


def levels(own_key, shape, pieces, low, largest):
    factor_of, own = 1.0, jax.random.fold_in(own_key, 6)
    for dim, parts in pieces:
        draws = jnp.exp(jax.random.uniform(jax.random.fold_in(own, dim), (parts,), jnp.float32, low / len(pieces), largest / len(pieces)))
        factor_of = factor_of * jnp.repeat(draws, shape[dim] // parts).reshape([-1 if axis == dim else 1 for axis in range(len(shape))])
    return factor_of


def noise(stream_key, extent, deviation, limit, cuts=(), kind=jnp.bfloat16):
    entries = jax.random.normal(stream_key, extent, jnp.float32) * deviation
    if len(cuts) > 0:
        entries = levels(stream_key, extent, cuts, -0.22, 0.18) * entries
    return jnp.clip(entries, min=-limit, max=limit).astype(kind)


def setup_inputs(seed: int = 0) -> dict:
    key_list = jax.random.split(jax.random.key(seed), 16)
    tokens = noise(key_list[0], (D, TOKENS), 1.0, 6.0, ((0, 2), (1, 16)))
    ln1_gain = jnp.clip(1.0 + 0.18 * jax.random.normal(key_list[1], (D,), jnp.float32), 0.1, 1.9)
    ln1_bias = noise(key_list[2], (D,), 0.5, 3.0, ((0, 2),), jnp.float32)
    qkv_weight = noise(key_list[3], (D, 3, D), D ** -0.5, 0.1875, ((0, 2), (2, 4)))
    qv_bias = noise(key_list[4], (2, D), 0.5, 3.0, ((1, 4),))
    out_weight = noise(key_list[5], (D, D), (D // 64) ** -0.5, 1.5, ((0, 4), (1, 2)))
    out_bias = noise(key_list[6], (D,), 0.5, 3.0, ((0, 2),))
    ln2_gain = jnp.clip(1.0 + 0.18 * jax.random.normal(key_list[7], (D,), jnp.float32), 0.1, 1.9)
    ln2_bias = noise(key_list[8], (D,), 0.5, 3.0, ((0, 2),), jnp.float32)
    fc_weight = noise(key_list[9], (D, FF), D ** -0.5, 0.1875, ((0, 2), (1, 4)))
    fc_bias = noise(key_list[10], (FF,), 0.5, 3.0, ((0, 4),))
    proj_weight = noise(key_list[11], (D, FF), FF ** -0.5, 0.09375, ((0, 2), (1, 4)))
    proj_bias = noise(key_list[12], (D,), 0.5, 3.0, ((0, 2),))
    doc_lengths = draw_doc_lengths(jax.random.fold_in(key_list[15], 71), 0)
    cotangent = noise(key_list[14], (D, TOKENS), 1.0, 6.0, ((0, 2), (1, 16)))
    return dict(tokens=tokens, ln1_gain=ln1_gain, ln1_bias=ln1_bias, qkv_weight=qkv_weight, qv_bias=qv_bias, out_weight=out_weight, out_bias=out_bias, ln2_gain=ln2_gain, ln2_bias=ln2_bias, fc_weight=fc_weight, fc_bias=fc_bias, proj_weight=proj_weight, proj_bias=proj_bias, doc_lengths=doc_lengths, cotangent=cotangent)


@jax.custom_vjp
def low(v):
    return lax.optimization_barrier(v.astype(jnp.bfloat16)).astype(jnp.float32)

@jax.custom_vjp
def low_back(v):
    return v

def low_keep(v):
    return (low(v), None)

def low_pass(kept, grad):
    return (grad,)

def back_keep(v):
    return (v, None)

def back_low(kept, grad):
    return (low(grad),)
low.defvjp(low_keep, low_pass)
low_back.defvjp(back_keep, back_low)
epsilon = 1e-05
score_scale = 0.125
masked_fill = -1e+30
block_limit = 512
highest = lax.Precision.HIGHEST

def layer_norm(values, gain_vec, shift_vec):
    center = lax.optimization_barrier(jnp.mean(values, axis=-1, keepdims=True))
    spread = lax.optimization_barrier(jnp.mean(values * values, axis=-1, keepdims=True)) - center * center
    return (values - center) * lax.rsqrt(spread + epsilon) * gain_vec + shift_vec

def segments_of(lengths, places):
    doc_ends = jnp.cumsum(lengths).astype(jnp.int32)
    segment = lax.optimization_barrier(jnp.sum((doc_ends[None, :] <= places[:, None]).astype(jnp.int32), axis=1, dtype=jnp.int32))
    return (segment, places >= doc_ends[-1])

def allowed_pairs(query_place, query_segment, query_padding, key_place, key_segment):
    causal = key_place[None, :] <= query_place[:, None]
    same_doc = key_segment[None, :] == query_segment[:, None]
    itself = key_place[None, :] == query_place[:, None]
    return causal & same_doc & (jnp.logical_not(query_padding)[:, None] | itself)

def sequence_attention(inputs):
    queries, keys_all, values_all, lengths = inputs
    places = jnp.arange(SEQ, dtype=jnp.int32)
    segment, padding = segments_of(lengths, places)
    block_rows = math.gcd(SEQ, block_limit)

    def one_block(number):
        first_row = number * block_rows
        query_rows = lax.dynamic_slice_in_dim(queries, first_row, block_rows, 0)
        query_place = lax.dynamic_slice_in_dim(places, first_row, block_rows, 0)
        query_segment = lax.dynamic_slice_in_dim(segment, first_row, block_rows, 0)
        query_padding = lax.dynamic_slice_in_dim(padding, first_row, block_rows, 0)
        scores = low_back(score_scale * jnp.einsum('qhd,khd->hqk', query_rows, keys_all, precision=highest))
        allowed = allowed_pairs(query_place, query_segment, query_padding, places, segment)[None]
        masked = jnp.where(allowed, scores, masked_fill)
        best_score = lax.optimization_barrier(jnp.max(masked, axis=-1, keepdims=True))
        weights = jnp.where(allowed, jnp.exp(masked - best_score), 0.0)
        probs_f = weights / lax.optimization_barrier(jnp.sum(weights, axis=-1, keepdims=True))
        return jnp.einsum('hqk,khd->qhd', low(probs_f), values_all, precision=highest)
    blocks = lax.map(jax.checkpoint(one_block), jnp.arange(SEQ // block_rows, dtype=jnp.int32))
    return blocks.reshape(SEQ, HEADS, HEAD_DIM)

def by_sequence(values):
    return values.reshape(SEQS, SEQ, HEADS, HEAD_DIM)

def forward(tokens_f, ln1_gain, ln1_bias, qkv_weight, qv_bias, out_weight, out_bias, ln2_gain, ln2_bias, fc_weight, fc_bias, proj_weight, proj_bias, doc_lengths):
    normed1 = low(layer_norm(tokens_f, ln1_gain, ln1_bias))
    mixed_qkv = jnp.dot(normed1, qkv_weight.reshape(D, 3 * D), precision=highest).reshape(TOKENS, 3, D)
    queries = low_back(low(mixed_qkv[:, 0] + qv_bias[0]))
    keys_all = low_back(low(mixed_qkv[:, 1]))
    values_all = low_back(low(mixed_qkv[:, 2] + qv_bias[1]))
    attended = lax.map(sequence_attention, (by_sequence(queries), by_sequence(keys_all), by_sequence(values_all), doc_lengths))
    attended = low_back(low(attended.reshape(TOKENS, D)))
    hidden = tokens_f + low_back(jnp.dot(attended, out_weight, precision=highest) + out_bias)
    normed2 = low(layer_norm(hidden, ln2_gain, ln2_bias))
    pre_act = low_back(jnp.dot(normed2, fc_weight, precision=highest) + fc_bias)
    active = low(jax.nn.gelu(pre_act, approximate=False))
    return hidden + jnp.dot(active, proj_weight.T, precision=highest) + proj_bias

def reference(tokens, ln1_gain, ln1_bias, qkv_weight, qv_bias, out_weight, out_bias, ln2_gain, ln2_bias, fc_weight, fc_bias, proj_weight, proj_bias, doc_lengths, cotangent):
    floats = (tokens.astype(jnp.float32).T,) + tuple((argument.astype(jnp.float32) for argument in (ln1_gain, ln1_bias, qkv_weight, qv_bias, out_weight, out_bias, ln2_gain, ln2_bias, fc_weight, fc_bias, proj_weight, proj_bias)))
    output, pullback = jax.vjp(partial(forward, doc_lengths=doc_lengths), *floats)
    gradients = pullback(cotangent.astype(jnp.float32).T)
    return (output.T.astype(jnp.bfloat16), gradients[0].T.astype(jnp.bfloat16), gradients[1], gradients[2], gradients[3], gradients[4], gradients[5], gradients[6], gradients[7], gradients[8], gradients[9], gradients[10], gradients[11], gradients[12])
```

```python
from functools import partial
import math

import jax
import jax.numpy as jnp
from jax import lax
from jax.experimental import pallas as pl
from jax.experimental.pallas import tpu as pltpu
from jax.sharding import PartitionSpec as P

HEAD_DIM = 64


epsilon = 1e-05
score_scale = 0.125
masked_fill = -1e30
block_limit = 512


def feature_sums(first_sum, second_sum):
    return lax.psum((first_sum, second_sum), "col")


def norm_forward(values, gain_vec, shift_vec):
    feature_count = values.shape[1] * lax.axis_size("col")
    total_sum, square_sum = feature_sums(jnp.sum(values, axis=1), jnp.sum(values * values, axis=1))
    center = total_sum / feature_count
    spread = square_sum / feature_count - center * center
    inv_std = lax.rsqrt(spread + epsilon)
    normal = (values - center[:, None]) * inv_std[:, None]
    return (normal, inv_std, normal * gain_vec + shift_vec)


def norm_backward(upstream, normal, inv_std, gain_vec):
    feature_count = upstream.shape[1] * lax.axis_size("col")
    scaled = upstream * gain_vec
    plain_sum, cross_sum = feature_sums(jnp.sum(scaled, axis=1), jnp.sum(scaled * normal, axis=1))
    return inv_std[:, None] * (
        scaled - plain_sum[:, None] / feature_count - normal * (cross_sum[:, None] / feature_count)
    )


def gather_rows(values):
    return lax.all_gather(values, "row", axis=0, tiled=True)


def gather_cols(values):
    return lax.all_gather(values, "col", axis=0, tiled=True)


def sum_over_rows(row_term, row_total):
    return lax.psum_scatter(
        row_term(jnp.int32(0), row_total * lax.axis_size("row")),
        "row",
        scatter_dimension=0,
        tiled=True,
    )


def sum_over_cols(row_term, row_total):
    return lax.psum_scatter(
        row_term(jnp.int32(0), row_total * lax.axis_size("col")),
        "col",
        scatter_dimension=0,
        tiled=True,
    )


def to_heads(values):
    return lax.all_to_all(values, "row", split_axis=0, concat_axis=2, tiled=True)


def to_tokens(values):
    return lax.all_to_all(values, "row", split_axis=2, concat_axis=0, tiled=True)


def product_term(full_rows, matrix):

    def row_term(first_row, row_count):
        return jnp.dot(full_rows, matrix, preferred_element_type=jnp.float32)

    return row_term


def product_term_back(full_rows, matrix):

    def row_term(first_row, row_count):
        return lax.dot_general(
            full_rows, matrix, (((1,), (1,)), ((), ())), preferred_element_type=jnp.float32
        )

    return row_term


def slice_term(full_rows):

    def row_term(first_row, row_count):
        return full_rows

    return row_term


def inner_rows(left_side, right_side):
    return lax.dot_general(
        left_side, right_side, (((0,), (0,)), ((), ())), preferred_element_type=jnp.float32
    )


def segments_of(lengths, places):
    doc_ends = jnp.cumsum(lengths)
    segment = jnp.sum(
        (doc_ends[None, :] <= places[:, None]).astype(jnp.int32), axis=1, dtype=jnp.int32
    )
    return (segment, places >= doc_ends[-1])


def allowed_pairs(query_place, query_segment, query_padding, key_place, key_segment):
    causal = key_place[None, :] <= query_place[:, None]
    same_doc = key_segment[None, :] == query_segment[:, None]
    itself = key_place[None, :] == query_place[:, None]
    return causal & same_doc & (jnp.logical_not(query_padding)[:, None] | itself)


def attention_parts(queries, keyvals, lengths, query_place):
    seq_total = keyvals.shape[0]
    key_block_size = math.gcd(seq_total, block_limit)
    block_count = seq_total // key_block_size
    key_place = jnp.arange(seq_total, dtype=jnp.int32)
    key_segment = segments_of(lengths, key_place)[0]
    query_segment, query_padding = segments_of(lengths, query_place)
    blocked = (
        keyvals.reshape((block_count, key_block_size) + keyvals.shape[1:]),
        key_place.reshape(block_count, key_block_size),
        key_segment.reshape(block_count, key_block_size),
    )

    def block_scores(key_rows, place_rows, segment_rows):
        raw_scores = (
            jnp.einsum("qhd,khd->hqk", queries, key_rows, preferred_element_type=jnp.float32)
            * score_scale
        )
        allowed = allowed_pairs(
            query_place, query_segment, query_padding, place_rows, segment_rows
        )[None]
        return (raw_scores, allowed)

    return (blocked, block_scores)


def attention_forward(queries, blocked, block_scores):
    query_count, head_count, head_width = queries.shape

    def max_step(running, inputs):
        best_score, mass_sum = running
        kv_block, place_rows, segment_rows = inputs
        raw_scores, allowed = block_scores(kv_block[:, 0], place_rows, segment_rows)
        masked = jnp.where(allowed, raw_scores, masked_fill)
        new_best = jnp.maximum(best_score, jnp.max(masked, axis=2))
        fresh = jnp.sum(jnp.where(allowed, jnp.exp(masked - new_best[:, :, None]), 0.0), axis=2)
        return ((new_best, mass_sum * jnp.exp(best_score - new_best) + fresh), None)

    start_best = jnp.full((head_count, query_count), masked_fill, jnp.float32)
    start_mass = jnp.zeros((head_count, query_count), jnp.float32)
    (best_score, mass_sum), unused = lax.scan(max_step, (start_best, start_mass), blocked)
    log_sum = best_score + jnp.log(mass_sum)

    def out_step(running, inputs):
        kv_block, place_rows, segment_rows = inputs
        raw_scores, allowed = block_scores(kv_block[:, 0], place_rows, segment_rows)
        probs_low = jnp.where(allowed, jnp.exp(raw_scores - log_sum[:, :, None]), 0.0).astype(
            jnp.bfloat16
        )
        return (
            running
            + jnp.einsum(
                "hqk,khd->qhd", probs_low, kv_block[:, 1], preferred_element_type=jnp.float32
            ),
            None,
        )

    attended, unused = lax.scan(
        out_step, jnp.zeros((query_count, head_count, head_width), jnp.float32), blocked
    )
    return (attended, log_sum)


def attention_backward(queries, blocked, block_scores, log_sum, grad_attended):
    query_count, head_count, head_width = queries.shape

    def probs_and_grads(inputs):
        kv_block, place_rows, segment_rows = inputs
        raw_scores, allowed = block_scores(kv_block[:, 0], place_rows, segment_rows)
        probs_f = jnp.where(allowed, jnp.exp(raw_scores - log_sum[:, :, None]), 0.0)
        grad_probs = jnp.einsum(
            "qhd,khd->hqk", grad_attended, kv_block[:, 1], preferred_element_type=jnp.float32
        )
        return (probs_f, grad_probs)

    def delta_step(running, inputs):
        probs_f, grad_probs = probs_and_grads(inputs)
        return (running + jnp.sum(probs_f * grad_probs, axis=2), None)

    delta_sum, unused = lax.scan(
        delta_step, jnp.zeros((head_count, query_count), jnp.float32), blocked
    )

    def grad_step(running, inputs):
        kv_block = inputs[0]
        probs_f, grad_probs = probs_and_grads(inputs)
        grad_scores = (probs_f * (grad_probs - delta_sum[:, :, None])).astype(jnp.bfloat16)
        running = running + jnp.einsum(
            "hqk,khd->qhd", grad_scores, kv_block[:, 0], preferred_element_type=jnp.float32
        )
        grad_keys = (
            jnp.einsum("hqk,qhd->khd", grad_scores, queries, preferred_element_type=jnp.float32)
            * score_scale
        )
        grad_values = jnp.einsum(
            "hqk,qhd->khd",
            probs_f.astype(jnp.bfloat16),
            grad_attended,
            preferred_element_type=jnp.float32,
        )
        return (running, jnp.stack([grad_keys, grad_values], axis=1))

    grad_queries, grad_keyvals = lax.scan(
        grad_step, jnp.zeros((query_count, head_count, head_width), jnp.float32), blocked
    )
    seq_total = grad_keyvals.shape[0] * grad_keyvals.shape[1]
    return (grad_queries * score_scale, grad_keyvals.reshape(seq_total, 2, head_count, head_width))


def body(
    tokens,
    ln1_gain,
    ln1_bias,
    qkv_weight,
    qv_bias,
    out_weight,
    out_bias,
    ln2_gain,
    ln2_bias,
    fc_weight,
    fc_bias,
    proj_weight,
    proj_bias,
    doc_lengths,
    cotangent,
):
    count_rows = lax.axis_size("row")
    count_cols = lax.axis_size("col")
    grid_rows = tokens.shape[1]
    col_width = tokens.shape[0]
    row_width = out_weight.shape[0]
    seq_rows = grid_rows * count_rows // count_cols
    query_rows = seq_rows // count_rows
    full_width = col_width * count_cols
    head_count = full_width // HEAD_DIM
    tokens_f = tokens.astype(jnp.float32).T
    normal1, inv_std1, shaped1 = norm_forward(tokens_f, ln1_gain, ln1_bias)
    qkv_flat = qkv_weight.reshape(col_width, 3 * row_width)
    gathered1 = gather_rows(shaped1.astype(jnp.bfloat16))
    mixed_qkv = sum_over_cols(product_term(gathered1, qkv_flat), seq_rows).reshape(
        seq_rows, 3, row_width
    )
    bias_three = jnp.stack([qv_bias[0], jnp.zeros_like(qv_bias[0]), qv_bias[1]])
    qkv_low = (mixed_qkv + bias_three).astype(jnp.bfloat16)
    local_qkv = to_heads(qkv_low).reshape(query_rows, 3, head_count, HEAD_DIM)
    queries = local_qkv[:, 0]
    keyvals = lax.all_gather(local_qkv[:, 1:], "row", axis=0, tiled=True)
    query_place = lax.axis_index("row") * query_rows + jnp.arange(query_rows, dtype=jnp.int32)
    blocked, block_scores = attention_parts(queries, keyvals, doc_lengths[0], query_place)
    attended_f, log_sum = attention_forward(queries, blocked, block_scores)
    attended_low = attended_f.reshape(query_rows, 1, full_width).astype(jnp.bfloat16)
    attended_grid = to_tokens(attended_low).reshape(seq_rows, row_width)
    gathered_att = gather_cols(attended_grid)
    branch = sum_over_rows(product_term(gathered_att, out_weight), grid_rows)
    hidden = tokens_f + (branch + out_bias)
    normal2, inv_std2, shaped2 = norm_forward(hidden, ln2_gain, ln2_bias)
    normed2 = shaped2.astype(jnp.bfloat16)
    gathered2 = gather_rows(normed2)
    pre_act = sum_over_cols(product_term(gathered2, fc_weight), seq_rows) + fc_bias
    active = jax.nn.gelu(pre_act, approximate=False).astype(jnp.bfloat16)
    gathered_act = gather_cols(active)
    projected = sum_over_rows(product_term_back(gathered_act, proj_weight), grid_rows)
    output = (hidden + projected + proj_bias).astype(jnp.bfloat16).T
    cotangent_rows = cotangent.T
    grad_out = cotangent_rows.astype(jnp.float32)
    unused, gelu_back = jax.vjp(partial(jax.nn.gelu, approximate=False), pre_act)
    grad_gathered = gather_rows(cotangent_rows)
    proj_weight_grad = inner_rows(grad_gathered, gathered_act)
    proj_bias_grad = jnp.sum(grad_gathered, axis=0, dtype=jnp.float32)
    grad_active = sum_over_cols(product_term(grad_gathered, proj_weight), seq_rows)
    grad_pre = gelu_back(grad_active)[0].astype(jnp.bfloat16)
    grad_pre_all = gather_cols(grad_pre)
    fc_weight_grad = inner_rows(gathered2, grad_pre_all)
    fc_bias_grad = jnp.sum(grad_pre_all, axis=0, dtype=jnp.float32)
    grad_normed2 = sum_over_rows(product_term_back(grad_pre_all, fc_weight), grid_rows)
    ln2_gain_part = jnp.sum(grad_normed2 * normal2, axis=0)
    ln2_bias_part = jnp.sum(grad_normed2, axis=0)
    grad_hidden = grad_out + norm_backward(grad_normed2, normal2, inv_std2, ln2_gain)
    branch_gathered = gather_rows(grad_hidden.astype(jnp.bfloat16))
    out_weight_grad = inner_rows(gathered_att, branch_gathered)
    out_bias_grad = jnp.sum(branch_gathered, axis=0, dtype=jnp.float32)
    grad_att_grid = sum_over_cols(product_term_back(branch_gathered, out_weight), seq_rows).astype(
        jnp.bfloat16
    )
    grad_attended = to_heads(grad_att_grid.reshape(seq_rows, 1, row_width)).reshape(
        query_rows, head_count, HEAD_DIM
    )
    grad_queries, grad_keyvals = attention_backward(
        queries, blocked, block_scores, log_sum, grad_attended
    )
    keyval_rows = sum_over_rows(slice_term(grad_keyvals), query_rows)
    grad_qkv_local = (
        jnp.concatenate([grad_queries[:, None], keyval_rows], axis=1)
        .astype(jnp.bfloat16)
        .reshape(query_rows, 3, full_width)
    )
    grad_qkv_grid = to_tokens(grad_qkv_local).reshape(seq_rows, 3 * row_width)
    qkv_gathered = gather_cols(grad_qkv_grid)
    qkv_weight_grad = inner_rows(gathered1, qkv_gathered).reshape(col_width, 3, row_width)
    qkv_bias_sums = jnp.sum(qkv_gathered, axis=0, dtype=jnp.float32).reshape(3, row_width)
    qv_bias_grad = jnp.stack([qkv_bias_sums[0], qkv_bias_sums[2]])
    grad_normed1 = sum_over_rows(product_term_back(qkv_gathered, qkv_flat), grid_rows)
    ln1_gain_part = jnp.sum(grad_normed1 * normal1, axis=0)
    ln1_bias_part = jnp.sum(grad_normed1, axis=0)
    input_grad = (
        (grad_hidden + norm_backward(grad_normed1, normal1, inv_std1, ln1_gain))
        .astype(jnp.bfloat16)
        .T
    )
    summed = lax.psum(
        (
            qkv_weight_grad,
            qv_bias_grad,
            out_weight_grad,
            out_bias_grad,
            fc_weight_grad,
            fc_bias_grad,
            proj_weight_grad,
            proj_bias_grad,
        ),
        "dp",
    )
    gain_sums = lax.psum(
        (ln1_gain_part, ln1_bias_part, ln2_gain_part, ln2_bias_part), ("dp", "row")
    )
    return (
        output,
        input_grad,
        gain_sums[0],
        gain_sums[1],
        summed[0],
        summed[1],
        summed[2],
        summed[3],
        gain_sums[2],
        gain_sums[3],
        summed[4],
        summed[5],
        summed[6],
        summed[7],
    )


BF = jnp.bfloat16
F32 = jnp.float32
MESH = pl.DeviceIdType.MESH
LANES = 128
KEY_TILE = 256
VEC_LN1_GAIN, VEC_LN1_BIAS, VEC_LN2_GAIN, VEC_LN2_BIAS, VEC_OUT_BIAS, VEC_PROJ_BIAS = range(6)


def dot_nn(left, right):
    return lax.dot_general(left, right, (((1,), (0,)), ((), ())), preferred_element_type=F32)


def dot_tn(left, right):
    return lax.dot_general(left, right, (((0,), (0,)), ((), ())), preferred_element_type=F32)


def dot_nt(left, right):
    return lax.dot_general(left, right, (((1,), (1,)), ((), ())), preferred_element_type=F32)


VMEM_LIMIT = 66_000_000


class Slots:
    def __init__(self):
        self.used = 0

    def take(self, count=1):
        first = self.used
        self.used += count
        return first


SEND_COUNT, RECV_COUNT, LOCAL_COUNT = 112, 128, 32


def layer_kernel(
    x_in,
    cot_in,
    w3_in,
    ow_in,
    ff_in,
    fcb_in,
    vec_in,
    doc_in,
    out_o,
    ing_o,
    gf_o,
    gq_o,
    vec_o,
    rf_hbm,
    rq_hbm,
    XG,
    CG,
    N1,
    WB,
    OWB,
    FB,
    FCB,
    FCC,
    VEC,
    DOC,
    MASK,
    QKV,
    LSE,
    ATT,
    HID,
    ST1,
    ST2,
    N2,
    ACT,
    GPRE,
    PGS,
    OPS,
    RCG,
    RCO,
    OPO,
    SZG,
    RZG,
    G2,
    SZO,
    RZO,
    RZN,
    DATT,
    GQKV,
    ACCK,
    ACCV,
    ZF,
    DQ,
    ZQ,
    ZT,
    GH,
    VGC,
    STX,
    SPR,
    SPZ,
    VOUT,
    SS,
    RS,
    LS,
    *,
    doc_count,
):
    H, T = x_in.shape
    R = w3_in.shape[1]
    HP = w3_in.shape[2]
    EXT = WB.shape[2]
    TAIL = EXT - R
    D = 2 * H
    S = 2 * T
    W = KEY_TILE
    Q = HEAD_DIM
    FW = ff_in.shape[1]
    per_tok = T // W
    n_tiles = S // W
    inv_d = 1.0 / D

    dp, z, c = lax.axis_index("dp"), lax.axis_index("row"), lax.axis_index("col")
    oc = 1 - c
    zz = lax.rem(z, 2)
    zp = z + 1 - 2 * zz
    z2 = lax.rem(z + 2, 4)
    j = lax.rem(z + 2 * c, 4)
    pair = z // 2
    core = (dp, z, oc)
    zdev = (dp, zp, c)
    xn = dp + 1 - 2 * lax.rem(dp, 2)
    yn = lax.rem(dp + 2, 4)
    dg = 3 - dp
    peers = (dg, xn, yn)
    first_core, second_core = c == 0, c == 1

    sends, recvs, locs = Slots(), Slots(), Slots()
    pending = []

    def remote(src, dst, s_idx, r_idx, dev):
        return pltpu.make_async_remote_copy(
            src_ref=src,
            dst_ref=dst,
            send_sem=SS.at[s_idx],
            recv_sem=RS.at[r_idx],
            device_id=dev,
            device_id_type=MESH,
        )

    def when(cond, fn):
        if cond is None:
            fn()
        else:
            pl.when(cond)(fn)

    def push(src, dst, r_idx, dev, cond=None):
        copy = remote(src, dst, sends.take(), r_idx, dev)
        when(cond, copy.start)
        entry = [cond, copy]
        pending.append(entry)
        return entry

    def sent(entry):
        when(entry[0], entry[1].wait_send)
        pending[:] = [other for other in pending if other is not entry]

    def arrived(dst, r_idx, cond=None):
        when(cond, remote(dst, dst, 0, r_idx, core).wait_recv)

    def local(src, dst, cond=None):
        copy = pltpu.make_async_copy(src, dst, LS.at[locs.take()])
        when(cond, copy.start)
        return (cond, copy)

    def done(entry):
        when(entry[0], entry[1].wait)

    barrier = pltpu.get_barrier_semaphore()
    for step in range(4):
        for side in range(2):
            if step == 0 and side == 0:
                continue
            target = (dp, lax.rem(z + step, 4), c if side == 0 else oc)
            pl.semaphore_signal(barrier, inc=1, device_id=target, device_id_type=MESH)
    for peer in peers:
        pl.semaphore_signal(barrier, inc=1, device_id=(peer, z, c), device_id_type=MESH)
    pl.semaphore_wait(barrier, 10)

    r_x_core, r_x_z, r_x_fwd = recvs.take(), recvs.take(), recvs.take()
    r_w_core, r_w_z, r_w_xy, r_w_tail = recvs.take(), recvs.take(2), recvs.take(4), recvs.take(2)
    r_vec, r_doc = recvs.take(), recvs.take()

    push(x_in, XG.at[zz, c], r_x_z, zdev)
    w_row = jnp.minimum(dp, 2)
    push(w3_in.at[w_row], WB.at[w_row, c, pl.ds(0, R)], r_w_z + c, (dp, z2, 1), dp < 3)
    has_before = z >= 1
    push(w3_in.at[:, pl.ds(0, TAIL)], WB.at[:, c, pl.ds(R, TAIL)], r_w_tail + c, (dp, jnp.maximum(z - 1, 0), 0), has_before)
    push(w3_in.at[:, pl.ds(0, TAIL)], WB.at[:, c, pl.ds(R, TAIL)], r_w_tail + c, (dp, lax.rem(z + 1, 4), 1), has_before)
    push(x_in, XG.at[zz, c], r_x_core, core)
    push(w3_in, WB.at[:, 1, pl.ds(0, R)], r_w_core, (dp, z, 0), second_core)
    push(doc_in, DOC.at[c], r_doc, core)
    push(vec_in, VEC.at[c], r_vec, core)
    l_x = local(x_in, XG.at[zz, c])
    l_w = local(w3_in, WB.at[:, 0, pl.ds(0, R)], first_core)
    l_doc = local(doc_in, DOC.at[c])
    l_vec = local(vec_in, VEC.at[c])

    pad_rows = HP - H
    ones_row = (lax.broadcasted_iota(jnp.int32, (pad_rows, T), 0) == 0).astype(BF)
    for t in range(2):
        for h in range(2):
            N1[t, h, H:, :] = ones_row
    VGC[...] = jnp.zeros_like(VGC)
    GQKV[...] = jnp.zeros_like(GQKV)

    def clear_tail():
        WB[:, :, R:, :] = jnp.zeros((3, 2, TAIL, HP), BF)

    pl.when(j == 3)(clear_tail)

    done(l_doc)
    arrived(DOC.at[oc], r_doc)
    lengths = DOC[pair][0:1, :]
    place_c = lax.broadcasted_iota(jnp.int32, (S, LANES), 0).astype(F32)
    place_r = lax.broadcasted_iota(jnp.int32, (8, S), 1).astype(F32)
    end = jnp.zeros((1, 1), F32)
    seg_c, seg_r = jnp.zeros_like(place_c), jnp.zeros_like(place_r)
    for number in range(doc_count):
        end = end + lengths[:, number : number + 1]
        seg_c = seg_c + jnp.where(end <= place_c, 1.0, 0.0)
        seg_r = seg_r + jnp.where(end <= place_r, 1.0, 0.0)
    seg_c = jnp.where(end <= place_c, place_c + 2.0 * S, seg_c)
    seg_r = jnp.where(end <= place_r, place_r + 2.0 * S, seg_r)
    for tile in range(n_tiles):
        rows = W * (tile + 1)
        first = W * tile * (tile + 1) // 2
        cols = slice(tile * W, (tile + 1) * W)
        key_seg = jnp.concatenate([seg_c[:rows]] * (W // LANES), axis=1)
        key_place = jnp.concatenate([place_c[:rows]] * (W // LANES), axis=1)
        ok = (key_seg == seg_r[0:1, cols]) & (key_place <= place_r[0:1, cols])
        MASK[first : first + rows, :] = jnp.where(ok, 0.0, masked_fill)

    done(l_vec)
    arrived(VEC.at[oc], r_vec)

    def column(h, which):
        return VEC[h, :, which : which + 1]

    def stats_of(first_half, second_half):
        center = (
            jnp.sum(first_half, axis=0, keepdims=True) + jnp.sum(second_half, axis=0, keepdims=True)
        ) * inv_d
        square = (
            jnp.sum(first_half * first_half, axis=0, keepdims=True)
            + jnp.sum(second_half * second_half, axis=0, keepdims=True)
        ) * inv_d
        return center, lax.rsqrt(square - center * center + epsilon)

    def first_norm(t):
        halves = [XG[t, h].astype(F32) for h in range(2)]
        center, inv_std = stats_of(*halves)
        ST1[t, 0:1, :] = center
        ST1[t, 1:2, :] = inv_std
        for h in range(2):
            shaped = (halves[h] - center) * inv_std * column(h, VEC_LN1_GAIN) + column(
                h, VEC_LN1_BIAS
            )
            N1[t, h, 0:H, :] = shaped.astype(BF)

    done(l_x)
    arrived(XG.at[zz, oc], r_x_core)
    first_norm(zz)

    w_from_z = second_core & (dp < 3)
    for h in range(2):
        arrived(WB.at[w_row, h, pl.ds(0, R)], r_w_z + h, w_from_z)
    for peer in peers:
        push(
            WB.at[w_row, :, pl.ds(0, R)],
            WB.at[w_row, :, pl.ds(0, R)],
            r_w_xy + w_row,
            (peer, z, 1),
            w_from_z,
        )
    arrived(XG.at[1 - zz, c], r_x_z)
    e_xf = push(XG.at[1 - zz, c], XG.at[1 - zz, c], r_x_fwd, core)

    quarter = ff_in.shape[0] // 4
    my_quarter = pl.ds(pl.multiple_of(dp * quarter, 16), quarter)
    r_f_core, r_f_z, r_f_xy, r_fcb = recvs.take(), recvs.take(2), recvs.take(4), recvs.take()
    push(ff_in.at[my_quarter], FB.at[c, my_quarter], r_f_z + c, (dp, z2, 1))
    push(ff_in, FB.at[1], r_f_core, (dp, z, 0), second_core)
    push(fcb_in, FCB, r_fcb, (dp, z2, 1), first_core)
    l_f = local(ff_in, FB.at[0], first_core)
    l_fcb = local(fcb_in, FCB, first_core)

    arrived(XG.at[1 - zz, oc], r_x_fwd)
    first_norm(1 - zz)

    done(l_w)
    arrived(WB.at[:, 1, pl.ds(0, R)], r_w_core, first_core)
    for m in range(3):
        arrived(WB.at[m, :, pl.ds(0, R)], r_w_xy + m, second_core & (dp != m))
    for h in range(2):
        arrived(WB.at[:, h, pl.ds(R, TAIL)], r_w_tail + h, j < 3)

    for t in range(2):
        for m in range(3):
            mixed = dot_nn(WB[m, 0], N1[t, 0]) + dot_nn(WB[m, 1], N1[t, 1])
            low = mixed.astype(BF)
            if m == 0:
                low = low * jnp.asarray(score_scale, BF)
            QKV[m, :, t * T : (t + 1) * T] = low

    r_o_core, r_o_z, r_o_fwd = recvs.take(), recvs.take(4), recvs.take(4)
    r_c_core, r_c_z, r_c_fwd = recvs.take(), recvs.take(), recvs.take()

    def block(number):
        return pl.ds(pl.multiple_of(number * R, 16), R)

    for step in (1, 3, 2):
        push(ow_in, OWB.at[c, block(z)], r_o_z + z, (dp, lax.rem(z + step, 4), c))
    push(cot_in, CG.at[zz, c], r_c_z, zdev)
    push(ow_in, OWB.at[c, block(z)], r_o_core, core)
    push(cot_in, CG.at[zz, c], r_c_core, core)
    l_o = local(ow_in, OWB.at[c, block(z)])
    l_c = local(cot_in, CG.at[zz, c])

    r_a_z, r_a_core, r_a_fwd = recvs.take(5), recvs.take(5), recvs.take(5)
    s_a_z, s_a_core, s_a_fwd = sends.take(5), sends.take(5), sends.take(5)
    first_slot = jnp.where(j == 0, 0, 1)

    def head_rows(owner, slot):
        return pl.ds(pl.multiple_of(owner * (4 * Q) + slot * Q, Q), Q)

    def slot_rows(slot):
        return pl.ds(pl.multiple_of(slot * Q - 16 * j, 16), Q)

    def att_copy(owner, slot, s_base, r_base, dev):
        rows = head_rows(owner, slot)
        return remote(ATT.at[rows], ATT.at[rows], s_base + slot, r_base + slot, dev)

    forward_slot = 3
    s_f_xy = sends.take(3)

    def ff_copy(number):
        part = FB.at[:, my_quarter]
        return remote(part, part, s_f_xy + number, r_f_xy + dp, (peers[number], z, 1))

    def forward_ff():
        for h in range(2):
            arrived(FB.at[h, my_quarter], r_f_z + h, second_core)
        for number in range(3):
            when(second_core, ff_copy(number).start)

    def attend(slot, carry):
        rows = slot_rows(slot)
        out_rows = head_rows(j, slot)
        queries = QKV[0, rows, :]
        keys = QKV[1, rows, :].T
        values = QKV[2, rows, :]
        for tile in range(n_tiles):
            count = W * (tile + 1)
            first = W * tile * (tile + 1) // 2
            cols = slice(tile * W, (tile + 1) * W)
            scores = dot_nn(keys[:count], queries[:, cols]) + MASK[first : first + count, :]
            best = jnp.max(scores, axis=0, keepdims=True)
            weights = jnp.exp(scores - best)
            mass = jnp.sum(weights, axis=0, keepdims=True)
            probs_low = (weights * (1.0 / mass)).astype(BF)
            ATT[out_rows, cols] = dot_nn(values[:, :count], probs_low).astype(BF)
            LSE[slot, 0:1, cols] = best + jnp.log(mass)
        att_copy(j, slot, s_a_z, r_a_z, zdev).start()
        att_copy(j, slot, s_a_core, r_a_core, core).start()

        @pl.when(slot == forward_slot)
        def _():
            forward_ff()

        return carry

    lax.fori_loop(first_slot, 5, attend, 0)

    arrived(CG.at[1 - zz, c], r_c_z)
    push(CG.at[1 - zz, c], CG.at[1 - zz, c], r_c_fwd, core)
    for step in (1, 3, 2):
        there = lax.rem(z + step, 4)
        arrived(OWB.at[c, block(there)], r_o_z + there)
        push(OWB.at[c, block(there)], OWB.at[c, block(there)], r_o_fwd + there, core)

    def owner_of(zv, cv):
        return lax.rem(zv + 2 * cv, 4)

    def slots_of(owner, body):
        lax.fori_loop(jnp.where(owner == 0, 0, 1), 5, lambda slot, carry: (body(slot), carry)[1], 0)

    def pass_on(slot):
        att_copy(owner_of(zp, c), slot, s_a_fwd, r_a_z, core).wait_recv()
        att_copy(owner_of(zp, c), slot, s_a_fwd, r_a_fwd, core).start()

    slots_of(owner_of(zp, c), pass_on)
    slots_of(owner_of(z, oc), lambda slot: att_copy(owner_of(z, oc), slot, s_a_core, r_a_core, core).wait_recv())
    slots_of(owner_of(zp, oc), lambda slot: att_copy(owner_of(zp, oc), slot, s_a_fwd, r_a_fwd, core).wait_recv())
    done(l_o)
    arrived(OWB.at[oc, block(z)], r_o_core)
    for step in range(1, 4):
        there = lax.rem(z + step, 4)
        arrived(OWB.at[oc, block(there)], r_o_fwd + there)

    def project(tile, carry):
        t = tile // per_tok
        cols = pl.ds(pl.multiple_of(lax.rem(tile, per_tok) * W, W), W)
        all_cols = pl.ds(pl.multiple_of(tile * W, W), W)
        att = ATT[:, all_cols]
        halves = []
        for h in range(2):
            branch = dot_tn(OWB[h], att)
            halves.append(XG[t, h, :, cols].astype(F32) + (branch + column(h, VEC_OUT_BIAS)))
            HID[t, h, :, cols] = halves[h]
        center, inv_std = stats_of(*halves)
        ST2[t, 0:1, cols] = center
        ST2[t, 1:2, cols] = inv_std
        for h in range(2):
            shaped = (halves[h] - center) * inv_std * column(h, VEC_LN2_GAIN) + column(
                h, VEC_LN2_BIAS
            )
            N2[t, h, :, cols] = shaped.astype(BF)
        return carry

    lax.fori_loop(0, n_tiles, project, 0)

    done(l_f)
    done(l_fcb)
    arrived(FB.at[1], r_f_core, first_core)
    arrived(FCB, r_fcb, second_core)
    for number in range(4):
        rows = pl.ds(number * quarter, quarter)
        arrived(FB.at[:, rows], r_f_xy + number, second_core & (dp != number))
    done(l_c)
    arrived(CG.at[zz, oc], r_c_core)
    arrived(CG.at[1 - zz, oc], r_c_fwd)

    one_row = (lax.broadcasted_iota(jnp.int32, (16, LANES), 0) == 0).astype(BF)
    FCC[...] = dot_tn(FCB[...], one_row)

    r_g_core, r_p_core, r_g_z = recvs.take(n_tiles), recvs.take(n_tiles), recvs.take(n_tiles)
    s_g_core, s_p_core, s_g_z = sends.take(n_tiles), sends.take(n_tiles), sends.take(n_tiles)

    def tile_at(tile):
        t = tile // per_tok
        return t, pl.ds(pl.multiple_of(lax.rem(tile, per_tok) * W, W), W)

    def part_copy(buf, dst, tile, s_base, r_base, dev):
        t, cols = tile_at(tile)
        return remote(buf.at[t, :, cols], dst.at[t, :, cols], s_base + tile, r_base + tile, dev)

    def feed(tile, carry):
        t, cols = tile_at(tile)
        all_cols = pl.ds(pl.multiple_of(tile * W, W), W)
        pre = (
            dot_tn(FB[0, 0:H], N2[t, 0, :, cols])
            + dot_tn(FB[1, 0:H], N2[t, 1, :, cols])
            + FCC[:, 0:1]
        )
        phi = 0.5 * (1.0 + lax.erf(pre * (2.0**-0.5)))
        ACT[:, all_cols] = (pre * phi).astype(BF)
        slope = phi + pre * jnp.exp(pre * pre * -0.5) * ((2.0 * math.pi) ** -0.5)
        grad_act = dot_tn(FB[0, H:D], CG[t, 0, :, cols]) + dot_tn(FB[1, H:D], CG[t, 1, :, cols])
        GPRE[:, all_cols] = (grad_act * slope).astype(BF)
        PGS[t, :, cols] = dot_nn(FB[oc, 0:H], GPRE[:, all_cols]).astype(BF)
        part_copy(PGS, RCG, tile, s_g_core, r_g_core, core).start()
        own = dot_nn(FB[c, 0:H], GPRE[:, all_cols])
        OPS[t, :, cols] = dot_nn(FB[oc, H:D], ACT[:, all_cols]).astype(BF)
        part_copy(OPS, RCO, tile, s_p_core, r_p_core, core).start()
        part_copy(PGS, RCG, tile, s_g_core, r_g_core, core).wait_recv()
        SZG[t, :, cols] = (own + RCG[t, :, cols].astype(F32)).astype(BF)
        part_copy(SZG, RZG, tile, s_g_z, r_g_z, zdev).start()
        OPO[t, :, cols] = dot_nn(FB[c, H:D], ACT[:, all_cols]).astype(BF)
        return carry

    lax.fori_loop(0, n_tiles, feed, 0)

    def wait_sends(tile, carry):
        part_copy(PGS, RCG, tile, s_g_core, r_g_core, core).wait_send()
        part_copy(OPS, RCO, tile, s_p_core, r_p_core, core).wait_send()
        return carry

    r_out_z = recvs.take()

    def wait_out(tile, carry):
        part_copy(OPS, RCO, tile, s_p_core, r_p_core, core).wait_recv()
        return carry

    lax.fori_loop(0, n_tiles, wait_out, 0)
    SZO[...] = (OPO[1 - zz].astype(F32) + RCO[1 - zz].astype(F32)).astype(BF)
    push(SZO, RZO, r_out_z, zdev)

    for number in range(3):
        when(second_core, ff_copy(number).wait_send)
    r_rf = recvs.take(4)
    rf_entries = []
    for number in range(4):
        rows = slice(number * quarter, (number + 1) * quarter)
        for h in range(2):
            if number < 2:
                left, right, low = N2, GPRE, number * quarter
            else:
                left, right, low = CG, ACT, (number - 2) * quarter
            total = dot_nt(left[0, h, low : low + quarter, :], right[:, 0:T]) + dot_nt(
                left[1, h, low : low + quarter, :], right[:, T:S]
            )
            FB[h, rows, :] = total.astype(BF)
        rf_entries.append(
            push(
                FB.at[:, pl.ds(number * quarter, quarter)],
                rf_hbm.at[dp],
                r_rf + dp,
                (number, z, c),
                dp != number,
            )
        )
    SPR[dp] = jnp.zeros(SPR.shape[1:], F32)
    SPR[dp, 6:7, :] = dot_nt(jnp.ones((16, S), BF), GPRE[...])[0:1, :]

    r_g_all = recvs.take(n_tiles)
    s_g_all = sends.take(n_tiles)

    def g2_copy(tile):
        t, cols = tile_at(tile)
        return remote(G2.at[t, c, :, cols], G2.at[t, c, :, cols], s_g_all + tile, r_g_all + tile, core)

    def g2_other(tile):
        t, cols = tile_at(tile)
        return remote(G2.at[t, oc, :, cols], G2.at[t, oc, :, cols], s_g_all + tile, r_g_all + tile, core)

    def join(tile, carry):
        t, cols = tile_at(tile)
        part_copy(SZG, RZG, tile, s_g_z, r_g_z, zdev).wait_recv()
        G2[t, c, :, cols] = (SZG[t, :, cols].astype(F32) + RZG[t, :, cols].astype(F32)).astype(BF)
        g2_copy(tile).start()
        return carry

    lax.fori_loop(0, n_tiles, join, 0)

    def norm_back(grads, normals, inv_std, gain_index):
        scaled = [grads[h] * column(h, gain_index) for h in range(2)]
        plain = sum(jnp.sum(scaled[h], axis=0, keepdims=True) for h in range(2)) * inv_d
        cross = sum(jnp.sum(scaled[h] * normals[h], axis=0, keepdims=True) for h in range(2)) * inv_d
        return [inv_std * (scaled[h] - plain - normals[h] * cross) for h in range(2)]

    def second_back(tile, carry):
        t, cols = tile_at(tile)
        g2_other(tile).wait_recv()
        center, inv_std = ST2[t, 0:1, cols], ST2[t, 1:2, cols]
        grads = [G2[t, h, :, cols].astype(F32) for h in range(2)]
        normals = [(HID[t, h, :, cols] - center) * inv_std for h in range(2)]
        back = norm_back(grads, normals, inv_std, VEC_LN2_GAIN)
        for h in range(2):
            grad_hidden = CG[t, h, :, cols].astype(F32) + back[h]
            XG[t, h, :, cols] = grad_hidden.astype(BF)

            @pl.when((t == zz) & (c == h))
            def _():
                GH[:, cols] = grad_hidden
                VGC[:, 2:3] = VGC[:, 2:3] + jnp.sum(grads[h] * normals[h], axis=1, keepdims=True)
                VGC[:, 3:4] = VGC[:, 3:4] + jnp.sum(grads[h], axis=1, keepdims=True)

        return carry

    sent(e_xf)
    lax.fori_loop(0, n_tiles, second_back, 0)
    GB = XG
    VGC[:, 4:5] = jnp.sum(GB[zz, c].astype(F32), axis=1, keepdims=True)
    VGC[:, 5:6] = jnp.sum(CG[zz, c].astype(F32), axis=1, keepdims=True)

    window = pl.ds(pl.multiple_of(j * (4 * Q), Q), 5 * Q)
    for t in range(2):
        DATT[:, t * T : (t + 1) * T] = (
            dot_nn(OWB[0, window, :], GB[t, 0]) + dot_nn(OWB[1, window, :], GB[t, 1])
        ).astype(BF)
    r_rq = recvs.take(4)
    rq_entries = []
    for h in range(2):
        total = dot_nt(ATT[block(j), 0:T], GB[0, h]) + dot_nt(ATT[block(j), T:S], GB[1, h])
        DQ[3, h, 0:R, 0:H] = total.astype(BF)
    rq_entries.append(push(DQ.at[3], rq_hbm.at[dp], r_rq + dp, (3, z, c), dp != 3))
    l_x2 = local(x_in, XG.at[zz, c])

    def attend_back(slot, carry):
        rows = slot_rows(slot)
        here = pl.ds(pl.multiple_of(slot * Q, Q), Q)
        queries = QKV[0, rows, :]
        keys_t = QKV[1, rows, :]
        keys = keys_t.T
        values = QKV[2, rows, :].T
        grads_out = DATT[here, :]
        for tile in reversed(range(n_tiles)):
            count = W * (tile + 1)
            first = W * tile * (tile + 1) // 2
            cols = slice(tile * W, (tile + 1) * W)
            scores = dot_nn(keys[:count], queries[:, cols]) + MASK[first : first + count, :]
            probs = jnp.exp(scores - LSE[slot, 0:1, cols])
            grad_probs = dot_nn(values[:count], grads_out[:, cols])
            delta = jnp.sum(probs * grad_probs, axis=0, keepdims=True)
            grad_scores = (probs * (grad_probs - delta)).astype(BF)
            probs_low = probs.astype(BF)
            part_v = dot_nt(grads_out[:, cols], probs_low)
            part_k = dot_nt(queries[:, cols], grad_scores)
            if tile == n_tiles - 1:
                ACCV[...] = part_v
                ACCK[...] = part_k
            else:
                ACCV[:, 0:count] = ACCV[:, 0:count] + part_v
                ACCK[:, 0:count] = ACCK[:, 0:count] + part_k
            GQKV[0, rows, cols] = (dot_nn(keys_t[:, :count], grad_scores) * score_scale).astype(BF)
        GQKV[1, rows, :] = ACCK[...].astype(BF)
        GQKV[2, rows, :] = ACCV[...].astype(BF)
        return carry

    lax.fori_loop(first_slot, 5, attend_back, 0)

    for m in range(3):
        for h in range(2):
            total = dot_nt(GQKV[m, :, 0:T], N1[0, h]) + dot_nt(GQKV[m, :, T:S], N1[1, h])
            DQ[m, h] = total.astype(BF)
        rq_entries.append(push(DQ.at[m], rq_hbm.at[dp], r_rq + dp, (m, z, c), dp != m))

    def wait_sends(tile, carry):
        part_copy(PGS, RCG, tile, s_g_core, r_g_core, core).wait_send()
        part_copy(OPS, RCO, tile, s_p_core, r_p_core, core).wait_send()
        part_copy(SZG, RZG, tile, s_g_z, r_g_z, zdev).wait_send()
        g2_copy(tile).wait_send()
        return carry

    lax.fori_loop(0, n_tiles, wait_sends, 0)
    r_n_core, r_n_z = recvs.take(n_tiles), recvs.take()
    s_n_core = sends.take(n_tiles)

    def back_rows(half, tile):
        all_cols = pl.ds(pl.multiple_of(tile * W, W), W)
        total = dot_tn(WB[0, half, :, 0:H], GQKV[0, :, all_cols])
        for m in range(1, 3):
            total = total + dot_tn(WB[m, half, :, 0:H], GQKV[m, :, all_cols])
        return total

    def first_part(tile, carry):
        t, cols = tile_at(tile)
        PGS[t, :, cols] = back_rows(oc, tile).astype(BF)
        part_copy(PGS, RCG, tile, s_n_core, r_n_core, core).start()
        OPS[t, :, cols] = back_rows(c, tile).astype(BF)
        return carry

    lax.fori_loop(0, n_tiles, first_part, 0)

    def wait_first(tile, carry):
        part_copy(PGS, RCG, tile, s_n_core, r_n_core, core).wait_recv()
        return carry

    lax.fori_loop(0, n_tiles, wait_first, 0)
    SZG[0] = (OPS[1 - zz].astype(F32) + RCG[1 - zz].astype(F32)).astype(BF)
    push(SZG.at[0], RZN, r_n_z, zdev)

    for entry in rf_entries:
        sent(entry)
    loads = []
    for number in range(4):
        other = dp != number
        arrived(rf_hbm.at[number], r_rf + number, other)
        loads.append(
            local(rf_hbm.at[number], FB.at[:, pl.ds(number * quarter, quarter)], other)
        )
    for entry in loads:
        done(entry)
    r_zf = recvs.take(2)
    first_rows = slice(0, quarter)
    for h in range(2):
        total = FB[h, 0:quarter, :].astype(F32)
        for number in range(1, 4):
            total = total + FB[h, number * quarter : (number + 1) * quarter, :].astype(F32)
        low = total.astype(BF)
        FB[h, 0:quarter, :] = low
        if h == 0:

            @pl.when(first_core)
            def _():
                ZF[0] = low

        push(FB.at[h, pl.ds(0, quarter)], ZF.at[1], r_zf + 1, (dp, z2, h), second_core)
        if h == 1:
            push(FB.at[h, pl.ds(0, quarter)], ZF.at[0], r_zf, (dp, z, 1), first_core)

    arrived(RZO, r_out_z)
    branch_out = OPO[zz].astype(F32) + RCO[zz].astype(F32) + RZO[...].astype(F32)
    OPO[0] = (HID[zz, c] + branch_out + VEC[c, :, VEC_PROJ_BIAS : VEC_PROJ_BIAS + 1]).astype(BF)
    l_out = local(OPO.at[0], out_o)

    done(l_x2)
    arrived(RZN, r_n_z)
    r_stat = recvs.take()
    grads = OPS[zz].astype(F32) + RCG[zz].astype(F32) + RZN[...].astype(F32)
    center, inv_std = ST1[zz, 0:1, :], ST1[zz, 1:2, :]
    normals = (XG[zz, c].astype(F32) - center) * inv_std
    scaled = grads * VEC[c, :, VEC_LN1_GAIN : VEC_LN1_GAIN + 1]
    STX[c, 0:1, :] = jnp.sum(scaled, axis=0, keepdims=True)
    STX[c, 1:2, :] = jnp.sum(scaled * normals, axis=0, keepdims=True)
    push(STX.at[c], STX.at[c], r_stat, core)
    VGC[:, 0:1] = jnp.sum(grads * normals, axis=1, keepdims=True)
    VGC[:, 1:2] = jnp.sum(grads, axis=1, keepdims=True)
    arrived(STX.at[oc], r_stat)
    sums = (STX[0] + STX[1]) * inv_d
    OPO[1] = (GH[...] + inv_std * (scaled - sums[0:1] - normals * sums[1:2])).astype(BF)
    l_ing = local(OPO.at[1], ing_o)

    r_sp, r_spz = recvs.take(4), recvs.take(8)
    turned = VGC[...].T
    SPR[dp, 0:6, 0:H] = turned[0:6, :]
    for peer in peers:
        push(SPR.at[dp], SPR.at[dp], r_sp + dp, (peer, z, c))

    for entry in rq_entries:
        sent(entry)
    loads = []
    for number in range(4):
        other = dp != number
        arrived(rq_hbm.at[number], r_rq + number, other)
        loads.append(local(rq_hbm.at[number], DQ.at[number], other))
    for entry in loads:
        done(entry)
    r_zq, r_zt = recvs.take(2), recvs.take(2)
    with_tail = (j < 3) & (dp < 3)
    next_block = jnp.minimum(j + 1, 3)
    for h in range(2):
        total = DQ[0, h].astype(F32)
        for number in range(1, 4):
            total = total + DQ[number, h].astype(F32)
        low = total.astype(BF)
        DQ[0, h] = low
        if h == 0:

            @pl.when(first_core)
            def _():
                ZQ[0] = low[0:R]

        push(DQ.at[0, h, pl.ds(0, R)], ZQ.at[1], r_zq + 1, (dp, z2, h), second_core)
        if h == 1:
            push(DQ.at[0, h, pl.ds(0, R)], ZQ.at[0], r_zq, (dp, z, 1), first_core)
        push(DQ.at[0, h, pl.ds(R, TAIL)], ZT.at[c], r_zt + c, (dp, next_block, h), with_tail)

    r_gf, r_gq = recvs.take(4), recvs.take(4)
    arrived(ZF.at[0], r_zf, second_core)
    arrived(ZF.at[1], r_zf + 1)
    ZF[0] = (ZF[0].astype(F32) + ZF[1].astype(F32)).astype(BF)
    l_gf = local(ZF.at[0], gf_o.at[my_quarter])
    for peer in peers:
        push(ZF.at[0], gf_o.at[my_quarter], r_gf + dp, (peer, z, c))

    for number in range(4):
        arrived(SPR.at[number], r_sp + number, dp != number)
    SPZ[z, c] = SPR[0] + SPR[1] + SPR[2] + SPR[3]
    for step in range(4):
        for side in range(2):
            if step == 0 and side == 0:
                continue
            target = (dp, lax.rem(z + step, 4), c if side == 0 else oc)
            push(SPZ.at[z, c], SPZ.at[z, c], r_spz + (2 * z + c), target)

    arrived(ZQ.at[0], r_zq, second_core)
    arrived(ZQ.at[1], r_zq + 1)
    gets_tail = (z >= 1) & (dp < 3)
    for side in range(2):
        arrived(ZT.at[side], r_zt + side, gets_tail)
    total = ZQ[0].astype(F32) + ZQ[1].astype(F32)
    ZQ[0] = total.astype(BF)

    @pl.when(gets_tail)
    def _():
        ZQ[0, 0:TAIL] = (total[0:TAIL] + ZT[0].astype(F32) + ZT[1].astype(F32)).astype(BF)

    l_gq = local(ZQ.at[0], gq_o.at[dp])
    for peer in peers:
        push(ZQ.at[0], gq_o.at[dp], r_gq + dp, (peer, z, c))

    for step in range(4):
        for side in range(2):
            if step == 0 and side == 0:
                continue
            zv, cv = lax.rem(z + step, 4), c if side == 0 else oc
            arrived(SPZ.at[zv, cv], r_spz + (2 * zv + cv))
    vectors = SPZ[0, c] + SPZ[1, c] + SPZ[2, c] + SPZ[3, c]
    VOUT[...] = vectors
    VOUT[6:7, :] = SPZ[z, 0, 6:7, :] + SPZ[z2, 1, 6:7, :]
    l_vec_o = local(VOUT, vec_o)

    for number in range(4):
        arrived(gf_o.at[pl.ds(number * quarter, quarter)], r_gf + number, dp != number)
        arrived(gq_o.at[number], r_gq + number, dp != number)
    for entry in (l_out, l_ing, l_gf, l_gq, l_vec_o):
        done(entry)

    def own_sends(slot):
        att_copy(j, slot, s_a_z, r_a_z, zdev).wait_send()
        att_copy(j, slot, s_a_core, r_a_core, core).wait_send()

    slots_of(j, own_sends)
    slots_of(
        owner_of(zp, c),
        lambda slot: att_copy(owner_of(zp, c), slot, s_a_fwd, r_a_fwd, core).wait_send(),
    )

    def last_sends(tile, carry):
        part_copy(PGS, RCG, tile, s_n_core, r_n_core, core).wait_send()
        return carry

    lax.fori_loop(0, n_tiles, last_sends, 0)
    for entry in list(pending):
        sent(entry)
    assert sends.used <= SEND_COUNT and recvs.used <= RECV_COUNT and locs.used <= LOCAL_COUNT


def fast_body(
    tokens,
    ln1_gain,
    ln1_bias,
    qkv_weight,
    qv_bias,
    out_weight,
    out_bias,
    ln2_gain,
    ln2_bias,
    fc_weight,
    fc_bias,
    proj_weight,
    proj_bias,
    doc_lengths,
    cotangent,
):
    H, T = tokens.shape
    R = out_weight.shape[0]
    FW = fc_weight.shape[1]
    D, S = 2 * H, 2 * T
    HP = (H // LANES + 1) * LANES
    EXT = 5 * HEAD_DIM
    NT = S // KEY_TILE
    doc_count = doc_lengths.shape[1]
    first_core = lax.axis_index("col") == 0
    low_bias = jnp.where(first_core, qv_bias, jnp.zeros_like(qv_bias))
    bias_three = jnp.stack([low_bias[0], jnp.zeros_like(low_bias[0]), low_bias[1]])
    w3 = jnp.concatenate(
        [
            jnp.transpose(qkv_weight, (1, 2, 0)),
            bias_three[:, :, None],
            jnp.zeros((3, R, HP - H - 1), BF),
        ],
        axis=2,
    )
    ff = jnp.concatenate([fc_weight, proj_weight], axis=0)
    fcb = jnp.pad(fc_bias[None], ((0, 15), (0, 0)))
    vec = jnp.stack(
        [ln1_gain, ln1_bias, ln2_gain, ln2_bias, out_bias.astype(F32), proj_bias.astype(F32)], axis=1
    )
    vec = jnp.pad(vec, ((0, 0), (0, LANES - 6)))
    doc = jnp.pad(doc_lengths.astype(F32), ((0, 7), (0, LANES - doc_count)))
    shape = jax.ShapeDtypeStruct
    anywhere = pl.BlockSpec(memory_space=pl.ANY)
    outs = [
        shape((H, T), BF),
        shape((H, T), BF),
        shape((2 * H, FW), BF),
        shape((4, R, HP), BF),
        shape((8, FW), F32),
        shape((4, 2, 2 * H // 4, FW), BF),
        shape((4, 2, EXT, HP), BF),
    ]
    vmem = pltpu.VMEM
    mask_rows = KEY_TILE * NT * (NT + 1) // 2
    scratch = [
        vmem((2, 2, H, T), BF),
        vmem((2, 2, H, T), BF),
        vmem((2, 2, HP, T), BF),
        vmem((3, 2, EXT, HP), BF),
        vmem((2, D, H), BF),
        vmem((2, 2 * H, FW), BF),
        vmem((16, FW), BF),
        vmem((FW, LANES), F32),
        vmem((2, H, LANES), F32),
        vmem((2, 8, LANES), F32),
        vmem((mask_rows, KEY_TILE), F32),
        vmem((3, EXT, S), BF),
        vmem((5, 8, S), F32),
        vmem((D, S), BF),
        vmem((2, 2, H, T), F32),
        vmem((2, 8, T), F32),
        vmem((2, 8, T), F32),
        vmem((2, 2, H, T), BF),
        vmem((FW, S), BF),
        vmem((FW, S), BF),
        vmem((2, H, T), BF),
        vmem((2, H, T), BF),
        vmem((2, H, T), BF),
        vmem((2, H, T), BF),
        vmem((2, H, T), BF),
        vmem((2, H, T), BF),
        vmem((2, H, T), BF),
        vmem((2, 2, H, T), BF),
        vmem((H, T), BF),
        vmem((H, T), BF),
        vmem((H, T), BF),
        vmem((EXT, S), BF),
        vmem((3, EXT, S), BF),
        vmem((HEAD_DIM, S), F32),
        vmem((HEAD_DIM, S), F32),
        vmem((2, 2 * H // 4, FW), BF),
        vmem((4, 2, EXT, HP), BF),
        vmem((2, R, HP), BF),
        vmem((2, EXT - R, HP), BF),
        vmem((H, T), F32),
        vmem((H, LANES), F32),
        vmem((2, 8, T), F32),
        vmem((4, 8, FW), F32),
        vmem((4, 2, 8, FW), F32),
        vmem((8, FW), F32),
        pltpu.SemaphoreType.DMA((SEND_COUNT,)),
        pltpu.SemaphoreType.DMA((RECV_COUNT,)),
        pltpu.SemaphoreType.DMA((LOCAL_COUNT,)),
    ]
    out_rows, in_rows, gf, gq, vectors, unused_rf, unused_rq = pl.pallas_call(
        partial(layer_kernel, doc_count=doc_count),
        out_shape=outs,
        in_specs=[anywhere] * 8,
        out_specs=[anywhere] * len(outs),
        scratch_shapes=scratch,
        compiler_params=pltpu.CompilerParams(
            collective_id=0, has_side_effects=True, vmem_limit_bytes=VMEM_LIMIT
        ),
    )(tokens, cotangent, w3, out_weight, ff, fcb, vec, doc)
    qkv_grad = jnp.transpose(gq[0:3, :, 0:H].astype(F32), (2, 0, 1))
    bias_grad = jnp.stack([gq[0, :, H], gq[2, :, H]]).astype(F32)
    return (
        out_rows,
        in_rows,
        vectors[0, :H],
        vectors[1, :H],
        qkv_grad,
        bias_grad,
        gq[3, :, 0:H].astype(F32),
        vectors[4, :H],
        vectors[2, :H],
        vectors[3, :H],
        gf[0:H].astype(F32),
        vectors[6],
        gf[H:].astype(F32),
        vectors[5, :H],
    )


def choose_body(*arrays):
    sizes = {axis: lax.axis_size(axis) for axis in ("dp", "row", "col")}
    H, R = arrays[0].shape[0], arrays[5].shape[0]
    fits = sizes == {"dp": 4, "row": 4, "col": 2} and 4 * R == 2 * H == 17 * HEAD_DIM
    return (fast_body if fits else body)(*arrays)


def solution(mesh):
    return jax.shard_map(
        choose_body,
        mesh=mesh,
        in_specs=(
            P("col", ("dp", "row")),
            P("col"),
            P("col"),
            P("col", None, "row"),
            P(None, "row"),
            P("row", "col"),
            P("col"),
            P("col"),
            P("col"),
            P("col", "row"),
            P("row"),
            P("col", "row"),
            P("col"),
            P(("dp", "col"), None),
            P("col", ("dp", "row")),
        ),
        out_specs=(
            P("col", ("dp", "row")),
            P("col", ("dp", "row")),
            P("col"),
            P("col"),
            P("col", None, "row"),
            P(None, "row"),
            P("row", "col"),
            P("col"),
            P("col"),
            P("col"),
            P("col", "row"),
            P("row"),
            P("col", "row"),
            P("col"),
        ),
        check_vma=False,
    )
```

```python
from functools import partial
import math

import jax
import jax.numpy as jnp
from jax import lax
from jax.experimental import pallas as pl
from jax.experimental.pallas import tpu as pltpu
from jax.sharding import PartitionSpec as P

HEAD_DIM = 64


epsilon = 1e-05
score_scale = 0.125
masked_fill = -1e30
block_limit = 512


def feature_sums(first_sum, second_sum):
    return lax.psum((first_sum, second_sum), "col")


def norm_forward(values, gain_vec, shift_vec):
    feature_count = values.shape[1] * lax.axis_size("col")
    total_sum, square_sum = feature_sums(jnp.sum(values, axis=1), jnp.sum(values * values, axis=1))
    center = total_sum / feature_count
    spread = square_sum / feature_count - center * center
    inv_std = lax.rsqrt(spread + epsilon)
    normal = (values - center[:, None]) * inv_std[:, None]
    return (normal, inv_std, normal * gain_vec + shift_vec)


def norm_backward(upstream, normal, inv_std, gain_vec):
    feature_count = upstream.shape[1] * lax.axis_size("col")
    scaled = upstream * gain_vec
    plain_sum, cross_sum = feature_sums(jnp.sum(scaled, axis=1), jnp.sum(scaled * normal, axis=1))
    return inv_std[:, None] * (
        scaled - plain_sum[:, None] / feature_count - normal * (cross_sum[:, None] / feature_count)
    )


def gather_rows(values):
    return lax.all_gather(values, "row", axis=0, tiled=True)


def gather_cols(values):
    return lax.all_gather(values, "col", axis=0, tiled=True)


def sum_over_rows(row_term, row_total):
    return lax.psum_scatter(
        row_term(jnp.int32(0), row_total * lax.axis_size("row")),
        "row",
        scatter_dimension=0,
        tiled=True,
    )


def sum_over_cols(row_term, row_total):
    return lax.psum_scatter(
        row_term(jnp.int32(0), row_total * lax.axis_size("col")),
        "col",
        scatter_dimension=0,
        tiled=True,
    )


def to_heads(values):
    return lax.all_to_all(values, "row", split_axis=0, concat_axis=2, tiled=True)


def to_tokens(values):
    return lax.all_to_all(values, "row", split_axis=2, concat_axis=0, tiled=True)


def product_term(full_rows, matrix):

    def row_term(first_row, row_count):
        return jnp.dot(full_rows, matrix, preferred_element_type=jnp.float32)

    return row_term


def product_term_back(full_rows, matrix):

    def row_term(first_row, row_count):
        return lax.dot_general(
            full_rows, matrix, (((1,), (1,)), ((), ())), preferred_element_type=jnp.float32
        )

    return row_term


def slice_term(full_rows):

    def row_term(first_row, row_count):
        return full_rows

    return row_term


def inner_rows(left_side, right_side):
    return lax.dot_general(
        left_side, right_side, (((0,), (0,)), ((), ())), preferred_element_type=jnp.float32
    )


def segments_of(lengths, places):
    doc_ends = jnp.cumsum(lengths)
    segment = jnp.sum(
        (doc_ends[None, :] <= places[:, None]).astype(jnp.int32), axis=1, dtype=jnp.int32
    )
    return (segment, places >= doc_ends[-1])


def allowed_pairs(query_place, query_segment, query_padding, key_place, key_segment):
    causal = key_place[None, :] <= query_place[:, None]
    same_doc = key_segment[None, :] == query_segment[:, None]
    itself = key_place[None, :] == query_place[:, None]
    return causal & same_doc & (jnp.logical_not(query_padding)[:, None] | itself)


def attention_parts(queries, keyvals, lengths, query_place):
    seq_total = keyvals.shape[0]
    key_block_size = math.gcd(seq_total, block_limit)
    block_count = seq_total // key_block_size
    key_place = jnp.arange(seq_total, dtype=jnp.int32)
    key_segment = segments_of(lengths, key_place)[0]
    query_segment, query_padding = segments_of(lengths, query_place)
    blocked = (
        keyvals.reshape((block_count, key_block_size) + keyvals.shape[1:]),
        key_place.reshape(block_count, key_block_size),
        key_segment.reshape(block_count, key_block_size),
    )

    def block_scores(key_rows, place_rows, segment_rows):
        raw_scores = (
            jnp.einsum("qhd,khd->hqk", queries, key_rows, preferred_element_type=jnp.float32)
            * score_scale
        )
        allowed = allowed_pairs(
            query_place, query_segment, query_padding, place_rows, segment_rows
        )[None]
        return (raw_scores, allowed)

    return (blocked, block_scores)


def attention_forward(queries, blocked, block_scores):
    query_count, head_count, head_width = queries.shape

    def max_step(running, inputs):
        best_score, mass_sum = running
        kv_block, place_rows, segment_rows = inputs
        raw_scores, allowed = block_scores(kv_block[:, 0], place_rows, segment_rows)
        masked = jnp.where(allowed, raw_scores, masked_fill)
        new_best = jnp.maximum(best_score, jnp.max(masked, axis=2))
        fresh = jnp.sum(jnp.where(allowed, jnp.exp(masked - new_best[:, :, None]), 0.0), axis=2)
        return ((new_best, mass_sum * jnp.exp(best_score - new_best) + fresh), None)

    start_best = jnp.full((head_count, query_count), masked_fill, jnp.float32)
    start_mass = jnp.zeros((head_count, query_count), jnp.float32)
    (best_score, mass_sum), unused = lax.scan(max_step, (start_best, start_mass), blocked)
    log_sum = best_score + jnp.log(mass_sum)

    def out_step(running, inputs):
        kv_block, place_rows, segment_rows = inputs
        raw_scores, allowed = block_scores(kv_block[:, 0], place_rows, segment_rows)
        probs_low = jnp.where(allowed, jnp.exp(raw_scores - log_sum[:, :, None]), 0.0).astype(
            jnp.bfloat16
        )
        return (
            running
            + jnp.einsum(
                "hqk,khd->qhd", probs_low, kv_block[:, 1], preferred_element_type=jnp.float32
            ),
            None,
        )

    attended, unused = lax.scan(
        out_step, jnp.zeros((query_count, head_count, head_width), jnp.float32), blocked
    )
    return (attended, log_sum)


def attention_backward(queries, blocked, block_scores, log_sum, grad_attended):
    query_count, head_count, head_width = queries.shape

    def probs_and_grads(inputs):
        kv_block, place_rows, segment_rows = inputs
        raw_scores, allowed = block_scores(kv_block[:, 0], place_rows, segment_rows)
        probs_f = jnp.where(allowed, jnp.exp(raw_scores - log_sum[:, :, None]), 0.0)
        grad_probs = jnp.einsum(
            "qhd,khd->hqk", grad_attended, kv_block[:, 1], preferred_element_type=jnp.float32
        )
        return (probs_f, grad_probs)

    def delta_step(running, inputs):
        probs_f, grad_probs = probs_and_grads(inputs)
        return (running + jnp.sum(probs_f * grad_probs, axis=2), None)

    delta_sum, unused = lax.scan(
        delta_step, jnp.zeros((head_count, query_count), jnp.float32), blocked
    )

    def grad_step(running, inputs):
        kv_block = inputs[0]
        probs_f, grad_probs = probs_and_grads(inputs)
        grad_scores = (probs_f * (grad_probs - delta_sum[:, :, None])).astype(jnp.bfloat16)
        running = running + jnp.einsum(
            "hqk,khd->qhd", grad_scores, kv_block[:, 0], preferred_element_type=jnp.float32
        )
        grad_keys = (
            jnp.einsum("hqk,qhd->khd", grad_scores, queries, preferred_element_type=jnp.float32)
            * score_scale
        )
        grad_values = jnp.einsum(
            "hqk,qhd->khd",
            probs_f.astype(jnp.bfloat16),
            grad_attended,
            preferred_element_type=jnp.float32,
        )
        return (running, jnp.stack([grad_keys, grad_values], axis=1))

    grad_queries, grad_keyvals = lax.scan(
        grad_step, jnp.zeros((query_count, head_count, head_width), jnp.float32), blocked
    )
    seq_total = grad_keyvals.shape[0] * grad_keyvals.shape[1]
    return (grad_queries * score_scale, grad_keyvals.reshape(seq_total, 2, head_count, head_width))


def body(
    tokens,
    ln1_gain,
    ln1_bias,
    qkv_weight,
    qv_bias,
    out_weight,
    out_bias,
    ln2_gain,
    ln2_bias,
    fc_weight,
    fc_bias,
    proj_weight,
    proj_bias,
    doc_lengths,
    cotangent,
):
    count_rows = lax.axis_size("row")
    count_cols = lax.axis_size("col")
    grid_rows = tokens.shape[1]
    col_width = tokens.shape[0]
    row_width = out_weight.shape[0]
    seq_rows = grid_rows * count_rows // count_cols
    query_rows = seq_rows // count_rows
    full_width = col_width * count_cols
    head_count = full_width // HEAD_DIM
    tokens_f = tokens.astype(jnp.float32).T
    normal1, inv_std1, shaped1 = norm_forward(tokens_f, ln1_gain, ln1_bias)
    qkv_flat = qkv_weight.reshape(col_width, 3 * row_width)
    gathered1 = gather_rows(shaped1.astype(jnp.bfloat16))
    mixed_qkv = sum_over_cols(product_term(gathered1, qkv_flat), seq_rows).reshape(
        seq_rows, 3, row_width
    )
    bias_three = jnp.stack([qv_bias[0], jnp.zeros_like(qv_bias[0]), qv_bias[1]])
    qkv_low = (mixed_qkv + bias_three).astype(jnp.bfloat16)
    local_qkv = to_heads(qkv_low).reshape(query_rows, 3, head_count, HEAD_DIM)
    queries = local_qkv[:, 0]
    keyvals = lax.all_gather(local_qkv[:, 1:], "row", axis=0, tiled=True)
    query_place = lax.axis_index("row") * query_rows + jnp.arange(query_rows, dtype=jnp.int32)
    blocked, block_scores = attention_parts(queries, keyvals, doc_lengths[0], query_place)
    attended_f, log_sum = attention_forward(queries, blocked, block_scores)
    attended_low = attended_f.reshape(query_rows, 1, full_width).astype(jnp.bfloat16)
    attended_grid = to_tokens(attended_low).reshape(seq_rows, row_width)
    gathered_att = gather_cols(attended_grid)
    branch = sum_over_rows(product_term(gathered_att, out_weight), grid_rows)
    hidden = tokens_f + (branch + out_bias)
    normal2, inv_std2, shaped2 = norm_forward(hidden, ln2_gain, ln2_bias)
    normed2 = shaped2.astype(jnp.bfloat16)
    gathered2 = gather_rows(normed2)
    pre_act = sum_over_cols(product_term(gathered2, fc_weight), seq_rows) + fc_bias
    active = jax.nn.gelu(pre_act, approximate=False).astype(jnp.bfloat16)
    gathered_act = gather_cols(active)
    projected = sum_over_rows(product_term_back(gathered_act, proj_weight), grid_rows)
    output = (hidden + projected + proj_bias).astype(jnp.bfloat16).T
    cotangent_rows = cotangent.T
    grad_out = cotangent_rows.astype(jnp.float32)
    unused, gelu_back = jax.vjp(partial(jax.nn.gelu, approximate=False), pre_act)
    grad_gathered = gather_rows(cotangent_rows)
    proj_weight_grad = inner_rows(grad_gathered, gathered_act)
    proj_bias_grad = jnp.sum(grad_gathered, axis=0, dtype=jnp.float32)
    grad_active = sum_over_cols(product_term(grad_gathered, proj_weight), seq_rows)
    grad_pre = gelu_back(grad_active)[0].astype(jnp.bfloat16)
    grad_pre_all = gather_cols(grad_pre)
    fc_weight_grad = inner_rows(gathered2, grad_pre_all)
    fc_bias_grad = jnp.sum(grad_pre_all, axis=0, dtype=jnp.float32)
    grad_normed2 = sum_over_rows(product_term_back(grad_pre_all, fc_weight), grid_rows)
    ln2_gain_part = jnp.sum(grad_normed2 * normal2, axis=0)
    ln2_bias_part = jnp.sum(grad_normed2, axis=0)
    grad_hidden = grad_out + norm_backward(grad_normed2, normal2, inv_std2, ln2_gain)
    branch_gathered = gather_rows(grad_hidden.astype(jnp.bfloat16))
    out_weight_grad = inner_rows(gathered_att, branch_gathered)
    out_bias_grad = jnp.sum(branch_gathered, axis=0, dtype=jnp.float32)
    grad_att_grid = sum_over_cols(product_term_back(branch_gathered, out_weight), seq_rows).astype(
        jnp.bfloat16
    )
    grad_attended = to_heads(grad_att_grid.reshape(seq_rows, 1, row_width)).reshape(
        query_rows, head_count, HEAD_DIM
    )
    grad_queries, grad_keyvals = attention_backward(
        queries, blocked, block_scores, log_sum, grad_attended
    )
    keyval_rows = sum_over_rows(slice_term(grad_keyvals), query_rows)
    grad_qkv_local = (
        jnp.concatenate([grad_queries[:, None], keyval_rows], axis=1)
        .astype(jnp.bfloat16)
        .reshape(query_rows, 3, full_width)
    )
    grad_qkv_grid = to_tokens(grad_qkv_local).reshape(seq_rows, 3 * row_width)
    qkv_gathered = gather_cols(grad_qkv_grid)
    qkv_weight_grad = inner_rows(gathered1, qkv_gathered).reshape(col_width, 3, row_width)
    qkv_bias_sums = jnp.sum(qkv_gathered, axis=0, dtype=jnp.float32).reshape(3, row_width)
    qv_bias_grad = jnp.stack([qkv_bias_sums[0], qkv_bias_sums[2]])
    grad_normed1 = sum_over_rows(product_term_back(qkv_gathered, qkv_flat), grid_rows)
    ln1_gain_part = jnp.sum(grad_normed1 * normal1, axis=0)
    ln1_bias_part = jnp.sum(grad_normed1, axis=0)
    input_grad = (
        (grad_hidden + norm_backward(grad_normed1, normal1, inv_std1, ln1_gain))
        .astype(jnp.bfloat16)
        .T
    )
    summed = lax.psum(
        (
            qkv_weight_grad,
            qv_bias_grad,
            out_weight_grad,
            out_bias_grad,
            fc_weight_grad,
            fc_bias_grad,
            proj_weight_grad,
            proj_bias_grad,
        ),
        "dp",
    )
    gain_sums = lax.psum(
        (ln1_gain_part, ln1_bias_part, ln2_gain_part, ln2_bias_part), ("dp", "row")
    )
    return (
        output,
        input_grad,
        gain_sums[0],
        gain_sums[1],
        summed[0],
        summed[1],
        summed[2],
        summed[3],
        gain_sums[2],
        gain_sums[3],
        summed[4],
        summed[5],
        summed[6],
        summed[7],
    )


BF = jnp.bfloat16
F32 = jnp.float32
MESH = pl.DeviceIdType.MESH
LANES = 128
KEY_TILE = 256
VEC_LN1_GAIN, VEC_LN1_BIAS, VEC_LN2_GAIN, VEC_LN2_BIAS, VEC_OUT_BIAS, VEC_PROJ_BIAS = range(6)


def dot_nn(left, right):
    return lax.dot_general(left, right, (((1,), (0,)), ((), ())), preferred_element_type=F32)


def dot_tn(left, right):
    return lax.dot_general(left, right, (((0,), (0,)), ((), ())), preferred_element_type=F32)


def dot_nt(left, right):
    return lax.dot_general(left, right, (((1,), (1,)), ((), ())), preferred_element_type=F32)


VMEM_LIMIT = 66_000_000


class Slots:
    def __init__(self):
        self.used = 0

    def take(self, count=1):
        first = self.used
        self.used += count
        return first


SEND_COUNT, RECV_COUNT, LOCAL_COUNT = 144, 160, 48


def layer_kernel(
    x_in,
    cot_in,
    w3_in,
    ow_in,
    fc_in,
    proj_in,
    pack_in,
    out_o,
    ing_o,
    gf_o,
    gq_o,
    vec_o,
    rf1_hbm,
    rf2_hbm,
    rq1_hbm,
    rq2_hbm,
    XG,
    CG,
    N1,
    WB,
    OWB,
    FB,
    COLS,
    PACK,
    PACKF,
    MASK,
    QKV,
    LSE,
    ATT,
    HID,
    ST1,
    ST2,
    N2,
    ACT,
    GPRE,
    PGS,
    OPS,
    RCG,
    RCO,
    OPO,
    SZG,
    RZG,
    G2,
    SZO,
    RZO,
    RZN,
    DATT,
    GQKV,
    ACCK,
    ACCV,
    ZF,
    DQ,
    ZQ,
    ZT,
    GH,
    VGC,
    STX,
    SPR,
    SPZ,
    VOUT,
    SS,
    RS,
    LS,
    *,
    doc_count,
):
    H, T = x_in.shape
    R = w3_in.shape[1]
    HP = w3_in.shape[2]
    EXT = WB.shape[2]
    TAIL = EXT - R
    D = 2 * H
    S = 2 * T
    W = KEY_TILE
    Q = HEAD_DIM
    FW = fc_in.shape[1]
    per_tok = T // W
    n_tiles = S // W
    inv_d = 1.0 / D

    dp, z, c = lax.axis_index("dp"), lax.axis_index("row"), lax.axis_index("col")
    oc = 1 - c
    zz = lax.rem(z, 2)
    zp = z + 1 - 2 * zz
    z2 = lax.rem(z + 2, 4)
    j = lax.rem(z + 2 * c, 4)
    pair = z // 2
    core = (dp, z, oc)
    zdev = (dp, zp, c)
    xn = dp + 1 - 2 * lax.rem(dp, 2)
    yn = lax.rem(dp + 2, 4)
    dg = 3 - dp
    peers = (dg, xn, yn)
    xb, yb = lax.rem(dp, 2), dp // 2
    xdev, ydev = (xn, z, c), (yn, z, c)
    first_core, second_core = c == 0, c == 1

    sends, recvs, locs = Slots(), Slots(), Slots()
    pending = []

    def remote(src, dst, s_idx, r_idx, dev):
        return pltpu.make_async_remote_copy(
            src_ref=src,
            dst_ref=dst,
            send_sem=SS.at[s_idx],
            recv_sem=RS.at[r_idx],
            device_id=dev,
            device_id_type=MESH,
        )

    def when(cond, fn):
        if cond is None:
            fn()
        else:
            pl.when(cond)(fn)

    def push(src, dst, r_idx, dev, cond=None):
        copy = remote(src, dst, sends.take(), r_idx, dev)
        when(cond, copy.start)
        entry = [cond, copy]
        pending.append(entry)
        return entry

    def sent(entry):
        when(entry[0], entry[1].wait_send)
        pending[:] = [other for other in pending if other is not entry]

    def arrived(dst, r_idx, cond=None):
        when(cond, remote(dst, dst, 0, r_idx, core).wait_recv)

    def local(src, dst, cond=None):
        copy = pltpu.make_async_copy(src, dst, LS.at[locs.take()])
        when(cond, copy.start)
        return (cond, copy)

    def done(entry):
        when(entry[0], entry[1].wait)

    barrier = pltpu.get_barrier_semaphore()
    for step in range(4):
        for side in range(2):
            if step == 0 and side == 0:
                continue
            target = (dp, lax.rem(z + step, 4), c if side == 0 else oc)
            pl.semaphore_signal(barrier, inc=1, device_id=target, device_id_type=MESH)
    for peer in peers:
        pl.semaphore_signal(barrier, inc=1, device_id=(peer, z, c), device_id_type=MESH)
    pl.semaphore_wait(barrier, 10)

    r_x_core, r_x_z, r_x_fwd = recvs.take(), recvs.take(), recvs.take()
    r_w_core, r_w_z, r_w_xy, r_w_tail = recvs.take(), recvs.take(2), recvs.take(4), recvs.take(2)
    r_pack, r_packf = recvs.take(), recvs.take()
    r_f_core, r_f_z, r_f_xy = recvs.take(2), recvs.take(2), recvs.take(4)
    r_o_core, r_o_z, r_o_z0, r_o_xy, r_o_fwd = (
        recvs.take(),
        recvs.take(4),
        recvs.take(4),
        recvs.take(16),
        recvs.take(4),
    )

    def block(number):
        return pl.ds(pl.multiple_of(number * R, 16), R)

    quarter = D // 4
    odd = R - 4 * (R // 64) * 16
    piece = R // 64 * 16

    def quarter_rows(number):
        return pl.ds(pl.multiple_of(number * quarter, 16), quarter)

    def ow_piece(number, plane):
        return pl.ds(pl.multiple_of(number * R + odd + plane * piece, 16), piece)

    def ow_odd(number):
        return pl.ds(pl.multiple_of(number * R, 16), odd)

    my_quarter = quarter_rows(dp)
    w_row = jnp.minimum(dp, 2)
    has_before = z >= 1
    push(w3_in.at[w_row], WB.at[w_row, c, pl.ds(0, R)], r_w_z + c, (dp, z2, 1), dp < 3)
    push(x_in, XG.at[zz, c], r_x_z, zdev)
    push(x_in, XG.at[zz, c], r_x_core, core)
    push(pack_in, PACK.at[c], r_pack, core)
    push(w3_in, WB.at[:, 1, pl.ds(0, R)], r_w_core, (dp, z, 0), second_core)
    push(w3_in.at[:, pl.ds(0, TAIL)], WB.at[:, c, pl.ds(R, TAIL)], r_w_tail + c, (dp, jnp.maximum(z - 1, 0), 0), has_before)
    push(w3_in.at[:, pl.ds(0, TAIL)], WB.at[:, c, pl.ds(R, TAIL)], r_w_tail + c, (dp, lax.rem(z + 1, 4), 1), has_before)
    push(pack_in, PACKF, r_packf, (dp, z2, 1), first_core)
    l_x = local(x_in, XG.at[zz, c])
    l_pack = local(pack_in, PACK.at[c])
    l_w = local(w3_in, WB.at[:, 0, pl.ds(0, R)], first_core)
    push(
        fc_in.at[quarter_rows(jnp.minimum(dp, 1))], FB.at[c, my_quarter], r_f_z + c, (dp, z2, 1), dp < 2
    )
    push(
        proj_in.at[quarter_rows(jnp.maximum(dp - 2, 0))],
        FB.at[c, my_quarter],
        r_f_z + c,
        (dp, z2, 1),
        dp >= 2,
    )
    for step in (1, 3, 2):
        target = (dp, lax.rem(z + step, 4), c)
        push(ow_in.at[ow_piece(0, dp)], OWB.at[c, ow_piece(z, dp)], r_o_z + z, target)
        push(ow_in.at[ow_odd(0)], OWB.at[c, ow_odd(z)], r_o_z0 + z, target)
    push(fc_in, FB.at[1, pl.ds(0, H)], r_f_core, (dp, z, 0), second_core)
    push(proj_in, FB.at[1, pl.ds(H, H)], r_f_core + 1, (dp, z, 0), second_core)
    push(ow_in, OWB.at[c, block(z)], r_o_core, core)
    l_f = local(fc_in, FB.at[0, pl.ds(0, H)], first_core)
    l_p = local(proj_in, FB.at[0, pl.ds(H, H)], first_core)
    l_o = local(ow_in, OWB.at[c, block(z)])

    KD = N1.shape[2]
    pad_rows = KD - H
    ones_row = (lax.broadcasted_iota(jnp.int32, (pad_rows, T), 0) == 0).astype(BF)
    for t in range(2):
        for h in range(2):
            N1[t, h, H:, :] = ones_row
    VGC[...] = jnp.zeros_like(VGC)
    GQKV[...] = jnp.zeros_like(GQKV)

    def clear_tail():
        WB[:, :, R:, :] = jnp.zeros((3, 2, TAIL, HP), BF)

    pl.when(j == 3)(clear_tail)

    done(l_pack)
    arrived(PACK.at[oc], r_pack)
    lengths = PACK[pair, 7:8, 0:LANES]
    place_c = lax.broadcasted_iota(jnp.int32, (S, LANES), 0).astype(F32)
    place_r = lax.broadcasted_iota(jnp.int32, (8, S), 1).astype(F32)
    end = jnp.zeros((1, 1), F32)
    seg_c, seg_r = jnp.zeros_like(place_c), jnp.zeros_like(place_r)
    for number in range(doc_count):
        end = end + lengths[:, number : number + 1]
        seg_c = seg_c + jnp.where(end <= place_c, 1.0, 0.0)
        seg_r = seg_r + jnp.where(end <= place_r, 1.0, 0.0)
    seg_c = jnp.where(end <= place_c, place_c + 2.0 * S, seg_c)
    seg_r = jnp.where(end <= place_r, place_r + 2.0 * S, seg_r)
    for tile in range(n_tiles):
        rows = W * (tile + 1)
        first = W * tile * (tile + 1) // 2
        cols = slice(tile * W, (tile + 1) * W)
        key_seg = jnp.concatenate([seg_c[:rows]] * (W // LANES), axis=1)
        key_place = jnp.concatenate([place_c[:rows]] * (W // LANES), axis=1)
        ok = (key_seg == seg_r[0:1, cols]) & (key_place <= place_r[0:1, cols])
        MASK[first : first + rows, :] = jnp.where(ok, 0.0, masked_fill)

    for h in range(2):
        COLS[h * H : (h + 1) * H, 0:6] = PACK[h].T[0:H, 0:6]

    def column(h, which):
        if isinstance(h, int):
            return COLS[h * H : (h + 1) * H, which : which + 1]
        return COLS[pl.ds(pl.multiple_of(h * H, 16), H), which : which + 1]

    def stats_of(first_half, second_half):
        center = (
            jnp.sum(first_half, axis=0, keepdims=True) + jnp.sum(second_half, axis=0, keepdims=True)
        ) * inv_d
        square = (
            jnp.sum(first_half * first_half, axis=0, keepdims=True)
            + jnp.sum(second_half * second_half, axis=0, keepdims=True)
        ) * inv_d
        return center, lax.rsqrt(square - center * center + epsilon)

    def first_norm(t):
        halves = [XG[t, h].astype(F32) for h in range(2)]
        center, inv_std = stats_of(*halves)
        ST1[t, 0:1, :] = center
        ST1[t, 1:2, :] = inv_std
        for h in range(2):
            shaped = (halves[h] - center) * inv_std * column(h, VEC_LN1_GAIN) + column(
                h, VEC_LN1_BIAS
            )
            N1[t, h, 0:H, :] = shaped.astype(BF)

    done(l_x)
    arrived(XG.at[zz, oc], r_x_core)
    first_norm(zz)

    w_from_z = second_core & (dp < 3)
    for h in range(2):
        arrived(WB.at[w_row, h, pl.ds(0, R)], r_w_z + h, w_from_z)
    for peer in peers:
        push(
            WB.at[w_row, :, pl.ds(0, R)],
            WB.at[w_row, :, pl.ds(0, R)],
            r_w_xy + w_row,
            (peer, z, 1),
            w_from_z,
        )
    arrived(XG.at[1 - zz, c], r_x_z)
    e_xf = push(XG.at[1 - zz, c], XG.at[1 - zz, c], r_x_fwd, core)

    arrived(XG.at[1 - zz, oc], r_x_fwd)
    first_norm(1 - zz)

    done(l_w)
    arrived(WB.at[:, 1, pl.ds(0, R)], r_w_core, first_core)
    for m in range(3):
        arrived(WB.at[m, :, pl.ds(0, R)], r_w_xy + m, second_core & (dp != m))
    for h in range(2):
        arrived(WB.at[:, h, pl.ds(R, TAIL)], r_w_tail + h, j < 3)

    for t in range(2):
        for m in range(3):
            mixed = dot_nn(WB[m, 0, :, 0:KD], N1[t, 0]) + dot_nn(WB[m, 1, :, 0:KD], N1[t, 1])
            low = mixed.astype(BF)
            if m == 0:
                low = low * jnp.asarray(score_scale, BF)
            QKV[m, :, t * T : (t + 1) * T] = low

    for h in range(2):
        arrived(FB.at[h, my_quarter], r_f_z + h, second_core)
    ff_entries = []
    for peer in peers:
        ff_entries.append(
            push(FB.at[:, my_quarter], FB.at[:, my_quarter], r_f_xy + dp, (peer, z, 1), second_core)
        )
    for step in (1, 3, 2):
        there = lax.rem(z + step, 4)
        arrived(OWB.at[c, ow_piece(there, dp)], r_o_z + there)
        for peer in peers:
            rows = ow_piece(there, dp)
            push(OWB.at[c, rows], OWB.at[c, rows], r_o_xy + (4 * dp + there), (peer, z, c))
    r_c_core, r_c_z, r_c_fwd = recvs.take(), recvs.take(), recvs.take()
    push(cot_in, CG.at[zz, c], r_c_z, zdev)
    push(cot_in, CG.at[zz, c], r_c_core, core)
    l_c = local(cot_in, CG.at[zz, c])

    r_a_z, r_a_core, r_a_fwd = recvs.take(5), recvs.take(5), recvs.take(5)
    s_a_z, s_a_core, s_a_fwd = sends.take(5), sends.take(5), sends.take(5)
    first_slot = jnp.where(j == 0, 0, 1)

    def head_rows(owner, slot):
        return pl.ds(pl.multiple_of(owner * (4 * Q) + slot * Q, Q), Q)

    def slot_rows(slot):
        return pl.ds(pl.multiple_of(slot * Q - 16 * j, 16), Q)

    def att_copy(owner, slot, s_base, r_base, dev):
        rows = head_rows(owner, slot)
        return remote(ATT.at[rows], ATT.at[rows], s_base + slot, r_base + slot, dev)

    def attend(slot, carry):
        rows = slot_rows(slot)
        out_rows = head_rows(j, slot)
        queries = QKV[0, rows, :]
        keys = QKV[1, rows, :].T
        values = QKV[2, rows, :]
        for tile in range(n_tiles):
            count = W * (tile + 1)
            first = W * tile * (tile + 1) // 2
            cols = slice(tile * W, (tile + 1) * W)
            scores = dot_nn(keys[:count], queries[:, cols]) + MASK[first : first + count, :]
            best = jnp.max(scores, axis=0, keepdims=True)
            weights = jnp.exp(scores - best)
            mass = jnp.sum(weights, axis=0, keepdims=True)
            probs_low = (weights * (1.0 / mass)).astype(BF)
            ATT[out_rows, cols] = dot_nn(values[:, :count], probs_low).astype(BF)
            LSE[slot, 0:1, cols] = best + jnp.log(mass)
        att_copy(j, slot, s_a_z, r_a_z, zdev).start()
        att_copy(j, slot, s_a_core, r_a_core, core).start()

        return carry

    lax.fori_loop(first_slot, 5, attend, 0)

    arrived(CG.at[1 - zz, c], r_c_z)
    push(CG.at[1 - zz, c], CG.at[1 - zz, c], r_c_fwd, core)
    for step in (1, 3, 2):
        there = lax.rem(z + step, 4)
        arrived(OWB.at[c, ow_odd(there)], r_o_z0 + there)
        for plane in range(4):
            arrived(OWB.at[c, ow_piece(there, plane)], r_o_xy + (4 * plane + there), dp != plane)
        push(OWB.at[c, block(there)], OWB.at[c, block(there)], r_o_fwd + there, core)

    def owner_of(zv, cv):
        return lax.rem(zv + 2 * cv, 4)

    def slots_of(owner, body):
        lax.fori_loop(jnp.where(owner == 0, 0, 1), 5, lambda slot, carry: (body(slot), carry)[1], 0)

    def pass_on(slot):
        att_copy(owner_of(zp, c), slot, s_a_fwd, r_a_z, core).wait_recv()
        att_copy(owner_of(zp, c), slot, s_a_fwd, r_a_fwd, core).start()

    slots_of(owner_of(zp, c), pass_on)
    slots_of(owner_of(z, oc), lambda slot: att_copy(owner_of(z, oc), slot, s_a_core, r_a_core, core).wait_recv())
    slots_of(owner_of(zp, oc), lambda slot: att_copy(owner_of(zp, oc), slot, s_a_fwd, r_a_fwd, core).wait_recv())
    done(l_o)
    arrived(OWB.at[oc, block(z)], r_o_core)
    for step in range(1, 4):
        there = lax.rem(z + step, 4)
        arrived(OWB.at[oc, block(there)], r_o_fwd + there)

    def project(tile, carry):
        t = tile // per_tok
        cols = pl.ds(pl.multiple_of(lax.rem(tile, per_tok) * W, W), W)
        all_cols = pl.ds(pl.multiple_of(tile * W, W), W)
        att = ATT[:, all_cols]
        halves = []
        for h in range(2):
            branch = dot_tn(OWB[h], att)
            halves.append(XG[t, h, :, cols].astype(F32) + (branch + column(h, VEC_OUT_BIAS)))
            HID[t, h, :, cols] = halves[h]
        center, inv_std = stats_of(*halves)
        ST2[t, 0:1, cols] = center
        ST2[t, 1:2, cols] = inv_std
        for h in range(2):
            shaped = (halves[h] - center) * inv_std * column(h, VEC_LN2_GAIN) + column(
                h, VEC_LN2_BIAS
            )
            N2[t, h, :, cols] = shaped.astype(BF)
        return carry

    lax.fori_loop(0, n_tiles, project, 0)

    done(l_f)
    done(l_p)
    for number in range(2):
        arrived(FB.at[1, pl.ds(number * H, H)], r_f_core + number, first_core)
    for number in range(4):
        arrived(FB.at[:, quarter_rows(number)], r_f_xy + number, second_core & (dp != number))
    arrived(PACKF, r_packf, second_core)

    @pl.when(first_core)
    def _():
        COLS[:, 6:7] = PACK[0].T[0:FW, 6:7]

    @pl.when(second_core)
    def _():
        COLS[:, 6:7] = PACKF[...].T[0:FW, 6:7]

    done(l_c)
    arrived(CG.at[zz, oc], r_c_core)
    arrived(CG.at[1 - zz, oc], r_c_fwd)

    r_g_core, r_p_core, r_g_z = recvs.take(n_tiles), recvs.take(n_tiles), recvs.take(n_tiles)
    s_g_core, s_p_core, s_g_z = sends.take(n_tiles), sends.take(n_tiles), sends.take(n_tiles)

    def tile_at(tile):
        t = tile // per_tok
        return t, pl.ds(pl.multiple_of(lax.rem(tile, per_tok) * W, W), W)

    def part_copy(buf, dst, tile, s_base, r_base, dev):
        t, cols = tile_at(tile)
        return remote(buf.at[t, :, cols], dst.at[t, :, cols], s_base + tile, r_base + tile, dev)

    def feed(tile, carry):
        t, cols = tile_at(tile)
        all_cols = pl.ds(pl.multiple_of(tile * W, W), W)
        pre = (
            dot_tn(FB[0, 0:H], N2[t, 0, :, cols])
            + dot_tn(FB[1, 0:H], N2[t, 1, :, cols])
            + COLS[:, 6:7]
        )
        phi = 0.5 * (1.0 + lax.erf(pre * (2.0**-0.5)))
        ACT[:, all_cols] = (pre * phi).astype(BF)
        slope = phi + pre * jnp.exp(pre * pre * -0.5) * ((2.0 * math.pi) ** -0.5)
        grad_act = dot_tn(FB[0, H:D], CG[t, 0, :, cols]) + dot_tn(FB[1, H:D], CG[t, 1, :, cols])
        GPRE[:, all_cols] = (grad_act * slope).astype(BF)
        PGS[t, :, cols] = dot_nn(FB[oc, 0:H], GPRE[:, all_cols]).astype(BF)
        part_copy(PGS, RCG, tile, s_g_core, r_g_core, core).start()
        own = dot_nn(FB[c, 0:H], GPRE[:, all_cols])
        part_copy(PGS, RCG, tile, s_g_core, r_g_core, core).wait_recv()
        SZG[t, :, cols] = (own + RCG[t, :, cols].astype(F32)).astype(BF)
        part_copy(SZG, RZG, tile, s_g_z, r_g_z, zdev).start()
        return carry

    lax.fori_loop(0, n_tiles, feed, 0)

    for entry in ff_entries:
        sent(entry)
    r_f1, r_f2 = recvs.take(4), recvs.take(2)
    f1_entries = []

    def ff_grads(number):
        for h in range(2):
            if number < 2:
                left, right, low = N2, GPRE, number * quarter
            else:
                left, right, low = CG, ACT, (number - 2) * quarter
            total = dot_nt(left[0, h, low : low + quarter, :], right[:, 0:T]) + dot_nt(
                left[1, h, low : low + quarter, :], right[:, T:S]
            )
            FB[h, number * quarter : (number + 1) * quarter, :] = total.astype(BF)

    def ff_part(h, number):
        return FB.at[h, quarter_rows(number)]

    def f1_push(h, number, place, dev, cond=None):
        f1_entries.append(push(ff_part(h, number), rf1_hbm.at[place], r_f1 + place, dev, cond))

    ff_grads(0)
    ff_grads(1)
    f1_push(0, 1 - xb, 0, xdev)
    for number in range(2):
        f1_push(1, number, 2 + number, ydev, yb == 1)

    def outward(tile, carry):
        t, cols = tile_at(tile)
        all_cols = pl.ds(pl.multiple_of(tile * W, W), W)
        OPS[t, :, cols] = dot_nn(FB[oc, H:D], ACT[:, all_cols]).astype(BF)
        part_copy(OPS, RCO, tile, s_p_core, r_p_core, core).start()
        OPO[t, :, cols] = dot_nn(FB[c, H:D], ACT[:, all_cols]).astype(BF)
        return carry

    lax.fori_loop(0, n_tiles, outward, 0)
    ff_grads(2)
    ff_grads(3)
    f1_push(0, 3 - xb, 1, xdev)
    for number in range(2):
        f1_push(1, 2 + number, 2 + number, ydev, yb == 0)

    SPR[dp] = jnp.zeros(SPR.shape[1:], F32)
    SPR[dp, 6:7, :] = dot_nt(jnp.ones((16, S), BF), GPRE[...])[0:1, :]

    r_g_all = recvs.take(n_tiles)
    s_g_all = sends.take(n_tiles)

    def g2_copy(tile):
        t, cols = tile_at(tile)
        return remote(G2.at[t, c, :, cols], G2.at[t, c, :, cols], s_g_all + tile, r_g_all + tile, core)

    def g2_other(tile):
        t, cols = tile_at(tile)
        return remote(G2.at[t, oc, :, cols], G2.at[t, oc, :, cols], s_g_all + tile, r_g_all + tile, core)

    def join(tile, carry):
        t, cols = tile_at(tile)
        part_copy(SZG, RZG, tile, s_g_z, r_g_z, zdev).wait_recv()
        G2[t, c, :, cols] = (SZG[t, :, cols].astype(F32) + RZG[t, :, cols].astype(F32)).astype(BF)
        g2_copy(tile).start()
        return carry

    lax.fori_loop(0, n_tiles, join, 0)

    def norm_back(grads, normals, inv_std, gain_index):
        scaled = [grads[h] * column(h, gain_index) for h in range(2)]
        plain = sum(jnp.sum(scaled[h], axis=0, keepdims=True) for h in range(2)) * inv_d
        cross = sum(jnp.sum(scaled[h] * normals[h], axis=0, keepdims=True) for h in range(2)) * inv_d
        return [inv_std * (scaled[h] - plain - normals[h] * cross) for h in range(2)]

    def second_back(tile, carry):
        t, cols = tile_at(tile)
        g2_other(tile).wait_recv()
        center, inv_std = ST2[t, 0:1, cols], ST2[t, 1:2, cols]
        grads = [G2[t, h, :, cols].astype(F32) for h in range(2)]
        normals = [(HID[t, h, :, cols] - center) * inv_std for h in range(2)]
        back = norm_back(grads, normals, inv_std, VEC_LN2_GAIN)
        for h in range(2):
            grad_hidden = CG[t, h, :, cols].astype(F32) + back[h]
            XG[t, h, :, cols] = grad_hidden.astype(BF)

            @pl.when((t == zz) & (c == h))
            def _():
                GH[:, cols] = grad_hidden
                VGC[:, 2:3] = VGC[:, 2:3] + jnp.sum(grads[h] * normals[h], axis=1, keepdims=True)
                VGC[:, 3:4] = VGC[:, 3:4] + jnp.sum(grads[h], axis=1, keepdims=True)

        return carry

    sent(e_xf)
    lax.fori_loop(0, n_tiles, second_back, 0)
    GB = XG

    r_out_z = recvs.take()

    def wait_out(tile, carry):
        part_copy(OPS, RCO, tile, s_p_core, r_p_core, core).wait_recv()
        return carry

    lax.fori_loop(0, n_tiles, wait_out, 0)
    SZO[...] = (OPO[1 - zz].astype(F32) + RCO[1 - zz].astype(F32)).astype(BF)
    push(SZO, RZO, r_out_z, zdev)
    VGC[:, 4:5] = jnp.sum(GB[zz, c].astype(F32), axis=1, keepdims=True)
    VGC[:, 5:6] = jnp.sum(CG[zz, c].astype(F32), axis=1, keepdims=True)

    window = pl.ds(pl.multiple_of(j * (4 * Q), Q), 5 * Q)
    for t in range(2):
        DATT[:, t * T : (t + 1) * T] = (
            dot_nn(OWB[0, window, :], GB[t, 0]) + dot_nn(OWB[1, window, :], GB[t, 1])
        ).astype(BF)
    r_q1, r_q2 = recvs.take(4), recvs.take(2)
    q1_entries = []

    def q1_push(h, number, place, dev, cond=None):
        q1_entries.append(push(DQ.at[number, h], rq1_hbm.at[place], r_q1 + place, dev, cond))

    for h in range(2):
        total = dot_nt(ATT[block(j), 0:T], GB[0, h]) + dot_nt(ATT[block(j), T:S], GB[1, h])
        DQ[3, h, 0:R, 0:H] = total.astype(BF)
    q1_push(0, 3, 1, xdev, xb == 0)
    q1_push(1, 3, 3, ydev, yb == 0)
    l_x2 = local(x_in, XG.at[zz, c])

    s_f2 = sends.take(2)
    l_f1, l_f2 = locs.take(4), locs.take(2)

    def f2_copy(place):
        if place == 0:
            return remote(ff_part(0, xb + 2 * (1 - yb)), rf2_hbm.at[0], s_f2, r_f2, ydev)
        return remote(ff_part(1, 2 * yb + 1 - xb), rf2_hbm.at[1], s_f2 + 1, r_f2 + 1, xdev)

    spare = ((0, 1 - xb), (0, 3 - xb), (1, 2 * (1 - yb)), (1, 2 * (1 - yb) + 1))
    kept = ((0, xb), (0, 2 + xb), (1, 2 * yb), (1, 2 * yb + 1))

    def first_join():
        for entry in f1_entries:
            when(entry[0], entry[1].wait_send)
        loads = []
        for place in range(4):
            arrived(rf1_hbm.at[place], r_f1 + place)
            load = pltpu.make_async_copy(rf1_hbm.at[place], ff_part(*spare[place]), LS.at[l_f1 + place])
            load.start()
            loads.append(load)
        for load in loads:
            load.wait()

        def add(place):
            h, number = kept[place]
            other = FB[spare[place][0], quarter_rows(spare[place][1]), :]
            rows = quarter_rows(number)
            FB[h, rows, :] = (FB[h, rows, :].astype(F32) + other.astype(F32)).astype(BF)

        for place in range(4):
            add(place)
        f2_copy(0).start()
        f2_copy(1).start()

    def attend_back(slot, carry):
        rows = slot_rows(slot)
        here = pl.ds(pl.multiple_of(slot * Q, Q), Q)
        queries = QKV[0, rows, :]
        keys_t = QKV[1, rows, :]
        keys = keys_t.T
        values = QKV[2, rows, :].T
        grads_out = DATT[here, :]
        for tile in reversed(range(n_tiles)):
            count = W * (tile + 1)
            first = W * tile * (tile + 1) // 2
            cols = slice(tile * W, (tile + 1) * W)
            scores = dot_nn(keys[:count], queries[:, cols]) + MASK[first : first + count, :]
            probs = jnp.exp(scores - LSE[slot, 0:1, cols])
            grad_probs = dot_nn(values[:count], grads_out[:, cols])
            delta = jnp.sum(probs * grad_probs, axis=0, keepdims=True)
            grad_scores = (probs * (grad_probs - delta)).astype(BF)
            probs_low = probs.astype(BF)
            part_v = dot_nt(grads_out[:, cols], probs_low)
            part_k = dot_nt(queries[:, cols], grad_scores)
            if tile == n_tiles - 1:
                ACCV[...] = part_v
                ACCK[...] = part_k
            else:
                ACCV[:, 0:count] = ACCV[:, 0:count] + part_v
                ACCK[:, 0:count] = ACCK[:, 0:count] + part_k
            GQKV[0, rows, cols] = (dot_nn(keys_t[:, :count], grad_scores) * score_scale).astype(BF)
        GQKV[1, rows, :] = ACCK[...].astype(BF)
        GQKV[2, rows, :] = ACCV[...].astype(BF)

        @pl.when(slot == 3)
        def _():
            first_join()

        return carry

    lax.fori_loop(first_slot, 5, attend_back, 0)

    for m in range(3):
        for h in range(2):
            total = dot_nt(GQKV[m, :, 0:T], N1[0, h]) + dot_nt(GQKV[m, :, T:S], N1[1, h])
            DQ[m, h, :, 0:KD] = total.astype(BF)
        q1_push(0, m, m // 2, xdev, xb != m % 2)
        q1_push(1, m, 2 + m % 2, ydev, yb != m // 2)

    def wait_sends(tile, carry):
        part_copy(PGS, RCG, tile, s_g_core, r_g_core, core).wait_send()
        part_copy(OPS, RCO, tile, s_p_core, r_p_core, core).wait_send()
        part_copy(SZG, RZG, tile, s_g_z, r_g_z, zdev).wait_send()
        g2_copy(tile).wait_send()
        return carry

    lax.fori_loop(0, n_tiles, wait_sends, 0)
    r_n_core, r_n_z = recvs.take(n_tiles), recvs.take()
    s_n_core = sends.take(n_tiles)

    def back_rows(half, tile):
        all_cols = pl.ds(pl.multiple_of(tile * W, W), W)
        total = dot_tn(WB[0, half, :, 0:H], GQKV[0, :, all_cols])
        for m in range(1, 3):
            total = total + dot_tn(WB[m, half, :, 0:H], GQKV[m, :, all_cols])
        return total

    def first_part(tile, carry):
        t, cols = tile_at(tile)
        PGS[t, :, cols] = back_rows(oc, tile).astype(BF)
        part_copy(PGS, RCG, tile, s_n_core, r_n_core, core).start()
        OPS[t, :, cols] = back_rows(c, tile).astype(BF)
        return carry

    lax.fori_loop(0, n_tiles, first_part, 0)

    def wait_first(tile, carry):
        part_copy(PGS, RCG, tile, s_n_core, r_n_core, core).wait_recv()
        return carry

    lax.fori_loop(0, n_tiles, wait_first, 0)
    SZG[0] = (OPS[1 - zz].astype(F32) + RCG[1 - zz].astype(F32)).astype(BF)
    push(SZG.at[0], RZN, r_n_z, zdev)

    for entry in f1_entries:
        pending[:] = [other for other in pending if other is not entry]
    loads = []
    for h in range(2):
        arrived(rf2_hbm.at[h], r_f2 + h)
        loads.append(local(rf2_hbm.at[h], ff_part(*spare[2 * h])))
    r_zf = recvs.take(2)
    for h in range(2):
        done(loads[h])
        low = (
            FB[h, my_quarter, :].astype(F32) + FB[h, quarter_rows(spare[2 * h][1]), :].astype(F32)
        ).astype(BF)
        FB[h, my_quarter, :] = low
        if h == 0:

            @pl.when(first_core)
            def _():
                ZF[0] = low

        push(FB.at[h, my_quarter], ZF.at[1], r_zf + 1, (dp, z2, h), second_core)
        if h == 1:
            push(FB.at[h, my_quarter], ZF.at[0], r_zf, (dp, z, 1), first_core)

    arrived(RZO, r_out_z)
    branch_out = OPO[zz].astype(F32) + RCO[zz].astype(F32) + RZO[...].astype(F32)
    OPO[0] = (HID[zz, c] + branch_out + column(c, VEC_PROJ_BIAS)).astype(BF)
    l_out = local(OPO.at[0], out_o)

    for entry in q1_entries:
        sent(entry)
    q_spare = ((1 - xb, 0), (3 - xb, 0), (2 * (1 - yb), 1), (2 * (1 - yb) + 1, 1))
    q_kept = ((xb, 0), (2 + xb, 0), (2 * yb, 1), (2 * yb + 1, 1))
    loads = []
    for place in range(4):
        arrived(rq1_hbm.at[place], r_q1 + place)
        loads.append(local(rq1_hbm.at[place], DQ.at[q_spare[place][0], q_spare[place][1]]))
    for place in range(4):
        done(loads[place])
        (there, h), (here, unused) = q_spare[place], q_kept[place]
        DQ[here, h] = (DQ[here, h].astype(F32) + DQ[there, h].astype(F32)).astype(BF)
    push(DQ.at[xb + 2 * (1 - yb), 0], rq2_hbm.at[0], r_q2, ydev)
    push(DQ.at[2 * yb + 1 - xb, 1], rq2_hbm.at[1], r_q2 + 1, xdev)

    done(l_x2)
    arrived(RZN, r_n_z)
    r_stat = recvs.take()
    grads = OPS[zz].astype(F32) + RCG[zz].astype(F32) + RZN[...].astype(F32)
    center, inv_std = ST1[zz, 0:1, :], ST1[zz, 1:2, :]
    normals = (XG[zz, c].astype(F32) - center) * inv_std
    scaled = grads * column(c, VEC_LN1_GAIN)
    STX[c, 0:1, :] = jnp.sum(scaled, axis=0, keepdims=True)
    STX[c, 1:2, :] = jnp.sum(scaled * normals, axis=0, keepdims=True)
    push(STX.at[c], STX.at[c], r_stat, core)
    VGC[:, 0:1] = jnp.sum(grads * normals, axis=1, keepdims=True)
    VGC[:, 1:2] = jnp.sum(grads, axis=1, keepdims=True)
    arrived(STX.at[oc], r_stat)
    sums = (STX[0] + STX[1]) * inv_d
    OPO[1] = (GH[...] + inv_std * (scaled - sums[0:1] - normals * sums[1:2])).astype(BF)
    l_ing = local(OPO.at[1], ing_o)

    r_sp, r_spz = recvs.take(4), recvs.take(8)
    turned = VGC[...].T
    SPR[dp, 0:6, 0:H] = turned[0:6, :]
    for peer in peers:
        push(SPR.at[dp], SPR.at[dp], r_sp + dp, (peer, z, c))

    r_gf, r_gq = recvs.take(4), recvs.take(4)
    arrived(ZF.at[0], r_zf, second_core)
    arrived(ZF.at[1], r_zf + 1)
    ZF[0] = (ZF[0].astype(F32) + ZF[1].astype(F32)).astype(BF)
    l_gf = local(ZF.at[0], gf_o.at[my_quarter])
    for peer in peers:
        push(ZF.at[0], gf_o.at[my_quarter], r_gf + dp, (peer, z, c))

    loads = []
    for h in range(2):
        arrived(rq2_hbm.at[h], r_q2 + h)
        loads.append(local(rq2_hbm.at[h], DQ.at[q_spare[2 * h][0], h]))
    r_zq, r_zt = recvs.take(2), recvs.take(2)
    with_tail = (j < 3) & (dp < 3)
    next_block = jnp.minimum(j + 1, 3)
    for h in range(2):
        done(loads[h])
        low = (DQ[dp, h].astype(F32) + DQ[q_spare[2 * h][0], h].astype(F32)).astype(BF)
        DQ[dp, h] = low
        if h == 0:

            @pl.when(first_core)
            def _():
                ZQ[0] = low[0:R]

        push(DQ.at[dp, h, pl.ds(0, R)], ZQ.at[1], r_zq + 1, (dp, z2, h), second_core)
        if h == 1:
            push(DQ.at[dp, h, pl.ds(0, R)], ZQ.at[0], r_zq, (dp, z, 1), first_core)
        push(DQ.at[dp, h, pl.ds(R, TAIL)], ZT.at[c], r_zt + c, (dp, next_block, h), with_tail)

    for number in range(4):
        arrived(SPR.at[number], r_sp + number, dp != number)
    SPZ[z, c] = SPR[0] + SPR[1] + SPR[2] + SPR[3]
    for step in range(4):
        for side in range(2):
            if step == 0 and side == 0:
                continue
            target = (dp, lax.rem(z + step, 4), c if side == 0 else oc)
            push(SPZ.at[z, c], SPZ.at[z, c], r_spz + (2 * z + c), target)

    arrived(ZQ.at[0], r_zq, second_core)
    arrived(ZQ.at[1], r_zq + 1)
    gets_tail = (z >= 1) & (dp < 3)
    for side in range(2):
        arrived(ZT.at[side], r_zt + side, gets_tail)
    total = ZQ[0].astype(F32) + ZQ[1].astype(F32)
    ZQ[0] = total.astype(BF)

    @pl.when(gets_tail)
    def _():
        ZQ[0, 0:TAIL] = (total[0:TAIL] + ZT[0].astype(F32) + ZT[1].astype(F32)).astype(BF)

    l_gq = local(ZQ.at[0], gq_o.at[dp])
    for peer in peers:
        push(ZQ.at[0], gq_o.at[dp], r_gq + dp, (peer, z, c))

    for step in range(4):
        for side in range(2):
            if step == 0 and side == 0:
                continue
            zv, cv = lax.rem(z + step, 4), c if side == 0 else oc
            arrived(SPZ.at[zv, cv], r_spz + (2 * zv + cv))
    vectors = SPZ[0, c] + SPZ[1, c] + SPZ[2, c] + SPZ[3, c]
    VOUT[...] = vectors
    VOUT[6:7, :] = SPZ[z, 0, 6:7, :] + SPZ[z2, 1, 6:7, :]
    l_vec_o = local(VOUT, vec_o)

    for number in range(4):
        arrived(gf_o.at[pl.ds(number * quarter, quarter)], r_gf + number, dp != number)
        arrived(gq_o.at[number], r_gq + number, dp != number)
    for entry in (l_out, l_ing, l_gf, l_gq, l_vec_o):
        done(entry)

    def own_sends(slot):
        att_copy(j, slot, s_a_z, r_a_z, zdev).wait_send()
        att_copy(j, slot, s_a_core, r_a_core, core).wait_send()

    slots_of(j, own_sends)
    slots_of(
        owner_of(zp, c),
        lambda slot: att_copy(owner_of(zp, c), slot, s_a_fwd, r_a_fwd, core).wait_send(),
    )

    f2_copy(0).wait_send()
    f2_copy(1).wait_send()

    def last_sends(tile, carry):
        part_copy(PGS, RCG, tile, s_n_core, r_n_core, core).wait_send()
        return carry

    lax.fori_loop(0, n_tiles, last_sends, 0)
    for entry in list(pending):
        sent(entry)
    assert sends.used <= SEND_COUNT and recvs.used <= RECV_COUNT and locs.used <= LOCAL_COUNT


def finish_kernel(
    out_in,
    ing_in,
    gf_in,
    gq_in,
    vec_in,
    out_o,
    ing_o,
    qkv_o,
    qvb_o,
    ow_o,
    fc_o,
    proj_o,
    v0,
    v1,
    v2,
    v3,
    v4,
    v5,
    v6,
    GF,
    GQ,
    FST,
    QST,
    SEM,
):
    R, H = ow_o.shape
    count = GF.shape[0] // R
    whole = [
        pltpu.make_async_copy(out_in, out_o, SEM.at[0]),
        pltpu.make_async_copy(ing_in, ing_o, SEM.at[1]),
    ]
    place = 2
    loads_q, loads_f = [], []
    for m in range(4):
        loads_q.append(pltpu.make_async_copy(gq_in.at[m], GQ.at[m], SEM.at[place + m]))
    place += 4
    for number in range(count):
        rows = pl.ds(number * R, R)
        loads_f.append(pltpu.make_async_copy(gf_in.at[rows], GF.at[rows], SEM.at[place + number]))
    place += count
    for copy in loads_f + loads_q + whole:
        copy.start()
    stores = []
    for number in range(count):
        loads_f[number].wait()
        rows = pl.ds(number * R, R)
        FST[rows, :] = GF[rows, :].astype(F32)
        half = count // 2
        dst = (fc_o if number < half else proj_o).at[pl.ds(number % half * R, R)]
        stores.append(pltpu.make_async_copy(FST.at[rows], dst, SEM.at[place + number]))
        stores[-1].start()
    place += count
    for m in range(4):
        loads_q[m].wait()
        QST[m] = GQ[m, :, 0:H].astype(F32)
        dst = qkv_o.at[m] if m < 3 else ow_o
        stores.append(pltpu.make_async_copy(QST.at[m], dst, SEM.at[place + m]))
        stores[-1].start()
    first = H // LANES * LANES
    for number, m in enumerate((0, 2)):
        turned = GQ[m, :, first : first + LANES].astype(F32).T
        qvb_o[number : number + 1, :] = turned[H - first : H - first + 1, :]
    for number, v in enumerate((v0, v1, v2, v3, v4, v5, v6)):
        v[...] = vec_in[number, 0 : v.shape[0]]
    for copy in stores + whole:
        copy.wait()


def fast_body(
    tokens,
    ln1_gain,
    ln1_bias,
    qkv_weight,
    qv_bias,
    out_weight,
    out_bias,
    ln2_gain,
    ln2_bias,
    fc_weight,
    fc_bias,
    proj_weight,
    proj_bias,
    doc_lengths,
    cotangent,
):
    H, T = tokens.shape
    R = out_weight.shape[0]
    FW = fc_weight.shape[1]
    D, S = 2 * H, 2 * T
    HP = (H // LANES + 1) * LANES
    EXT = 5 * HEAD_DIM
    NT = S // KEY_TILE
    doc_count = doc_lengths.shape[1]
    first_core = lax.axis_index("col") == 0
    low_bias = jnp.where(first_core, qv_bias, jnp.zeros_like(qv_bias))
    bias_three = jnp.stack([low_bias[0], jnp.zeros_like(low_bias[0]), low_bias[1]])
    w3 = jnp.concatenate(
        [
            jnp.transpose(qkv_weight, (1, 2, 0)),
            bias_three[:, :, None],
            jnp.zeros((3, R, HP - H - 1), BF),
        ],
        axis=2,
    )
    rows = [ln1_gain, ln1_bias, ln2_gain, ln2_bias, out_bias, proj_bias, fc_bias, doc_lengths[0]]
    wide = (FW // LANES + 1) * LANES
    pack = jnp.concatenate(
        [jnp.pad(row.astype(F32)[None], ((0, 0), (0, wide - row.shape[0]))) for row in rows], axis=0
    )
    shape = jax.ShapeDtypeStruct
    anywhere = pl.BlockSpec(memory_space=pl.ANY)
    outs = [
        shape((H, T), BF),
        shape((H, T), BF),
        shape((2 * H, FW), BF),
        shape((4, R, HP), BF),
        shape((8, FW), F32),
        shape((4, D // 4, FW), BF),
        shape((2, D // 4, FW), BF),
        shape((4, EXT, HP), BF),
        shape((2, EXT, HP), BF),
    ]
    vmem = pltpu.VMEM
    mask_rows = KEY_TILE * NT * (NT + 1) // 2
    scratch = [
        vmem((2, 2, H, T), BF),
        vmem((2, 2, H, T), BF),
        vmem((2, 2, H + 16, T), BF),
        vmem((3, 2, EXT, HP), BF),
        vmem((2, D, H), BF),
        vmem((2, 2 * H, FW), BF),
        vmem((FW, LANES), F32),
        vmem((2, 8, wide), F32),
        vmem((8, wide), F32),
        vmem((mask_rows, KEY_TILE), F32),
        vmem((3, EXT, S), BF),
        vmem((5, 8, S), F32),
        vmem((D, S), BF),
        vmem((2, 2, H, T), F32),
        vmem((2, 8, T), F32),
        vmem((2, 8, T), F32),
        vmem((2, 2, H, T), BF),
        vmem((FW, S), BF),
        vmem((FW, S), BF),
        vmem((2, H, T), BF),
        vmem((2, H, T), BF),
        vmem((2, H, T), BF),
        vmem((2, H, T), BF),
        vmem((2, H, T), BF),
        vmem((2, H, T), BF),
        vmem((2, H, T), BF),
        vmem((2, 2, H, T), BF),
        vmem((H, T), BF),
        vmem((H, T), BF),
        vmem((H, T), BF),
        vmem((EXT, S), BF),
        vmem((3, EXT, S), BF),
        vmem((HEAD_DIM, S), F32),
        vmem((HEAD_DIM, S), F32),
        vmem((2, 2 * H // 4, FW), BF),
        vmem((4, 2, EXT, HP), BF),
        vmem((2, R, HP), BF),
        vmem((2, EXT - R, HP), BF),
        vmem((H, T), F32),
        vmem((H, LANES), F32),
        vmem((2, 8, T), F32),
        vmem((4, 8, FW), F32),
        vmem((4, 2, 8, FW), F32),
        vmem((8, FW), F32),
        pltpu.SemaphoreType.DMA((SEND_COUNT,)),
        pltpu.SemaphoreType.DMA((RECV_COUNT,)),
        pltpu.SemaphoreType.DMA((LOCAL_COUNT,)),
    ]
    out_rows, in_rows, gf, gq, vectors = pl.pallas_call(
        partial(layer_kernel, doc_count=doc_count),
        out_shape=outs,
        in_specs=[anywhere] * 7,
        out_specs=[anywhere] * len(outs),
        scratch_shapes=scratch,
        compiler_params=pltpu.CompilerParams(
            collective_id=0, has_side_effects=True, vmem_limit_bytes=VMEM_LIMIT
        ),
    )(tokens, cotangent, w3, out_weight, fc_weight, proj_weight, pack)[:5]
    in_vmem = pl.BlockSpec(memory_space=vmem)
    finals = pl.pallas_call(
        finish_kernel,
        out_shape=[
            shape((H, T), BF),
            shape((H, T), BF),
            shape((3, R, H), F32),
            shape((2, R), F32),
            shape((R, H), F32),
            shape((H, FW), F32),
            shape((H, FW), F32),
        ]
        + [shape((H,), F32)] * 6
        + [shape((FW,), F32)],
        in_specs=[anywhere] * 4 + [in_vmem],
        out_specs=[anywhere] * 3 + [in_vmem] + [anywhere] * 3 + [in_vmem] * 7,
        scratch_shapes=[
            vmem((D, FW), BF),
            vmem((4, R, HP), BF),
            vmem((D, FW), F32),
            vmem((4, R, H), F32),
            pltpu.SemaphoreType.DMA((32,)),
        ],
        compiler_params=pltpu.CompilerParams(vmem_limit_bytes=32_000_000),
    )(out_rows, in_rows, gf, gq, vectors)
    out_final, in_final, qkv_rows, bias_grad, ow_grad, fc_grad, proj_grad = finals[:7]
    ln1_gain_g, ln1_bias_g, ln2_gain_g, ln2_bias_g, out_bias_g, proj_bias_g, fc_bias_g = finals[7:]
    return (
        out_final,
        in_final,
        ln1_gain_g,
        ln1_bias_g,
        jnp.transpose(qkv_rows, (2, 0, 1)),
        bias_grad,
        ow_grad,
        out_bias_g,
        ln2_gain_g,
        ln2_bias_g,
        fc_grad,
        fc_bias_g,
        proj_grad,
        proj_bias_g,
    )


def choose_body(*arrays):
    sizes = {axis: lax.axis_size(axis) for axis in ("dp", "row", "col")}
    H, R = arrays[0].shape[0], arrays[5].shape[0]
    fits = sizes == {"dp": 4, "row": 4, "col": 2} and 4 * R == 2 * H == 17 * HEAD_DIM
    return (fast_body if fits else body)(*arrays)


def solution(mesh):
    return jax.shard_map(
        choose_body,
        mesh=mesh,
        in_specs=(
            P("col", ("dp", "row")),
            P("col"),
            P("col"),
            P("col", None, "row"),
            P(None, "row"),
            P("row", "col"),
            P("col"),
            P("col"),
            P("col"),
            P("col", "row"),
            P("row"),
            P("col", "row"),
            P("col"),
            P(("dp", "col"), None),
            P("col", ("dp", "row")),
        ),
        out_specs=(
            P("col", ("dp", "row")),
            P("col", ("dp", "row")),
            P("col"),
            P("col"),
            P("col", None, "row"),
            P(None, "row"),
            P("row", "col"),
            P("col"),
            P("col"),
            P("col"),
            P("col", "row"),
            P("row"),
            P("col", "row"),
            P("col"),
        ),
        check_vma=False,
    )
```

```python
from functools import partial
import math

import jax
import jax.numpy as jnp
from jax import lax
from jax.experimental import pallas as pl
from jax.experimental.pallas import tpu as pltpu
from jax.sharding import PartitionSpec as P

HEAD_DIM = 64


epsilon = 1e-05
score_scale = 0.125
masked_fill = -1e30
block_limit = 512


def feature_sums(first_sum, second_sum):
    return lax.psum((first_sum, second_sum), "col")


def norm_forward(values, gain_vec, shift_vec):
    feature_count = values.shape[1] * lax.axis_size("col")
    total_sum, square_sum = feature_sums(jnp.sum(values, axis=1), jnp.sum(values * values, axis=1))
    center = total_sum / feature_count
    spread = square_sum / feature_count - center * center
    inv_std = lax.rsqrt(spread + epsilon)
    normal = (values - center[:, None]) * inv_std[:, None]
    return (normal, inv_std, normal * gain_vec + shift_vec)


def norm_backward(upstream, normal, inv_std, gain_vec):
    feature_count = upstream.shape[1] * lax.axis_size("col")
    scaled = upstream * gain_vec
    plain_sum, cross_sum = feature_sums(jnp.sum(scaled, axis=1), jnp.sum(scaled * normal, axis=1))
    return inv_std[:, None] * (
        scaled - plain_sum[:, None] / feature_count - normal * (cross_sum[:, None] / feature_count)
    )


def gather_rows(values):
    return lax.all_gather(values, "row", axis=0, tiled=True)


def gather_cols(values):
    return lax.all_gather(values, "col", axis=0, tiled=True)


def sum_over_rows(row_term, row_total):
    return lax.psum_scatter(
        row_term(jnp.int32(0), row_total * lax.axis_size("row")),
        "row",
        scatter_dimension=0,
        tiled=True,
    )


def sum_over_cols(row_term, row_total):
    return lax.psum_scatter(
        row_term(jnp.int32(0), row_total * lax.axis_size("col")),
        "col",
        scatter_dimension=0,
        tiled=True,
    )


def to_heads(values):
    return lax.all_to_all(values, "row", split_axis=0, concat_axis=2, tiled=True)


def to_tokens(values):
    return lax.all_to_all(values, "row", split_axis=2, concat_axis=0, tiled=True)


def product_term(full_rows, matrix):

    def row_term(first_row, row_count):
        return jnp.dot(full_rows, matrix, preferred_element_type=jnp.float32)

    return row_term


def product_term_back(full_rows, matrix):

    def row_term(first_row, row_count):
        return lax.dot_general(
            full_rows, matrix, (((1,), (1,)), ((), ())), preferred_element_type=jnp.float32
        )

    return row_term


def slice_term(full_rows):

    def row_term(first_row, row_count):
        return full_rows

    return row_term


def inner_rows(left_side, right_side):
    return lax.dot_general(
        left_side, right_side, (((0,), (0,)), ((), ())), preferred_element_type=jnp.float32
    )


def segments_of(lengths, places):
    doc_ends = jnp.cumsum(lengths)
    segment = jnp.sum(
        (doc_ends[None, :] <= places[:, None]).astype(jnp.int32), axis=1, dtype=jnp.int32
    )
    return (segment, places >= doc_ends[-1])


def allowed_pairs(query_place, query_segment, query_padding, key_place, key_segment):
    causal = key_place[None, :] <= query_place[:, None]
    same_doc = key_segment[None, :] == query_segment[:, None]
    itself = key_place[None, :] == query_place[:, None]
    return causal & same_doc & (jnp.logical_not(query_padding)[:, None] | itself)


def attention_parts(queries, keyvals, lengths, query_place):
    seq_total = keyvals.shape[0]
    key_block_size = math.gcd(seq_total, block_limit)
    block_count = seq_total // key_block_size
    key_place = jnp.arange(seq_total, dtype=jnp.int32)
    key_segment = segments_of(lengths, key_place)[0]
    query_segment, query_padding = segments_of(lengths, query_place)
    blocked = (
        keyvals.reshape((block_count, key_block_size) + keyvals.shape[1:]),
        key_place.reshape(block_count, key_block_size),
        key_segment.reshape(block_count, key_block_size),
    )

    def block_scores(key_rows, place_rows, segment_rows):
        raw_scores = (
            jnp.einsum("qhd,khd->hqk", queries, key_rows, preferred_element_type=jnp.float32)
            * score_scale
        )
        allowed = allowed_pairs(
            query_place, query_segment, query_padding, place_rows, segment_rows
        )[None]
        return (raw_scores, allowed)

    return (blocked, block_scores)


def attention_forward(queries, blocked, block_scores):
    query_count, head_count, head_width = queries.shape

    def max_step(running, inputs):
        best_score, mass_sum = running
        kv_block, place_rows, segment_rows = inputs
        raw_scores, allowed = block_scores(kv_block[:, 0], place_rows, segment_rows)
        masked = jnp.where(allowed, raw_scores, masked_fill)
        new_best = jnp.maximum(best_score, jnp.max(masked, axis=2))
        fresh = jnp.sum(jnp.where(allowed, jnp.exp(masked - new_best[:, :, None]), 0.0), axis=2)
        return ((new_best, mass_sum * jnp.exp(best_score - new_best) + fresh), None)

    start_best = jnp.full((head_count, query_count), masked_fill, jnp.float32)
    start_mass = jnp.zeros((head_count, query_count), jnp.float32)
    (best_score, mass_sum), unused = lax.scan(max_step, (start_best, start_mass), blocked)
    log_sum = best_score + jnp.log(mass_sum)

    def out_step(running, inputs):
        kv_block, place_rows, segment_rows = inputs
        raw_scores, allowed = block_scores(kv_block[:, 0], place_rows, segment_rows)
        probs_low = jnp.where(allowed, jnp.exp(raw_scores - log_sum[:, :, None]), 0.0).astype(
            jnp.bfloat16
        )
        return (
            running
            + jnp.einsum(
                "hqk,khd->qhd", probs_low, kv_block[:, 1], preferred_element_type=jnp.float32
            ),
            None,
        )

    attended, unused = lax.scan(
        out_step, jnp.zeros((query_count, head_count, head_width), jnp.float32), blocked
    )
    return (attended, log_sum)


def attention_backward(queries, blocked, block_scores, log_sum, grad_attended):
    query_count, head_count, head_width = queries.shape

    def probs_and_grads(inputs):
        kv_block, place_rows, segment_rows = inputs
        raw_scores, allowed = block_scores(kv_block[:, 0], place_rows, segment_rows)
        probs_f = jnp.where(allowed, jnp.exp(raw_scores - log_sum[:, :, None]), 0.0)
        grad_probs = jnp.einsum(
            "qhd,khd->hqk", grad_attended, kv_block[:, 1], preferred_element_type=jnp.float32
        )
        return (probs_f, grad_probs)

    def delta_step(running, inputs):
        probs_f, grad_probs = probs_and_grads(inputs)
        return (running + jnp.sum(probs_f * grad_probs, axis=2), None)

    delta_sum, unused = lax.scan(
        delta_step, jnp.zeros((head_count, query_count), jnp.float32), blocked
    )

    def grad_step(running, inputs):
        kv_block = inputs[0]
        probs_f, grad_probs = probs_and_grads(inputs)
        grad_scores = (probs_f * (grad_probs - delta_sum[:, :, None])).astype(jnp.bfloat16)
        running = running + jnp.einsum(
            "hqk,khd->qhd", grad_scores, kv_block[:, 0], preferred_element_type=jnp.float32
        )
        grad_keys = (
            jnp.einsum("hqk,qhd->khd", grad_scores, queries, preferred_element_type=jnp.float32)
            * score_scale
        )
        grad_values = jnp.einsum(
            "hqk,qhd->khd",
            probs_f.astype(jnp.bfloat16),
            grad_attended,
            preferred_element_type=jnp.float32,
        )
        return (running, jnp.stack([grad_keys, grad_values], axis=1))

    grad_queries, grad_keyvals = lax.scan(
        grad_step, jnp.zeros((query_count, head_count, head_width), jnp.float32), blocked
    )
    seq_total = grad_keyvals.shape[0] * grad_keyvals.shape[1]
    return (grad_queries * score_scale, grad_keyvals.reshape(seq_total, 2, head_count, head_width))


def body(
    tokens,
    ln1_gain,
    ln1_bias,
    qkv_weight,
    qv_bias,
    out_weight,
    out_bias,
    ln2_gain,
    ln2_bias,
    fc_weight,
    fc_bias,
    proj_weight,
    proj_bias,
    doc_lengths,
    cotangent,
):
    count_rows = lax.axis_size("row")
    count_cols = lax.axis_size("col")
    grid_rows = tokens.shape[1]
    col_width = tokens.shape[0]
    row_width = out_weight.shape[0]
    seq_rows = grid_rows * count_rows // count_cols
    query_rows = seq_rows // count_rows
    full_width = col_width * count_cols
    head_count = full_width // HEAD_DIM
    tokens_f = tokens.astype(jnp.float32).T
    normal1, inv_std1, shaped1 = norm_forward(tokens_f, ln1_gain, ln1_bias)
    qkv_flat = qkv_weight.reshape(col_width, 3 * row_width)
    gathered1 = gather_rows(shaped1.astype(jnp.bfloat16))
    mixed_qkv = sum_over_cols(product_term(gathered1, qkv_flat), seq_rows).reshape(
        seq_rows, 3, row_width
    )
    bias_three = jnp.stack([qv_bias[0], jnp.zeros_like(qv_bias[0]), qv_bias[1]])
    qkv_low = (mixed_qkv + bias_three).astype(jnp.bfloat16)
    local_qkv = to_heads(qkv_low).reshape(query_rows, 3, head_count, HEAD_DIM)
    queries = local_qkv[:, 0]
    keyvals = lax.all_gather(local_qkv[:, 1:], "row", axis=0, tiled=True)
    query_place = lax.axis_index("row") * query_rows + jnp.arange(query_rows, dtype=jnp.int32)
    blocked, block_scores = attention_parts(queries, keyvals, doc_lengths[0], query_place)
    attended_f, log_sum = attention_forward(queries, blocked, block_scores)
    attended_low = attended_f.reshape(query_rows, 1, full_width).astype(jnp.bfloat16)
    attended_grid = to_tokens(attended_low).reshape(seq_rows, row_width)
    gathered_att = gather_cols(attended_grid)
    branch = sum_over_rows(product_term(gathered_att, out_weight), grid_rows)
    hidden = tokens_f + (branch + out_bias)
    normal2, inv_std2, shaped2 = norm_forward(hidden, ln2_gain, ln2_bias)
    normed2 = shaped2.astype(jnp.bfloat16)
    gathered2 = gather_rows(normed2)
    pre_act = sum_over_cols(product_term(gathered2, fc_weight), seq_rows) + fc_bias
    active = jax.nn.gelu(pre_act, approximate=False).astype(jnp.bfloat16)
    gathered_act = gather_cols(active)
    projected = sum_over_rows(product_term_back(gathered_act, proj_weight), grid_rows)
    output = (hidden + projected + proj_bias).astype(jnp.bfloat16).T
    cotangent_rows = cotangent.T
    grad_out = cotangent_rows.astype(jnp.float32)
    unused, gelu_back = jax.vjp(partial(jax.nn.gelu, approximate=False), pre_act)
    grad_gathered = gather_rows(cotangent_rows)
    proj_weight_grad = inner_rows(grad_gathered, gathered_act)
    proj_bias_grad = jnp.sum(grad_gathered, axis=0, dtype=jnp.float32)
    grad_active = sum_over_cols(product_term(grad_gathered, proj_weight), seq_rows)
    grad_pre = gelu_back(grad_active)[0].astype(jnp.bfloat16)
    grad_pre_all = gather_cols(grad_pre)
    fc_weight_grad = inner_rows(gathered2, grad_pre_all)
    fc_bias_grad = jnp.sum(grad_pre_all, axis=0, dtype=jnp.float32)
    grad_normed2 = sum_over_rows(product_term_back(grad_pre_all, fc_weight), grid_rows)
    ln2_gain_part = jnp.sum(grad_normed2 * normal2, axis=0)
    ln2_bias_part = jnp.sum(grad_normed2, axis=0)
    grad_hidden = grad_out + norm_backward(grad_normed2, normal2, inv_std2, ln2_gain)
    branch_gathered = gather_rows(grad_hidden.astype(jnp.bfloat16))
    out_weight_grad = inner_rows(gathered_att, branch_gathered)
    out_bias_grad = jnp.sum(branch_gathered, axis=0, dtype=jnp.float32)
    grad_att_grid = sum_over_cols(product_term_back(branch_gathered, out_weight), seq_rows).astype(
        jnp.bfloat16
    )
    grad_attended = to_heads(grad_att_grid.reshape(seq_rows, 1, row_width)).reshape(
        query_rows, head_count, HEAD_DIM
    )
    grad_queries, grad_keyvals = attention_backward(
        queries, blocked, block_scores, log_sum, grad_attended
    )
    keyval_rows = sum_over_rows(slice_term(grad_keyvals), query_rows)
    grad_qkv_local = (
        jnp.concatenate([grad_queries[:, None], keyval_rows], axis=1)
        .astype(jnp.bfloat16)
        .reshape(query_rows, 3, full_width)
    )
    grad_qkv_grid = to_tokens(grad_qkv_local).reshape(seq_rows, 3 * row_width)
    qkv_gathered = gather_cols(grad_qkv_grid)
    qkv_weight_grad = inner_rows(gathered1, qkv_gathered).reshape(col_width, 3, row_width)
    qkv_bias_sums = jnp.sum(qkv_gathered, axis=0, dtype=jnp.float32).reshape(3, row_width)
    qv_bias_grad = jnp.stack([qkv_bias_sums[0], qkv_bias_sums[2]])
    grad_normed1 = sum_over_rows(product_term_back(qkv_gathered, qkv_flat), grid_rows)
    ln1_gain_part = jnp.sum(grad_normed1 * normal1, axis=0)
    ln1_bias_part = jnp.sum(grad_normed1, axis=0)
    input_grad = (
        (grad_hidden + norm_backward(grad_normed1, normal1, inv_std1, ln1_gain))
        .astype(jnp.bfloat16)
        .T
    )
    summed = lax.psum(
        (
            qkv_weight_grad,
            qv_bias_grad,
            out_weight_grad,
            out_bias_grad,
            fc_weight_grad,
            fc_bias_grad,
            proj_weight_grad,
            proj_bias_grad,
        ),
        "dp",
    )
    gain_sums = lax.psum(
        (ln1_gain_part, ln1_bias_part, ln2_gain_part, ln2_bias_part), ("dp", "row")
    )
    return (
        output,
        input_grad,
        gain_sums[0],
        gain_sums[1],
        summed[0],
        summed[1],
        summed[2],
        summed[3],
        gain_sums[2],
        gain_sums[3],
        summed[4],
        summed[5],
        summed[6],
        summed[7],
    )


BF = jnp.bfloat16
F32 = jnp.float32
MESH = pl.DeviceIdType.MESH
LANES = 128
KEY_TILE = 256
VEC_LN1_GAIN, VEC_LN1_BIAS, VEC_LN2_GAIN, VEC_LN2_BIAS, VEC_OUT_BIAS, VEC_PROJ_BIAS = range(6)


def dot_nn(left, right):
    return lax.dot_general(left, right, (((1,), (0,)), ((), ())), preferred_element_type=F32)


def dot_tn(left, right):
    return lax.dot_general(left, right, (((0,), (0,)), ((), ())), preferred_element_type=F32)


def dot_nt(left, right):
    return lax.dot_general(left, right, (((1,), (1,)), ((), ())), preferred_element_type=F32)


VMEM_LIMIT = 66_000_000


class Slots:
    def __init__(self):
        self.used = 0

    def take(self, count=1):
        first = self.used
        self.used += count
        return first


SEND_COUNT, RECV_COUNT, LOCAL_COUNT = 144, 160, 48


def layer_kernel(
    x_in,
    cot_in,
    w3_in,
    ow_in,
    fc_in,
    proj_in,
    ln1_gain_in,
    ln1_bias_in,
    ln2_gain_in,
    ln2_bias_in,
    out_bias_in,
    proj_bias_in,
    fc_bias_in,
    qv_bias_in,
    doc_in,
    out_o,
    ing_o,
    gf_o,
    gq_o,
    vec_o,
    rf1_hbm,
    rf2_hbm,
    rq1_hbm,
    rq2_hbm,
    XG,
    CG,
    N1,
    WB,
    QB,
    OWB,
    FB,
    COLS,
    PACK,
    PACKF,
    PACKN,
    MASK,
    QKV,
    LSE,
    ATT,
    HID,
    ST1,
    ST2,
    N2,
    ACT,
    GPRE,
    PGS,
    OPS,
    RCG,
    RCO,
    OPO,
    SZG,
    RZG,
    G2,
    SZO,
    RZO,
    RZN,
    DATT,
    GQKV,
    ACCK,
    ACCV,
    ZF,
    DQ,
    ZQ,
    ZT,
    GH,
    VGC,
    STX,
    SPR,
    SPZ,
    VOUT,
    SS,
    RS,
    LS,
):
    H, T = x_in.shape
    R = w3_in.shape[1]
    HP = DQ.shape[3]
    EXT = WB.shape[2]
    TAIL = EXT - R
    D = 2 * H
    S = 2 * T
    W = KEY_TILE
    Q = HEAD_DIM
    FW = fc_in.shape[1]
    per_tok = T // W
    n_tiles = S // W
    inv_d = 1.0 / D

    dp, z, c = lax.axis_index("dp"), lax.axis_index("row"), lax.axis_index("col")
    oc = 1 - c
    zz = lax.rem(z, 2)
    zp = z + 1 - 2 * zz
    z2 = lax.rem(z + 2, 4)
    j = lax.rem(z + 2 * c, 4)
    pair = z // 2
    core = (dp, z, oc)
    zdev = (dp, zp, c)
    xn = dp + 1 - 2 * lax.rem(dp, 2)
    yn = lax.rem(dp + 2, 4)
    dg = 3 - dp
    peers = (dg, xn, yn)
    xb, yb = lax.rem(dp, 2), dp // 2
    xdev, ydev = (xn, z, c), (yn, z, c)
    first_core, second_core = c == 0, c == 1

    sends, recvs, locs = Slots(), Slots(), Slots()
    pending = []

    def remote(src, dst, s_idx, r_idx, dev):
        return pltpu.make_async_remote_copy(
            src_ref=src,
            dst_ref=dst,
            send_sem=SS.at[s_idx],
            recv_sem=RS.at[r_idx],
            device_id=dev,
            device_id_type=MESH,
        )

    def when(cond, fn):
        if cond is None:
            fn()
        else:
            pl.when(cond)(fn)

    def push(src, dst, r_idx, dev, cond=None):
        copy = remote(src, dst, sends.take(), r_idx, dev)
        when(cond, copy.start)
        entry = [cond, copy]
        pending.append(entry)
        return entry

    def sent(entry):
        when(entry[0], entry[1].wait_send)
        pending[:] = [other for other in pending if other is not entry]

    def arrived(dst, r_idx, cond=None):
        when(cond, remote(dst, dst, 0, r_idx, core).wait_recv)

    def local(src, dst, cond=None):
        copy = pltpu.make_async_copy(src, dst, LS.at[locs.take()])
        when(cond, copy.start)
        return (cond, copy)

    def done(entry):
        when(entry[0], entry[1].wait)

    barrier = pltpu.get_barrier_semaphore()
    for step in range(4):
        for side in range(2):
            if step == 0 and side == 0:
                continue
            target = (dp, lax.rem(z + step, 4), c if side == 0 else oc)
            pl.semaphore_signal(barrier, inc=1, device_id=target, device_id_type=MESH)
    for peer in peers:
        pl.semaphore_signal(barrier, inc=1, device_id=(peer, z, c), device_id_type=MESH)
    pl.semaphore_wait(barrier, 10)

    r_x_core, r_x_z, r_x_fwd = recvs.take(), recvs.take(), recvs.take()
    r_w_core, r_w_z, r_w_xy, r_w_tail = recvs.take(), recvs.take(2), recvs.take(4), recvs.take(2)
    r_pack, r_packf, r_packn = recvs.take(), recvs.take(), recvs.take()
    r_f_core, r_f_z, r_f_xy = recvs.take(2), recvs.take(2), recvs.take(4)
    r_o_core, r_o_z, r_o_z0, r_o_xy, r_o_fwd = (
        recvs.take(),
        recvs.take(4),
        recvs.take(4),
        recvs.take(16),
        recvs.take(4),
    )

    def block(number):
        return pl.ds(pl.multiple_of(number * R, 16), R)

    quarter = D // 4
    odd = R - 4 * (R // 64) * 16
    piece = R // 64 * 16

    def quarter_rows(number):
        return pl.ds(pl.multiple_of(number * quarter, 16), quarter)

    def ow_piece(number, plane):
        return pl.ds(pl.multiple_of(number * R + odd + plane * piece, 16), piece)

    def ow_odd(number):
        return pl.ds(pl.multiple_of(number * R, 16), odd)

    my_quarter = quarter_rows(dp)
    w_row = jnp.minimum(dp, 2)
    has_before = z >= 1
    bias_first = (LANES, LANES + (R // LANES + 1) * LANES)
    doc_count = doc_in.shape[1]
    push(w3_in.at[w_row], WB.at[w_row, c, pl.ds(0, R)], r_w_z + c, (dp, z2, 1), dp < 3)
    pack = PACK.at[c]
    PACK[c] = jnp.zeros(PACK.shape[1:], F32)
    vectors_in = (ln1_gain_in, ln1_bias_in, ln2_gain_in, ln2_bias_in, out_bias_in, proj_bias_in, fc_bias_in)
    for number, vector in enumerate(vectors_in):
        PACK[c, number : number + 1, 0 : vector.shape[0]] = vector[...].astype(F32).reshape(1, -1)
    PACK[c, 7:8, 0:doc_count] = doc_in[...].astype(F32)
    for number in range(2):
        PACK[c, 7:8, bias_first[number] : bias_first[number] + R] = qv_bias_in[number : number + 1, :].astype(F32)
    push(x_in, XG.at[zz, c], r_x_z, zdev)
    push(x_in, XG.at[zz, c], r_x_core, core)
    push(pack, pack, r_pack, core)
    push(w3_in, WB.at[:, 1, pl.ds(0, R)], r_w_core, (dp, z, 0), second_core)
    push(w3_in.at[:, pl.ds(0, TAIL)], WB.at[:, c, pl.ds(R, TAIL)], r_w_tail + c, (dp, jnp.maximum(z - 1, 0), 0), has_before)
    push(w3_in.at[:, pl.ds(0, TAIL)], WB.at[:, c, pl.ds(R, TAIL)], r_w_tail + c, (dp, lax.rem(z + 1, 4), 1), has_before)
    push(pack, PACKF, r_packf, (dp, z2, 1), first_core)
    push(pack, PACKN, r_packn, (dp, jnp.maximum(z - 1, 0), 0), has_before & first_core)
    push(pack, PACKN, r_packn, (dp, lax.rem(z + 1, 4), 1), has_before & first_core)
    l_x = local(x_in, XG.at[zz, c])
    l_w = local(w3_in, WB.at[:, 0, pl.ds(0, R)], first_core)
    push(fc_in, FB.at[1, pl.ds(0, H)], r_f_core, (dp, z, 0), second_core)
    push(proj_in, FB.at[1, pl.ds(H, H)], r_f_core + 1, (dp, z, 0), second_core)
    push(ow_in, OWB.at[c, block(z)], r_o_core, core)
    l_f = local(fc_in, FB.at[0, pl.ds(0, H)], first_core)
    l_p = local(proj_in, FB.at[0, pl.ds(H, H)], first_core)
    l_o = local(ow_in, OWB.at[c, block(z)])

    VGC[...] = jnp.zeros_like(VGC)
    GQKV[...] = jnp.zeros_like(GQKV)

    def clear_tail():
        WB[:, :, R:, :] = jnp.zeros((3, 2, TAIL, H), BF)

    pl.when(j == 3)(clear_tail)

    arrived(PACK.at[oc], r_pack)
    lengths = PACK[pair, 7:8, 0:LANES]
    place_c = lax.broadcasted_iota(jnp.int32, (S, LANES), 0).astype(F32)
    place_r = lax.broadcasted_iota(jnp.int32, (8, S), 1).astype(F32)
    end = jnp.zeros((1, 1), F32)
    seg_c, seg_r = jnp.zeros_like(place_c), jnp.zeros_like(place_r)
    for number in range(doc_count):
        end = end + lengths[:, number : number + 1]
        seg_c = seg_c + jnp.where(end <= place_c, 1.0, 0.0)
        seg_r = seg_r + jnp.where(end <= place_r, 1.0, 0.0)
    seg_c = jnp.where(end <= place_c, place_c + 2.0 * S, seg_c)
    seg_r = jnp.where(end <= place_r, place_r + 2.0 * S, seg_r)
    for tile in range(n_tiles):
        rows = W * (tile + 1)
        first = W * tile * (tile + 1) // 2
        cols = slice(tile * W, (tile + 1) * W)
        key_seg = jnp.concatenate([seg_c[:rows]] * (W // LANES), axis=1)
        key_place = jnp.concatenate([place_c[:rows]] * (W // LANES), axis=1)
        ok = (key_seg == seg_r[0:1, cols]) & (key_place <= place_r[0:1, cols])
        MASK[first : first + rows, :] = jnp.where(ok, 0.0, masked_fill)

    for h in range(2):
        COLS[h * H : (h + 1) * H, 0:6] = PACK[h].T[0:H, 0:6]

    def column(h, which):
        if isinstance(h, int):
            return COLS[h * H : (h + 1) * H, which : which + 1]
        return COLS[pl.ds(pl.multiple_of(h * H, 16), H), which : which + 1]

    def stats_of(first_half, second_half):
        center = (
            jnp.sum(first_half, axis=0, keepdims=True) + jnp.sum(second_half, axis=0, keepdims=True)
        ) * inv_d
        square = (
            jnp.sum(first_half * first_half, axis=0, keepdims=True)
            + jnp.sum(second_half * second_half, axis=0, keepdims=True)
        ) * inv_d
        return center, lax.rsqrt(square - center * center + epsilon)

    def first_norm(t):
        halves = [XG[t, h].astype(F32) for h in range(2)]
        center, inv_std = stats_of(*halves)
        ST1[t, 0:1, :] = center
        ST1[t, 1:2, :] = inv_std
        for h in range(2):
            shaped = (halves[h] - center) * inv_std * column(h, VEC_LN1_GAIN) + column(
                h, VEC_LN1_BIAS
            )
            N1[t, h, 0:H, :] = shaped.astype(BF)

    done(l_x)
    arrived(XG.at[zz, oc], r_x_core)
    first_norm(zz)

    w_from_z = second_core & (dp < 3)
    for h in range(2):
        arrived(WB.at[w_row, h, pl.ds(0, R)], r_w_z + h, w_from_z)
    for peer in peers:
        push(
            WB.at[w_row, :, pl.ds(0, R)],
            WB.at[w_row, :, pl.ds(0, R)],
            r_w_xy + w_row,
            (peer, z, 1),
            w_from_z,
        )
    arrived(XG.at[1 - zz, c], r_x_z)
    e_xf = push(XG.at[1 - zz, c], XG.at[1 - zz, c], r_x_fwd, core)
    for step in (1, 3, 2):
        target = (dp, lax.rem(z + step, 4), c)
        push(ow_in.at[ow_piece(0, dp)], OWB.at[c, ow_piece(z, dp)], r_o_z + z, target)
        push(ow_in.at[ow_odd(0)], OWB.at[c, ow_odd(z)], r_o_z0 + z, target)
    push(
        fc_in.at[quarter_rows(jnp.minimum(dp, 1))], FB.at[c, my_quarter], r_f_z + c, (dp, z2, 1), dp < 2
    )
    push(
        proj_in.at[quarter_rows(jnp.maximum(dp - 2, 0))],
        FB.at[c, my_quarter],
        r_f_z + c,
        (dp, z2, 1),
        dp >= 2,
    )

    arrived(XG.at[1 - zz, oc], r_x_fwd)
    first_norm(1 - zz)

    done(l_w)
    arrived(WB.at[:, 1, pl.ds(0, R)], r_w_core, first_core)
    for m in range(3):
        arrived(WB.at[m, :, pl.ds(0, R)], r_w_xy + m, second_core & (dp != m))
    for h in range(2):
        arrived(WB.at[:, h, pl.ds(R, TAIL)], r_w_tail + h, j < 3)

    arrived(PACKF, r_packf, second_core)
    arrived(PACKN, r_packn, j < 3)

    def bias_columns(source, rows, count):
        turned = source.T
        for m, first in ((0, bias_first[0]), (2, bias_first[1])):
            QB[rows : rows + count, m : m + 1] = turned[first : first + count, 7:8]

    QB[...] = jnp.zeros_like(QB)
    pl.when(first_core)(lambda: bias_columns(PACK[0], 0, R))
    pl.when(second_core)(lambda: bias_columns(PACKF[...], 0, R))
    pl.when(j < 3)(lambda: bias_columns(PACKN[...], R, TAIL))

    for t in range(2):
        for m in range(3):
            mixed = dot_nn(WB[m, 0], N1[t, 0]) + dot_nn(WB[m, 1], N1[t, 1])
            if m != 1:
                mixed = mixed + QB[:, m : m + 1]
            low = mixed.astype(BF)
            if m == 0:
                low = low * jnp.asarray(score_scale, BF)
            QKV[m, :, t * T : (t + 1) * T] = low

    for step in (1, 3, 2):
        there = lax.rem(z + step, 4)
        arrived(OWB.at[c, ow_piece(there, dp)], r_o_z + there)
        for peer in peers:
            rows = ow_piece(there, dp)
            push(OWB.at[c, rows], OWB.at[c, rows], r_o_xy + (4 * dp + there), (peer, z, c))
    r_a_z, r_a_core, r_a_fwd = recvs.take(5), recvs.take(5), recvs.take(5)
    s_a_z, s_a_core, s_a_fwd = sends.take(5), sends.take(5), sends.take(5)
    first_slot = jnp.where(j == 0, 0, 1)

    def head_rows(owner, slot):
        return pl.ds(pl.multiple_of(owner * (4 * Q) + slot * Q, Q), Q)

    def slot_rows(slot):
        return pl.ds(pl.multiple_of(slot * Q - 16 * j, 16), Q)

    def att_copy(owner, slot, s_base, r_base, dev):
        rows = head_rows(owner, slot)
        return remote(ATT.at[rows], ATT.at[rows], s_base + slot, r_base + slot, dev)

    s_f_xy = sends.take(3)

    def ff_copy(number):
        part = FB.at[:, my_quarter]
        return remote(part, part, s_f_xy + number, r_f_xy + dp, (peers[number], z, 1))

    def attend(slot, carry):
        @pl.when((slot == 4) & second_core)
        def _():
            for h in range(2):
                arrived(FB.at[h, my_quarter], r_f_z + h)
            for number in range(3):
                ff_copy(number).start()

        rows = slot_rows(slot)
        out_rows = head_rows(j, slot)
        queries = QKV[0, rows, :]
        keys = QKV[1, rows, :].T
        values = QKV[2, rows, :]
        for tile in range(n_tiles):
            count = W * (tile + 1)
            first = W * tile * (tile + 1) // 2
            cols = slice(tile * W, (tile + 1) * W)
            scores = dot_nn(keys[:count], queries[:, cols]) + MASK[first : first + count, :]
            best = jnp.max(scores, axis=0, keepdims=True)
            weights = jnp.exp(scores - best)
            mass = jnp.sum(weights, axis=0, keepdims=True)
            probs_low = (weights * (1.0 / mass)).astype(BF)
            ATT[out_rows, cols] = dot_nn(values[:, :count], probs_low).astype(BF)
            LSE[slot, 0:1, cols] = best + jnp.log(mass)
        att_copy(j, slot, s_a_z, r_a_z, zdev).start()
        att_copy(j, slot, s_a_core, r_a_core, core).start()

        return carry

    lax.fori_loop(first_slot, 5, attend, 0)

    r_c_core, r_c_z, r_c_fwd = recvs.take(), recvs.take(), recvs.take()
    push(cot_in, CG.at[zz, c], r_c_z, zdev)
    push(cot_in, CG.at[zz, c], r_c_core, core)
    l_c = local(cot_in, CG.at[zz, c])

    for step in (1, 3, 2):
        there = lax.rem(z + step, 4)
        arrived(OWB.at[c, ow_odd(there)], r_o_z0 + there)
        for plane in range(4):
            arrived(OWB.at[c, ow_piece(there, plane)], r_o_xy + (4 * plane + there), dp != plane)
        push(OWB.at[c, block(there)], OWB.at[c, block(there)], r_o_fwd + there, core)

    def owner_of(zv, cv):
        return lax.rem(zv + 2 * cv, 4)

    def slots_of(owner, body):
        lax.fori_loop(jnp.where(owner == 0, 0, 1), 5, lambda slot, carry: (body(slot), carry)[1], 0)

    def pass_on(slot):
        att_copy(owner_of(zp, c), slot, s_a_fwd, r_a_z, core).wait_recv()
        att_copy(owner_of(zp, c), slot, s_a_fwd, r_a_fwd, core).start()

    slots_of(owner_of(zp, c), pass_on)
    slots_of(owner_of(z, oc), lambda slot: att_copy(owner_of(z, oc), slot, s_a_core, r_a_core, core).wait_recv())
    slots_of(owner_of(zp, oc), lambda slot: att_copy(owner_of(zp, oc), slot, s_a_fwd, r_a_fwd, core).wait_recv())
    done(l_o)
    arrived(OWB.at[oc, block(z)], r_o_core)
    for step in range(1, 4):
        there = lax.rem(z + step, 4)
        arrived(OWB.at[oc, block(there)], r_o_fwd + there)

    def project(tile, carry):
        t = tile // per_tok
        cols = pl.ds(pl.multiple_of(lax.rem(tile, per_tok) * W, W), W)
        all_cols = pl.ds(pl.multiple_of(tile * W, W), W)
        att = ATT[:, all_cols]
        halves = []
        for h in range(2):
            branch = dot_tn(OWB[h], att)
            halves.append(XG[t, h, :, cols].astype(F32) + (branch + column(h, VEC_OUT_BIAS)))
            HID[t, h, :, cols] = halves[h]
        center, inv_std = stats_of(*halves)
        ST2[t, 0:1, cols] = center
        ST2[t, 1:2, cols] = inv_std
        for h in range(2):
            shaped = (halves[h] - center) * inv_std * column(h, VEC_LN2_GAIN) + column(
                h, VEC_LN2_BIAS
            )
            N2[t, h, :, cols] = shaped.astype(BF)
        return carry

    lax.fori_loop(0, n_tiles, project, 0)

    done(l_f)
    done(l_p)
    for number in range(2):
        arrived(FB.at[1, pl.ds(number * H, H)], r_f_core + number, first_core)
    for number in range(4):
        arrived(FB.at[:, quarter_rows(number)], r_f_xy + number, second_core & (dp != number))
    @pl.when(first_core)
    def _():
        COLS[:, 6:7] = PACK[0].T[0:FW, 6:7]

    @pl.when(second_core)
    def _():
        COLS[:, 6:7] = PACKF[...].T[0:FW, 6:7]

    arrived(CG.at[1 - zz, c], r_c_z)
    push(CG.at[1 - zz, c], CG.at[1 - zz, c], r_c_fwd, core)
    done(l_c)
    arrived(CG.at[zz, oc], r_c_core)
    arrived(CG.at[1 - zz, oc], r_c_fwd)

    r_g_core, r_p_core, r_g_z = recvs.take(n_tiles), recvs.take(n_tiles), recvs.take(n_tiles)
    s_g_core, s_p_core, s_g_z = sends.take(n_tiles), sends.take(n_tiles), sends.take(n_tiles)

    def tile_at(tile):
        t = tile // per_tok
        return t, pl.ds(pl.multiple_of(lax.rem(tile, per_tok) * W, W), W)

    def part_copy(buf, dst, tile, s_base, r_base, dev):
        t, cols = tile_at(tile)
        return remote(buf.at[t, :, cols], dst.at[t, :, cols], s_base + tile, r_base + tile, dev)

    def feed(tile, carry):
        t, cols = tile_at(tile)
        all_cols = pl.ds(pl.multiple_of(tile * W, W), W)
        pre = (
            dot_tn(FB[0, 0:H], N2[t, 0, :, cols])
            + dot_tn(FB[1, 0:H], N2[t, 1, :, cols])
            + COLS[:, 6:7]
        )
        phi = 0.5 * (1.0 + lax.erf(pre * (2.0**-0.5)))
        ACT[:, all_cols] = (pre * phi).astype(BF)
        slope = phi + pre * jnp.exp(pre * pre * -0.5) * ((2.0 * math.pi) ** -0.5)
        grad_act = dot_tn(FB[0, H:D], CG[t, 0, :, cols]) + dot_tn(FB[1, H:D], CG[t, 1, :, cols])
        GPRE[:, all_cols] = (grad_act * slope).astype(BF)
        PGS[t, :, cols] = dot_nn(FB[oc, 0:H], GPRE[:, all_cols]).astype(BF)
        part_copy(PGS, RCG, tile, s_g_core, r_g_core, core).start()
        own = dot_nn(FB[c, 0:H], GPRE[:, all_cols])
        part_copy(PGS, RCG, tile, s_g_core, r_g_core, core).wait_recv()
        SZG[t, :, cols] = (own + RCG[t, :, cols].astype(F32)).astype(BF)
        part_copy(SZG, RZG, tile, s_g_z, r_g_z, zdev).start()
        return carry

    lax.fori_loop(0, n_tiles, feed, 0)

    for number in range(3):
        when(second_core, ff_copy(number).wait_send)
    r_f1, r_f2 = recvs.take(4), recvs.take(2)
    f1_entries = []

    def ff_grads(number):
        for h in range(2):
            if number < 2:
                left, right, low = N2, GPRE, number * quarter
            else:
                left, right, low = CG, ACT, (number - 2) * quarter
            total = dot_nt(left[0, h, low : low + quarter, :], right[:, 0:T]) + dot_nt(
                left[1, h, low : low + quarter, :], right[:, T:S]
            )
            FB[h, number * quarter : (number + 1) * quarter, :] = total.astype(BF)

    def ff_part(h, number):
        return FB.at[h, quarter_rows(number)]

    def f1_push(h, number, place, dev, cond=None):
        f1_entries.append(push(ff_part(h, number), rf1_hbm.at[place], r_f1 + place, dev, cond))

    ff_grads(0)
    ff_grads(1)
    f1_push(0, 1 - xb, 0, xdev)
    for number in range(2):
        f1_push(1, number, 2 + number, ydev, yb == 1)

    def outward(tile, carry):
        t, cols = tile_at(tile)
        all_cols = pl.ds(pl.multiple_of(tile * W, W), W)
        OPS[t, :, cols] = dot_nn(FB[oc, H:D], ACT[:, all_cols]).astype(BF)
        part_copy(OPS, RCO, tile, s_p_core, r_p_core, core).start()
        OPO[t, :, cols] = dot_nn(FB[c, H:D], ACT[:, all_cols]).astype(BF)
        return carry

    lax.fori_loop(0, n_tiles, outward, 0)
    ff_grads(2)
    ff_grads(3)
    f1_push(0, 3 - xb, 1, xdev)
    for number in range(2):
        f1_push(1, 2 + number, 2 + number, ydev, yb == 0)

    SPR[dp] = jnp.zeros(SPR.shape[1:], F32)
    SPR[dp, 6:7, :] = dot_nt(jnp.ones((16, S), BF), GPRE[...])[0:1, :]

    r_g_all = recvs.take(n_tiles)
    s_g_all = sends.take(n_tiles)

    def g2_copy(tile):
        t, cols = tile_at(tile)
        return remote(G2.at[t, c, :, cols], G2.at[t, c, :, cols], s_g_all + tile, r_g_all + tile, core)

    def g2_other(tile):
        t, cols = tile_at(tile)
        return remote(G2.at[t, oc, :, cols], G2.at[t, oc, :, cols], s_g_all + tile, r_g_all + tile, core)

    def join(tile, carry):
        t, cols = tile_at(tile)
        part_copy(SZG, RZG, tile, s_g_z, r_g_z, zdev).wait_recv()
        G2[t, c, :, cols] = (SZG[t, :, cols].astype(F32) + RZG[t, :, cols].astype(F32)).astype(BF)
        g2_copy(tile).start()
        return carry

    lax.fori_loop(0, n_tiles, join, 0)

    def norm_back(grads, normals, inv_std, gain_index):
        scaled = [grads[h] * column(h, gain_index) for h in range(2)]
        plain = sum(jnp.sum(scaled[h], axis=0, keepdims=True) for h in range(2)) * inv_d
        cross = sum(jnp.sum(scaled[h] * normals[h], axis=0, keepdims=True) for h in range(2)) * inv_d
        return [inv_std * (scaled[h] - plain - normals[h] * cross) for h in range(2)]

    def second_back(tile, carry):
        t, cols = tile_at(tile)
        g2_other(tile).wait_recv()
        center, inv_std = ST2[t, 0:1, cols], ST2[t, 1:2, cols]
        grads = [G2[t, h, :, cols].astype(F32) for h in range(2)]
        normals = [(HID[t, h, :, cols] - center) * inv_std for h in range(2)]
        back = norm_back(grads, normals, inv_std, VEC_LN2_GAIN)
        for h in range(2):
            grad_hidden = CG[t, h, :, cols].astype(F32) + back[h]
            XG[t, h, :, cols] = grad_hidden.astype(BF)

            @pl.when((t == zz) & (c == h))
            def _():
                GH[:, cols] = grad_hidden
                VGC[:, 2:3] = VGC[:, 2:3] + jnp.sum(grads[h] * normals[h], axis=1, keepdims=True)
                VGC[:, 3:4] = VGC[:, 3:4] + jnp.sum(grads[h], axis=1, keepdims=True)

        return carry

    sent(e_xf)
    lax.fori_loop(0, n_tiles, second_back, 0)
    GB = XG

    r_out_z = recvs.take()

    def wait_out(tile, carry):
        part_copy(OPS, RCO, tile, s_p_core, r_p_core, core).wait_recv()
        return carry

    lax.fori_loop(0, n_tiles, wait_out, 0)
    SZO[...] = (OPO[1 - zz].astype(F32) + RCO[1 - zz].astype(F32)).astype(BF)
    push(SZO, RZO, r_out_z, zdev)
    VGC[:, 4:5] = jnp.sum(GB[zz, c].astype(F32), axis=1, keepdims=True)
    VGC[:, 5:6] = jnp.sum(CG[zz, c].astype(F32), axis=1, keepdims=True)

    window = pl.ds(pl.multiple_of(j * (4 * Q), Q), 5 * Q)
    for t in range(2):
        DATT[:, t * T : (t + 1) * T] = (
            dot_nn(OWB[0, window, :], GB[t, 0]) + dot_nn(OWB[1, window, :], GB[t, 1])
        ).astype(BF)
    r_q1, r_q2 = recvs.take(4), recvs.take(2)
    q1_entries = []

    def q1_push(h, number, place, dev, cond=None):
        q1_entries.append(push(DQ.at[number, h], rq1_hbm.at[place], r_q1 + place, dev, cond))

    for h in range(2):
        total = dot_nt(ATT[block(j), 0:T], GB[0, h]) + dot_nt(ATT[block(j), T:S], GB[1, h])
        DQ[3, h, 0:R, 0:H] = total.astype(BF)
    q1_push(0, 3, 1, xdev, xb == 0)
    q1_push(1, 3, 3, ydev, yb == 0)
    l_x2 = local(x_in, XG.at[zz, c])

    s_f2 = sends.take(2)
    l_f1, l_f2 = locs.take(4), locs.take(2)

    def f2_copy(place):
        if place == 0:
            return remote(ff_part(0, xb + 2 * (1 - yb)), rf2_hbm.at[0], s_f2, r_f2, ydev)
        return remote(ff_part(1, 2 * yb + 1 - xb), rf2_hbm.at[1], s_f2 + 1, r_f2 + 1, xdev)

    spare = ((0, 1 - xb), (0, 3 - xb), (1, 2 * (1 - yb)), (1, 2 * (1 - yb) + 1))
    kept = ((0, xb), (0, 2 + xb), (1, 2 * yb), (1, 2 * yb + 1))

    def first_join():
        for entry in f1_entries:
            when(entry[0], entry[1].wait_send)
        loads = []
        for place in range(4):
            arrived(rf1_hbm.at[place], r_f1 + place)
            load = pltpu.make_async_copy(rf1_hbm.at[place], ff_part(*spare[place]), LS.at[l_f1 + place])
            load.start()
            loads.append(load)
        for load in loads:
            load.wait()

        def add(place):
            h, number = kept[place]
            other = FB[spare[place][0], quarter_rows(spare[place][1]), :]
            rows = quarter_rows(number)
            FB[h, rows, :] = (FB[h, rows, :].astype(F32) + other.astype(F32)).astype(BF)

        for place in range(4):
            add(place)
        f2_copy(0).start()
        f2_copy(1).start()

    def attend_back(slot, carry):
        rows = slot_rows(slot)
        here = pl.ds(pl.multiple_of(slot * Q, Q), Q)
        queries = QKV[0, rows, :]
        keys_t = QKV[1, rows, :]
        keys = keys_t.T
        values = QKV[2, rows, :].T
        grads_out = DATT[here, :]
        for tile in reversed(range(n_tiles)):
            count = W * (tile + 1)
            first = W * tile * (tile + 1) // 2
            cols = slice(tile * W, (tile + 1) * W)
            scores = dot_nn(keys[:count], queries[:, cols]) + MASK[first : first + count, :]
            probs = jnp.exp(scores - LSE[slot, 0:1, cols])
            grad_probs = dot_nn(values[:count], grads_out[:, cols])
            delta = jnp.sum(probs * grad_probs, axis=0, keepdims=True)
            grad_scores = (probs * (grad_probs - delta)).astype(BF)
            probs_low = probs.astype(BF)
            part_v = dot_nt(grads_out[:, cols], probs_low)
            part_k = dot_nt(queries[:, cols], grad_scores)
            if tile == n_tiles - 1:
                ACCV[...] = part_v
                ACCK[...] = part_k
            else:
                ACCV[:, 0:count] = ACCV[:, 0:count] + part_v
                ACCK[:, 0:count] = ACCK[:, 0:count] + part_k
            GQKV[0, rows, cols] = (dot_nn(keys_t[:, :count], grad_scores) * score_scale).astype(BF)
        GQKV[1, rows, :] = ACCK[...].astype(BF)
        GQKV[2, rows, :] = ACCV[...].astype(BF)

        @pl.when(slot == 3)
        def _():
            first_join()

        return carry

    lax.fori_loop(first_slot, 5, attend_back, 0)

    for m in range(3):
        if m != 1:
            bias_sum = jnp.sum(GQKV[m].astype(F32), axis=1, keepdims=True)
        for h in range(2):
            total = dot_nt(GQKV[m, :, 0:T], N1[0, h]) + dot_nt(GQKV[m, :, T:S], N1[1, h])
            DQ[m, h, :, 0:H] = total.astype(BF)
            if m != 1:
                DQ[m, h, :, H : H + 1] = bias_sum.astype(BF)
        q1_push(0, m, m // 2, xdev, xb != m % 2)
        q1_push(1, m, 2 + m % 2, ydev, yb != m // 2)

    def wait_sends(tile, carry):
        part_copy(PGS, RCG, tile, s_g_core, r_g_core, core).wait_send()
        part_copy(OPS, RCO, tile, s_p_core, r_p_core, core).wait_send()
        part_copy(SZG, RZG, tile, s_g_z, r_g_z, zdev).wait_send()
        g2_copy(tile).wait_send()
        return carry

    lax.fori_loop(0, n_tiles, wait_sends, 0)
    r_n_core, r_n_z = recvs.take(n_tiles), recvs.take()
    s_n_core = sends.take(n_tiles)

    def back_rows(half, tile):
        all_cols = pl.ds(pl.multiple_of(tile * W, W), W)
        total = dot_tn(WB[0, half], GQKV[0, :, all_cols])
        for m in range(1, 3):
            total = total + dot_tn(WB[m, half], GQKV[m, :, all_cols])
        return total

    def first_part(tile, carry):
        t, cols = tile_at(tile)
        PGS[t, :, cols] = back_rows(oc, tile).astype(BF)
        part_copy(PGS, RCG, tile, s_n_core, r_n_core, core).start()
        OPS[t, :, cols] = back_rows(c, tile).astype(BF)
        return carry

    lax.fori_loop(0, n_tiles, first_part, 0)

    def wait_first(tile, carry):
        part_copy(PGS, RCG, tile, s_n_core, r_n_core, core).wait_recv()
        return carry

    lax.fori_loop(0, n_tiles, wait_first, 0)
    SZG[0] = (OPS[1 - zz].astype(F32) + RCG[1 - zz].astype(F32)).astype(BF)
    push(SZG.at[0], RZN, r_n_z, zdev)

    for entry in f1_entries:
        pending[:] = [other for other in pending if other is not entry]
    loads = []
    for h in range(2):
        arrived(rf2_hbm.at[h], r_f2 + h)
        loads.append(local(rf2_hbm.at[h], ff_part(*spare[2 * h])))
    r_zf = recvs.take(2)
    for h in range(2):
        done(loads[h])
        low = (
            FB[h, my_quarter, :].astype(F32) + FB[h, quarter_rows(spare[2 * h][1]), :].astype(F32)
        ).astype(BF)
        FB[h, my_quarter, :] = low
        if h == 0:

            @pl.when(first_core)
            def _():
                ZF[0] = low

        push(FB.at[h, my_quarter], ZF.at[1], r_zf + 1, (dp, z2, h), second_core)
        if h == 1:
            push(FB.at[h, my_quarter], ZF.at[0], r_zf, (dp, z, 1), first_core)

    arrived(RZO, r_out_z)
    branch_out = OPO[zz].astype(F32) + RCO[zz].astype(F32) + RZO[...].astype(F32)
    OPO[0] = (HID[zz, c] + branch_out + column(c, VEC_PROJ_BIAS)).astype(BF)
    l_out = local(OPO.at[0], out_o)

    for entry in q1_entries:
        sent(entry)
    q_spare = ((1 - xb, 0), (3 - xb, 0), (2 * (1 - yb), 1), (2 * (1 - yb) + 1, 1))
    q_kept = ((xb, 0), (2 + xb, 0), (2 * yb, 1), (2 * yb + 1, 1))
    loads = []
    for place in range(4):
        arrived(rq1_hbm.at[place], r_q1 + place)
        loads.append(local(rq1_hbm.at[place], DQ.at[q_spare[place][0], q_spare[place][1]]))
    for place in range(4):
        done(loads[place])
        (there, h), (here, unused) = q_spare[place], q_kept[place]
        DQ[here, h] = (DQ[here, h].astype(F32) + DQ[there, h].astype(F32)).astype(BF)
    push(DQ.at[xb + 2 * (1 - yb), 0], rq2_hbm.at[0], r_q2, ydev)
    push(DQ.at[2 * yb + 1 - xb, 1], rq2_hbm.at[1], r_q2 + 1, xdev)

    done(l_x2)
    arrived(RZN, r_n_z)
    r_stat = recvs.take()
    grads = OPS[zz].astype(F32) + RCG[zz].astype(F32) + RZN[...].astype(F32)
    center, inv_std = ST1[zz, 0:1, :], ST1[zz, 1:2, :]
    normals = (XG[zz, c].astype(F32) - center) * inv_std
    scaled = grads * column(c, VEC_LN1_GAIN)
    STX[c, 0:1, :] = jnp.sum(scaled, axis=0, keepdims=True)
    STX[c, 1:2, :] = jnp.sum(scaled * normals, axis=0, keepdims=True)
    push(STX.at[c], STX.at[c], r_stat, core)
    VGC[:, 0:1] = jnp.sum(grads * normals, axis=1, keepdims=True)
    VGC[:, 1:2] = jnp.sum(grads, axis=1, keepdims=True)
    arrived(STX.at[oc], r_stat)
    sums = (STX[0] + STX[1]) * inv_d
    OPO[1] = (GH[...] + inv_std * (scaled - sums[0:1] - normals * sums[1:2])).astype(BF)
    l_ing = local(OPO.at[1], ing_o)

    r_sp, r_spz = recvs.take(4), recvs.take(8)
    turned = VGC[...].T
    SPR[dp, 0:6, 0:H] = turned[0:6, :]
    for peer in peers:
        push(SPR.at[dp], SPR.at[dp], r_sp + dp, (peer, z, c))

    r_gf, r_gq = recvs.take(4), recvs.take(4)
    arrived(ZF.at[0], r_zf, second_core)
    arrived(ZF.at[1], r_zf + 1)
    ZF[0] = (ZF[0].astype(F32) + ZF[1].astype(F32)).astype(BF)
    l_gf = local(ZF.at[0], gf_o.at[my_quarter])
    for peer in peers:
        push(ZF.at[0], gf_o.at[my_quarter], r_gf + dp, (peer, z, c))

    loads = []
    for h in range(2):
        arrived(rq2_hbm.at[h], r_q2 + h)
        loads.append(local(rq2_hbm.at[h], DQ.at[q_spare[2 * h][0], h]))
    r_zq, r_zt = recvs.take(2), recvs.take(2)
    with_tail = (j < 3) & (dp < 3)
    next_block = jnp.minimum(j + 1, 3)
    for h in range(2):
        done(loads[h])
        low = (DQ[dp, h].astype(F32) + DQ[q_spare[2 * h][0], h].astype(F32)).astype(BF)
        DQ[dp, h] = low
        if h == 0:

            @pl.when(first_core)
            def _():
                ZQ[0] = low[0:R]

        push(DQ.at[dp, h, pl.ds(0, R)], ZQ.at[1], r_zq + 1, (dp, z2, h), second_core)
        if h == 1:
            push(DQ.at[dp, h, pl.ds(0, R)], ZQ.at[0], r_zq, (dp, z, 1), first_core)
        push(DQ.at[dp, h, pl.ds(R, TAIL)], ZT.at[c], r_zt + c, (dp, next_block, h), with_tail)

    for number in range(4):
        arrived(SPR.at[number], r_sp + number, dp != number)
    SPZ[z, c] = SPR[0] + SPR[1] + SPR[2] + SPR[3]
    for step in range(4):
        for side in range(2):
            if step == 0 and side == 0:
                continue
            target = (dp, lax.rem(z + step, 4), c if side == 0 else oc)
            push(SPZ.at[z, c], SPZ.at[z, c], r_spz + (2 * z + c), target)

    arrived(ZQ.at[0], r_zq, second_core)
    arrived(ZQ.at[1], r_zq + 1)
    gets_tail = (z >= 1) & (dp < 3)
    for side in range(2):
        arrived(ZT.at[side], r_zt + side, gets_tail)
    total = ZQ[0].astype(F32) + ZQ[1].astype(F32)
    ZQ[0] = total.astype(BF)

    @pl.when(gets_tail)
    def _():
        ZQ[0, 0:TAIL] = (total[0:TAIL] + ZT[0].astype(F32) + ZT[1].astype(F32)).astype(BF)

    l_gq = local(ZQ.at[0], gq_o.at[dp])
    for peer in peers:
        push(ZQ.at[0], gq_o.at[dp], r_gq + dp, (peer, z, c))

    for step in range(4):
        for side in range(2):
            if step == 0 and side == 0:
                continue
            zv, cv = lax.rem(z + step, 4), c if side == 0 else oc
            arrived(SPZ.at[zv, cv], r_spz + (2 * zv + cv))
    vectors = SPZ[0, c] + SPZ[1, c] + SPZ[2, c] + SPZ[3, c]
    VOUT[...] = vectors
    VOUT[6:7, :] = SPZ[z, 0, 6:7, :] + SPZ[z2, 1, 6:7, :]
    l_vec_o = local(VOUT, vec_o)

    for number in range(4):
        arrived(gf_o.at[pl.ds(number * quarter, quarter)], r_gf + number, dp != number)
        arrived(gq_o.at[number], r_gq + number, dp != number)
    for entry in (l_out, l_ing, l_gf, l_gq, l_vec_o):
        done(entry)

    def own_sends(slot):
        att_copy(j, slot, s_a_z, r_a_z, zdev).wait_send()
        att_copy(j, slot, s_a_core, r_a_core, core).wait_send()

    slots_of(j, own_sends)
    slots_of(
        owner_of(zp, c),
        lambda slot: att_copy(owner_of(zp, c), slot, s_a_fwd, r_a_fwd, core).wait_send(),
    )

    f2_copy(0).wait_send()
    f2_copy(1).wait_send()

    def last_sends(tile, carry):
        part_copy(PGS, RCG, tile, s_n_core, r_n_core, core).wait_send()
        return carry

    lax.fori_loop(0, n_tiles, last_sends, 0)
    for entry in list(pending):
        sent(entry)
    assert sends.used <= SEND_COUNT and recvs.used <= RECV_COUNT and locs.used <= LOCAL_COUNT


def finish_kernel(
    out_in,
    ing_in,
    gf_in,
    gq_in,
    vec_in,
    out_o,
    ing_o,
    qkv_o,
    qvb_o,
    ow_o,
    fc_o,
    proj_o,
    v0,
    v1,
    v2,
    v3,
    v4,
    v5,
    v6,
    GF,
    GQ,
    FST,
    QST,
    OB,
    SEM,
):
    R, H = ow_o.shape
    count = GF.shape[0] // R
    whole = [
        pltpu.make_async_copy(out_in, OB.at[0], SEM.at[0]),
        pltpu.make_async_copy(ing_in, OB.at[1], SEM.at[1]),
    ]
    place = 2
    loads_q, loads_f = [], []
    for m in range(4):
        loads_q.append(pltpu.make_async_copy(gq_in.at[m], GQ.at[m], SEM.at[place + m]))
    place += 4
    for number in range(count):
        rows = pl.ds(number * R, R)
        loads_f.append(pltpu.make_async_copy(gf_in.at[rows], GF.at[rows], SEM.at[place + number]))
    place += count
    for copy in loads_f + loads_q + whole:
        copy.start()
    stores = []
    for number in range(count):
        loads_f[number].wait()
        rows = pl.ds(number * R, R)
        FST[rows, :] = GF[rows, :].astype(F32)
        half = count // 2
        dst = (fc_o if number < half else proj_o).at[pl.ds(number % half * R, R)]
        stores.append(pltpu.make_async_copy(FST.at[rows], dst, SEM.at[place + number]))
        stores[-1].start()
    place += count
    for m in range(4):
        loads_q[m].wait()
        QST[m] = GQ[m, :, 0:H].astype(F32)
        dst = qkv_o.at[m] if m < 3 else ow_o
        stores.append(pltpu.make_async_copy(QST.at[m], dst, SEM.at[place + m]))
        stores[-1].start()
    place += 4
    for number, dst in enumerate((out_o, ing_o)):
        whole[number].wait()
        stores.append(pltpu.make_async_copy(OB.at[number], dst, SEM.at[place + number]))
        stores[-1].start()
    first = H // LANES * LANES
    for number, m in enumerate((0, 2)):
        turned = GQ[m, :, first : first + LANES].astype(F32).T
        qvb_o[number : number + 1, :] = turned[H - first : H - first + 1, :]
    for number, v in enumerate((v0, v1, v2, v3, v4, v5, v6)):
        v[...] = vec_in[number, 0 : v.shape[0]]
    for copy in stores:
        copy.wait()


def fast_body(
    tokens,
    ln1_gain,
    ln1_bias,
    qkv_weight,
    qv_bias,
    out_weight,
    out_bias,
    ln2_gain,
    ln2_bias,
    fc_weight,
    fc_bias,
    proj_weight,
    proj_bias,
    doc_lengths,
    cotangent,
):
    H, T = tokens.shape
    R = out_weight.shape[0]
    FW = fc_weight.shape[1]
    D, S = 2 * H, 2 * T
    HP = (H // LANES + 1) * LANES
    EXT = 5 * HEAD_DIM
    NT = S // KEY_TILE
    wide = (FW // LANES + 1) * LANES
    w3 = jnp.transpose(qkv_weight, (1, 2, 0))
    shape = jax.ShapeDtypeStruct
    anywhere = pl.BlockSpec(memory_space=pl.ANY)
    outs = [
        shape((H, T), BF),
        shape((H, T), BF),
        shape((2 * H, FW), BF),
        shape((4, R, HP), BF),
        shape((8, FW), F32),
        shape((4, D // 4, FW), BF),
        shape((2, D // 4, FW), BF),
        shape((4, EXT, HP), BF),
        shape((2, EXT, HP), BF),
    ]
    vmem = pltpu.VMEM
    mask_rows = KEY_TILE * NT * (NT + 1) // 2
    scratch = [
        vmem((2, 2, H, T), BF),
        vmem((2, 2, H, T), BF),
        vmem((2, 2, H, T), BF),
        vmem((3, 2, EXT, H), BF),
        vmem((EXT, LANES), F32),
        vmem((2, D, H), BF),
        vmem((2, 2 * H, FW), BF),
        vmem((FW, LANES), F32),
        vmem((2, 8, wide), F32),
        vmem((8, wide), F32),
        vmem((8, wide), F32),
        vmem((mask_rows, KEY_TILE), F32),
        vmem((3, EXT, S), BF),
        vmem((5, 8, S), F32),
        vmem((D, S), BF),
        vmem((2, 2, H, T), F32),
        vmem((2, 8, T), F32),
        vmem((2, 8, T), F32),
        vmem((2, 2, H, T), BF),
        vmem((FW, S), BF),
        vmem((FW, S), BF),
        vmem((2, H, T), BF),
        vmem((2, H, T), BF),
        vmem((2, H, T), BF),
        vmem((2, H, T), BF),
        vmem((2, H, T), BF),
        vmem((2, H, T), BF),
        vmem((2, H, T), BF),
        vmem((2, 2, H, T), BF),
        vmem((H, T), BF),
        vmem((H, T), BF),
        vmem((H, T), BF),
        vmem((EXT, S), BF),
        vmem((3, EXT, S), BF),
        vmem((HEAD_DIM, S), F32),
        vmem((HEAD_DIM, S), F32),
        vmem((2, 2 * H // 4, FW), BF),
        vmem((4, 2, EXT, HP), BF),
        vmem((2, R, HP), BF),
        vmem((2, EXT - R, HP), BF),
        vmem((H, T), F32),
        vmem((H, LANES), F32),
        vmem((2, 8, T), F32),
        vmem((4, 8, FW), F32),
        vmem((4, 2, 8, FW), F32),
        vmem((8, FW), F32),
        pltpu.SemaphoreType.DMA((SEND_COUNT,)),
        pltpu.SemaphoreType.DMA((RECV_COUNT,)),
        pltpu.SemaphoreType.DMA((LOCAL_COUNT,)),
    ]
    out_rows, in_rows, gf, gq, vectors = pl.pallas_call(
        layer_kernel,
        out_shape=outs,
        in_specs=[anywhere] * 6 + [pl.BlockSpec(memory_space=vmem)] * 9,
        out_specs=[anywhere] * len(outs),
        scratch_shapes=scratch,
        compiler_params=pltpu.CompilerParams(
            collective_id=0, has_side_effects=True, vmem_limit_bytes=VMEM_LIMIT
        ),
    )(
        tokens,
        cotangent,
        w3,
        out_weight,
        fc_weight,
        proj_weight,
        ln1_gain,
        ln1_bias,
        ln2_gain,
        ln2_bias,
        out_bias,
        proj_bias,
        fc_bias,
        qv_bias,
        doc_lengths,
    )[:5]
    in_vmem = pl.BlockSpec(memory_space=vmem)
    finals = pl.pallas_call(
        finish_kernel,
        out_shape=[
            shape((H, T), BF),
            shape((H, T), BF),
            shape((3, R, H), F32),
            shape((2, R), F32),
            shape((R, H), F32),
            shape((H, FW), F32),
            shape((H, FW), F32),
        ]
        + [shape((H,), F32)] * 6
        + [shape((FW,), F32)],
        in_specs=[anywhere] * 4 + [in_vmem],
        out_specs=[anywhere] * 3 + [in_vmem] + [anywhere] * 3 + [in_vmem] * 7,
        scratch_shapes=[
            vmem((D, FW), BF),
            vmem((4, R, HP), BF),
            vmem((D, FW), F32),
            vmem((4, R, H), F32),
            vmem((2, H, T), BF),
            pltpu.SemaphoreType.DMA((32,)),
        ],
        compiler_params=pltpu.CompilerParams(vmem_limit_bytes=VMEM_LIMIT),
    )(out_rows, in_rows, gf, gq, vectors)
    out_final, in_final, qkv_rows, bias_grad, ow_grad, fc_grad, proj_grad = finals[:7]
    ln1_gain_g, ln1_bias_g, ln2_gain_g, ln2_bias_g, out_bias_g, proj_bias_g, fc_bias_g = finals[7:]
    return (
        out_final,
        in_final,
        ln1_gain_g,
        ln1_bias_g,
        jnp.transpose(qkv_rows, (2, 0, 1)),
        bias_grad,
        ow_grad,
        out_bias_g,
        ln2_gain_g,
        ln2_bias_g,
        fc_grad,
        fc_bias_g,
        proj_grad,
        proj_bias_g,
    )


def choose_body(*arrays):
    sizes = {axis: lax.axis_size(axis) for axis in ("dp", "row", "col")}
    H, R = arrays[0].shape[0], arrays[5].shape[0]
    fits = sizes == {"dp": 4, "row": 4, "col": 2} and 4 * R == 2 * H == 17 * HEAD_DIM
    return (fast_body if fits else body)(*arrays)


def solution(mesh):
    return jax.shard_map(
        choose_body,
        mesh=mesh,
        in_specs=(
            P("col", ("dp", "row")),
            P("col"),
            P("col"),
            P("col", None, "row"),
            P(None, "row"),
            P("row", "col"),
            P("col"),
            P("col"),
            P("col"),
            P("col", "row"),
            P("row"),
            P("col", "row"),
            P("col"),
            P(("dp", "col"), None),
            P("col", ("dp", "row")),
        ),
        out_specs=(
            P("col", ("dp", "row")),
            P("col", ("dp", "row")),
            P("col"),
            P("col"),
            P("col", None, "row"),
            P(None, "row"),
            P("row", "col"),
            P("col"),
            P("col"),
            P("col"),
            P("col", "row"),
            P("row"),
            P("col", "row"),
            P("col"),
        ),
        check_vma=False,
    )
```

```python
from functools import partial
import math

import jax
import jax.numpy as jnp
from jax import lax
from jax.experimental import pallas as pl
from jax.experimental.pallas import tpu as pltpu
from jax.sharding import PartitionSpec as P

HEAD_DIM = 64


epsilon = 1e-05
score_scale = 0.125
masked_fill = -1e30
block_limit = 512


def feature_sums(first_sum, second_sum):
    return lax.psum((first_sum, second_sum), "col")


def norm_forward(values, gain_vec, shift_vec):
    feature_count = values.shape[1] * lax.axis_size("col")
    total_sum, square_sum = feature_sums(jnp.sum(values, axis=1), jnp.sum(values * values, axis=1))
    center = total_sum / feature_count
    spread = square_sum / feature_count - center * center
    inv_std = lax.rsqrt(spread + epsilon)
    normal = (values - center[:, None]) * inv_std[:, None]
    return (normal, inv_std, normal * gain_vec + shift_vec)


def norm_backward(upstream, normal, inv_std, gain_vec):
    feature_count = upstream.shape[1] * lax.axis_size("col")
    scaled = upstream * gain_vec
    plain_sum, cross_sum = feature_sums(jnp.sum(scaled, axis=1), jnp.sum(scaled * normal, axis=1))
    return inv_std[:, None] * (
        scaled - plain_sum[:, None] / feature_count - normal * (cross_sum[:, None] / feature_count)
    )


def gather_rows(values):
    return lax.all_gather(values, "row", axis=0, tiled=True)


def gather_cols(values):
    return lax.all_gather(values, "col", axis=0, tiled=True)


def sum_over_rows(row_term, row_total):
    return lax.psum_scatter(
        row_term(jnp.int32(0), row_total * lax.axis_size("row")),
        "row",
        scatter_dimension=0,
        tiled=True,
    )


def sum_over_cols(row_term, row_total):
    return lax.psum_scatter(
        row_term(jnp.int32(0), row_total * lax.axis_size("col")),
        "col",
        scatter_dimension=0,
        tiled=True,
    )


def to_heads(values):
    return lax.all_to_all(values, "row", split_axis=0, concat_axis=2, tiled=True)


def to_tokens(values):
    return lax.all_to_all(values, "row", split_axis=2, concat_axis=0, tiled=True)


def product_term(full_rows, matrix):

    def row_term(first_row, row_count):
        return jnp.dot(full_rows, matrix, preferred_element_type=jnp.float32)

    return row_term


def product_term_back(full_rows, matrix):

    def row_term(first_row, row_count):
        return lax.dot_general(
            full_rows, matrix, (((1,), (1,)), ((), ())), preferred_element_type=jnp.float32
        )

    return row_term


def slice_term(full_rows):

    def row_term(first_row, row_count):
        return full_rows

    return row_term


def inner_rows(left_side, right_side):
    return lax.dot_general(
        left_side, right_side, (((0,), (0,)), ((), ())), preferred_element_type=jnp.float32
    )


def segments_of(lengths, places):
    doc_ends = jnp.cumsum(lengths)
    segment = jnp.sum(
        (doc_ends[None, :] <= places[:, None]).astype(jnp.int32), axis=1, dtype=jnp.int32
    )
    return (segment, places >= doc_ends[-1])


def allowed_pairs(query_place, query_segment, query_padding, key_place, key_segment):
    causal = key_place[None, :] <= query_place[:, None]
    same_doc = key_segment[None, :] == query_segment[:, None]
    itself = key_place[None, :] == query_place[:, None]
    return causal & same_doc & (jnp.logical_not(query_padding)[:, None] | itself)


def attention_parts(queries, keyvals, lengths, query_place):
    seq_total = keyvals.shape[0]
    key_block_size = math.gcd(seq_total, block_limit)
    block_count = seq_total // key_block_size
    key_place = jnp.arange(seq_total, dtype=jnp.int32)
    key_segment = segments_of(lengths, key_place)[0]
    query_segment, query_padding = segments_of(lengths, query_place)
    blocked = (
        keyvals.reshape((block_count, key_block_size) + keyvals.shape[1:]),
        key_place.reshape(block_count, key_block_size),
        key_segment.reshape(block_count, key_block_size),
    )

    def block_scores(key_rows, place_rows, segment_rows):
        raw_scores = (
            jnp.einsum("qhd,khd->hqk", queries, key_rows, preferred_element_type=jnp.float32)
            * score_scale
        )
        allowed = allowed_pairs(
            query_place, query_segment, query_padding, place_rows, segment_rows
        )[None]
        return (raw_scores, allowed)

    return (blocked, block_scores)


def attention_forward(queries, blocked, block_scores):
    query_count, head_count, head_width = queries.shape

    def max_step(running, inputs):
        best_score, mass_sum = running
        kv_block, place_rows, segment_rows = inputs
        raw_scores, allowed = block_scores(kv_block[:, 0], place_rows, segment_rows)
        masked = jnp.where(allowed, raw_scores, masked_fill)
        new_best = jnp.maximum(best_score, jnp.max(masked, axis=2))
        fresh = jnp.sum(jnp.where(allowed, jnp.exp(masked - new_best[:, :, None]), 0.0), axis=2)
        return ((new_best, mass_sum * jnp.exp(best_score - new_best) + fresh), None)

    start_best = jnp.full((head_count, query_count), masked_fill, jnp.float32)
    start_mass = jnp.zeros((head_count, query_count), jnp.float32)
    (best_score, mass_sum), unused = lax.scan(max_step, (start_best, start_mass), blocked)
    log_sum = best_score + jnp.log(mass_sum)

    def out_step(running, inputs):
        kv_block, place_rows, segment_rows = inputs
        raw_scores, allowed = block_scores(kv_block[:, 0], place_rows, segment_rows)
        probs_low = jnp.where(allowed, jnp.exp(raw_scores - log_sum[:, :, None]), 0.0).astype(
            jnp.bfloat16
        )
        return (
            running
            + jnp.einsum(
                "hqk,khd->qhd", probs_low, kv_block[:, 1], preferred_element_type=jnp.float32
            ),
            None,
        )

    attended, unused = lax.scan(
        out_step, jnp.zeros((query_count, head_count, head_width), jnp.float32), blocked
    )
    return (attended, log_sum)


def attention_backward(queries, blocked, block_scores, log_sum, grad_attended):
    query_count, head_count, head_width = queries.shape

    def probs_and_grads(inputs):
        kv_block, place_rows, segment_rows = inputs
        raw_scores, allowed = block_scores(kv_block[:, 0], place_rows, segment_rows)
        probs_f = jnp.where(allowed, jnp.exp(raw_scores - log_sum[:, :, None]), 0.0)
        grad_probs = jnp.einsum(
            "qhd,khd->hqk", grad_attended, kv_block[:, 1], preferred_element_type=jnp.float32
        )
        return (probs_f, grad_probs)

    def delta_step(running, inputs):
        probs_f, grad_probs = probs_and_grads(inputs)
        return (running + jnp.sum(probs_f * grad_probs, axis=2), None)

    delta_sum, unused = lax.scan(
        delta_step, jnp.zeros((head_count, query_count), jnp.float32), blocked
    )

    def grad_step(running, inputs):
        kv_block = inputs[0]
        probs_f, grad_probs = probs_and_grads(inputs)
        grad_scores = (probs_f * (grad_probs - delta_sum[:, :, None])).astype(jnp.bfloat16)
        running = running + jnp.einsum(
            "hqk,khd->qhd", grad_scores, kv_block[:, 0], preferred_element_type=jnp.float32
        )
        grad_keys = (
            jnp.einsum("hqk,qhd->khd", grad_scores, queries, preferred_element_type=jnp.float32)
            * score_scale
        )
        grad_values = jnp.einsum(
            "hqk,qhd->khd",
            probs_f.astype(jnp.bfloat16),
            grad_attended,
            preferred_element_type=jnp.float32,
        )
        return (running, jnp.stack([grad_keys, grad_values], axis=1))

    grad_queries, grad_keyvals = lax.scan(
        grad_step, jnp.zeros((query_count, head_count, head_width), jnp.float32), blocked
    )
    seq_total = grad_keyvals.shape[0] * grad_keyvals.shape[1]
    return (grad_queries * score_scale, grad_keyvals.reshape(seq_total, 2, head_count, head_width))


def body(
    tokens,
    ln1_gain,
    ln1_bias,
    qkv_weight,
    qv_bias,
    out_weight,
    out_bias,
    ln2_gain,
    ln2_bias,
    fc_weight,
    fc_bias,
    proj_weight,
    proj_bias,
    doc_lengths,
    cotangent,
):
    count_rows = lax.axis_size("row")
    count_cols = lax.axis_size("col")
    grid_rows = tokens.shape[1]
    col_width = tokens.shape[0]
    row_width = out_weight.shape[0]
    seq_rows = grid_rows * count_rows // count_cols
    query_rows = seq_rows // count_rows
    full_width = col_width * count_cols
    head_count = full_width // HEAD_DIM
    tokens_f = tokens.astype(jnp.float32).T
    normal1, inv_std1, shaped1 = norm_forward(tokens_f, ln1_gain, ln1_bias)
    qkv_flat = qkv_weight.reshape(col_width, 3 * row_width)
    gathered1 = gather_rows(shaped1.astype(jnp.bfloat16))
    mixed_qkv = sum_over_cols(product_term(gathered1, qkv_flat), seq_rows).reshape(
        seq_rows, 3, row_width
    )
    bias_three = jnp.stack([qv_bias[0], jnp.zeros_like(qv_bias[0]), qv_bias[1]])
    qkv_low = (mixed_qkv + bias_three).astype(jnp.bfloat16)
    local_qkv = to_heads(qkv_low).reshape(query_rows, 3, head_count, HEAD_DIM)
    queries = local_qkv[:, 0]
    keyvals = lax.all_gather(local_qkv[:, 1:], "row", axis=0, tiled=True)
    query_place = lax.axis_index("row") * query_rows + jnp.arange(query_rows, dtype=jnp.int32)
    blocked, block_scores = attention_parts(queries, keyvals, doc_lengths[0], query_place)
    attended_f, log_sum = attention_forward(queries, blocked, block_scores)
    attended_low = attended_f.reshape(query_rows, 1, full_width).astype(jnp.bfloat16)
    attended_grid = to_tokens(attended_low).reshape(seq_rows, row_width)
    gathered_att = gather_cols(attended_grid)
    branch = sum_over_rows(product_term(gathered_att, out_weight), grid_rows)
    hidden = tokens_f + (branch + out_bias)
    normal2, inv_std2, shaped2 = norm_forward(hidden, ln2_gain, ln2_bias)
    normed2 = shaped2.astype(jnp.bfloat16)
    gathered2 = gather_rows(normed2)
    pre_act = sum_over_cols(product_term(gathered2, fc_weight), seq_rows) + fc_bias
    active = jax.nn.gelu(pre_act, approximate=False).astype(jnp.bfloat16)
    gathered_act = gather_cols(active)
    projected = sum_over_rows(product_term_back(gathered_act, proj_weight), grid_rows)
    output = (hidden + projected + proj_bias).astype(jnp.bfloat16).T
    cotangent_rows = cotangent.T
    grad_out = cotangent_rows.astype(jnp.float32)
    unused, gelu_back = jax.vjp(partial(jax.nn.gelu, approximate=False), pre_act)
    grad_gathered = gather_rows(cotangent_rows)
    proj_weight_grad = inner_rows(grad_gathered, gathered_act)
    proj_bias_grad = jnp.sum(grad_gathered, axis=0, dtype=jnp.float32)
    grad_active = sum_over_cols(product_term(grad_gathered, proj_weight), seq_rows)
    grad_pre = gelu_back(grad_active)[0].astype(jnp.bfloat16)
    grad_pre_all = gather_cols(grad_pre)
    fc_weight_grad = inner_rows(gathered2, grad_pre_all)
    fc_bias_grad = jnp.sum(grad_pre_all, axis=0, dtype=jnp.float32)
    grad_normed2 = sum_over_rows(product_term_back(grad_pre_all, fc_weight), grid_rows)
    ln2_gain_part = jnp.sum(grad_normed2 * normal2, axis=0)
    ln2_bias_part = jnp.sum(grad_normed2, axis=0)
    grad_hidden = grad_out + norm_backward(grad_normed2, normal2, inv_std2, ln2_gain)
    branch_gathered = gather_rows(grad_hidden.astype(jnp.bfloat16))
    out_weight_grad = inner_rows(gathered_att, branch_gathered)
    out_bias_grad = jnp.sum(branch_gathered, axis=0, dtype=jnp.float32)
    grad_att_grid = sum_over_cols(product_term_back(branch_gathered, out_weight), seq_rows).astype(
        jnp.bfloat16
    )
    grad_attended = to_heads(grad_att_grid.reshape(seq_rows, 1, row_width)).reshape(
        query_rows, head_count, HEAD_DIM
    )
    grad_queries, grad_keyvals = attention_backward(
        queries, blocked, block_scores, log_sum, grad_attended
    )
    keyval_rows = sum_over_rows(slice_term(grad_keyvals), query_rows)
    grad_qkv_local = (
        jnp.concatenate([grad_queries[:, None], keyval_rows], axis=1)
        .astype(jnp.bfloat16)
        .reshape(query_rows, 3, full_width)
    )
    grad_qkv_grid = to_tokens(grad_qkv_local).reshape(seq_rows, 3 * row_width)
    qkv_gathered = gather_cols(grad_qkv_grid)
    qkv_weight_grad = inner_rows(gathered1, qkv_gathered).reshape(col_width, 3, row_width)
    qkv_bias_sums = jnp.sum(qkv_gathered, axis=0, dtype=jnp.float32).reshape(3, row_width)
    qv_bias_grad = jnp.stack([qkv_bias_sums[0], qkv_bias_sums[2]])
    grad_normed1 = sum_over_rows(product_term_back(qkv_gathered, qkv_flat), grid_rows)
    ln1_gain_part = jnp.sum(grad_normed1 * normal1, axis=0)
    ln1_bias_part = jnp.sum(grad_normed1, axis=0)
    input_grad = (
        (grad_hidden + norm_backward(grad_normed1, normal1, inv_std1, ln1_gain))
        .astype(jnp.bfloat16)
        .T
    )
    summed = lax.psum(
        (
            qkv_weight_grad,
            qv_bias_grad,
            out_weight_grad,
            out_bias_grad,
            fc_weight_grad,
            fc_bias_grad,
            proj_weight_grad,
            proj_bias_grad,
        ),
        "dp",
    )
    gain_sums = lax.psum(
        (ln1_gain_part, ln1_bias_part, ln2_gain_part, ln2_bias_part), ("dp", "row")
    )
    return (
        output,
        input_grad,
        gain_sums[0],
        gain_sums[1],
        summed[0],
        summed[1],
        summed[2],
        summed[3],
        gain_sums[2],
        gain_sums[3],
        summed[4],
        summed[5],
        summed[6],
        summed[7],
    )


BF = jnp.bfloat16
F32 = jnp.float32
MESH = pl.DeviceIdType.MESH
LANES = 128
KEY_TILE = 256
VEC_LN1_GAIN, VEC_LN1_BIAS, VEC_LN2_GAIN, VEC_LN2_BIAS, VEC_OUT_BIAS, VEC_PROJ_BIAS = range(6)


def dot_nn(left, right):
    return lax.dot_general(left, right, (((1,), (0,)), ((), ())), preferred_element_type=F32)


def dot_tn(left, right):
    return lax.dot_general(left, right, (((0,), (0,)), ((), ())), preferred_element_type=F32)


def dot_nt(left, right):
    return lax.dot_general(left, right, (((1,), (1,)), ((), ())), preferred_element_type=F32)


VMEM_LIMIT = 66_000_000


class Slots:
    def __init__(self):
        self.used = 0

    def take(self, count=1):
        first = self.used
        self.used += count
        return first


SEND_COUNT, RECV_COUNT, LOCAL_COUNT = 176, 192, 48


def layer_kernel(
    x_in,
    cot_in,
    w3_in,
    ow_in,
    fc_in,
    proj_in,
    ln1_gain_in,
    ln1_bias_in,
    ln2_gain_in,
    ln2_bias_in,
    out_bias_in,
    proj_bias_in,
    fc_bias_in,
    qv_bias_in,
    doc_in,
    out_o,
    ing_o,
    gf_o,
    gq_o,
    vec_o,
    rf1_hbm,
    rf2_hbm,
    rq1_hbm,
    rq2_hbm,
    XG,
    CG,
    N1,
    WB,
    QB,
    OWB,
    FB,
    COLS,
    PACK,
    PACKF,
    PACKN,
    MASK,
    QKV,
    LSE,
    ATT,
    HID,
    ST1,
    ST2,
    N2,
    ACT,
    GPRE,
    PGS,
    OPS,
    RCG,
    RCO,
    OPO,
    SZG,
    RZG,
    G2,
    SZO,
    RZO,
    RZN,
    DATT,
    GQKV,
    ACCK,
    ACCV,
    ZF,
    DQ,
    ZQ,
    ZT,
    GH,
    VGC,
    STX,
    SPR,
    SPZ,
    VOUT,
    SS,
    RS,
    LS,
):
    H, T = x_in.shape
    R = w3_in.shape[1]
    HP = DQ.shape[3]
    EXT = WB.shape[2]
    TAIL = EXT - R
    D = 2 * H
    S = 2 * T
    W = KEY_TILE
    Q = HEAD_DIM
    FW = fc_in.shape[1]
    per_tok = T // W
    n_tiles = S // W
    inv_d = 1.0 / D

    dp, z, c = lax.axis_index("dp"), lax.axis_index("row"), lax.axis_index("col")
    oc = 1 - c
    zz = lax.rem(z, 2)
    zp = z + 1 - 2 * zz
    z2 = lax.rem(z + 2, 4)
    j = lax.rem(z + 2 * c, 4)
    pair = z // 2
    core = (dp, z, oc)
    zdev = (dp, zp, c)
    xn = dp + 1 - 2 * lax.rem(dp, 2)
    yn = lax.rem(dp + 2, 4)
    dg = 3 - dp
    peers = (dg, xn, yn)
    xb, yb = lax.rem(dp, 2), dp // 2
    xdev, ydev = (xn, z, c), (yn, z, c)
    first_core, second_core = c == 0, c == 1

    sends, recvs, locs = Slots(), Slots(), Slots()
    pending = []

    def remote(src, dst, s_idx, r_idx, dev):
        return pltpu.make_async_remote_copy(
            src_ref=src,
            dst_ref=dst,
            send_sem=SS.at[s_idx],
            recv_sem=RS.at[r_idx],
            device_id=dev,
            device_id_type=MESH,
        )

    def when(cond, fn):
        if cond is None:
            fn()
        else:
            pl.when(cond)(fn)

    def push(src, dst, r_idx, dev, cond=None):
        copy = remote(src, dst, sends.take(), r_idx, dev)
        when(cond, copy.start)
        entry = [cond, copy]
        pending.append(entry)
        return entry

    def sent(entry):
        when(entry[0], entry[1].wait_send)
        pending[:] = [other for other in pending if other is not entry]

    def arrived(dst, r_idx, cond=None):
        when(cond, remote(dst, dst, 0, r_idx, core).wait_recv)

    def local(src, dst, cond=None):
        copy = pltpu.make_async_copy(src, dst, LS.at[locs.take()])
        when(cond, copy.start)
        return (cond, copy)

    def done(entry):
        when(entry[0], entry[1].wait)

    barrier = pltpu.get_barrier_semaphore()
    for step in range(4):
        for side in range(2):
            if step == 0 and side == 0:
                continue
            target = (dp, lax.rem(z + step, 4), c if side == 0 else oc)
            pl.semaphore_signal(barrier, inc=1, device_id=target, device_id_type=MESH)
    for peer in peers:
        pl.semaphore_signal(barrier, inc=1, device_id=(peer, z, c), device_id_type=MESH)
    pl.semaphore_wait(barrier, 10)

    r_x_core, r_x_z, r_x_fwd = recvs.take(), recvs.take(), recvs.take()
    r_w_core, r_w_z, r_w_xy, r_w_tail = recvs.take(), recvs.take(16), recvs.take(8), recvs.take(2)
    r_pack, r_packf, r_packn = recvs.take(), recvs.take(), recvs.take()
    r_f_core, r_f_z, r_f_xy = recvs.take(2), recvs.take(4), recvs.take(8)
    r_o_core, r_o_z, r_o_z0, r_o_xy, r_o_fwd = (
        recvs.take(),
        recvs.take(4),
        recvs.take(4),
        recvs.take(16),
        recvs.take(4),
    )

    def block(number):
        return pl.ds(pl.multiple_of(number * R, 16), R)

    quarter = D // 4
    odd = R - 4 * (R // 64) * 16
    piece = R // 64 * 16

    def quarter_rows(number):
        return pl.ds(pl.multiple_of(number * quarter, 16), quarter)

    def ow_piece(number, plane):
        return pl.ds(pl.multiple_of(number * R + odd + plane * piece, 16), piece)

    def ow_odd(number):
        return pl.ds(pl.multiple_of(number * R, 16), odd)

    my_quarter = quarter_rows(dp)
    more = H // 16 % 4
    share = H // 64 * 16

    def ff_share(plane, large):
        if large:
            return pl.ds(pl.multiple_of(plane * (share + 16), 16), share + 16)
        return pl.ds(pl.multiple_of(more * 16 + plane * share, 16), share)

    ff_kinds = ((True, dp < more), (False, dp >= more))
    w_pieces, row = [], 0
    for plane in range(4):
        left = (3 * R // 16 // 4 + (1 if plane < 3 * R // 16 % 4 else 0)) * 16
        while left:
            rows = min(left, R - row % R)
            w_pieces.append((plane, row // R, row % R, rows))
            row, left = row + rows, left - rows
    has_before = z >= 1
    bias_first = (LANES, LANES + (R // LANES + 1) * LANES)
    doc_count = doc_in.shape[1]
    w_entries = []
    for number, (plane, m, first, size) in enumerate(w_pieces):
        rows = pl.ds(first, size)
        w_entries.append(
            push(
                w3_in.at[m, rows], WB.at[m, c, rows], r_w_z + (2 * number + c), (dp, z2, 1), dp == plane
            )
        )
    pack = PACK.at[c]
    PACK[c] = jnp.zeros(PACK.shape[1:], F32)
    vectors_in = (ln1_gain_in, ln1_bias_in, ln2_gain_in, ln2_bias_in, out_bias_in, proj_bias_in, fc_bias_in)
    for number, vector in enumerate(vectors_in):
        PACK[c, number : number + 1, 0 : vector.shape[0]] = vector[...].astype(F32).reshape(1, -1)
    PACK[c, 7:8, 0:doc_count] = doc_in[...].astype(F32)
    for number in range(2):
        PACK[c, 7:8, bias_first[number] : bias_first[number] + R] = qv_bias_in[number : number + 1, :].astype(F32)
    push(x_in, XG.at[zz, c], r_x_z, zdev)
    push(x_in, XG.at[zz, c], r_x_core, core)
    push(pack, pack, r_pack, core)
    push(w3_in, WB.at[:, 1, pl.ds(0, R)], r_w_core, (dp, z, 0), second_core)
    push(w3_in.at[:, pl.ds(0, TAIL)], WB.at[:, c, pl.ds(R, TAIL)], r_w_tail + c, (dp, jnp.maximum(z - 1, 0), 0), has_before)
    push(w3_in.at[:, pl.ds(0, TAIL)], WB.at[:, c, pl.ds(R, TAIL)], r_w_tail + c, (dp, lax.rem(z + 1, 4), 1), has_before)
    push(pack, PACKF, r_packf, (dp, z2, 1), first_core)
    push(pack, PACKN, r_packn, (dp, jnp.maximum(z - 1, 0), 0), has_before & first_core)
    push(pack, PACKN, r_packn, (dp, lax.rem(z + 1, 4), 1), has_before & first_core)
    l_x = local(x_in, XG.at[zz, c])
    l_w = local(w3_in, WB.at[:, 0, pl.ds(0, R)], first_core)
    push(fc_in, FB.at[0, 1], r_f_core, (dp, z, 0), second_core)
    push(proj_in, FB.at[1, 1], r_f_core + 1, (dp, z, 0), second_core)
    push(ow_in, OWB.at[c, block(z)], r_o_core, core)
    l_f = local(fc_in, FB.at[0, 0], first_core)
    l_p = local(proj_in, FB.at[1, 0], first_core)
    l_o = local(ow_in, OWB.at[c, block(z)])

    ff_entries = []

    def send_ff(kind):
        source = (fc_in, proj_in)[kind]
        for large, cond in ff_kinds:
            rows = ff_share(dp, large)
            push(source.at[rows], FB.at[kind, c, rows], r_f_z + (2 * kind + c), (dp, z2, 1), cond)

    def pass_ff(kind):
        for large, cond in ff_kinds:
            rows = ff_share(dp, large)
            for h in range(2):
                arrived(FB.at[kind, h, rows], r_f_z + (2 * kind + h), second_core & cond)
            part = FB.at[kind, :, rows]
            for peer in peers:
                ff_entries.append(
                    push(part, part, r_f_xy + (4 * kind + dp), (peer, z, 1), second_core & cond)
                )

    def ff_ready(kind):
        arrived(FB.at[kind, 1], r_f_core + kind, first_core)
        for plane in range(4):
            arrived(
                FB.at[kind, :, ff_share(plane, plane < more)],
                r_f_xy + (4 * kind + plane),
                second_core & (dp != plane),
            )

    for entry in w_entries:
        sent(entry)
    send_ff(0)

    VGC[...] = jnp.zeros_like(VGC)
    GQKV[...] = jnp.zeros_like(GQKV)

    def clear_tail():
        WB[:, :, R:, :] = jnp.zeros((3, 2, TAIL, H), BF)

    pl.when(j == 3)(clear_tail)

    arrived(PACK.at[oc], r_pack)
    lengths = PACK[pair, 7:8, 0:LANES]
    place_c = lax.broadcasted_iota(jnp.int32, (S, LANES), 0).astype(F32)
    place_r = lax.broadcasted_iota(jnp.int32, (8, S), 1).astype(F32)
    end = jnp.zeros((1, 1), F32)
    seg_c, seg_r = jnp.zeros_like(place_c), jnp.zeros_like(place_r)
    for number in range(doc_count):
        end = end + lengths[:, number : number + 1]
        seg_c = seg_c + jnp.where(end <= place_c, 1.0, 0.0)
        seg_r = seg_r + jnp.where(end <= place_r, 1.0, 0.0)
    seg_c = jnp.where(end <= place_c, place_c + 2.0 * S, seg_c)
    seg_r = jnp.where(end <= place_r, place_r + 2.0 * S, seg_r)
    for tile in range(n_tiles):
        rows = W * (tile + 1)
        first = W * tile * (tile + 1) // 2
        cols = slice(tile * W, (tile + 1) * W)
        key_seg = jnp.concatenate([seg_c[:rows]] * (W // LANES), axis=1)
        key_place = jnp.concatenate([place_c[:rows]] * (W // LANES), axis=1)
        ok = (key_seg == seg_r[0:1, cols]) & (key_place <= place_r[0:1, cols])
        MASK[first : first + rows, :] = jnp.where(ok, 0.0, masked_fill)

    for h in range(2):
        COLS[h * H : (h + 1) * H, 0:6] = PACK[h].T[0:H, 0:6]

    def column(h, which):
        if isinstance(h, int):
            return COLS[h * H : (h + 1) * H, which : which + 1]
        return COLS[pl.ds(pl.multiple_of(h * H, 16), H), which : which + 1]

    def stats_of(first_half, second_half):
        center = (
            jnp.sum(first_half, axis=0, keepdims=True) + jnp.sum(second_half, axis=0, keepdims=True)
        ) * inv_d
        square = (
            jnp.sum(first_half * first_half, axis=0, keepdims=True)
            + jnp.sum(second_half * second_half, axis=0, keepdims=True)
        ) * inv_d
        return center, lax.rsqrt(square - center * center + epsilon)

    def first_norm(t):
        halves = [XG[t, h].astype(F32) for h in range(2)]
        center, inv_std = stats_of(*halves)
        ST1[t, 0:1, :] = center
        ST1[t, 1:2, :] = inv_std
        for h in range(2):
            shaped = (halves[h] - center) * inv_std * column(h, VEC_LN1_GAIN) + column(
                h, VEC_LN1_BIAS
            )
            N1[t, h, 0:H, :] = shaped.astype(BF)

    done(l_x)
    arrived(XG.at[zz, oc], r_x_core)
    first_norm(zz)

    for number, (plane, m, first, size) in enumerate(w_pieces):
        cond = second_core & (dp == plane)
        rows = pl.ds(first, size)
        for h in range(2):
            arrived(WB.at[m, h, rows], r_w_z + (2 * number + h), cond)
        for peer in peers:
            push(WB.at[m, :, rows], WB.at[m, :, rows], r_w_xy + number, (peer, z, 1), cond)
    arrived(XG.at[1 - zz, c], r_x_z)
    e_xf = push(XG.at[1 - zz, c], XG.at[1 - zz, c], r_x_fwd, core)
    arrived(XG.at[1 - zz, oc], r_x_fwd)
    first_norm(1 - zz)

    done(l_w)
    pass_ff(0)
    for step in (1, 3, 2):
        target = (dp, lax.rem(z + step, 4), c)
        push(ow_in.at[ow_piece(0, dp)], OWB.at[c, ow_piece(z, dp)], r_o_z + z, target)
        push(ow_in.at[ow_odd(0)], OWB.at[c, ow_odd(z)], r_o_z0 + z, target)
    arrived(WB.at[:, 1, pl.ds(0, R)], r_w_core, first_core)
    for number, (plane, m, first, size) in enumerate(w_pieces):
        arrived(WB.at[m, :, pl.ds(first, size)], r_w_xy + number, second_core & (dp != plane))
    for h in range(2):
        arrived(WB.at[:, h, pl.ds(R, TAIL)], r_w_tail + h, j < 3)

    arrived(PACKF, r_packf, second_core)
    arrived(PACKN, r_packn, j < 3)

    def bias_columns(source, rows, count):
        turned = source.T
        for m, first in ((0, bias_first[0]), (2, bias_first[1])):
            QB[rows : rows + count, m : m + 1] = turned[first : first + count, 7:8]

    QB[...] = jnp.zeros_like(QB)
    pl.when(first_core)(lambda: bias_columns(PACK[0], 0, R))
    pl.when(second_core)(lambda: bias_columns(PACKF[...], 0, R))
    pl.when(j < 3)(lambda: bias_columns(PACKN[...], R, TAIL))

    for t in range(2):
        for m in range(3):
            mixed = dot_nn(WB[m, 0], N1[t, 0]) + dot_nn(WB[m, 1], N1[t, 1])
            if m != 1:
                mixed = mixed + QB[:, m : m + 1]
            low = mixed.astype(BF)
            if m == 0:
                low = low * jnp.asarray(score_scale, BF)
            QKV[m, :, t * T : (t + 1) * T] = low

    send_ff(1)

    r_a_z, r_a_core, r_a_fwd = recvs.take(5), recvs.take(5), recvs.take(5)
    s_a_z, s_a_core, s_a_fwd = sends.take(5), sends.take(5), sends.take(5)
    first_slot = jnp.where(j == 0, 0, 1)

    def head_rows(owner, slot):
        return pl.ds(pl.multiple_of(owner * (4 * Q) + slot * Q, Q), Q)

    def slot_rows(slot):
        return pl.ds(pl.multiple_of(slot * Q - 16 * j, 16), Q)

    def att_copy(owner, slot, s_base, r_base, dev):
        rows = head_rows(owner, slot)
        return remote(ATT.at[rows], ATT.at[rows], s_base + slot, r_base + slot, dev)

    s_o_xy = sends.take(9)

    def ow_copy(step, number):
        there = lax.rem(z + step, 4)
        rows = OWB.at[c, ow_piece(there, dp)]
        return remote(
            rows, rows, s_o_xy + (3 * (step - 1) + number), r_o_xy + (4 * dp + there), (peers[number], z, c)
        )

    def pass_ow():
        for step in (1, 3, 2):
            there = lax.rem(z + step, 4)
            arrived(OWB.at[c, ow_piece(there, dp)], r_o_z + there)
            for number in range(3):
                ow_copy(step, number).start()

    def attend(slot, carry):
        @pl.when(slot == 2)
        def _():
            pass_ow()

        rows = slot_rows(slot)
        out_rows = head_rows(j, slot)
        queries = QKV[0, rows, :]
        keys = QKV[1, rows, :].T
        values = QKV[2, rows, :]
        for tile in range(n_tiles):
            count = W * (tile + 1)
            first = W * tile * (tile + 1) // 2
            cols = slice(tile * W, (tile + 1) * W)
            scores = dot_nn(keys[:count], queries[:, cols]) + MASK[first : first + count, :]
            best = jnp.max(scores, axis=0, keepdims=True)
            weights = jnp.exp(scores - best)
            mass = jnp.sum(weights, axis=0, keepdims=True)
            probs_low = (weights * (1.0 / mass)).astype(BF)
            ATT[out_rows, cols] = dot_nn(values[:, :count], probs_low).astype(BF)
            LSE[slot, 0:1, cols] = best + jnp.log(mass)
        att_copy(j, slot, s_a_z, r_a_z, zdev).start()
        att_copy(j, slot, s_a_core, r_a_core, core).start()

        return carry

    lax.fori_loop(first_slot, 5, attend, 0)

    r_c_core, r_c_z, r_c_fwd = recvs.take(), recvs.take(), recvs.take()
    push(cot_in, CG.at[zz, c], r_c_z, zdev)
    push(cot_in, CG.at[zz, c], r_c_core, core)
    l_c = local(cot_in, CG.at[zz, c])

    pass_ff(1)

    for step in (1, 3, 2):
        there = lax.rem(z + step, 4)
        arrived(OWB.at[c, ow_odd(there)], r_o_z0 + there)
        for plane in range(4):
            arrived(OWB.at[c, ow_piece(there, plane)], r_o_xy + (4 * plane + there), dp != plane)
        push(OWB.at[c, block(there)], OWB.at[c, block(there)], r_o_fwd + there, core)

    def owner_of(zv, cv):
        return lax.rem(zv + 2 * cv, 4)

    def slots_of(owner, body):
        lax.fori_loop(jnp.where(owner == 0, 0, 1), 5, lambda slot, carry: (body(slot), carry)[1], 0)

    def pass_on(slot):
        att_copy(owner_of(zp, c), slot, s_a_fwd, r_a_z, core).wait_recv()
        att_copy(owner_of(zp, c), slot, s_a_fwd, r_a_fwd, core).start()

    slots_of(owner_of(zp, c), pass_on)
    slots_of(owner_of(z, oc), lambda slot: att_copy(owner_of(z, oc), slot, s_a_core, r_a_core, core).wait_recv())
    slots_of(owner_of(zp, oc), lambda slot: att_copy(owner_of(zp, oc), slot, s_a_fwd, r_a_fwd, core).wait_recv())
    done(l_o)
    arrived(OWB.at[oc, block(z)], r_o_core)
    for step in range(1, 4):
        there = lax.rem(z + step, 4)
        arrived(OWB.at[oc, block(there)], r_o_fwd + there)

    def project(tile, carry):
        t = tile // per_tok
        cols = pl.ds(pl.multiple_of(lax.rem(tile, per_tok) * W, W), W)
        all_cols = pl.ds(pl.multiple_of(tile * W, W), W)
        att = ATT[:, all_cols]
        halves = []
        for h in range(2):
            branch = dot_tn(OWB[h], att)
            halves.append(XG[t, h, :, cols].astype(F32) + (branch + column(h, VEC_OUT_BIAS)))
            HID[t, h, :, cols] = halves[h]
        center, inv_std = stats_of(*halves)
        ST2[t, 0:1, cols] = center
        ST2[t, 1:2, cols] = inv_std
        for h in range(2):
            shaped = (halves[h] - center) * inv_std * column(h, VEC_LN2_GAIN) + column(
                h, VEC_LN2_BIAS
            )
            N2[t, h, :, cols] = shaped.astype(BF)
        return carry

    lax.fori_loop(0, n_tiles, project, 0)

    done(l_f)
    ff_ready(0)

    @pl.when(first_core)
    def _():
        COLS[:, 6:7] = PACK[0].T[0:FW, 6:7]

    @pl.when(second_core)
    def _():
        COLS[:, 6:7] = PACKF[...].T[0:FW, 6:7]

    s_c_fwd = sends.take()

    def cot_forward():
        return remote(CG.at[1 - zz, c], CG.at[1 - zz, c], s_c_fwd, r_c_fwd, core)

    def other_cotangent():
        arrived(CG.at[1 - zz, c], r_c_z)
        cot_forward().start()
        arrived(CG.at[1 - zz, oc], r_c_fwd)


    r_g_core, r_p_core, r_g_z = recvs.take(n_tiles), recvs.take(n_tiles), recvs.take(n_tiles)
    s_g_core, s_p_core, s_g_z = sends.take(n_tiles), sends.take(n_tiles), sends.take(n_tiles)

    def tile_at(tile):
        t = tile // per_tok
        return t, pl.ds(pl.multiple_of(lax.rem(tile, per_tok) * W, W), W)

    def part_copy(buf, dst, tile, s_base, r_base, dev):
        t, cols = tile_at(tile)
        return remote(buf.at[t, :, cols], dst.at[t, :, cols], s_base + tile, r_base + tile, dev)

    def feed(tile, carry):
        t, cols = tile_at(tile)
        all_cols = pl.ds(pl.multiple_of(tile * W, W), W)
        pre = dot_tn(FB[0].reshape(D, FW), N2[t, :, :, cols].reshape(D, W)) + COLS[:, 6:7]
        phi = 0.5 * (1.0 + lax.erf(pre * (2.0**-0.5)))
        ACT[:, all_cols] = (pre * phi).astype(BF)
        slope = phi + pre * jnp.exp(pre * pre * -0.5) * ((2.0 * math.pi) ** -0.5)
        GPRE[:, all_cols] = slope.astype(BF)
        return carry

    lax.fori_loop(0, n_tiles, feed, 0)
    done(l_p)
    ff_ready(1)
    done(l_c)
    arrived(CG.at[zz, oc], r_c_core)

    def feed_back(order, carry):
        t = lax.rem(order + zz, 2)
        pl.when(order == 1)(other_cotangent)
        for number in range(per_tok):
            cols = slice(number * W, (number + 1) * W)
            all_cols = pl.ds(pl.multiple_of(t * T + number * W, W), W)
            grad_act = dot_tn(FB[1].reshape(D, FW), CG[t, :, :, cols].reshape(D, W))
            GPRE[:, all_cols] = (grad_act * GPRE[:, all_cols].astype(F32)).astype(BF)
            PGS[t, :, cols] = dot_nn(FB[0, oc], GPRE[:, all_cols]).astype(BF)
            part_copy(PGS, RCG, t * per_tok + number, s_g_core, r_g_core, core).start()
        for number in range(per_tok):
            cols = slice(number * W, (number + 1) * W)
            all_cols = pl.ds(pl.multiple_of(t * T + number * W, W), W)
            tile = t * per_tok + number
            own = dot_nn(FB[0, c], GPRE[:, all_cols])
            part_copy(PGS, RCG, tile, s_g_core, r_g_core, core).wait_recv()
            SZG[t, :, cols] = (own + RCG[t, :, cols].astype(F32)).astype(BF)
            part_copy(SZG, RZG, tile, s_g_z, r_g_z, zdev).start()
        return carry

    lax.fori_loop(0, 2, feed_back, 0)

    for entry in ff_entries:
        sent(entry)
    r_f1, r_f2 = recvs.take(4), recvs.take(2)
    f1_entries = []

    def ff_grads(number):
        for h in range(2):
            left, right = (N2, GPRE) if number < 2 else (CG, ACT)
            rows = slice(number % 2 * quarter, (number % 2 + 1) * quarter)
            total = dot_nt(left[0, h, rows, :], right[:, 0:T]) + dot_nt(left[1, h, rows, :], right[:, T:S])
            FB[number // 2, h, rows, :] = total.astype(BF)

    def ff_rows(number):
        return quarter_rows(lax.rem(number, 2))

    def ff_part(h, number):
        return FB.at[number // 2, h, ff_rows(number)]

    def ff_value(h, number):
        return FB[number // 2, h, ff_rows(number), :].astype(F32)

    def f1_push(h, number, place, dev, cond=None):
        f1_entries.append(push(ff_part(h, number), rf1_hbm.at[place], r_f1 + place, dev, cond))

    ff_grads(0)
    ff_grads(1)
    f1_push(0, 1 - xb, 0, xdev)
    for number in range(2):
        f1_push(1, number, 2 + number, ydev, yb == 1)

    def outward(tile, carry):
        t, cols = tile_at(tile)
        all_cols = pl.ds(pl.multiple_of(tile * W, W), W)
        OPS[t, :, cols] = dot_nn(FB[1, oc], ACT[:, all_cols]).astype(BF)
        part_copy(OPS, RCO, tile, s_p_core, r_p_core, core).start()
        OPO[t, :, cols] = dot_nn(FB[1, c], ACT[:, all_cols]).astype(BF)
        return carry

    lax.fori_loop(0, n_tiles, outward, 0)
    ff_grads(2)
    ff_grads(3)
    f1_push(0, 3 - xb, 1, xdev)
    for number in range(2):
        f1_push(1, 2 + number, 2 + number, ydev, yb == 0)

    SPR[dp] = jnp.zeros(SPR.shape[1:], F32)
    SPR[dp, 6:7, :] = dot_nt(jnp.ones((16, S), BF), GPRE[...])[0:1, :]

    r_g_all = recvs.take(n_tiles)
    s_g_all = sends.take(n_tiles)

    def g2_copy(tile):
        t, cols = tile_at(tile)
        return remote(G2.at[t, c, :, cols], G2.at[t, c, :, cols], s_g_all + tile, r_g_all + tile, core)

    def g2_other(tile):
        t, cols = tile_at(tile)
        return remote(G2.at[t, oc, :, cols], G2.at[t, oc, :, cols], s_g_all + tile, r_g_all + tile, core)

    def join(tile, carry):
        t, cols = tile_at(tile)
        part_copy(SZG, RZG, tile, s_g_z, r_g_z, zdev).wait_recv()
        G2[t, c, :, cols] = (SZG[t, :, cols].astype(F32) + RZG[t, :, cols].astype(F32)).astype(BF)
        g2_copy(tile).start()
        return carry

    lax.fori_loop(0, n_tiles, join, 0)

    def norm_back(grads, normals, inv_std, gain_index):
        scaled = [grads[h] * column(h, gain_index) for h in range(2)]
        plain = sum(jnp.sum(scaled[h], axis=0, keepdims=True) for h in range(2)) * inv_d
        cross = sum(jnp.sum(scaled[h] * normals[h], axis=0, keepdims=True) for h in range(2)) * inv_d
        return [inv_std * (scaled[h] - plain - normals[h] * cross) for h in range(2)]

    def second_back(tile, carry):
        t, cols = tile_at(tile)
        g2_other(tile).wait_recv()
        center, inv_std = ST2[t, 0:1, cols], ST2[t, 1:2, cols]
        grads = [G2[t, h, :, cols].astype(F32) for h in range(2)]
        normals = [(HID[t, h, :, cols] - center) * inv_std for h in range(2)]
        back = norm_back(grads, normals, inv_std, VEC_LN2_GAIN)
        for h in range(2):
            grad_hidden = CG[t, h, :, cols].astype(F32) + back[h]
            XG[t, h, :, cols] = grad_hidden.astype(BF)

            @pl.when((t == zz) & (c == h))
            def _():
                GH[:, cols] = grad_hidden
                VGC[:, 2:3] = VGC[:, 2:3] + jnp.sum(grads[h] * normals[h], axis=1, keepdims=True)
                VGC[:, 3:4] = VGC[:, 3:4] + jnp.sum(grads[h], axis=1, keepdims=True)

        return carry

    sent(e_xf)
    lax.fori_loop(0, n_tiles, second_back, 0)
    GB = XG

    r_out_z = recvs.take()

    def wait_out(tile, carry):
        part_copy(OPS, RCO, tile, s_p_core, r_p_core, core).wait_recv()
        return carry

    lax.fori_loop(0, n_tiles, wait_out, 0)
    SZO[...] = (OPO[1 - zz].astype(F32) + RCO[1 - zz].astype(F32)).astype(BF)
    push(SZO, RZO, r_out_z, zdev)
    VGC[:, 4:5] = jnp.sum(GB[zz, c].astype(F32), axis=1, keepdims=True)
    VGC[:, 5:6] = jnp.sum(CG[zz, c].astype(F32), axis=1, keepdims=True)

    window = pl.ds(pl.multiple_of(j * (4 * Q), Q), 5 * Q)
    for t in range(2):
        DATT[:, t * T : (t + 1) * T] = (
            dot_nn(OWB[0, window, :], GB[t, 0]) + dot_nn(OWB[1, window, :], GB[t, 1])
        ).astype(BF)
    r_q1, r_q2 = recvs.take(4), recvs.take(2)
    q1_entries = []

    def q1_push(h, number, place, dev, cond=None):
        q1_entries.append(push(DQ.at[number, h], rq1_hbm.at[place], r_q1 + place, dev, cond))

    for h in range(2):
        total = dot_nt(ATT[block(j), 0:T], GB[0, h]) + dot_nt(ATT[block(j), T:S], GB[1, h])
        DQ[3, h, 0:R, 0:H] = total.astype(BF)
    q1_push(0, 3, 1, xdev, xb == 0)
    q1_push(1, 3, 3, ydev, yb == 0)
    l_x2 = local(x_in, XG.at[zz, c])

    s_f2 = sends.take(2)
    l_f1, l_f2 = locs.take(4), locs.take(2)

    def f2_copy(place):
        if place == 0:
            return remote(ff_part(0, xb + 2 * (1 - yb)), rf2_hbm.at[0], s_f2, r_f2, ydev)
        return remote(ff_part(1, 2 * yb + 1 - xb), rf2_hbm.at[1], s_f2 + 1, r_f2 + 1, xdev)

    spare = ((0, 1 - xb), (0, 3 - xb), (1, 2 * (1 - yb)), (1, 2 * (1 - yb) + 1))
    kept = ((0, xb), (0, 2 + xb), (1, 2 * yb), (1, 2 * yb + 1))

    def first_join():
        for entry in f1_entries:
            when(entry[0], entry[1].wait_send)
        loads = []
        for place in range(4):
            arrived(rf1_hbm.at[place], r_f1 + place)
            load = pltpu.make_async_copy(rf1_hbm.at[place], ff_part(*spare[place]), LS.at[l_f1 + place])
            load.start()
            loads.append(load)
        for load in loads:
            load.wait()

        def add(place):
            h, number = kept[place]
            total = ff_value(h, number) + ff_value(*spare[place])
            FB[number // 2, h, ff_rows(number), :] = total.astype(BF)

        for place in range(4):
            add(place)
        f2_copy(0).start()
        f2_copy(1).start()

    def attend_back(slot, carry):
        rows = slot_rows(slot)
        here = pl.ds(pl.multiple_of(slot * Q, Q), Q)
        queries = QKV[0, rows, :]
        keys_t = QKV[1, rows, :]
        keys = keys_t.T
        values = QKV[2, rows, :].T
        grads_out = DATT[here, :]
        for tile in reversed(range(n_tiles)):
            count = W * (tile + 1)
            first = W * tile * (tile + 1) // 2
            cols = slice(tile * W, (tile + 1) * W)
            scores = dot_nn(keys[:count], queries[:, cols]) + MASK[first : first + count, :]
            probs = jnp.exp(scores - LSE[slot, 0:1, cols])
            grad_probs = dot_nn(values[:count], grads_out[:, cols])
            delta = jnp.sum(probs * grad_probs, axis=0, keepdims=True)
            grad_scores = (probs * (grad_probs - delta)).astype(BF)
            probs_low = probs.astype(BF)
            part_v = dot_nt(grads_out[:, cols], probs_low)
            part_k = dot_nt(queries[:, cols], grad_scores)
            if tile == n_tiles - 1:
                ACCV[...] = part_v
                ACCK[...] = part_k
            else:
                ACCV[:, 0:count] = ACCV[:, 0:count] + part_v
                ACCK[:, 0:count] = ACCK[:, 0:count] + part_k
            GQKV[0, rows, cols] = (dot_nn(keys_t[:, :count], grad_scores) * score_scale).astype(BF)
        GQKV[1, rows, :] = ACCK[...].astype(BF)
        GQKV[2, rows, :] = ACCV[...].astype(BF)

        @pl.when(slot == 3)
        def _():
            first_join()

        return carry

    lax.fori_loop(first_slot, 5, attend_back, 0)

    for m in range(3):
        if m != 1:
            bias_sum = jnp.sum(GQKV[m].astype(F32), axis=1, keepdims=True)
        for h in range(2):
            total = dot_nt(GQKV[m, :, 0:T], N1[0, h]) + dot_nt(GQKV[m, :, T:S], N1[1, h])
            DQ[m, h, :, 0:H] = total.astype(BF)
            if m != 1:
                DQ[m, h, :, H : H + 1] = bias_sum.astype(BF)
        q1_push(0, m, m // 2, xdev, xb != m % 2)
        q1_push(1, m, 2 + m % 2, ydev, yb != m // 2)

    def wait_sends(tile, carry):
        part_copy(PGS, RCG, tile, s_g_core, r_g_core, core).wait_send()
        part_copy(OPS, RCO, tile, s_p_core, r_p_core, core).wait_send()
        part_copy(SZG, RZG, tile, s_g_z, r_g_z, zdev).wait_send()
        g2_copy(tile).wait_send()
        return carry

    lax.fori_loop(0, n_tiles, wait_sends, 0)
    r_n_core, r_n_z = recvs.take(n_tiles), recvs.take()
    s_n_core = sends.take(n_tiles)

    def back_rows(half, tile):
        all_cols = pl.ds(pl.multiple_of(tile * W, W), W)
        total = dot_tn(WB[0, half], GQKV[0, :, all_cols])
        for m in range(1, 3):
            total = total + dot_tn(WB[m, half], GQKV[m, :, all_cols])
        return total

    def first_part(tile, carry):
        t, cols = tile_at(tile)
        PGS[t, :, cols] = back_rows(oc, tile).astype(BF)
        part_copy(PGS, RCG, tile, s_n_core, r_n_core, core).start()
        OPS[t, :, cols] = back_rows(c, tile).astype(BF)
        return carry

    lax.fori_loop(0, n_tiles, first_part, 0)

    def wait_first(tile, carry):
        part_copy(PGS, RCG, tile, s_n_core, r_n_core, core).wait_recv()
        return carry

    lax.fori_loop(0, n_tiles, wait_first, 0)
    SZG[0] = (OPS[1 - zz].astype(F32) + RCG[1 - zz].astype(F32)).astype(BF)
    push(SZG.at[0], RZN, r_n_z, zdev)

    for entry in f1_entries:
        pending[:] = [other for other in pending if other is not entry]
    loads = []
    for h in range(2):
        arrived(rf2_hbm.at[h], r_f2 + h)
        loads.append(local(rf2_hbm.at[h], ff_part(*spare[2 * h])))
    r_zf = recvs.take(2)
    for h in range(2):
        done(loads[h])
        low = (ff_value(h, dp) + ff_value(*spare[2 * h])).astype(BF)
        FB[dp // 2, h, ff_rows(dp), :] = low
        if h == 0:

            @pl.when(first_core)
            def _():
                ZF[0] = low

        push(ff_part(h, dp), ZF.at[1], r_zf + 1, (dp, z2, h), second_core)
        if h == 1:
            push(ff_part(h, dp), ZF.at[0], r_zf, (dp, z, 1), first_core)

    arrived(RZO, r_out_z)
    branch_out = OPO[zz].astype(F32) + RCO[zz].astype(F32) + RZO[...].astype(F32)
    OPO[0] = (HID[zz, c] + branch_out + column(c, VEC_PROJ_BIAS)).astype(BF)
    l_out = local(OPO.at[0], out_o)

    for entry in q1_entries:
        sent(entry)
    q_spare = ((1 - xb, 0), (3 - xb, 0), (2 * (1 - yb), 1), (2 * (1 - yb) + 1, 1))
    q_kept = ((xb, 0), (2 + xb, 0), (2 * yb, 1), (2 * yb + 1, 1))
    loads = []
    for place in range(4):
        arrived(rq1_hbm.at[place], r_q1 + place)
        loads.append(local(rq1_hbm.at[place], DQ.at[q_spare[place][0], q_spare[place][1]]))
    for place in range(4):
        done(loads[place])
        (there, h), (here, unused) = q_spare[place], q_kept[place]
        DQ[here, h] = (DQ[here, h].astype(F32) + DQ[there, h].astype(F32)).astype(BF)
    push(DQ.at[xb + 2 * (1 - yb), 0], rq2_hbm.at[0], r_q2, ydev)
    push(DQ.at[2 * yb + 1 - xb, 1], rq2_hbm.at[1], r_q2 + 1, xdev)

    done(l_x2)
    arrived(RZN, r_n_z)
    r_stat = recvs.take()
    grads = OPS[zz].astype(F32) + RCG[zz].astype(F32) + RZN[...].astype(F32)
    center, inv_std = ST1[zz, 0:1, :], ST1[zz, 1:2, :]
    normals = (XG[zz, c].astype(F32) - center) * inv_std
    scaled = grads * column(c, VEC_LN1_GAIN)
    STX[c, 0:1, :] = jnp.sum(scaled, axis=0, keepdims=True)
    STX[c, 1:2, :] = jnp.sum(scaled * normals, axis=0, keepdims=True)
    push(STX.at[c], STX.at[c], r_stat, core)
    VGC[:, 0:1] = jnp.sum(grads * normals, axis=1, keepdims=True)
    VGC[:, 1:2] = jnp.sum(grads, axis=1, keepdims=True)
    arrived(STX.at[oc], r_stat)
    sums = (STX[0] + STX[1]) * inv_d
    OPO[1] = (GH[...] + inv_std * (scaled - sums[0:1] - normals * sums[1:2])).astype(BF)
    l_ing = local(OPO.at[1], ing_o)

    r_sp, r_spz = recvs.take(4), recvs.take(8)
    turned = VGC[...].T
    SPR[dp, 0:6, 0:H] = turned[0:6, :]
    for peer in peers:
        push(SPR.at[dp], SPR.at[dp], r_sp + dp, (peer, z, c))

    r_gf, r_gq = recvs.take(4), recvs.take(4)

    def spread(src, out_at, size, r_base):
        push(src, out_at(dp, 0, size), r_base, xdev)
        push(src, out_at(dp, 0, size), r_base + 1, ydev)

    def spread_on(out_at, size, r_base):
        half = size // 32 * 16
        arrived(out_at(xn, 0, size), r_base)
        push(out_at(xn, 0, half), out_at(xn, 0, half), r_base + 2, ydev)
        arrived(out_at(yn, 0, size), r_base + 1)
        push(out_at(yn, half, size - half), out_at(yn, half, size - half), r_base + 3, xdev)

    def spread_end(out_at, size, r_base):
        half = size // 32 * 16
        arrived(out_at(dg, 0, half), r_base + 2)
        arrived(out_at(dg, half, size - half), r_base + 3)

    def gf_at(plane, first, size):
        return gf_o.at[pl.ds(pl.multiple_of(plane * quarter + first, 16), size)]

    def gq_at(plane, first, size):
        return gq_o.at[plane, pl.ds(first, size)]

    arrived(ZF.at[0], r_zf, second_core)
    arrived(ZF.at[1], r_zf + 1)
    ZF[0] = (ZF[0].astype(F32) + ZF[1].astype(F32)).astype(BF)
    l_gf = local(ZF.at[0], gf_o.at[my_quarter])
    spread(ZF.at[0], gf_at, quarter, r_gf)

    loads = []
    for h in range(2):
        arrived(rq2_hbm.at[h], r_q2 + h)
        loads.append(local(rq2_hbm.at[h], DQ.at[q_spare[2 * h][0], h]))
    r_zq, r_zt = recvs.take(2), recvs.take(2)
    with_tail = (j < 3) & (dp < 3)
    next_block = jnp.minimum(j + 1, 3)
    for h in range(2):
        done(loads[h])
        low = (DQ[dp, h].astype(F32) + DQ[q_spare[2 * h][0], h].astype(F32)).astype(BF)
        DQ[dp, h] = low
        if h == 0:

            @pl.when(first_core)
            def _():
                ZQ[0] = low[0:R]

        push(DQ.at[dp, h, pl.ds(0, R)], ZQ.at[1], r_zq + 1, (dp, z2, h), second_core)
        if h == 1:
            push(DQ.at[dp, h, pl.ds(0, R)], ZQ.at[0], r_zq, (dp, z, 1), first_core)
        push(DQ.at[dp, h, pl.ds(R, TAIL)], ZT.at[c], r_zt + c, (dp, next_block, h), with_tail)

    for number in range(4):
        arrived(SPR.at[number], r_sp + number, dp != number)
    SPZ[z, c] = SPR[0] + SPR[1] + SPR[2] + SPR[3]
    for step in range(4):
        for side in range(2):
            if step == 0 and side == 0:
                continue
            target = (dp, lax.rem(z + step, 4), c if side == 0 else oc)
            push(SPZ.at[z, c], SPZ.at[z, c], r_spz + (2 * z + c), target)

    arrived(ZQ.at[0], r_zq, second_core)
    arrived(ZQ.at[1], r_zq + 1)
    gets_tail = (z >= 1) & (dp < 3)
    for side in range(2):
        arrived(ZT.at[side], r_zt + side, gets_tail)
    total = ZQ[0].astype(F32) + ZQ[1].astype(F32)
    ZQ[0] = total.astype(BF)

    @pl.when(gets_tail)
    def _():
        ZQ[0, 0:TAIL] = (total[0:TAIL] + ZT[0].astype(F32) + ZT[1].astype(F32)).astype(BF)

    l_gq = local(ZQ.at[0], gq_o.at[dp])
    spread(ZQ.at[0], gq_at, R, r_gq)
    spread_on(gf_at, quarter, r_gf)

    for step in range(4):
        for side in range(2):
            if step == 0 and side == 0:
                continue
            zv, cv = lax.rem(z + step, 4), c if side == 0 else oc
            arrived(SPZ.at[zv, cv], r_spz + (2 * zv + cv))
    vectors = SPZ[0, c] + SPZ[1, c] + SPZ[2, c] + SPZ[3, c]
    VOUT[...] = vectors
    VOUT[6:7, :] = SPZ[z, 0, 6:7, :] + SPZ[z2, 1, 6:7, :]
    l_vec_o = local(VOUT, vec_o)

    spread_on(gq_at, R, r_gq)
    spread_end(gf_at, quarter, r_gf)
    spread_end(gq_at, R, r_gq)
    for entry in (l_out, l_ing, l_gf, l_gq, l_vec_o):
        done(entry)

    def own_sends(slot):
        att_copy(j, slot, s_a_z, r_a_z, zdev).wait_send()
        att_copy(j, slot, s_a_core, r_a_core, core).wait_send()

    slots_of(j, own_sends)
    slots_of(
        owner_of(zp, c),
        lambda slot: att_copy(owner_of(zp, c), slot, s_a_fwd, r_a_fwd, core).wait_send(),
    )

    f2_copy(0).wait_send()
    f2_copy(1).wait_send()
    cot_forward().wait_send()

    for step in (1, 3, 2):
        for number in range(3):
            ow_copy(step, number).wait_send()

    def last_sends(tile, carry):
        part_copy(PGS, RCG, tile, s_n_core, r_n_core, core).wait_send()
        return carry

    lax.fori_loop(0, n_tiles, last_sends, 0)
    for entry in list(pending):
        sent(entry)
    assert sends.used <= SEND_COUNT and recvs.used <= RECV_COUNT and locs.used <= LOCAL_COUNT


def finish_kernel(
    out_in,
    ing_in,
    gf_in,
    gq_in,
    vec_in,
    out_o,
    ing_o,
    qkv_o,
    qvb_o,
    ow_o,
    fc_o,
    proj_o,
    v0,
    v1,
    v2,
    v3,
    v4,
    v5,
    v6,
    GF,
    GQ,
    FST,
    QST,
    OB,
    SEM,
):
    R, H = ow_o.shape
    count = GF.shape[0] // R
    whole = [
        pltpu.make_async_copy(out_in, OB.at[0], SEM.at[0]),
        pltpu.make_async_copy(ing_in, OB.at[1], SEM.at[1]),
    ]
    place = 2
    loads_q, loads_f = [], []
    for m in range(4):
        loads_q.append(pltpu.make_async_copy(gq_in.at[m], GQ.at[m], SEM.at[place + m]))
    place += 4
    for number in range(count):
        rows = pl.ds(number * R, R)
        loads_f.append(pltpu.make_async_copy(gf_in.at[rows], GF.at[rows], SEM.at[place + number]))
    place += count
    for copy in loads_f + loads_q + whole:
        copy.start()
    stores = []
    for number in range(count):
        loads_f[number].wait()
        rows = pl.ds(number * R, R)
        FST[rows, :] = GF[rows, :].astype(F32)
        half = count // 2
        dst = (fc_o if number < half else proj_o).at[pl.ds(number % half * R, R)]
        stores.append(pltpu.make_async_copy(FST.at[rows], dst, SEM.at[place + number]))
        stores[-1].start()
    place += count
    for m in range(4):
        loads_q[m].wait()
        QST[m] = GQ[m, :, 0:H].astype(F32)
        dst = qkv_o.at[m] if m < 3 else ow_o
        stores.append(pltpu.make_async_copy(QST.at[m], dst, SEM.at[place + m]))
        stores[-1].start()
    place += 4
    for number, dst in enumerate((out_o, ing_o)):
        whole[number].wait()
        stores.append(pltpu.make_async_copy(OB.at[number], dst, SEM.at[place + number]))
        stores[-1].start()
    first = H // LANES * LANES
    for number, m in enumerate((0, 2)):
        turned = GQ[m, :, first : first + LANES].astype(F32).T
        qvb_o[number : number + 1, :] = turned[H - first : H - first + 1, :]
    for number, v in enumerate((v0, v1, v2, v3, v4, v5, v6)):
        v[...] = vec_in[number, 0 : v.shape[0]]
    for copy in stores:
        copy.wait()


def fast_body(
    tokens,
    ln1_gain,
    ln1_bias,
    qkv_weight,
    qv_bias,
    out_weight,
    out_bias,
    ln2_gain,
    ln2_bias,
    fc_weight,
    fc_bias,
    proj_weight,
    proj_bias,
    doc_lengths,
    cotangent,
):
    H, T = tokens.shape
    R = out_weight.shape[0]
    FW = fc_weight.shape[1]
    D, S = 2 * H, 2 * T
    HP = (H // LANES + 1) * LANES
    EXT = 5 * HEAD_DIM
    NT = S // KEY_TILE
    wide = (FW // LANES + 1) * LANES
    w3 = jnp.transpose(qkv_weight, (1, 2, 0))
    shape = jax.ShapeDtypeStruct
    anywhere = pl.BlockSpec(memory_space=pl.ANY)
    outs = [
        shape((H, T), BF),
        shape((H, T), BF),
        shape((2 * H, FW), BF),
        shape((4, R, HP), BF),
        shape((8, FW), F32),
        shape((4, D // 4, FW), BF),
        shape((2, D // 4, FW), BF),
        shape((4, EXT, HP), BF),
        shape((2, EXT, HP), BF),
    ]
    vmem = pltpu.VMEM
    mask_rows = KEY_TILE * NT * (NT + 1) // 2
    scratch = [
        vmem((2, 2, H, T), BF),
        vmem((2, 2, H, T), BF),
        vmem((2, 2, H, T), BF),
        vmem((3, 2, EXT, H), BF),
        vmem((EXT, LANES), F32),
        vmem((2, D, H), BF),
        vmem((2, 2, H, FW), BF),
        vmem((FW, LANES), F32),
        vmem((2, 8, wide), F32),
        vmem((8, wide), F32),
        vmem((8, wide), F32),
        vmem((mask_rows, KEY_TILE), F32),
        vmem((3, EXT, S), BF),
        vmem((5, 8, S), F32),
        vmem((D, S), BF),
        vmem((2, 2, H, T), F32),
        vmem((2, 8, T), F32),
        vmem((2, 8, T), F32),
        vmem((2, 2, H, T), BF),
        vmem((FW, S), BF),
        vmem((FW, S), BF),
        vmem((2, H, T), BF),
        vmem((2, H, T), BF),
        vmem((2, H, T), BF),
        vmem((2, H, T), BF),
        vmem((2, H, T), BF),
        vmem((2, H, T), BF),
        vmem((2, H, T), BF),
        vmem((2, 2, H, T), BF),
        vmem((H, T), BF),
        vmem((H, T), BF),
        vmem((H, T), BF),
        vmem((EXT, S), BF),
        vmem((3, EXT, S), BF),
        vmem((HEAD_DIM, S), F32),
        vmem((HEAD_DIM, S), F32),
        vmem((2, 2 * H // 4, FW), BF),
        vmem((4, 2, EXT, HP), BF),
        vmem((2, R, HP), BF),
        vmem((2, EXT - R, HP), BF),
        vmem((H, T), F32),
        vmem((H, LANES), F32),
        vmem((2, 8, T), F32),
        vmem((4, 8, FW), F32),
        vmem((4, 2, 8, FW), F32),
        vmem((8, FW), F32),
        pltpu.SemaphoreType.DMA((SEND_COUNT,)),
        pltpu.SemaphoreType.DMA((RECV_COUNT,)),
        pltpu.SemaphoreType.DMA((LOCAL_COUNT,)),
    ]
    out_rows, in_rows, gf, gq, vectors = pl.pallas_call(
        layer_kernel,
        out_shape=outs,
        in_specs=[anywhere] * 6 + [pl.BlockSpec(memory_space=vmem)] * 9,
        out_specs=[anywhere] * len(outs),
        scratch_shapes=scratch,
        compiler_params=pltpu.CompilerParams(
            collective_id=0, has_side_effects=True, vmem_limit_bytes=VMEM_LIMIT
        ),
    )(
        tokens,
        cotangent,
        w3,
        out_weight,
        fc_weight,
        proj_weight,
        ln1_gain,
        ln1_bias,
        ln2_gain,
        ln2_bias,
        out_bias,
        proj_bias,
        fc_bias,
        qv_bias,
        doc_lengths,
    )[:5]
    in_vmem = pl.BlockSpec(memory_space=vmem)
    finals = pl.pallas_call(
        finish_kernel,
        out_shape=[
            shape((H, T), BF),
            shape((H, T), BF),
            shape((3, R, H), F32),
            shape((2, R), F32),
            shape((R, H), F32),
            shape((H, FW), F32),
            shape((H, FW), F32),
        ]
        + [shape((H,), F32)] * 6
        + [shape((FW,), F32)],
        in_specs=[anywhere] * 4 + [in_vmem],
        out_specs=[anywhere] * 3 + [in_vmem] + [anywhere] * 3 + [in_vmem] * 7,
        scratch_shapes=[
            vmem((D, FW), BF),
            vmem((4, R, HP), BF),
            vmem((D, FW), F32),
            vmem((4, R, H), F32),
            vmem((2, H, T), BF),
            pltpu.SemaphoreType.DMA((32,)),
        ],
        compiler_params=pltpu.CompilerParams(vmem_limit_bytes=VMEM_LIMIT),
    )(out_rows, in_rows, gf, gq, vectors)
    out_final, in_final, qkv_rows, bias_grad, ow_grad, fc_grad, proj_grad = finals[:7]
    ln1_gain_g, ln1_bias_g, ln2_gain_g, ln2_bias_g, out_bias_g, proj_bias_g, fc_bias_g = finals[7:]
    return (
        out_final,
        in_final,
        ln1_gain_g,
        ln1_bias_g,
        jnp.transpose(qkv_rows, (2, 0, 1)),
        bias_grad,
        ow_grad,
        out_bias_g,
        ln2_gain_g,
        ln2_bias_g,
        fc_grad,
        fc_bias_g,
        proj_grad,
        proj_bias_g,
    )


def choose_body(*arrays):
    sizes = {axis: lax.axis_size(axis) for axis in ("dp", "row", "col")}
    H, R = arrays[0].shape[0], arrays[5].shape[0]
    fits = sizes == {"dp": 4, "row": 4, "col": 2} and 4 * R == 2 * H == 17 * HEAD_DIM
    return (fast_body if fits else body)(*arrays)


def solution(mesh):
    return jax.shard_map(
        choose_body,
        mesh=mesh,
        in_specs=(
            P("col", ("dp", "row")),
            P("col"),
            P("col"),
            P("col", None, "row"),
            P(None, "row"),
            P("row", "col"),
            P("col"),
            P("col"),
            P("col"),
            P("col", "row"),
            P("row"),
            P("col", "row"),
            P("col"),
            P(("dp", "col"), None),
            P("col", ("dp", "row")),
        ),
        out_specs=(
            P("col", ("dp", "row")),
            P("col", ("dp", "row")),
            P("col"),
            P("col"),
            P("col", None, "row"),
            P(None, "row"),
            P("row", "col"),
            P("col"),
            P("col"),
            P("col"),
            P("col", "row"),
            P("row"),
            P("col", "row"),
            P("col"),
        ),
        check_vma=False,
    )
```

```python
from functools import partial
import math

import jax
import jax.numpy as jnp
from jax import lax
from jax.experimental import pallas as pl
from jax.experimental.pallas import tpu as pltpu
from jax.sharding import PartitionSpec as P

HEAD_DIM = 64


epsilon = 1e-05
score_scale = 0.125
masked_fill = -1e30
block_limit = 512


def feature_sums(first_sum, second_sum):
    return lax.psum((first_sum, second_sum), "col")


def norm_forward(values, gain_vec, shift_vec):
    feature_count = values.shape[1] * lax.axis_size("col")
    total_sum, square_sum = feature_sums(jnp.sum(values, axis=1), jnp.sum(values * values, axis=1))
    center = total_sum / feature_count
    spread = square_sum / feature_count - center * center
    inv_std = lax.rsqrt(spread + epsilon)
    normal = (values - center[:, None]) * inv_std[:, None]
    return (normal, inv_std, normal * gain_vec + shift_vec)


def norm_backward(upstream, normal, inv_std, gain_vec):
    feature_count = upstream.shape[1] * lax.axis_size("col")
    scaled = upstream * gain_vec
    plain_sum, cross_sum = feature_sums(jnp.sum(scaled, axis=1), jnp.sum(scaled * normal, axis=1))
    return inv_std[:, None] * (
        scaled - plain_sum[:, None] / feature_count - normal * (cross_sum[:, None] / feature_count)
    )


def gather_rows(values):
    return lax.all_gather(values, "row", axis=0, tiled=True)


def gather_cols(values):
    return lax.all_gather(values, "col", axis=0, tiled=True)


def sum_over_rows(row_term, row_total):
    return lax.psum_scatter(
        row_term(jnp.int32(0), row_total * lax.axis_size("row")),
        "row",
        scatter_dimension=0,
        tiled=True,
    )


def sum_over_cols(row_term, row_total):
    return lax.psum_scatter(
        row_term(jnp.int32(0), row_total * lax.axis_size("col")),
        "col",
        scatter_dimension=0,
        tiled=True,
    )


def to_heads(values):
    return lax.all_to_all(values, "row", split_axis=0, concat_axis=2, tiled=True)


def to_tokens(values):
    return lax.all_to_all(values, "row", split_axis=2, concat_axis=0, tiled=True)


def product_term(full_rows, matrix):

    def row_term(first_row, row_count):
        return jnp.dot(full_rows, matrix, preferred_element_type=jnp.float32)

    return row_term


def product_term_back(full_rows, matrix):

    def row_term(first_row, row_count):
        return lax.dot_general(
            full_rows, matrix, (((1,), (1,)), ((), ())), preferred_element_type=jnp.float32
        )

    return row_term


def slice_term(full_rows):

    def row_term(first_row, row_count):
        return full_rows

    return row_term


def inner_rows(left_side, right_side):
    return lax.dot_general(
        left_side, right_side, (((0,), (0,)), ((), ())), preferred_element_type=jnp.float32
    )


def segments_of(lengths, places):
    doc_ends = jnp.cumsum(lengths)
    segment = jnp.sum(
        (doc_ends[None, :] <= places[:, None]).astype(jnp.int32), axis=1, dtype=jnp.int32
    )
    return (segment, places >= doc_ends[-1])


def allowed_pairs(query_place, query_segment, query_padding, key_place, key_segment):
    causal = key_place[None, :] <= query_place[:, None]
    same_doc = key_segment[None, :] == query_segment[:, None]
    itself = key_place[None, :] == query_place[:, None]
    return causal & same_doc & (jnp.logical_not(query_padding)[:, None] | itself)


def attention_parts(queries, keyvals, lengths, query_place):
    seq_total = keyvals.shape[0]
    key_block_size = math.gcd(seq_total, block_limit)
    block_count = seq_total // key_block_size
    key_place = jnp.arange(seq_total, dtype=jnp.int32)
    key_segment = segments_of(lengths, key_place)[0]
    query_segment, query_padding = segments_of(lengths, query_place)
    blocked = (
        keyvals.reshape((block_count, key_block_size) + keyvals.shape[1:]),
        key_place.reshape(block_count, key_block_size),
        key_segment.reshape(block_count, key_block_size),
    )

    def block_scores(key_rows, place_rows, segment_rows):
        raw_scores = (
            jnp.einsum("qhd,khd->hqk", queries, key_rows, preferred_element_type=jnp.float32)
            * score_scale
        )
        allowed = allowed_pairs(
            query_place, query_segment, query_padding, place_rows, segment_rows
        )[None]
        return (raw_scores, allowed)

    return (blocked, block_scores)


def attention_forward(queries, blocked, block_scores):
    query_count, head_count, head_width = queries.shape

    def max_step(running, inputs):
        best_score, mass_sum = running
        kv_block, place_rows, segment_rows = inputs
        raw_scores, allowed = block_scores(kv_block[:, 0], place_rows, segment_rows)
        masked = jnp.where(allowed, raw_scores, masked_fill)
        new_best = jnp.maximum(best_score, jnp.max(masked, axis=2))
        fresh = jnp.sum(jnp.where(allowed, jnp.exp(masked - new_best[:, :, None]), 0.0), axis=2)
        return ((new_best, mass_sum * jnp.exp(best_score - new_best) + fresh), None)

    start_best = jnp.full((head_count, query_count), masked_fill, jnp.float32)
    start_mass = jnp.zeros((head_count, query_count), jnp.float32)
    (best_score, mass_sum), unused = lax.scan(max_step, (start_best, start_mass), blocked)
    log_sum = best_score + jnp.log(mass_sum)

    def out_step(running, inputs):
        kv_block, place_rows, segment_rows = inputs
        raw_scores, allowed = block_scores(kv_block[:, 0], place_rows, segment_rows)
        probs_low = jnp.where(allowed, jnp.exp(raw_scores - log_sum[:, :, None]), 0.0).astype(
            jnp.bfloat16
        )
        return (
            running
            + jnp.einsum(
                "hqk,khd->qhd", probs_low, kv_block[:, 1], preferred_element_type=jnp.float32
            ),
            None,
        )

    attended, unused = lax.scan(
        out_step, jnp.zeros((query_count, head_count, head_width), jnp.float32), blocked
    )
    return (attended, log_sum)


def attention_backward(queries, blocked, block_scores, log_sum, grad_attended):
    query_count, head_count, head_width = queries.shape

    def probs_and_grads(inputs):
        kv_block, place_rows, segment_rows = inputs
        raw_scores, allowed = block_scores(kv_block[:, 0], place_rows, segment_rows)
        probs_f = jnp.where(allowed, jnp.exp(raw_scores - log_sum[:, :, None]), 0.0)
        grad_probs = jnp.einsum(
            "qhd,khd->hqk", grad_attended, kv_block[:, 1], preferred_element_type=jnp.float32
        )
        return (probs_f, grad_probs)

    def delta_step(running, inputs):
        probs_f, grad_probs = probs_and_grads(inputs)
        return (running + jnp.sum(probs_f * grad_probs, axis=2), None)

    delta_sum, unused = lax.scan(
        delta_step, jnp.zeros((head_count, query_count), jnp.float32), blocked
    )

    def grad_step(running, inputs):
        kv_block = inputs[0]
        probs_f, grad_probs = probs_and_grads(inputs)
        grad_scores = (probs_f * (grad_probs - delta_sum[:, :, None])).astype(jnp.bfloat16)
        running = running + jnp.einsum(
            "hqk,khd->qhd", grad_scores, kv_block[:, 0], preferred_element_type=jnp.float32
        )
        grad_keys = (
            jnp.einsum("hqk,qhd->khd", grad_scores, queries, preferred_element_type=jnp.float32)
            * score_scale
        )
        grad_values = jnp.einsum(
            "hqk,qhd->khd",
            probs_f.astype(jnp.bfloat16),
            grad_attended,
            preferred_element_type=jnp.float32,
        )
        return (running, jnp.stack([grad_keys, grad_values], axis=1))

    grad_queries, grad_keyvals = lax.scan(
        grad_step, jnp.zeros((query_count, head_count, head_width), jnp.float32), blocked
    )
    seq_total = grad_keyvals.shape[0] * grad_keyvals.shape[1]
    return (grad_queries * score_scale, grad_keyvals.reshape(seq_total, 2, head_count, head_width))


def body(
    tokens,
    ln1_gain,
    ln1_bias,
    qkv_weight,
    qv_bias,
    out_weight,
    out_bias,
    ln2_gain,
    ln2_bias,
    fc_weight,
    fc_bias,
    proj_weight,
    proj_bias,
    doc_lengths,
    cotangent,
):
    count_rows = lax.axis_size("row")
    count_cols = lax.axis_size("col")
    grid_rows = tokens.shape[1]
    col_width = tokens.shape[0]
    row_width = out_weight.shape[0]
    seq_rows = grid_rows * count_rows // count_cols
    query_rows = seq_rows // count_rows
    full_width = col_width * count_cols
    head_count = full_width // HEAD_DIM
    tokens_f = tokens.astype(jnp.float32).T
    normal1, inv_std1, shaped1 = norm_forward(tokens_f, ln1_gain, ln1_bias)
    qkv_flat = qkv_weight.reshape(col_width, 3 * row_width)
    gathered1 = gather_rows(shaped1.astype(jnp.bfloat16))
    mixed_qkv = sum_over_cols(product_term(gathered1, qkv_flat), seq_rows).reshape(
        seq_rows, 3, row_width
    )
    bias_three = jnp.stack([qv_bias[0], jnp.zeros_like(qv_bias[0]), qv_bias[1]])
    qkv_low = (mixed_qkv + bias_three).astype(jnp.bfloat16)
    local_qkv = to_heads(qkv_low).reshape(query_rows, 3, head_count, HEAD_DIM)
    queries = local_qkv[:, 0]
    keyvals = lax.all_gather(local_qkv[:, 1:], "row", axis=0, tiled=True)
    query_place = lax.axis_index("row") * query_rows + jnp.arange(query_rows, dtype=jnp.int32)
    blocked, block_scores = attention_parts(queries, keyvals, doc_lengths[0], query_place)
    attended_f, log_sum = attention_forward(queries, blocked, block_scores)
    attended_low = attended_f.reshape(query_rows, 1, full_width).astype(jnp.bfloat16)
    attended_grid = to_tokens(attended_low).reshape(seq_rows, row_width)
    gathered_att = gather_cols(attended_grid)
    branch = sum_over_rows(product_term(gathered_att, out_weight), grid_rows)
    hidden = tokens_f + (branch + out_bias)
    normal2, inv_std2, shaped2 = norm_forward(hidden, ln2_gain, ln2_bias)
    normed2 = shaped2.astype(jnp.bfloat16)
    gathered2 = gather_rows(normed2)
    pre_act = sum_over_cols(product_term(gathered2, fc_weight), seq_rows) + fc_bias
    active = jax.nn.gelu(pre_act, approximate=False).astype(jnp.bfloat16)
    gathered_act = gather_cols(active)
    projected = sum_over_rows(product_term_back(gathered_act, proj_weight), grid_rows)
    output = (hidden + projected + proj_bias).astype(jnp.bfloat16).T
    cotangent_rows = cotangent.T
    grad_out = cotangent_rows.astype(jnp.float32)
    unused, gelu_back = jax.vjp(partial(jax.nn.gelu, approximate=False), pre_act)
    grad_gathered = gather_rows(cotangent_rows)
    proj_weight_grad = inner_rows(grad_gathered, gathered_act)
    proj_bias_grad = jnp.sum(grad_gathered, axis=0, dtype=jnp.float32)
    grad_active = sum_over_cols(product_term(grad_gathered, proj_weight), seq_rows)
    grad_pre = gelu_back(grad_active)[0].astype(jnp.bfloat16)
    grad_pre_all = gather_cols(grad_pre)
    fc_weight_grad = inner_rows(gathered2, grad_pre_all)
    fc_bias_grad = jnp.sum(grad_pre_all, axis=0, dtype=jnp.float32)
    grad_normed2 = sum_over_rows(product_term_back(grad_pre_all, fc_weight), grid_rows)
    ln2_gain_part = jnp.sum(grad_normed2 * normal2, axis=0)
    ln2_bias_part = jnp.sum(grad_normed2, axis=0)
    grad_hidden = grad_out + norm_backward(grad_normed2, normal2, inv_std2, ln2_gain)
    branch_gathered = gather_rows(grad_hidden.astype(jnp.bfloat16))
    out_weight_grad = inner_rows(gathered_att, branch_gathered)
    out_bias_grad = jnp.sum(branch_gathered, axis=0, dtype=jnp.float32)
    grad_att_grid = sum_over_cols(product_term_back(branch_gathered, out_weight), seq_rows).astype(
        jnp.bfloat16
    )
    grad_attended = to_heads(grad_att_grid.reshape(seq_rows, 1, row_width)).reshape(
        query_rows, head_count, HEAD_DIM
    )
    grad_queries, grad_keyvals = attention_backward(
        queries, blocked, block_scores, log_sum, grad_attended
    )
    keyval_rows = sum_over_rows(slice_term(grad_keyvals), query_rows)
    grad_qkv_local = (
        jnp.concatenate([grad_queries[:, None], keyval_rows], axis=1)
        .astype(jnp.bfloat16)
        .reshape(query_rows, 3, full_width)
    )
    grad_qkv_grid = to_tokens(grad_qkv_local).reshape(seq_rows, 3 * row_width)
    qkv_gathered = gather_cols(grad_qkv_grid)
    qkv_weight_grad = inner_rows(gathered1, qkv_gathered).reshape(col_width, 3, row_width)
    qkv_bias_sums = jnp.sum(qkv_gathered, axis=0, dtype=jnp.float32).reshape(3, row_width)
    qv_bias_grad = jnp.stack([qkv_bias_sums[0], qkv_bias_sums[2]])
    grad_normed1 = sum_over_rows(product_term_back(qkv_gathered, qkv_flat), grid_rows)
    ln1_gain_part = jnp.sum(grad_normed1 * normal1, axis=0)
    ln1_bias_part = jnp.sum(grad_normed1, axis=0)
    input_grad = (
        (grad_hidden + norm_backward(grad_normed1, normal1, inv_std1, ln1_gain))
        .astype(jnp.bfloat16)
        .T
    )
    summed = lax.psum(
        (
            qkv_weight_grad,
            qv_bias_grad,
            out_weight_grad,
            out_bias_grad,
            fc_weight_grad,
            fc_bias_grad,
            proj_weight_grad,
            proj_bias_grad,
        ),
        "dp",
    )
    gain_sums = lax.psum(
        (ln1_gain_part, ln1_bias_part, ln2_gain_part, ln2_bias_part), ("dp", "row")
    )
    return (
        output,
        input_grad,
        gain_sums[0],
        gain_sums[1],
        summed[0],
        summed[1],
        summed[2],
        summed[3],
        gain_sums[2],
        gain_sums[3],
        summed[4],
        summed[5],
        summed[6],
        summed[7],
    )


BF = jnp.bfloat16
F32 = jnp.float32
MESH = pl.DeviceIdType.MESH
LANES = 128
KEY_TILE = 256
VEC_LN1_GAIN, VEC_LN1_BIAS, VEC_LN2_GAIN, VEC_LN2_BIAS, VEC_OUT_BIAS, VEC_PROJ_BIAS = range(6)


def dot_nn(left, right):
    return lax.dot_general(left, right, (((1,), (0,)), ((), ())), preferred_element_type=F32)


def dot_tn(left, right):
    return lax.dot_general(left, right, (((0,), (0,)), ((), ())), preferred_element_type=F32)


def dot_nt(left, right):
    return lax.dot_general(left, right, (((1,), (1,)), ((), ())), preferred_element_type=F32)


VMEM_LIMIT = 66_000_000


class Slots:
    def __init__(self):
        self.used = 0

    def take(self, count=1):
        first = self.used
        self.used += count
        return first


SEND_COUNT, RECV_COUNT, LOCAL_COUNT = 208, 208, 48


def layer_kernel(
    x_in,
    cot_in,
    w3_in,
    ow_in,
    fc_in,
    proj_in,
    ln1_gain_in,
    ln1_bias_in,
    ln2_gain_in,
    ln2_bias_in,
    out_bias_in,
    proj_bias_in,
    fc_bias_in,
    qv_bias_in,
    doc_in,
    out_o,
    ing_o,
    gf_o,
    gq_o,
    vec_o,
    rf1_hbm,
    rf2_hbm,
    rq1_hbm,
    rq2_hbm,
    XG,
    CG,
    N1,
    WB,
    QB,
    OWB,
    FB,
    COLS,
    PACK,
    PACKF,
    PACKN,
    MASK,
    QKV,
    LSE,
    ATT,
    HID,
    ST1,
    ST2,
    N2,
    ACT,
    GPRE,
    PGS,
    OPS,
    RCG,
    RCO,
    OPO,
    SZG,
    RZG,
    G2,
    SZO,
    RZO,
    RZN,
    DATT,
    GQKV,
    ACCK,
    ACCV,
    ZF,
    DQ,
    ZQ,
    ZT,
    GH,
    VGC,
    STX,
    SPR,
    SPZ,
    VOUT,
    SS,
    RS,
    LS,
):
    H, T = x_in.shape
    R = w3_in.shape[1]
    HP = DQ.shape[3]
    EXT = WB.shape[2]
    TAIL = EXT - R
    D = 2 * H
    S = 2 * T
    W = KEY_TILE
    Q = HEAD_DIM
    FW = fc_in.shape[1]
    per_tok = T // W
    n_tiles = S // W
    inv_d = 1.0 / D

    dp, z, c = lax.axis_index("dp"), lax.axis_index("row"), lax.axis_index("col")
    oc = 1 - c
    zz = lax.rem(z, 2)
    zp = z + 1 - 2 * zz
    z2 = lax.rem(z + 2, 4)
    j = lax.rem(z + 2 * c, 4)
    pair = z // 2
    core = (dp, z, oc)
    zdev = (dp, zp, c)
    xn = dp + 1 - 2 * lax.rem(dp, 2)
    yn = lax.rem(dp + 2, 4)
    dg = 3 - dp
    peers = (dg, xn, yn)
    xb, yb = lax.rem(dp, 2), dp // 2
    xdev, ydev = (xn, z, c), (yn, z, c)
    first_core, second_core = c == 0, c == 1

    sends, recvs, locs = Slots(), Slots(), Slots()
    pending = []

    def remote(src, dst, s_idx, r_idx, dev):
        return pltpu.make_async_remote_copy(
            src_ref=src,
            dst_ref=dst,
            send_sem=SS.at[s_idx],
            recv_sem=RS.at[r_idx],
            device_id=dev,
            device_id_type=MESH,
        )

    def when(cond, fn):
        if cond is None:
            fn()
        else:
            pl.when(cond)(fn)

    def push(src, dst, r_idx, dev, cond=None):
        copy = remote(src, dst, sends.take(), r_idx, dev)
        when(cond, copy.start)
        entry = [cond, copy]
        pending.append(entry)
        return entry

    def sent(entry):
        when(entry[0], entry[1].wait_send)
        pending[:] = [other for other in pending if other is not entry]

    def arrived(dst, r_idx, cond=None):
        when(cond, remote(dst, dst, 0, r_idx, core).wait_recv)

    def local(src, dst, cond=None):
        copy = pltpu.make_async_copy(src, dst, LS.at[locs.take()])
        when(cond, copy.start)
        return (cond, copy)

    def done(entry):
        when(entry[0], entry[1].wait)

    barrier = pltpu.get_barrier_semaphore()
    for step in range(4):
        for side in range(2):
            if step == 0 and side == 0:
                continue
            target = (dp, lax.rem(z + step, 4), c if side == 0 else oc)
            pl.semaphore_signal(barrier, inc=1, device_id=target, device_id_type=MESH)
    for peer in peers:
        pl.semaphore_signal(barrier, inc=1, device_id=(peer, z, c), device_id_type=MESH)
    pl.semaphore_wait(barrier, 10)

    r_x_core, r_x_z, r_x_fwd = recvs.take(), recvs.take(), recvs.take()
    r_w_core, r_w_z, r_w_xy, r_w_tail = recvs.take(), recvs.take(16), recvs.take(8), recvs.take(2)
    r_pack, r_packf, r_packn = recvs.take(), recvs.take(), recvs.take()
    r_f_core, r_f_z, r_f_xy = recvs.take(2), recvs.take(4), recvs.take(8)
    r_o_core, r_o_z, r_o_z0, r_o_xy, r_o_fwd = (
        recvs.take(),
        recvs.take(4),
        recvs.take(4),
        recvs.take(16),
        recvs.take(4),
    )

    def block(number):
        return pl.ds(pl.multiple_of(number * R, 16), R)

    quarter = D // 4
    odd = R - 4 * (R // 64) * 16
    piece = R // 64 * 16

    def quarter_rows(number):
        return pl.ds(pl.multiple_of(number * quarter, 16), quarter)

    def ow_piece(number, plane):
        return pl.ds(pl.multiple_of(number * R + odd + plane * piece, 16), piece)

    def ow_odd(number):
        return pl.ds(pl.multiple_of(number * R, 16), odd)

    my_quarter = quarter_rows(dp)
    more = H // 16 % 4
    share = H // 64 * 16

    def ff_share(plane, large):
        if large:
            return pl.ds(pl.multiple_of(plane * (share + 16), 16), share + 16)
        return pl.ds(pl.multiple_of(more * 16 + plane * share, 16), share)

    ff_kinds = ((True, dp < more), (False, dp >= more))
    w_pieces, row = [], 0
    for plane in range(4):
        left = (3 * R // 16 // 4 + (1 if plane < 3 * R // 16 % 4 else 0)) * 16
        while left:
            rows = min(left, R - row % R)
            w_pieces.append((plane, row // R, row % R, rows))
            row, left = row + rows, left - rows
    has_before = z >= 1
    bias_first = (LANES, LANES + (R // LANES + 1) * LANES)
    doc_count = doc_in.shape[1]
    w_entries = []
    for number, (plane, m, first, size) in enumerate(w_pieces):
        rows = pl.ds(first, size)
        w_entries.append(
            push(
                w3_in.at[m, rows], WB.at[m, c, rows], r_w_z + (2 * number + c), (dp, z2, 1), dp == plane
            )
        )
    pack = PACK.at[c]
    PACK[c] = jnp.zeros(PACK.shape[1:], F32)
    vectors_in = (ln1_gain_in, ln1_bias_in, ln2_gain_in, ln2_bias_in, out_bias_in, proj_bias_in, fc_bias_in)
    for number, vector in enumerate(vectors_in):
        PACK[c, number : number + 1, 0 : vector.shape[0]] = vector[...].astype(F32).reshape(1, -1)
    PACK[c, 7:8, 0:doc_count] = doc_in[...].astype(F32)
    for number in range(2):
        PACK[c, 7:8, bias_first[number] : bias_first[number] + R] = qv_bias_in[number : number + 1, :].astype(F32)
    push(x_in, XG.at[zz, c], r_x_z, zdev)
    push(x_in, XG.at[zz, c], r_x_core, core)
    push(pack, pack, r_pack, core)
    push(w3_in, WB.at[:, 1, pl.ds(0, R)], r_w_core, (dp, z, 0), second_core)
    push(w3_in.at[:, pl.ds(0, TAIL)], WB.at[:, c, pl.ds(R, TAIL)], r_w_tail + c, (dp, jnp.maximum(z - 1, 0), 0), has_before)
    push(w3_in.at[:, pl.ds(0, TAIL)], WB.at[:, c, pl.ds(R, TAIL)], r_w_tail + c, (dp, lax.rem(z + 1, 4), 1), has_before)
    push(pack, PACKF, r_packf, (dp, z2, 1), first_core)
    push(pack, PACKN, r_packn, (dp, jnp.maximum(z - 1, 0), 0), has_before & first_core)
    push(pack, PACKN, r_packn, (dp, lax.rem(z + 1, 4), 1), has_before & first_core)
    l_x = local(x_in, XG.at[zz, c])
    l_w = local(w3_in, WB.at[:, 0, pl.ds(0, R)], first_core)
    push(fc_in, FB.at[0, 1], r_f_core, (dp, z, 0), second_core)
    push(proj_in, FB.at[1, 1], r_f_core + 1, (dp, z, 0), second_core)
    push(ow_in, OWB.at[c, block(z)], r_o_core, core)
    l_f = local(fc_in, FB.at[0, 0], first_core)
    l_p = local(proj_in, FB.at[1, 0], first_core)
    l_o = local(ow_in, OWB.at[c, block(z)])

    ff_entries = []

    def send_ff(kind):
        source = (fc_in, proj_in)[kind]
        for large, cond in ff_kinds:
            rows = ff_share(dp, large)
            push(source.at[rows], FB.at[kind, c, rows], r_f_z + (2 * kind + c), (dp, z2, 1), cond)

    def pass_ff(kind):
        for large, cond in ff_kinds:
            rows = ff_share(dp, large)
            for h in range(2):
                arrived(FB.at[kind, h, rows], r_f_z + (2 * kind + h), second_core & cond)
            part = FB.at[kind, :, rows]
            for peer in peers:
                ff_entries.append(
                    push(part, part, r_f_xy + (4 * kind + dp), (peer, z, 1), second_core & cond)
                )

    def ff_ready(kind):
        arrived(FB.at[kind, 1], r_f_core + kind, first_core)
        for plane in range(4):
            arrived(
                FB.at[kind, :, ff_share(plane, plane < more)],
                r_f_xy + (4 * kind + plane),
                second_core & (dp != plane),
            )

    for entry in w_entries:
        sent(entry)
    send_ff(0)

    VGC[...] = jnp.zeros_like(VGC)
    GQKV[...] = jnp.zeros_like(GQKV)

    def clear_tail():
        WB[:, :, R:, :] = jnp.zeros((3, 2, TAIL, H), BF)

    pl.when(j == 3)(clear_tail)

    arrived(PACK.at[oc], r_pack)
    lengths = PACK[pair, 7:8, 0:LANES]
    place_c = lax.broadcasted_iota(jnp.int32, (S, LANES), 0).astype(F32)
    place_r = lax.broadcasted_iota(jnp.int32, (8, S), 1).astype(F32)
    end = jnp.zeros((1, 1), F32)
    seg_c, seg_r = jnp.zeros_like(place_c), jnp.zeros_like(place_r)
    for number in range(doc_count):
        end = end + lengths[:, number : number + 1]
        seg_c = seg_c + jnp.where(end <= place_c, 1.0, 0.0)
        seg_r = seg_r + jnp.where(end <= place_r, 1.0, 0.0)
    seg_c = jnp.where(end <= place_c, place_c + 2.0 * S, seg_c)
    seg_r = jnp.where(end <= place_r, place_r + 2.0 * S, seg_r)
    for tile in range(n_tiles):
        rows = W * (tile + 1)
        first = W * tile * (tile + 1) // 2
        cols = slice(tile * W, (tile + 1) * W)
        key_seg = jnp.concatenate([seg_c[:rows]] * (W // LANES), axis=1)
        key_place = jnp.concatenate([place_c[:rows]] * (W // LANES), axis=1)
        ok = (key_seg == seg_r[0:1, cols]) & (key_place <= place_r[0:1, cols])
        MASK[first : first + rows, :] = jnp.where(ok, 0.0, masked_fill)

    for h in range(2):
        COLS[h * H : (h + 1) * H, 0:6] = PACK[h].T[0:H, 0:6]

    def column(h, which):
        if isinstance(h, int):
            return COLS[h * H : (h + 1) * H, which : which + 1]
        return COLS[pl.ds(pl.multiple_of(h * H, 16), H), which : which + 1]

    def stats_of(first_half, second_half):
        center = (
            jnp.sum(first_half, axis=0, keepdims=True) + jnp.sum(second_half, axis=0, keepdims=True)
        ) * inv_d
        square = (
            jnp.sum(first_half * first_half, axis=0, keepdims=True)
            + jnp.sum(second_half * second_half, axis=0, keepdims=True)
        ) * inv_d
        return center, lax.rsqrt(square - center * center + epsilon)

    def first_norm(t):
        halves = [XG[t, h].astype(F32) for h in range(2)]
        center, inv_std = stats_of(*halves)
        ST1[t, 0:1, :] = center
        ST1[t, 1:2, :] = inv_std
        for h in range(2):
            shaped = (halves[h] - center) * inv_std * column(h, VEC_LN1_GAIN) + column(
                h, VEC_LN1_BIAS
            )
            N1[t, h, 0:H, :] = shaped.astype(BF)

    done(l_x)
    arrived(XG.at[zz, oc], r_x_core)
    first_norm(zz)

    for number, (plane, m, first, size) in enumerate(w_pieces):
        cond = second_core & (dp == plane)
        rows = pl.ds(first, size)
        for h in range(2):
            arrived(WB.at[m, h, rows], r_w_z + (2 * number + h), cond)
        for peer in peers:
            push(WB.at[m, :, rows], WB.at[m, :, rows], r_w_xy + number, (peer, z, 1), cond)
    arrived(XG.at[1 - zz, c], r_x_z)
    e_xf = push(XG.at[1 - zz, c], XG.at[1 - zz, c], r_x_fwd, core)
    arrived(XG.at[1 - zz, oc], r_x_fwd)
    first_norm(1 - zz)

    done(l_w)
    pass_ff(0)
    for step in (1, 3, 2):
        target = (dp, lax.rem(z + step, 4), c)
        push(ow_in.at[ow_piece(0, dp)], OWB.at[c, ow_piece(z, dp)], r_o_z + z, target)
        push(ow_in.at[ow_odd(0)], OWB.at[c, ow_odd(z)], r_o_z0 + z, target)
    arrived(WB.at[:, 1, pl.ds(0, R)], r_w_core, first_core)
    for number, (plane, m, first, size) in enumerate(w_pieces):
        arrived(WB.at[m, :, pl.ds(first, size)], r_w_xy + number, second_core & (dp != plane))
    for h in range(2):
        arrived(WB.at[:, h, pl.ds(R, TAIL)], r_w_tail + h, j < 3)

    arrived(PACKF, r_packf, second_core)
    arrived(PACKN, r_packn, j < 3)

    def bias_columns(source, rows, count):
        turned = source.T
        for m, first in ((0, bias_first[0]), (2, bias_first[1])):
            QB[rows : rows + count, m : m + 1] = turned[first : first + count, 7:8]

    QB[...] = jnp.zeros_like(QB)
    pl.when(first_core)(lambda: bias_columns(PACK[0], 0, R))
    pl.when(second_core)(lambda: bias_columns(PACKF[...], 0, R))
    pl.when(j < 3)(lambda: bias_columns(PACKN[...], R, TAIL))

    for t in range(2):
        for m in range(3):
            mixed = dot_nn(WB[m, 0], N1[t, 0]) + dot_nn(WB[m, 1], N1[t, 1])
            if m != 1:
                mixed = mixed + QB[:, m : m + 1]
            low = mixed.astype(BF)
            if m == 0:
                low = low * jnp.asarray(score_scale, BF)
            QKV[m, :, t * T : (t + 1) * T] = low

    send_ff(1)

    r_a_z, r_a_core, r_a_fwd = recvs.take(5), recvs.take(5), recvs.take(5)
    s_a_z, s_a_core, s_a_fwd = sends.take(5), sends.take(5), sends.take(5)
    first_slot = jnp.where(j == 0, 0, 1)

    def head_rows(owner, slot):
        return pl.ds(pl.multiple_of(owner * (4 * Q) + slot * Q, Q), Q)

    def slot_rows(slot):
        return pl.ds(pl.multiple_of(slot * Q - 16 * j, 16), Q)

    def att_copy(owner, slot, s_base, r_base, dev):
        rows = head_rows(owner, slot)
        return remote(ATT.at[rows], ATT.at[rows], s_base + slot, r_base + slot, dev)

    s_o_xy = sends.take(9)

    def ow_copy(step, number):
        there = lax.rem(z + step, 4)
        rows = OWB.at[c, ow_piece(there, dp)]
        return remote(
            rows, rows, s_o_xy + (3 * (step - 1) + number), r_o_xy + (4 * dp + there), (peers[number], z, c)
        )

    def pass_ow():
        for step in (1, 3, 2):
            there = lax.rem(z + step, 4)
            arrived(OWB.at[c, ow_piece(there, dp)], r_o_z + there)
            for number in range(3):
                ow_copy(step, number).start()

    def attend(slot, carry):
        @pl.when(slot == 2)
        def _():
            pass_ow()

        rows = slot_rows(slot)
        out_rows = head_rows(j, slot)
        queries = QKV[0, rows, :]
        keys = QKV[1, rows, :].T
        values = QKV[2, rows, :]
        for tile in range(n_tiles):
            count = W * (tile + 1)
            first = W * tile * (tile + 1) // 2
            cols = slice(tile * W, (tile + 1) * W)
            scores = dot_nn(keys[:count], queries[:, cols]) + MASK[first : first + count, :]
            best = jnp.max(scores, axis=0, keepdims=True)
            weights = jnp.exp(scores - best)
            mass = jnp.sum(weights, axis=0, keepdims=True)
            probs_low = (weights * (1.0 / mass)).astype(BF)
            ATT[out_rows, cols] = dot_nn(values[:, :count], probs_low).astype(BF)
            LSE[slot, 0:1, cols] = best + jnp.log(mass)
        att_copy(j, slot, s_a_z, r_a_z, zdev).start()
        att_copy(j, slot, s_a_core, r_a_core, core).start()

        return carry

    lax.fori_loop(first_slot, 5, attend, 0)

    r_c_core, r_c_z, r_c_fwd = recvs.take(), recvs.take(), recvs.take()
    push(cot_in, CG.at[zz, c], r_c_z, zdev)
    push(cot_in, CG.at[zz, c], r_c_core, core)
    l_c = local(cot_in, CG.at[zz, c])

    pass_ff(1)

    for step in (1, 3, 2):
        there = lax.rem(z + step, 4)
        arrived(OWB.at[c, ow_odd(there)], r_o_z0 + there)
        for plane in range(4):
            arrived(OWB.at[c, ow_piece(there, plane)], r_o_xy + (4 * plane + there), dp != plane)
        push(OWB.at[c, block(there)], OWB.at[c, block(there)], r_o_fwd + there, core)

    def owner_of(zv, cv):
        return lax.rem(zv + 2 * cv, 4)

    def slots_of(owner, body):
        lax.fori_loop(jnp.where(owner == 0, 0, 1), 5, lambda slot, carry: (body(slot), carry)[1], 0)

    def pass_on(slot):
        att_copy(owner_of(zp, c), slot, s_a_fwd, r_a_z, core).wait_recv()
        att_copy(owner_of(zp, c), slot, s_a_fwd, r_a_fwd, core).start()

    slots_of(owner_of(zp, c), pass_on)
    slots_of(owner_of(z, oc), lambda slot: att_copy(owner_of(z, oc), slot, s_a_core, r_a_core, core).wait_recv())
    slots_of(owner_of(zp, oc), lambda slot: att_copy(owner_of(zp, oc), slot, s_a_fwd, r_a_fwd, core).wait_recv())
    done(l_o)
    arrived(OWB.at[oc, block(z)], r_o_core)
    for step in range(1, 4):
        there = lax.rem(z + step, 4)
        arrived(OWB.at[oc, block(there)], r_o_fwd + there)

    def project(tile, carry):
        t = tile // per_tok
        cols = pl.ds(pl.multiple_of(lax.rem(tile, per_tok) * W, W), W)
        all_cols = pl.ds(pl.multiple_of(tile * W, W), W)
        att = ATT[:, all_cols]
        halves = []
        for h in range(2):
            branch = dot_tn(OWB[h], att)
            halves.append(XG[t, h, :, cols].astype(F32) + (branch + column(h, VEC_OUT_BIAS)))
            HID[t, h, :, cols] = halves[h]
        center, inv_std = stats_of(*halves)
        ST2[t, 0:1, cols] = center
        ST2[t, 1:2, cols] = inv_std
        for h in range(2):
            shaped = (halves[h] - center) * inv_std * column(h, VEC_LN2_GAIN) + column(
                h, VEC_LN2_BIAS
            )
            N2[t, h, :, cols] = shaped.astype(BF)
        return carry

    lax.fori_loop(0, n_tiles, project, 0)

    done(l_f)
    ff_ready(0)

    @pl.when(first_core)
    def _():
        COLS[:, 6:7] = PACK[0].T[0:FW, 6:7]

    @pl.when(second_core)
    def _():
        COLS[:, 6:7] = PACKF[...].T[0:FW, 6:7]

    s_c_fwd = sends.take()

    def cot_forward():
        return remote(CG.at[1 - zz, c], CG.at[1 - zz, c], s_c_fwd, r_c_fwd, core)

    def other_cotangent():
        arrived(CG.at[1 - zz, c], r_c_z)
        cot_forward().start()
        arrived(CG.at[1 - zz, oc], r_c_fwd)


    r_g_core, r_p_core, r_g_z = recvs.take(n_tiles), recvs.take(n_tiles), recvs.take(n_tiles)
    s_g_core, s_p_core, s_g_z = sends.take(n_tiles), sends.take(n_tiles), sends.take(n_tiles)

    def tile_at(tile):
        t = tile // per_tok
        return t, pl.ds(pl.multiple_of(lax.rem(tile, per_tok) * W, W), W)

    def part_copy(buf, dst, tile, s_base, r_base, dev):
        t, cols = tile_at(tile)
        return remote(buf.at[t, :, cols], dst.at[t, :, cols], s_base + tile, r_base + tile, dev)

    def feed(tile, carry):
        t, cols = tile_at(tile)
        all_cols = pl.ds(pl.multiple_of(tile * W, W), W)
        pre = dot_tn(FB[0].reshape(D, FW), N2[t, :, :, cols].reshape(D, W)) + COLS[:, 6:7]
        phi = 0.5 * (1.0 + lax.erf(pre * (2.0**-0.5)))
        ACT[:, all_cols] = (pre * phi).astype(BF)
        slope = phi + pre * jnp.exp(pre * pre * -0.5) * ((2.0 * math.pi) ** -0.5)
        GPRE[:, all_cols] = slope.astype(BF)
        return carry

    lax.fori_loop(0, n_tiles, feed, 0)
    done(l_p)
    ff_ready(1)
    done(l_c)
    arrived(CG.at[zz, oc], r_c_core)

    def feed_back(order, carry):
        t = lax.rem(order + zz, 2)
        pl.when(order == 1)(other_cotangent)
        for number in range(per_tok):
            cols = slice(number * W, (number + 1) * W)
            all_cols = pl.ds(pl.multiple_of(t * T + number * W, W), W)
            grad_act = dot_tn(FB[1].reshape(D, FW), CG[t, :, :, cols].reshape(D, W))
            GPRE[:, all_cols] = (grad_act * GPRE[:, all_cols].astype(F32)).astype(BF)
            PGS[t, :, cols] = dot_nn(FB[0, oc], GPRE[:, all_cols]).astype(BF)
            part_copy(PGS, RCG, t * per_tok + number, s_g_core, r_g_core, core).start()
        for number in range(per_tok):
            cols = slice(number * W, (number + 1) * W)
            all_cols = pl.ds(pl.multiple_of(t * T + number * W, W), W)
            tile = t * per_tok + number
            own = dot_nn(FB[0, c], GPRE[:, all_cols])
            part_copy(PGS, RCG, tile, s_g_core, r_g_core, core).wait_recv()
            SZG[t, :, cols] = (own + RCG[t, :, cols].astype(F32)).astype(BF)
            part_copy(SZG, RZG, tile, s_g_z, r_g_z, zdev).start()
        return carry

    lax.fori_loop(0, 2, feed_back, 0)

    for entry in ff_entries:
        sent(entry)
    r_f1, r_f2 = recvs.take(4), recvs.take(2)
    f1_entries = []

    def ff_grads(number):
        for h in range(2):
            left, right = (N2, GPRE) if number < 2 else (CG, ACT)
            rows = slice(number % 2 * quarter, (number % 2 + 1) * quarter)
            total = dot_nt(left[0, h, rows, :], right[:, 0:T]) + dot_nt(left[1, h, rows, :], right[:, T:S])
            FB[number // 2, h, rows, :] = total.astype(BF)

    def ff_rows(number):
        return quarter_rows(lax.rem(number, 2))

    def ff_part(h, number):
        return FB.at[number // 2, h, ff_rows(number)]

    def ff_value(h, number):
        return FB[number // 2, h, ff_rows(number), :].astype(F32)

    def f1_push(h, number, place, dev, cond=None):
        f1_entries.append(push(ff_part(h, number), rf1_hbm.at[place], r_f1 + place, dev, cond))

    ff_grads(0)
    ff_grads(1)
    f1_push(0, 1 - xb, 0, xdev)
    for number in range(2):
        f1_push(1, number, 2 + number, ydev, yb == 1)

    def outward(tile, carry):
        t, cols = tile_at(tile)
        all_cols = pl.ds(pl.multiple_of(tile * W, W), W)
        OPS[t, :, cols] = dot_nn(FB[1, oc], ACT[:, all_cols]).astype(BF)
        part_copy(OPS, RCO, tile, s_p_core, r_p_core, core).start()
        OPO[t, :, cols] = dot_nn(FB[1, c], ACT[:, all_cols]).astype(BF)
        return carry

    lax.fori_loop(0, n_tiles, outward, 0)
    ff_grads(2)
    ff_grads(3)
    f1_push(0, 3 - xb, 1, xdev)
    for number in range(2):
        f1_push(1, 2 + number, 2 + number, ydev, yb == 0)

    SPR[dp] = jnp.zeros(SPR.shape[1:], F32)
    SPR[dp, 6:7, :] = dot_nt(jnp.ones((16, S), BF), GPRE[...])[0:1, :]

    r_g_all = recvs.take(n_tiles)
    s_g_all = sends.take(n_tiles)

    def g2_copy(tile):
        t, cols = tile_at(tile)
        return remote(G2.at[t, c, :, cols], G2.at[t, c, :, cols], s_g_all + tile, r_g_all + tile, core)

    def g2_other(tile):
        t, cols = tile_at(tile)
        return remote(G2.at[t, oc, :, cols], G2.at[t, oc, :, cols], s_g_all + tile, r_g_all + tile, core)

    def join(tile, carry):
        t, cols = tile_at(tile)
        part_copy(SZG, RZG, tile, s_g_z, r_g_z, zdev).wait_recv()
        G2[t, c, :, cols] = (SZG[t, :, cols].astype(F32) + RZG[t, :, cols].astype(F32)).astype(BF)
        g2_copy(tile).start()
        return carry

    lax.fori_loop(0, n_tiles, join, 0)

    def norm_back(grads, normals, inv_std, gain_index):
        scaled = [grads[h] * column(h, gain_index) for h in range(2)]
        plain = sum(jnp.sum(scaled[h], axis=0, keepdims=True) for h in range(2)) * inv_d
        cross = sum(jnp.sum(scaled[h] * normals[h], axis=0, keepdims=True) for h in range(2)) * inv_d
        return [inv_std * (scaled[h] - plain - normals[h] * cross) for h in range(2)]

    def second_back(tile, carry):
        t, cols = tile_at(tile)
        g2_other(tile).wait_recv()
        center, inv_std = ST2[t, 0:1, cols], ST2[t, 1:2, cols]
        grads = [G2[t, h, :, cols].astype(F32) for h in range(2)]
        normals = [(HID[t, h, :, cols] - center) * inv_std for h in range(2)]
        back = norm_back(grads, normals, inv_std, VEC_LN2_GAIN)
        for h in range(2):
            grad_hidden = CG[t, h, :, cols].astype(F32) + back[h]
            XG[t, h, :, cols] = grad_hidden.astype(BF)

            @pl.when((t == zz) & (c == h))
            def _():
                GH[:, cols] = grad_hidden
                VGC[:, 2:3] = VGC[:, 2:3] + jnp.sum(grads[h] * normals[h], axis=1, keepdims=True)
                VGC[:, 3:4] = VGC[:, 3:4] + jnp.sum(grads[h], axis=1, keepdims=True)

        return carry

    sent(e_xf)
    lax.fori_loop(0, n_tiles, second_back, 0)
    GB = XG

    r_out_z = recvs.take()

    def wait_out(tile, carry):
        part_copy(OPS, RCO, tile, s_p_core, r_p_core, core).wait_recv()
        return carry

    lax.fori_loop(0, n_tiles, wait_out, 0)
    SZO[...] = (OPO[1 - zz].astype(F32) + RCO[1 - zz].astype(F32)).astype(BF)
    push(SZO, RZO, r_out_z, zdev)
    VGC[:, 4:5] = jnp.sum(GB[zz, c].astype(F32), axis=1, keepdims=True)
    VGC[:, 5:6] = jnp.sum(CG[zz, c].astype(F32), axis=1, keepdims=True)

    window = pl.ds(pl.multiple_of(j * (4 * Q), Q), 5 * Q)
    for t in range(2):
        DATT[:, t * T : (t + 1) * T] = (
            dot_nn(OWB[0, window, :], GB[t, 0]) + dot_nn(OWB[1, window, :], GB[t, 1])
        ).astype(BF)
    r_q1, r_q2 = recvs.take(4), recvs.take(2)
    q1_entries = []

    def q1_push(h, number, place, dev, cond=None):
        q1_entries.append(push(DQ.at[number, h], rq1_hbm.at[place], r_q1 + place, dev, cond))

    for h in range(2):
        total = dot_nt(ATT[block(j), 0:T], GB[0, h]) + dot_nt(ATT[block(j), T:S], GB[1, h])
        DQ[3, h, 0:R, 0:H] = total.astype(BF)
    q1_push(0, 3, 1, xdev, xb == 0)
    q1_push(1, 3, 3, ydev, yb == 0)
    l_x2 = local(x_in, XG.at[zz, c])

    s_f2 = sends.take(2)
    l_f1, l_f2 = locs.take(4), locs.take(2)

    def f2_copy(place):
        if place == 0:
            return remote(ff_part(0, xb + 2 * (1 - yb)), rf2_hbm.at[0], s_f2, r_f2, ydev)
        return remote(ff_part(1, 2 * yb + 1 - xb), rf2_hbm.at[1], s_f2 + 1, r_f2 + 1, xdev)

    spare = ((0, 1 - xb), (0, 3 - xb), (1, 2 * (1 - yb)), (1, 2 * (1 - yb) + 1))
    kept = ((0, xb), (0, 2 + xb), (1, 2 * yb), (1, 2 * yb + 1))

    def first_join():
        for entry in f1_entries:
            when(entry[0], entry[1].wait_send)
        loads = []
        for place in range(4):
            arrived(rf1_hbm.at[place], r_f1 + place)
            load = pltpu.make_async_copy(rf1_hbm.at[place], ff_part(*spare[place]), LS.at[l_f1 + place])
            load.start()
            loads.append(load)
        for load in loads:
            load.wait()

        def add(place):
            h, number = kept[place]
            total = ff_value(h, number) + ff_value(*spare[place])
            FB[number // 2, h, ff_rows(number), :] = total.astype(BF)

        for place in range(4):
            add(place)
        f2_copy(0).start()
        f2_copy(1).start()

    def attend_back(slot, carry):
        rows = slot_rows(slot)
        here = pl.ds(pl.multiple_of(slot * Q, Q), Q)
        queries = QKV[0, rows, :]
        keys_t = QKV[1, rows, :]
        keys = keys_t.T
        values = QKV[2, rows, :].T
        grads_out = DATT[here, :]
        for tile in reversed(range(n_tiles)):
            count = W * (tile + 1)
            first = W * tile * (tile + 1) // 2
            cols = slice(tile * W, (tile + 1) * W)
            scores = dot_nn(keys[:count], queries[:, cols]) + MASK[first : first + count, :]
            probs = jnp.exp(scores - LSE[slot, 0:1, cols])
            grad_probs = dot_nn(values[:count], grads_out[:, cols])
            delta = jnp.sum(probs * grad_probs, axis=0, keepdims=True)
            grad_scores = (probs * (grad_probs - delta)).astype(BF)
            probs_low = probs.astype(BF)
            part_v = dot_nt(grads_out[:, cols], probs_low)
            part_k = dot_nt(queries[:, cols], grad_scores)
            if tile == n_tiles - 1:
                ACCV[...] = part_v
                ACCK[...] = part_k
            else:
                ACCV[:, 0:count] = ACCV[:, 0:count] + part_v
                ACCK[:, 0:count] = ACCK[:, 0:count] + part_k
            GQKV[0, rows, cols] = (dot_nn(keys_t[:, :count], grad_scores) * score_scale).astype(BF)
        GQKV[1, rows, :] = ACCK[...].astype(BF)
        GQKV[2, rows, :] = ACCV[...].astype(BF)

        @pl.when(slot == 3)
        def _():
            first_join()

        return carry

    lax.fori_loop(first_slot, 5, attend_back, 0)

    for m in range(3):
        if m != 1:
            bias_sum = jnp.sum(GQKV[m].astype(F32), axis=1, keepdims=True)
        for h in range(2):
            total = dot_nt(GQKV[m, :, 0:T], N1[0, h]) + dot_nt(GQKV[m, :, T:S], N1[1, h])
            DQ[m, h, :, 0:H] = total.astype(BF)
            if m != 1:
                DQ[m, h, :, H : H + 1] = bias_sum.astype(BF)
        q1_push(0, m, m // 2, xdev, xb != m % 2)
        q1_push(1, m, 2 + m % 2, ydev, yb != m // 2)

    def wait_sends(tile, carry):
        part_copy(PGS, RCG, tile, s_g_core, r_g_core, core).wait_send()
        part_copy(OPS, RCO, tile, s_p_core, r_p_core, core).wait_send()
        part_copy(SZG, RZG, tile, s_g_z, r_g_z, zdev).wait_send()
        g2_copy(tile).wait_send()
        return carry

    lax.fori_loop(0, n_tiles, wait_sends, 0)
    r_n_core, r_n_z = recvs.take(n_tiles), recvs.take()
    s_n_core = sends.take(n_tiles)

    def back_rows(half, tile):
        all_cols = pl.ds(pl.multiple_of(tile * W, W), W)
        total = dot_tn(WB[0, half], GQKV[0, :, all_cols])
        for m in range(1, 3):
            total = total + dot_tn(WB[m, half], GQKV[m, :, all_cols])
        return total

    def first_part(tile, carry):
        t, cols = tile_at(tile)
        PGS[t, :, cols] = back_rows(oc, tile).astype(BF)
        part_copy(PGS, RCG, tile, s_n_core, r_n_core, core).start()
        OPS[t, :, cols] = back_rows(c, tile).astype(BF)
        return carry

    lax.fori_loop(0, n_tiles, first_part, 0)

    def wait_first(tile, carry):
        part_copy(PGS, RCG, tile, s_n_core, r_n_core, core).wait_recv()
        return carry

    lax.fori_loop(0, n_tiles, wait_first, 0)
    SZG[0] = (OPS[1 - zz].astype(F32) + RCG[1 - zz].astype(F32)).astype(BF)
    push(SZG.at[0], RZN, r_n_z, zdev)

    for entry in f1_entries:
        pending[:] = [other for other in pending if other is not entry]
    loads = []
    for h in range(2):
        arrived(rf2_hbm.at[h], r_f2 + h)
        loads.append(local(rf2_hbm.at[h], ff_part(*spare[2 * h])))
    r_zf = recvs.take(4)
    final_cut = (R // 16 + 1) // 2 * 16
    final_chunks = ((0, final_cut), (final_cut, R - final_cut))
    for h in range(2):
        done(loads[h])
        low = (ff_value(h, dp) + ff_value(*spare[2 * h])).astype(BF)
        FB[dp // 2, h, ff_rows(dp), :] = low
        if h == 0:

            @pl.when(first_core)
            def _():
                ZF[0] = low

        for chunk, (start, size) in enumerate(final_chunks):
            part = FB.at[dp // 2, h, pl.ds(pl.multiple_of(lax.rem(dp, 2) * quarter + start, 16), size)]
            rows = pl.ds(start, size)
            push(part, ZF.at[1, rows], r_zf + (2 + chunk), (dp, z2, h), second_core)
            if h == 1:
                push(part, ZF.at[0, rows], r_zf + chunk, (dp, z, 1), first_core)

    arrived(RZO, r_out_z)
    branch_out = OPO[zz].astype(F32) + RCO[zz].astype(F32) + RZO[...].astype(F32)
    OPO[0] = (HID[zz, c] + branch_out + column(c, VEC_PROJ_BIAS)).astype(BF)
    l_out = local(OPO.at[0], out_o)

    for entry in q1_entries:
        sent(entry)
    q_spare = ((1 - xb, 0), (3 - xb, 0), (2 * (1 - yb), 1), (2 * (1 - yb) + 1, 1))
    q_kept = ((xb, 0), (2 + xb, 0), (2 * yb, 1), (2 * yb + 1, 1))
    loads = []
    for place in range(4):
        arrived(rq1_hbm.at[place], r_q1 + place)
        loads.append(local(rq1_hbm.at[place], DQ.at[q_spare[place][0], q_spare[place][1]]))
    for place in range(4):
        done(loads[place])
        (there, h), (here, unused) = q_spare[place], q_kept[place]
        DQ[here, h] = (DQ[here, h].astype(F32) + DQ[there, h].astype(F32)).astype(BF)
    push(DQ.at[xb + 2 * (1 - yb), 0], rq2_hbm.at[0], r_q2, ydev)
    push(DQ.at[2 * yb + 1 - xb, 1], rq2_hbm.at[1], r_q2 + 1, xdev)

    r_gf, r_gq = recvs.take(8), recvs.take(8)

    def gf_at(plane, first, size):
        return gf_o.at[pl.ds(pl.multiple_of(plane * quarter + first, 16), size)]

    def gq_at(plane, first, size):
        return gq_o.at[plane, pl.ds(first, size)]

    def spread(buf, out_at, chunk, r_base):
        first, size = final_chunks[chunk]
        push(buf.at[0, pl.ds(first, size)], out_at(dp, first, size), r_base + 4 * chunk, xdev)
        push(buf.at[0, pl.ds(first, size)], out_at(dp, first, size), r_base + (4 * chunk + 1), ydev)
        return local(buf.at[0, pl.ds(first, size)], out_at(dp, first, size))

    def spread_on(out_at, chunk, r_base):
        first, size = final_chunks[chunk]
        half = size // 32 * 16
        arrived(out_at(xn, first, size), r_base + 4 * chunk)
        part = out_at(xn, first, half)
        push(part, part, r_base + (4 * chunk + 2), ydev)
        arrived(out_at(yn, first, size), r_base + (4 * chunk + 1))
        part = out_at(yn, first + half, size - half)
        push(part, part, r_base + (4 * chunk + 3), xdev)

    def spread_end(out_at, chunk, r_base):
        first, size = final_chunks[chunk]
        half = size // 32 * 16
        arrived(out_at(dg, first, half), r_base + (4 * chunk + 2))
        arrived(out_at(dg, first + half, size - half), r_base + (4 * chunk + 3))

    def ff_final(chunk):
        first, size = final_chunks[chunk]
        rows = pl.ds(first, size)
        arrived(ZF.at[0, rows], r_zf + chunk, second_core)
        arrived(ZF.at[1, rows], r_zf + (2 + chunk))
        here = slice(first, first + size)
        ZF[0, here] = (ZF[0, here].astype(F32) + ZF[1, here].astype(F32)).astype(BF)
        return spread(ZF, gf_at, chunk, r_gf)

    l_gf = [ff_final(0)]

    done(l_x2)
    arrived(RZN, r_n_z)
    r_stat = recvs.take()
    grads = OPS[zz].astype(F32) + RCG[zz].astype(F32) + RZN[...].astype(F32)
    center, inv_std = ST1[zz, 0:1, :], ST1[zz, 1:2, :]
    normals = (XG[zz, c].astype(F32) - center) * inv_std
    scaled = grads * column(c, VEC_LN1_GAIN)
    STX[c, 0:1, :] = jnp.sum(scaled, axis=0, keepdims=True)
    STX[c, 1:2, :] = jnp.sum(scaled * normals, axis=0, keepdims=True)
    push(STX.at[c], STX.at[c], r_stat, core)
    VGC[:, 0:1] = jnp.sum(grads * normals, axis=1, keepdims=True)
    VGC[:, 1:2] = jnp.sum(grads, axis=1, keepdims=True)
    arrived(STX.at[oc], r_stat)
    sums = (STX[0] + STX[1]) * inv_d
    OPO[1] = (GH[...] + inv_std * (scaled - sums[0:1] - normals * sums[1:2])).astype(BF)
    l_ing = local(OPO.at[1], ing_o)

    r_sp, r_spz = recvs.take(4), recvs.take(8)
    turned = VGC[...].T
    SPR[dp, 0:6, 0:H] = turned[0:6, :]
    for peer in peers:
        push(SPR.at[dp], SPR.at[dp], r_sp + dp, (peer, z, c))

    loads = []
    for h in range(2):
        arrived(rq2_hbm.at[h], r_q2 + h)
        loads.append(local(rq2_hbm.at[h], DQ.at[q_spare[2 * h][0], h]))
    r_zq, r_zt = recvs.take(4), recvs.take(2)
    with_tail = (j < 3) & (dp < 3)
    next_block = jnp.minimum(j + 1, 3)
    for h in range(2):
        done(loads[h])
        low = (DQ[dp, h].astype(F32) + DQ[q_spare[2 * h][0], h].astype(F32)).astype(BF)
        DQ[dp, h] = low
        if h == 0:

            @pl.when(first_core)
            def _():
                ZQ[0] = low[0:R]

        push(DQ.at[dp, h, pl.ds(R, TAIL)], ZT.at[c], r_zt + c, (dp, next_block, h), with_tail)
    for chunk, (start, size) in enumerate(final_chunks):
        rows = pl.ds(start, size)
        for h in range(2):
            push(DQ.at[dp, h, rows], ZQ.at[1, rows], r_zq + (2 + chunk), (dp, z2, h), second_core)
        push(DQ.at[dp, 1, rows], ZQ.at[0, rows], r_zq + chunk, (dp, z, 1), first_core)

    l_gf.append(ff_final(1))
    spread_on(gf_at, 0, r_gf)

    for number in range(4):
        arrived(SPR.at[number], r_sp + number, dp != number)
    SPZ[z, c] = SPR[0] + SPR[1] + SPR[2] + SPR[3]
    for step in range(4):
        for side in range(2):
            if step == 0 and side == 0:
                continue
            target = (dp, lax.rem(z + step, 4), c if side == 0 else oc)
            push(SPZ.at[z, c], SPZ.at[z, c], r_spz + (2 * z + c), target)

    gets_tail = (z >= 1) & (dp < 3)

    def qkv_final(chunk):
        first, size = final_chunks[chunk]
        rows = pl.ds(first, size)
        arrived(ZQ.at[0, rows], r_zq + chunk, second_core)
        arrived(ZQ.at[1, rows], r_zq + (2 + chunk))
        here = slice(first, first + size)
        total = ZQ[0, here].astype(F32) + ZQ[1, here].astype(F32)
        ZQ[0, here] = total.astype(BF)
        if chunk == 0:
            for side in range(2):
                arrived(ZT.at[side], r_zt + side, gets_tail)

            @pl.when(gets_tail)
            def _():
                ZQ[0, 0:TAIL] = (total[0:TAIL] + ZT[0].astype(F32) + ZT[1].astype(F32)).astype(BF)

        return spread(ZQ, gq_at, chunk, r_gq)

    l_gq = [qkv_final(0)]
    spread_on(gf_at, 1, r_gf)
    l_gq.append(qkv_final(1))

    for step in range(4):
        for side in range(2):
            if step == 0 and side == 0:
                continue
            zv, cv = lax.rem(z + step, 4), c if side == 0 else oc
            arrived(SPZ.at[zv, cv], r_spz + (2 * zv + cv))
    vectors = SPZ[0, c] + SPZ[1, c] + SPZ[2, c] + SPZ[3, c]
    VOUT[...] = vectors
    VOUT[6:7, :] = SPZ[z, 0, 6:7, :] + SPZ[z2, 1, 6:7, :]
    l_vec_o = local(VOUT, vec_o)

    for chunk in range(2):
        spread_on(gq_at, chunk, r_gq)
    for chunk in range(2):
        spread_end(gf_at, chunk, r_gf)
        spread_end(gq_at, chunk, r_gq)
    for entry in (l_out, l_ing, l_vec_o, *l_gf, *l_gq):
        done(entry)

    def own_sends(slot):
        att_copy(j, slot, s_a_z, r_a_z, zdev).wait_send()
        att_copy(j, slot, s_a_core, r_a_core, core).wait_send()

    slots_of(j, own_sends)
    slots_of(
        owner_of(zp, c),
        lambda slot: att_copy(owner_of(zp, c), slot, s_a_fwd, r_a_fwd, core).wait_send(),
    )

    f2_copy(0).wait_send()
    f2_copy(1).wait_send()
    cot_forward().wait_send()

    for step in (1, 3, 2):
        for number in range(3):
            ow_copy(step, number).wait_send()

    def last_sends(tile, carry):
        part_copy(PGS, RCG, tile, s_n_core, r_n_core, core).wait_send()
        return carry

    lax.fori_loop(0, n_tiles, last_sends, 0)
    for entry in list(pending):
        sent(entry)
    assert sends.used <= SEND_COUNT and recvs.used <= RECV_COUNT and locs.used <= LOCAL_COUNT


def finish_kernel(
    out_in,
    ing_in,
    gf_in,
    gq_in,
    vec_in,
    out_o,
    ing_o,
    qkv_o,
    qvb_o,
    ow_o,
    fc_o,
    proj_o,
    v0,
    v1,
    v2,
    v3,
    v4,
    v5,
    v6,
    GF,
    GQ,
    FST,
    QST,
    OB,
    SEM,
):
    R, H = ow_o.shape
    count = GF.shape[0] // R
    whole = [
        pltpu.make_async_copy(out_in, OB.at[0], SEM.at[0]),
        pltpu.make_async_copy(ing_in, OB.at[1], SEM.at[1]),
    ]
    place = 2
    loads_q, loads_f = [], []
    for m in range(4):
        loads_q.append(pltpu.make_async_copy(gq_in.at[m], GQ.at[m], SEM.at[place + m]))
    place += 4
    for number in range(count):
        rows = pl.ds(number * R, R)
        loads_f.append(pltpu.make_async_copy(gf_in.at[rows], GF.at[rows], SEM.at[place + number]))
    place += count
    for copy in loads_f + loads_q + whole:
        copy.start()
    stores = []
    for number in range(count):
        loads_f[number].wait()
        rows = pl.ds(number * R, R)
        FST[rows, :] = GF[rows, :].astype(F32)
        half = count // 2
        dst = (fc_o if number < half else proj_o).at[pl.ds(number % half * R, R)]
        stores.append(pltpu.make_async_copy(FST.at[rows], dst, SEM.at[place + number]))
        stores[-1].start()
    place += count
    for m in range(4):
        loads_q[m].wait()
        QST[m] = GQ[m, :, 0:H].astype(F32)
        dst = qkv_o.at[m] if m < 3 else ow_o
        stores.append(pltpu.make_async_copy(QST.at[m], dst, SEM.at[place + m]))
        stores[-1].start()
    place += 4
    for number, dst in enumerate((out_o, ing_o)):
        whole[number].wait()
        stores.append(pltpu.make_async_copy(OB.at[number], dst, SEM.at[place + number]))
        stores[-1].start()
    first = H // LANES * LANES
    for number, m in enumerate((0, 2)):
        turned = GQ[m, :, first : first + LANES].astype(F32).T
        qvb_o[number : number + 1, :] = turned[H - first : H - first + 1, :]
    for number, v in enumerate((v0, v1, v2, v3, v4, v5, v6)):
        v[...] = vec_in[number, 0 : v.shape[0]]
    for copy in stores:
        copy.wait()


def fast_body(
    tokens,
    ln1_gain,
    ln1_bias,
    qkv_weight,
    qv_bias,
    out_weight,
    out_bias,
    ln2_gain,
    ln2_bias,
    fc_weight,
    fc_bias,
    proj_weight,
    proj_bias,
    doc_lengths,
    cotangent,
):
    H, T = tokens.shape
    R = out_weight.shape[0]
    FW = fc_weight.shape[1]
    D, S = 2 * H, 2 * T
    HP = (H // LANES + 1) * LANES
    EXT = 5 * HEAD_DIM
    NT = S // KEY_TILE
    wide = (FW // LANES + 1) * LANES
    w3 = jnp.transpose(qkv_weight, (1, 2, 0))
    shape = jax.ShapeDtypeStruct
    anywhere = pl.BlockSpec(memory_space=pl.ANY)
    outs = [
        shape((H, T), BF),
        shape((H, T), BF),
        shape((2 * H, FW), BF),
        shape((4, R, HP), BF),
        shape((8, FW), F32),
        shape((4, D // 4, FW), BF),
        shape((2, D // 4, FW), BF),
        shape((4, EXT, HP), BF),
        shape((2, EXT, HP), BF),
    ]
    vmem = pltpu.VMEM
    mask_rows = KEY_TILE * NT * (NT + 1) // 2
    scratch = [
        vmem((2, 2, H, T), BF),
        vmem((2, 2, H, T), BF),
        vmem((2, 2, H, T), BF),
        vmem((3, 2, EXT, H), BF),
        vmem((EXT, LANES), F32),
        vmem((2, D, H), BF),
        vmem((2, 2, H, FW), BF),
        vmem((FW, LANES), F32),
        vmem((2, 8, wide), F32),
        vmem((8, wide), F32),
        vmem((8, wide), F32),
        vmem((mask_rows, KEY_TILE), F32),
        vmem((3, EXT, S), BF),
        vmem((5, 8, S), F32),
        vmem((D, S), BF),
        vmem((2, 2, H, T), F32),
        vmem((2, 8, T), F32),
        vmem((2, 8, T), F32),
        vmem((2, 2, H, T), BF),
        vmem((FW, S), BF),
        vmem((FW, S), BF),
        vmem((2, H, T), BF),
        vmem((2, H, T), BF),
        vmem((2, H, T), BF),
        vmem((2, H, T), BF),
        vmem((2, H, T), BF),
        vmem((2, H, T), BF),
        vmem((2, H, T), BF),
        vmem((2, 2, H, T), BF),
        vmem((H, T), BF),
        vmem((H, T), BF),
        vmem((H, T), BF),
        vmem((EXT, S), BF),
        vmem((3, EXT, S), BF),
        vmem((HEAD_DIM, S), F32),
        vmem((HEAD_DIM, S), F32),
        vmem((2, 2 * H // 4, FW), BF),
        vmem((4, 2, EXT, HP), BF),
        vmem((2, R, HP), BF),
        vmem((2, EXT - R, HP), BF),
        vmem((H, T), F32),
        vmem((H, LANES), F32),
        vmem((2, 8, T), F32),
        vmem((4, 8, FW), F32),
        vmem((4, 2, 8, FW), F32),
        vmem((8, FW), F32),
        pltpu.SemaphoreType.DMA((SEND_COUNT,)),
        pltpu.SemaphoreType.DMA((RECV_COUNT,)),
        pltpu.SemaphoreType.DMA((LOCAL_COUNT,)),
    ]
    out_rows, in_rows, gf, gq, vectors = pl.pallas_call(
        layer_kernel,
        out_shape=outs,
        in_specs=[anywhere] * 6 + [pl.BlockSpec(memory_space=vmem)] * 9,
        out_specs=[anywhere] * len(outs),
        scratch_shapes=scratch,
        compiler_params=pltpu.CompilerParams(
            collective_id=0, has_side_effects=True, vmem_limit_bytes=VMEM_LIMIT
        ),
    )(
        tokens,
        cotangent,
        w3,
        out_weight,
        fc_weight,
        proj_weight,
        ln1_gain,
        ln1_bias,
        ln2_gain,
        ln2_bias,
        out_bias,
        proj_bias,
        fc_bias,
        qv_bias,
        doc_lengths,
    )[:5]
    in_vmem = pl.BlockSpec(memory_space=vmem)
    finals = pl.pallas_call(
        finish_kernel,
        out_shape=[
            shape((H, T), BF),
            shape((H, T), BF),
            shape((3, R, H), F32),
            shape((2, R), F32),
            shape((R, H), F32),
            shape((H, FW), F32),
            shape((H, FW), F32),
        ]
        + [shape((H,), F32)] * 6
        + [shape((FW,), F32)],
        in_specs=[anywhere] * 4 + [in_vmem],
        out_specs=[anywhere] * 3 + [in_vmem] + [anywhere] * 3 + [in_vmem] * 7,
        scratch_shapes=[
            vmem((D, FW), BF),
            vmem((4, R, HP), BF),
            vmem((D, FW), F32),
            vmem((4, R, H), F32),
            vmem((2, H, T), BF),
            pltpu.SemaphoreType.DMA((32,)),
        ],
        compiler_params=pltpu.CompilerParams(vmem_limit_bytes=VMEM_LIMIT),
    )(out_rows, in_rows, gf, gq, vectors)
    out_final, in_final, qkv_rows, bias_grad, ow_grad, fc_grad, proj_grad = finals[:7]
    ln1_gain_g, ln1_bias_g, ln2_gain_g, ln2_bias_g, out_bias_g, proj_bias_g, fc_bias_g = finals[7:]
    return (
        out_final,
        in_final,
        ln1_gain_g,
        ln1_bias_g,
        jnp.transpose(qkv_rows, (2, 0, 1)),
        bias_grad,
        ow_grad,
        out_bias_g,
        ln2_gain_g,
        ln2_bias_g,
        fc_grad,
        fc_bias_g,
        proj_grad,
        proj_bias_g,
    )


def choose_body(*arrays):
    sizes = {axis: lax.axis_size(axis) for axis in ("dp", "row", "col")}
    H, R = arrays[0].shape[0], arrays[5].shape[0]
    fits = sizes == {"dp": 4, "row": 4, "col": 2} and 4 * R == 2 * H == 17 * HEAD_DIM
    return (fast_body if fits else body)(*arrays)


def solution(mesh):
    return jax.shard_map(
        choose_body,
        mesh=mesh,
        in_specs=(
            P("col", ("dp", "row")),
            P("col"),
            P("col"),
            P("col", None, "row"),
            P(None, "row"),
            P("row", "col"),
            P("col"),
            P("col"),
            P("col"),
            P("col", "row"),
            P("row"),
            P("col", "row"),
            P("col"),
            P(("dp", "col"), None),
            P("col", ("dp", "row")),
        ),
        out_specs=(
            P("col", ("dp", "row")),
            P("col", ("dp", "row")),
            P("col"),
            P("col"),
            P("col", None, "row"),
            P(None, "row"),
            P("row", "col"),
            P("col"),
            P("col"),
            P("col"),
            P("col", "row"),
            P("row"),
            P("col", "row"),
            P("col"),
        ),
        check_vma=False,
    )
```

```python
from functools import partial
import math

import jax
import jax.numpy as jnp
from jax import lax
from jax.experimental import pallas as pl
from jax.experimental.pallas import tpu as pltpu
from jax.sharding import PartitionSpec as P

HEAD_DIM = 64


epsilon = 1e-05
score_scale = 0.125
masked_fill = -1e30
block_limit = 512


def feature_sums(first_sum, second_sum):
    return lax.psum((first_sum, second_sum), "col")


def norm_forward(values, gain_vec, shift_vec):
    feature_count = values.shape[1] * lax.axis_size("col")
    total_sum, square_sum = feature_sums(jnp.sum(values, axis=1), jnp.sum(values * values, axis=1))
    center = total_sum / feature_count
    spread = square_sum / feature_count - center * center
    inv_std = lax.rsqrt(spread + epsilon)
    normal = (values - center[:, None]) * inv_std[:, None]
    return (normal, inv_std, normal * gain_vec + shift_vec)


def norm_backward(upstream, normal, inv_std, gain_vec):
    feature_count = upstream.shape[1] * lax.axis_size("col")
    scaled = upstream * gain_vec
    plain_sum, cross_sum = feature_sums(jnp.sum(scaled, axis=1), jnp.sum(scaled * normal, axis=1))
    return inv_std[:, None] * (
        scaled - plain_sum[:, None] / feature_count - normal * (cross_sum[:, None] / feature_count)
    )


def gather_rows(values):
    return lax.all_gather(values, "row", axis=0, tiled=True)


def gather_cols(values):
    return lax.all_gather(values, "col", axis=0, tiled=True)


def sum_over_rows(row_term, row_total):
    return lax.psum_scatter(
        row_term(jnp.int32(0), row_total * lax.axis_size("row")),
        "row",
        scatter_dimension=0,
        tiled=True,
    )


def sum_over_cols(row_term, row_total):
    return lax.psum_scatter(
        row_term(jnp.int32(0), row_total * lax.axis_size("col")),
        "col",
        scatter_dimension=0,
        tiled=True,
    )


def to_heads(values):
    return lax.all_to_all(values, "row", split_axis=0, concat_axis=2, tiled=True)


def to_tokens(values):
    return lax.all_to_all(values, "row", split_axis=2, concat_axis=0, tiled=True)


def product_term(full_rows, matrix):

    def row_term(first_row, row_count):
        return jnp.dot(full_rows, matrix, preferred_element_type=jnp.float32)

    return row_term


def product_term_back(full_rows, matrix):

    def row_term(first_row, row_count):
        return lax.dot_general(
            full_rows, matrix, (((1,), (1,)), ((), ())), preferred_element_type=jnp.float32
        )

    return row_term


def slice_term(full_rows):

    def row_term(first_row, row_count):
        return full_rows

    return row_term


def inner_rows(left_side, right_side):
    return lax.dot_general(
        left_side, right_side, (((0,), (0,)), ((), ())), preferred_element_type=jnp.float32
    )


def segments_of(lengths, places):
    doc_ends = jnp.cumsum(lengths)
    segment = jnp.sum(
        (doc_ends[None, :] <= places[:, None]).astype(jnp.int32), axis=1, dtype=jnp.int32
    )
    return (segment, places >= doc_ends[-1])


def allowed_pairs(query_place, query_segment, query_padding, key_place, key_segment):
    causal = key_place[None, :] <= query_place[:, None]
    same_doc = key_segment[None, :] == query_segment[:, None]
    itself = key_place[None, :] == query_place[:, None]
    return causal & same_doc & (jnp.logical_not(query_padding)[:, None] | itself)


def attention_parts(queries, keyvals, lengths, query_place):
    seq_total = keyvals.shape[0]
    key_block_size = math.gcd(seq_total, block_limit)
    block_count = seq_total // key_block_size
    key_place = jnp.arange(seq_total, dtype=jnp.int32)
    key_segment = segments_of(lengths, key_place)[0]
    query_segment, query_padding = segments_of(lengths, query_place)
    blocked = (
        keyvals.reshape((block_count, key_block_size) + keyvals.shape[1:]),
        key_place.reshape(block_count, key_block_size),
        key_segment.reshape(block_count, key_block_size),
    )

    def block_scores(key_rows, place_rows, segment_rows):
        raw_scores = (
            jnp.einsum("qhd,khd->hqk", queries, key_rows, preferred_element_type=jnp.float32)
            * score_scale
        )
        allowed = allowed_pairs(
            query_place, query_segment, query_padding, place_rows, segment_rows
        )[None]
        return (raw_scores, allowed)

    return (blocked, block_scores)


def attention_forward(queries, blocked, block_scores):
    query_count, head_count, head_width = queries.shape

    def max_step(running, inputs):
        best_score, mass_sum = running
        kv_block, place_rows, segment_rows = inputs
        raw_scores, allowed = block_scores(kv_block[:, 0], place_rows, segment_rows)
        masked = jnp.where(allowed, raw_scores, masked_fill)
        new_best = jnp.maximum(best_score, jnp.max(masked, axis=2))
        fresh = jnp.sum(jnp.where(allowed, jnp.exp(masked - new_best[:, :, None]), 0.0), axis=2)
        return ((new_best, mass_sum * jnp.exp(best_score - new_best) + fresh), None)

    start_best = jnp.full((head_count, query_count), masked_fill, jnp.float32)
    start_mass = jnp.zeros((head_count, query_count), jnp.float32)
    (best_score, mass_sum), unused = lax.scan(max_step, (start_best, start_mass), blocked)
    log_sum = best_score + jnp.log(mass_sum)

    def out_step(running, inputs):
        kv_block, place_rows, segment_rows = inputs
        raw_scores, allowed = block_scores(kv_block[:, 0], place_rows, segment_rows)
        probs_low = jnp.where(allowed, jnp.exp(raw_scores - log_sum[:, :, None]), 0.0).astype(
            jnp.bfloat16
        )
        return (
            running
            + jnp.einsum(
                "hqk,khd->qhd", probs_low, kv_block[:, 1], preferred_element_type=jnp.float32
            ),
            None,
        )

    attended, unused = lax.scan(
        out_step, jnp.zeros((query_count, head_count, head_width), jnp.float32), blocked
    )
    return (attended, log_sum)


def attention_backward(queries, blocked, block_scores, log_sum, grad_attended):
    query_count, head_count, head_width = queries.shape

    def probs_and_grads(inputs):
        kv_block, place_rows, segment_rows = inputs
        raw_scores, allowed = block_scores(kv_block[:, 0], place_rows, segment_rows)
        probs_f = jnp.where(allowed, jnp.exp(raw_scores - log_sum[:, :, None]), 0.0)
        grad_probs = jnp.einsum(
            "qhd,khd->hqk", grad_attended, kv_block[:, 1], preferred_element_type=jnp.float32
        )
        return (probs_f, grad_probs)

    def delta_step(running, inputs):
        probs_f, grad_probs = probs_and_grads(inputs)
        return (running + jnp.sum(probs_f * grad_probs, axis=2), None)

    delta_sum, unused = lax.scan(
        delta_step, jnp.zeros((head_count, query_count), jnp.float32), blocked
    )

    def grad_step(running, inputs):
        kv_block = inputs[0]
        probs_f, grad_probs = probs_and_grads(inputs)
        grad_scores = (probs_f * (grad_probs - delta_sum[:, :, None])).astype(jnp.bfloat16)
        running = running + jnp.einsum(
            "hqk,khd->qhd", grad_scores, kv_block[:, 0], preferred_element_type=jnp.float32
        )
        grad_keys = (
            jnp.einsum("hqk,qhd->khd", grad_scores, queries, preferred_element_type=jnp.float32)
            * score_scale
        )
        grad_values = jnp.einsum(
            "hqk,qhd->khd",
            probs_f.astype(jnp.bfloat16),
            grad_attended,
            preferred_element_type=jnp.float32,
        )
        return (running, jnp.stack([grad_keys, grad_values], axis=1))

    grad_queries, grad_keyvals = lax.scan(
        grad_step, jnp.zeros((query_count, head_count, head_width), jnp.float32), blocked
    )
    seq_total = grad_keyvals.shape[0] * grad_keyvals.shape[1]
    return (grad_queries * score_scale, grad_keyvals.reshape(seq_total, 2, head_count, head_width))


def body(
    tokens,
    ln1_gain,
    ln1_bias,
    qkv_weight,
    qv_bias,
    out_weight,
    out_bias,
    ln2_gain,
    ln2_bias,
    fc_weight,
    fc_bias,
    proj_weight,
    proj_bias,
    doc_lengths,
    cotangent,
):
    count_rows = lax.axis_size("row")
    count_cols = lax.axis_size("col")
    grid_rows = tokens.shape[1]
    col_width = tokens.shape[0]
    row_width = out_weight.shape[0]
    seq_rows = grid_rows * count_rows // count_cols
    query_rows = seq_rows // count_rows
    full_width = col_width * count_cols
    head_count = full_width // HEAD_DIM
    tokens_f = tokens.astype(jnp.float32).T
    normal1, inv_std1, shaped1 = norm_forward(tokens_f, ln1_gain, ln1_bias)
    qkv_flat = qkv_weight.reshape(col_width, 3 * row_width)
    gathered1 = gather_rows(shaped1.astype(jnp.bfloat16))
    mixed_qkv = sum_over_cols(product_term(gathered1, qkv_flat), seq_rows).reshape(
        seq_rows, 3, row_width
    )
    bias_three = jnp.stack([qv_bias[0], jnp.zeros_like(qv_bias[0]), qv_bias[1]])
    qkv_low = (mixed_qkv + bias_three).astype(jnp.bfloat16)
    local_qkv = to_heads(qkv_low).reshape(query_rows, 3, head_count, HEAD_DIM)
    queries = local_qkv[:, 0]
    keyvals = lax.all_gather(local_qkv[:, 1:], "row", axis=0, tiled=True)
    query_place = lax.axis_index("row") * query_rows + jnp.arange(query_rows, dtype=jnp.int32)
    blocked, block_scores = attention_parts(queries, keyvals, doc_lengths[0], query_place)
    attended_f, log_sum = attention_forward(queries, blocked, block_scores)
    attended_low = attended_f.reshape(query_rows, 1, full_width).astype(jnp.bfloat16)
    attended_grid = to_tokens(attended_low).reshape(seq_rows, row_width)
    gathered_att = gather_cols(attended_grid)
    branch = sum_over_rows(product_term(gathered_att, out_weight), grid_rows)
    hidden = tokens_f + (branch + out_bias)
    normal2, inv_std2, shaped2 = norm_forward(hidden, ln2_gain, ln2_bias)
    normed2 = shaped2.astype(jnp.bfloat16)
    gathered2 = gather_rows(normed2)
    pre_act = sum_over_cols(product_term(gathered2, fc_weight), seq_rows) + fc_bias
    active = jax.nn.gelu(pre_act, approximate=False).astype(jnp.bfloat16)
    gathered_act = gather_cols(active)
    projected = sum_over_rows(product_term_back(gathered_act, proj_weight), grid_rows)
    output = (hidden + projected + proj_bias).astype(jnp.bfloat16).T
    cotangent_rows = cotangent.T
    grad_out = cotangent_rows.astype(jnp.float32)
    unused, gelu_back = jax.vjp(partial(jax.nn.gelu, approximate=False), pre_act)
    grad_gathered = gather_rows(cotangent_rows)
    proj_weight_grad = inner_rows(grad_gathered, gathered_act)
    proj_bias_grad = jnp.sum(grad_gathered, axis=0, dtype=jnp.float32)
    grad_active = sum_over_cols(product_term(grad_gathered, proj_weight), seq_rows)
    grad_pre = gelu_back(grad_active)[0].astype(jnp.bfloat16)
    grad_pre_all = gather_cols(grad_pre)
    fc_weight_grad = inner_rows(gathered2, grad_pre_all)
    fc_bias_grad = jnp.sum(grad_pre_all, axis=0, dtype=jnp.float32)
    grad_normed2 = sum_over_rows(product_term_back(grad_pre_all, fc_weight), grid_rows)
    ln2_gain_part = jnp.sum(grad_normed2 * normal2, axis=0)
    ln2_bias_part = jnp.sum(grad_normed2, axis=0)
    grad_hidden = grad_out + norm_backward(grad_normed2, normal2, inv_std2, ln2_gain)
    branch_gathered = gather_rows(grad_hidden.astype(jnp.bfloat16))
    out_weight_grad = inner_rows(gathered_att, branch_gathered)
    out_bias_grad = jnp.sum(branch_gathered, axis=0, dtype=jnp.float32)
    grad_att_grid = sum_over_cols(product_term_back(branch_gathered, out_weight), seq_rows).astype(
        jnp.bfloat16
    )
    grad_attended = to_heads(grad_att_grid.reshape(seq_rows, 1, row_width)).reshape(
        query_rows, head_count, HEAD_DIM
    )
    grad_queries, grad_keyvals = attention_backward(
        queries, blocked, block_scores, log_sum, grad_attended
    )
    keyval_rows = sum_over_rows(slice_term(grad_keyvals), query_rows)
    grad_qkv_local = (
        jnp.concatenate([grad_queries[:, None], keyval_rows], axis=1)
        .astype(jnp.bfloat16)
        .reshape(query_rows, 3, full_width)
    )
    grad_qkv_grid = to_tokens(grad_qkv_local).reshape(seq_rows, 3 * row_width)
    qkv_gathered = gather_cols(grad_qkv_grid)
    qkv_weight_grad = inner_rows(gathered1, qkv_gathered).reshape(col_width, 3, row_width)
    qkv_bias_sums = jnp.sum(qkv_gathered, axis=0, dtype=jnp.float32).reshape(3, row_width)
    qv_bias_grad = jnp.stack([qkv_bias_sums[0], qkv_bias_sums[2]])
    grad_normed1 = sum_over_rows(product_term_back(qkv_gathered, qkv_flat), grid_rows)
    ln1_gain_part = jnp.sum(grad_normed1 * normal1, axis=0)
    ln1_bias_part = jnp.sum(grad_normed1, axis=0)
    input_grad = (
        (grad_hidden + norm_backward(grad_normed1, normal1, inv_std1, ln1_gain))
        .astype(jnp.bfloat16)
        .T
    )
    summed = lax.psum(
        (
            qkv_weight_grad,
            qv_bias_grad,
            out_weight_grad,
            out_bias_grad,
            fc_weight_grad,
            fc_bias_grad,
            proj_weight_grad,
            proj_bias_grad,
        ),
        "dp",
    )
    gain_sums = lax.psum(
        (ln1_gain_part, ln1_bias_part, ln2_gain_part, ln2_bias_part), ("dp", "row")
    )
    return (
        output,
        input_grad,
        gain_sums[0],
        gain_sums[1],
        summed[0],
        summed[1],
        summed[2],
        summed[3],
        gain_sums[2],
        gain_sums[3],
        summed[4],
        summed[5],
        summed[6],
        summed[7],
    )


BF = jnp.bfloat16
F32 = jnp.float32
MESH = pl.DeviceIdType.MESH
LANES = 128
KEY_TILE = 256
VEC_LN1_GAIN, VEC_LN1_BIAS, VEC_LN2_GAIN, VEC_LN2_BIAS, VEC_OUT_BIAS, VEC_PROJ_BIAS = range(6)


def dot_nn(left, right):
    return lax.dot_general(left, right, (((1,), (0,)), ((), ())), preferred_element_type=F32)


def dot_tn(left, right):
    return lax.dot_general(left, right, (((0,), (0,)), ((), ())), preferred_element_type=F32)


def dot_nt(left, right):
    return lax.dot_general(left, right, (((1,), (1,)), ((), ())), preferred_element_type=F32)


VMEM_LIMIT = 66_000_000


class Slots:
    def __init__(self):
        self.used = 0

    def take(self, count=1):
        first = self.used
        self.used += count
        return first


SEND_COUNT, RECV_COUNT, LOCAL_COUNT = 208, 208, 48


def layer_kernel(
    x_in,
    cot_in,
    w3_in,
    ow_in,
    fc_in,
    proj_in,
    ln1_gain_in,
    ln1_bias_in,
    ln2_gain_in,
    ln2_bias_in,
    out_bias_in,
    proj_bias_in,
    fc_bias_in,
    qv_bias_in,
    doc_in,
    out_o,
    ing_o,
    gf_o,
    gq_o,
    vec_o,
    rf1_hbm,
    rf2_hbm,
    rq1_hbm,
    rq2_hbm,
    XG,
    CG,
    N1,
    WB,
    QB,
    OWB,
    FB,
    COLS,
    PACK,
    PACKF,
    PACKN,
    MASK,
    QKV,
    LSE,
    ATT,
    HID,
    ST1,
    ST2,
    N2,
    ACT,
    GPRE,
    PGS,
    OPS,
    RCG,
    RCO,
    OPO,
    SZG,
    RZG,
    G2,
    SZO,
    RZO,
    RZN,
    DATT,
    GQKV,
    ACCK,
    ACCV,
    ZF,
    DQ,
    ZQ,
    ZT,
    GH,
    VGC,
    STX,
    SPR,
    SPZ,
    VOUT,
    SS,
    RS,
    LS,
):
    H, T = x_in.shape
    R = w3_in.shape[1]
    HP = DQ.shape[3]
    EXT = WB.shape[2]
    TAIL = EXT - R
    D = 2 * H
    S = 2 * T
    W = KEY_TILE
    Q = HEAD_DIM
    FW = fc_in.shape[1]
    per_tok = T // W
    n_tiles = S // W
    inv_d = 1.0 / D

    dp, z, c = lax.axis_index("dp"), lax.axis_index("row"), lax.axis_index("col")
    oc = 1 - c
    zz = lax.rem(z, 2)
    zp = z + 1 - 2 * zz
    z2 = lax.rem(z + 2, 4)
    j = lax.rem(z + 2 * c, 4)
    pair = z // 2
    core = (dp, z, oc)
    zdev = (dp, zp, c)
    xn = dp + 1 - 2 * lax.rem(dp, 2)
    yn = lax.rem(dp + 2, 4)
    dg = 3 - dp
    peers = (dg, xn, yn)
    xb, yb = lax.rem(dp, 2), dp // 2
    xdev, ydev = (xn, z, c), (yn, z, c)
    first_core, second_core = c == 0, c == 1

    sends, recvs, locs = Slots(), Slots(), Slots()
    pending = []

    def remote(src, dst, s_idx, r_idx, dev):
        return pltpu.make_async_remote_copy(
            src_ref=src,
            dst_ref=dst,
            send_sem=SS.at[s_idx],
            recv_sem=RS.at[r_idx],
            device_id=dev,
            device_id_type=MESH,
        )

    def when(cond, fn):
        if cond is None:
            fn()
        else:
            pl.when(cond)(fn)

    def push(src, dst, r_idx, dev, cond=None):
        copy = remote(src, dst, sends.take(), r_idx, dev)
        when(cond, copy.start)
        entry = [cond, copy]
        pending.append(entry)
        return entry

    def sent(entry):
        when(entry[0], entry[1].wait_send)
        pending[:] = [other for other in pending if other is not entry]

    def arrived(dst, r_idx, cond=None):
        when(cond, remote(dst, dst, 0, r_idx, core).wait_recv)

    def local(src, dst, cond=None):
        copy = pltpu.make_async_copy(src, dst, LS.at[locs.take()])
        when(cond, copy.start)
        return (cond, copy)

    def done(entry):
        when(entry[0], entry[1].wait)

    barrier = pltpu.get_barrier_semaphore()
    for step in range(4):
        for side in range(2):
            if step == 0 and side == 0:
                continue
            target = (dp, lax.rem(z + step, 4), c if side == 0 else oc)
            pl.semaphore_signal(barrier, inc=1, device_id=target, device_id_type=MESH)
    for peer in peers:
        pl.semaphore_signal(barrier, inc=1, device_id=(peer, z, c), device_id_type=MESH)
    pl.semaphore_wait(barrier, 10)

    r_x_core, r_x_z, r_x_fwd = recvs.take(), recvs.take(), recvs.take()
    r_w_core, r_w_z, r_w_xy, r_w_tail = recvs.take(), recvs.take(16), recvs.take(8), recvs.take(2)
    r_pack, r_packf, r_packn = recvs.take(), recvs.take(), recvs.take()
    r_f_core, r_f_z, r_f_xy = recvs.take(2), recvs.take(4), recvs.take(8)
    r_o_core, r_o_z, r_o_z0, r_o_xy, r_o_fwd = (
        recvs.take(),
        recvs.take(4),
        recvs.take(4),
        recvs.take(16),
        recvs.take(4),
    )

    def block(number):
        return pl.ds(pl.multiple_of(number * R, 16), R)

    quarter = D // 4
    odd = R - 4 * (R // 64) * 16
    piece = R // 64 * 16

    def quarter_rows(number):
        return pl.ds(pl.multiple_of(number * quarter, 16), quarter)

    def ow_piece(number, plane):
        return pl.ds(pl.multiple_of(number * R + odd + plane * piece, 16), piece)

    def ow_odd(number):
        return pl.ds(pl.multiple_of(number * R, 16), odd)

    my_quarter = quarter_rows(dp)
    more = H // 16 % 4
    share = H // 64 * 16

    def ff_share(plane, large):
        if large:
            return pl.ds(pl.multiple_of(plane * (share + 16), 16), share + 16)
        return pl.ds(pl.multiple_of(more * 16 + plane * share, 16), share)

    ff_kinds = ((True, dp < more), (False, dp >= more))
    w_pieces, row = [], 0
    for plane in range(4):
        left = (3 * R // 16 // 4 + (1 if plane < 3 * R // 16 % 4 else 0)) * 16
        while left:
            rows = min(left, R - row % R)
            w_pieces.append((plane, row // R, row % R, rows))
            row, left = row + rows, left - rows
    has_before = z >= 1
    bias_first = (LANES, LANES + (R // LANES + 1) * LANES)
    doc_count = doc_in.shape[1]
    w_entries = []
    for number, (plane, m, first, size) in enumerate(w_pieces):
        rows = pl.ds(first, size)
        w_entries.append(
            push(
                w3_in.at[m, rows], WB.at[m, c, rows], r_w_z + (2 * number + c), (dp, z2, 1), dp == plane
            )
        )
    pack = PACK.at[c]
    PACK[c] = jnp.zeros(PACK.shape[1:], F32)
    vectors_in = (ln1_gain_in, ln1_bias_in, ln2_gain_in, ln2_bias_in, out_bias_in, proj_bias_in, fc_bias_in)
    for number, vector in enumerate(vectors_in):
        PACK[c, number : number + 1, 0 : vector.shape[0]] = vector[...].astype(F32).reshape(1, -1)
    PACK[c, 7:8, 0:doc_count] = doc_in[...].astype(F32)
    for number in range(2):
        PACK[c, 7:8, bias_first[number] : bias_first[number] + R] = qv_bias_in[number : number + 1, :].astype(F32)
    push(x_in, XG.at[zz, c], r_x_z, zdev)
    push(x_in, XG.at[zz, c], r_x_core, core)
    push(pack, pack, r_pack, core)
    push(w3_in, WB.at[:, 1, pl.ds(0, R)], r_w_core, (dp, z, 0), second_core)
    for place in range(1, 4):
        rows = TAIL - 16 * (place - 1)
        head = w3_in.at[:, pl.ds(0, rows)]
        there = WB.at[:, c, pl.ds(R, rows)]
        push(head, there, r_w_tail + c, (dp, place - 1, 0), z == place)
        push(head, there, r_w_tail + c, (dp, (place + 1) % 4, 1), z == place)
    push(pack, PACKF, r_packf, (dp, z2, 1), first_core)
    push(pack, PACKN, r_packn, (dp, jnp.maximum(z - 1, 0), 0), has_before & first_core)
    push(pack, PACKN, r_packn, (dp, lax.rem(z + 1, 4), 1), has_before & first_core)
    l_x = local(x_in, XG.at[zz, c])
    l_w = local(w3_in, WB.at[:, 0, pl.ds(0, R)], first_core)
    push(fc_in, FB.at[0, 1], r_f_core, (dp, z, 0), second_core)
    push(proj_in, FB.at[1, 1], r_f_core + 1, (dp, z, 0), second_core)
    push(ow_in, OWB.at[c, block(z)], r_o_core, core)
    l_f = local(fc_in, FB.at[0, 0], first_core)
    l_p = local(proj_in, FB.at[1, 0], first_core)
    l_o = local(ow_in, OWB.at[c, block(z)])

    ff_entries = []

    def send_ff(kind):
        source = (fc_in, proj_in)[kind]
        for large, cond in ff_kinds:
            rows = ff_share(dp, large)
            push(source.at[rows], FB.at[kind, c, rows], r_f_z + (2 * kind + c), (dp, z2, 1), cond)

    def pass_ff(kind):
        for large, cond in ff_kinds:
            rows = ff_share(dp, large)
            for h in range(2):
                arrived(FB.at[kind, h, rows], r_f_z + (2 * kind + h), second_core & cond)
            part = FB.at[kind, :, rows]
            for peer in peers:
                ff_entries.append(
                    push(part, part, r_f_xy + (4 * kind + dp), (peer, z, 1), second_core & cond)
                )

    def ff_ready(kind):
        arrived(FB.at[kind, 1], r_f_core + kind, first_core)
        for plane in range(4):
            arrived(
                FB.at[kind, :, ff_share(plane, plane < more)],
                r_f_xy + (4 * kind + plane),
                second_core & (dp != plane),
            )

    for entry in w_entries:
        sent(entry)
    send_ff(0)

    VGC[...] = jnp.zeros_like(VGC)
    GQKV[...] = jnp.zeros_like(GQKV)

    def clear_tail(rows):
        WB[:, :, EXT - rows :, :] = jnp.zeros((3, 2, rows, H), BF)

    for place in range(1, 4):
        pl.when(j == place)(partial(clear_tail, 16 * place))

    arrived(PACK.at[oc], r_pack)
    lengths = PACK[pair, 7:8, 0:LANES]
    place_c = lax.broadcasted_iota(jnp.int32, (S, LANES), 0).astype(F32)
    place_r = lax.broadcasted_iota(jnp.int32, (8, S), 1).astype(F32)
    end = jnp.zeros((1, 1), F32)
    seg_c, seg_r = jnp.zeros_like(place_c), jnp.zeros_like(place_r)
    for number in range(doc_count):
        end = end + lengths[:, number : number + 1]
        seg_c = seg_c + jnp.where(end <= place_c, 1.0, 0.0)
        seg_r = seg_r + jnp.where(end <= place_r, 1.0, 0.0)
    seg_c = jnp.where(end <= place_c, place_c + 2.0 * S, seg_c)
    seg_r = jnp.where(end <= place_r, place_r + 2.0 * S, seg_r)
    for tile in range(n_tiles):
        rows = W * (tile + 1)
        first = W * tile * (tile + 1) // 2
        cols = slice(tile * W, (tile + 1) * W)
        key_seg = jnp.concatenate([seg_c[:rows]] * (W // LANES), axis=1)
        key_place = jnp.concatenate([place_c[:rows]] * (W // LANES), axis=1)
        ok = (key_seg == seg_r[0:1, cols]) & (key_place <= place_r[0:1, cols])
        MASK[first : first + rows, :] = jnp.where(ok, 0.0, masked_fill)

    for h in range(2):
        COLS[h * H : (h + 1) * H, 0:6] = PACK[h].T[0:H, 0:6]

    def column(h, which):
        if isinstance(h, int):
            return COLS[h * H : (h + 1) * H, which : which + 1]
        return COLS[pl.ds(pl.multiple_of(h * H, 16), H), which : which + 1]

    def stats_of(first_half, second_half):
        center = (
            jnp.sum(first_half, axis=0, keepdims=True) + jnp.sum(second_half, axis=0, keepdims=True)
        ) * inv_d
        square = (
            jnp.sum(first_half * first_half, axis=0, keepdims=True)
            + jnp.sum(second_half * second_half, axis=0, keepdims=True)
        ) * inv_d
        return center, lax.rsqrt(square - center * center + epsilon)

    def first_norm(t):
        halves = [XG[t, h].astype(F32) for h in range(2)]
        center, inv_std = stats_of(*halves)
        ST1[t, 0:1, :] = center
        ST1[t, 1:2, :] = inv_std
        for h in range(2):
            shaped = (halves[h] - center) * inv_std * column(h, VEC_LN1_GAIN) + column(
                h, VEC_LN1_BIAS
            )
            N1[t, h, 0:H, :] = shaped.astype(BF)

    done(l_x)
    arrived(XG.at[zz, oc], r_x_core)
    first_norm(zz)

    for number, (plane, m, first, size) in enumerate(w_pieces):
        cond = second_core & (dp == plane)
        rows = pl.ds(first, size)
        for h in range(2):
            arrived(WB.at[m, h, rows], r_w_z + (2 * number + h), cond)
        for peer in peers:
            push(WB.at[m, :, rows], WB.at[m, :, rows], r_w_xy + number, (peer, z, 1), cond)
    arrived(XG.at[1 - zz, c], r_x_z)
    e_xf = push(XG.at[1 - zz, c], XG.at[1 - zz, c], r_x_fwd, core)
    arrived(XG.at[1 - zz, oc], r_x_fwd)
    first_norm(1 - zz)

    done(l_w)
    pass_ff(0)
    for step in (1, 3, 2):
        target = (dp, lax.rem(z + step, 4), c)
        push(ow_in.at[ow_piece(0, dp)], OWB.at[c, ow_piece(z, dp)], r_o_z + z, target)
        push(ow_in.at[ow_odd(0)], OWB.at[c, ow_odd(z)], r_o_z0 + z, target)
    send_ff(1)
    arrived(WB.at[:, 1, pl.ds(0, R)], r_w_core, first_core)
    for number, (plane, m, first, size) in enumerate(w_pieces):
        arrived(WB.at[m, :, pl.ds(first, size)], r_w_xy + number, second_core & (dp != plane))
    for h in range(2):
        for place in range(3):
            arrived(WB.at[:, h, pl.ds(R, TAIL - 16 * place)], r_w_tail + h, j == place)

    arrived(PACKF, r_packf, second_core)
    arrived(PACKN, r_packn, j < 3)

    def bias_columns(source, rows, count):
        turned = source.T
        for m, first in ((0, bias_first[0]), (2, bias_first[1])):
            QB[rows : rows + count, m : m + 1] = turned[first : first + count, 7:8]

    QB[...] = jnp.zeros_like(QB)
    pl.when(first_core)(lambda: bias_columns(PACK[0], 0, R))
    pl.when(second_core)(lambda: bias_columns(PACKF[...], 0, R))
    pl.when(j < 3)(lambda: bias_columns(PACKN[...], R, TAIL))

    for t in range(2):
        for m in range(3):
            mixed = dot_nn(WB[m, 0], N1[t, 0]) + dot_nn(WB[m, 1], N1[t, 1])
            if m != 1:
                mixed = mixed + QB[:, m : m + 1]
            low = mixed.astype(BF)
            if m == 0:
                low = low * jnp.asarray(score_scale, BF)
            QKV[m, :, t * T : (t + 1) * T] = low


    r_a_z, r_a_core, r_a_fwd = recvs.take(5), recvs.take(5), recvs.take(5)
    s_a_z, s_a_core, s_a_fwd = sends.take(5), sends.take(5), sends.take(5)
    first_slot = jnp.where(j == 0, 0, 1)

    def head_rows(owner, slot):
        return pl.ds(pl.multiple_of(owner * (4 * Q) + slot * Q, Q), Q)

    def slot_rows(slot):
        return pl.ds(pl.multiple_of(slot * Q - 16 * j, 16), Q)

    def att_copy(owner, slot, s_base, r_base, dev):
        rows = head_rows(owner, slot)
        return remote(ATT.at[rows], ATT.at[rows], s_base + slot, r_base + slot, dev)

    s_o_xy = sends.take(9)

    def ow_copy(step, number):
        there = lax.rem(z + step, 4)
        rows = OWB.at[c, ow_piece(there, dp)]
        return remote(
            rows, rows, s_o_xy + (3 * (step - 1) + number), r_o_xy + (4 * dp + there), (peers[number], z, c)
        )

    def pass_ow():
        for step in (1, 3, 2):
            there = lax.rem(z + step, 4)
            arrived(OWB.at[c, ow_piece(there, dp)], r_o_z + there)
            for number in range(3):
                ow_copy(step, number).start()

    def attend(slot, carry):
        @pl.when(slot == 2)
        def _():
            pass_ow()

        rows = slot_rows(slot)
        out_rows = head_rows(j, slot)
        queries = QKV[0, rows, :]
        keys = QKV[1, rows, :].T
        values = QKV[2, rows, :]
        for tile in range(n_tiles):
            count = W * (tile + 1)
            first = W * tile * (tile + 1) // 2
            cols = slice(tile * W, (tile + 1) * W)
            scores = dot_nn(keys[:count], queries[:, cols]) + MASK[first : first + count, :]
            best = jnp.max(scores, axis=0, keepdims=True)
            weights = jnp.exp(scores - best)
            mass = jnp.sum(weights, axis=0, keepdims=True)
            probs_low = (weights * (1.0 / mass)).astype(BF)
            ATT[out_rows, cols] = dot_nn(values[:, :count], probs_low).astype(BF)
            LSE[slot, 0:1, cols] = best + jnp.log(mass)
        att_copy(j, slot, s_a_z, r_a_z, zdev).start()
        att_copy(j, slot, s_a_core, r_a_core, core).start()

        return carry

    lax.fori_loop(first_slot, 5, attend, 0)

    r_c_core, r_c_z, r_c_fwd = recvs.take(), recvs.take(), recvs.take()
    push(cot_in, CG.at[zz, c], r_c_z, zdev)
    push(cot_in, CG.at[zz, c], r_c_core, core)
    l_c = local(cot_in, CG.at[zz, c])

    pass_ff(1)

    for step in (1, 3, 2):
        there = lax.rem(z + step, 4)
        arrived(OWB.at[c, ow_odd(there)], r_o_z0 + there)
        for plane in range(4):
            arrived(OWB.at[c, ow_piece(there, plane)], r_o_xy + (4 * plane + there), dp != plane)
        push(OWB.at[c, block(there)], OWB.at[c, block(there)], r_o_fwd + there, core)

    def owner_of(zv, cv):
        return lax.rem(zv + 2 * cv, 4)

    def slots_of(owner, body):
        lax.fori_loop(jnp.where(owner == 0, 0, 1), 5, lambda slot, carry: (body(slot), carry)[1], 0)

    def pass_on(slot):
        att_copy(owner_of(zp, c), slot, s_a_fwd, r_a_z, core).wait_recv()
        att_copy(owner_of(zp, c), slot, s_a_fwd, r_a_fwd, core).start()

    slots_of(owner_of(zp, c), pass_on)
    slots_of(owner_of(z, oc), lambda slot: att_copy(owner_of(z, oc), slot, s_a_core, r_a_core, core).wait_recv())
    slots_of(owner_of(zp, oc), lambda slot: att_copy(owner_of(zp, oc), slot, s_a_fwd, r_a_fwd, core).wait_recv())
    done(l_o)
    arrived(OWB.at[oc, block(z)], r_o_core)
    for step in range(1, 4):
        there = lax.rem(z + step, 4)
        arrived(OWB.at[oc, block(there)], r_o_fwd + there)

    def project(tile, carry):
        t = tile // per_tok
        cols = pl.ds(pl.multiple_of(lax.rem(tile, per_tok) * W, W), W)
        all_cols = pl.ds(pl.multiple_of(tile * W, W), W)
        att = ATT[:, all_cols]
        halves = []
        for h in range(2):
            branch = dot_tn(OWB[h], att)
            halves.append(XG[t, h, :, cols].astype(F32) + (branch + column(h, VEC_OUT_BIAS)))
            HID[t, h, :, cols] = halves[h]
        center, inv_std = stats_of(*halves)
        ST2[t, 0:1, cols] = center
        ST2[t, 1:2, cols] = inv_std
        for h in range(2):
            shaped = (halves[h] - center) * inv_std * column(h, VEC_LN2_GAIN) + column(
                h, VEC_LN2_BIAS
            )
            N2[t, h, :, cols] = shaped.astype(BF)
        return carry

    lax.fori_loop(0, n_tiles, project, 0)

    done(l_f)
    ff_ready(0)

    @pl.when(first_core)
    def _():
        COLS[:, 6:7] = PACK[0].T[0:FW, 6:7]

    @pl.when(second_core)
    def _():
        COLS[:, 6:7] = PACKF[...].T[0:FW, 6:7]

    s_c_fwd = sends.take()

    def cot_forward():
        return remote(CG.at[1 - zz, c], CG.at[1 - zz, c], s_c_fwd, r_c_fwd, core)

    def other_cotangent():
        arrived(CG.at[1 - zz, c], r_c_z)
        cot_forward().start()
        arrived(CG.at[1 - zz, oc], r_c_fwd)


    r_g_core, r_p_core, r_g_z = recvs.take(n_tiles), recvs.take(n_tiles), recvs.take(n_tiles)
    s_g_core, s_p_core, s_g_z = sends.take(n_tiles), sends.take(n_tiles), sends.take(n_tiles)

    def tile_at(tile):
        t = tile // per_tok
        return t, pl.ds(pl.multiple_of(lax.rem(tile, per_tok) * W, W), W)

    def part_copy(buf, dst, tile, s_base, r_base, dev):
        t, cols = tile_at(tile)
        return remote(buf.at[t, :, cols], dst.at[t, :, cols], s_base + tile, r_base + tile, dev)

    def feed(tile, carry):
        t, cols = tile_at(tile)
        all_cols = pl.ds(pl.multiple_of(tile * W, W), W)
        pre = dot_tn(FB[0].reshape(D, FW), N2[t, :, :, cols].reshape(D, W)) + COLS[:, 6:7]
        phi = 0.5 * (1.0 + lax.erf(pre * (2.0**-0.5)))
        ACT[:, all_cols] = (pre * phi).astype(BF)
        slope = phi + pre * jnp.exp(pre * pre * -0.5) * ((2.0 * math.pi) ** -0.5)
        GPRE[:, all_cols] = slope.astype(BF)
        return carry

    lax.fori_loop(0, n_tiles, feed, 0)
    done(l_p)
    ff_ready(1)
    done(l_c)
    arrived(CG.at[zz, oc], r_c_core)

    def feed_back(order, carry):
        t = lax.rem(order + zz, 2)
        pl.when(order == 1)(other_cotangent)
        for number in range(per_tok):
            cols = slice(number * W, (number + 1) * W)
            all_cols = pl.ds(pl.multiple_of(t * T + number * W, W), W)
            grad_act = dot_tn(FB[1].reshape(D, FW), CG[t, :, :, cols].reshape(D, W))
            GPRE[:, all_cols] = (grad_act * GPRE[:, all_cols].astype(F32)).astype(BF)
            PGS[t, :, cols] = dot_nn(FB[0, oc], GPRE[:, all_cols]).astype(BF)
            part_copy(PGS, RCG, t * per_tok + number, s_g_core, r_g_core, core).start()
        for number in range(per_tok):
            cols = slice(number * W, (number + 1) * W)
            all_cols = pl.ds(pl.multiple_of(t * T + number * W, W), W)
            tile = t * per_tok + number
            own = dot_nn(FB[0, c], GPRE[:, all_cols])
            part_copy(PGS, RCG, tile, s_g_core, r_g_core, core).wait_recv()
            SZG[t, :, cols] = (own + RCG[t, :, cols].astype(F32)).astype(BF)
            part_copy(SZG, RZG, tile, s_g_z, r_g_z, zdev).start()
        return carry

    lax.fori_loop(0, 2, feed_back, 0)

    for entry in ff_entries:
        sent(entry)
    r_f1, r_f2 = recvs.take(4), recvs.take(2)
    f1_entries = []

    def ff_grads(number):
        for h in range(2):
            left, right = (N2, GPRE) if number < 2 else (CG, ACT)
            rows = slice(number % 2 * quarter, (number % 2 + 1) * quarter)
            total = dot_nt(left[0, h, rows, :], right[:, 0:T]) + dot_nt(left[1, h, rows, :], right[:, T:S])
            FB[number // 2, h, rows, :] = total.astype(BF)

    def ff_rows(number):
        return quarter_rows(lax.rem(number, 2))

    def ff_part(h, number):
        return FB.at[number // 2, h, ff_rows(number)]

    def ff_value(h, number):
        return FB[number // 2, h, ff_rows(number), :].astype(F32)

    def f1_push(h, number, place, dev, cond=None):
        f1_entries.append(push(ff_part(h, number), rf1_hbm.at[place], r_f1 + place, dev, cond))

    for number in range(2):
        ff_grads(number)
        f1_push(0, number, 0, xdev, xb != number)
        f1_push(1, number, 2 + number, ydev, yb == 1)

    def outward(tile, carry):
        t, cols = tile_at(tile)
        all_cols = pl.ds(pl.multiple_of(tile * W, W), W)
        OPS[t, :, cols] = dot_nn(FB[1, oc], ACT[:, all_cols]).astype(BF)
        part_copy(OPS, RCO, tile, s_p_core, r_p_core, core).start()
        OPO[t, :, cols] = dot_nn(FB[1, c], ACT[:, all_cols]).astype(BF)
        return carry

    lax.fori_loop(0, n_tiles, outward, 0)
    for number in range(2):
        ff_grads(2 + number)
        f1_push(0, 2 + number, 1, xdev, xb != number)
        f1_push(1, 2 + number, 2 + number, ydev, yb == 0)

    SPR[dp] = jnp.zeros(SPR.shape[1:], F32)
    SPR[dp, 6:7, :] = dot_nt(jnp.ones((16, S), BF), GPRE[...])[0:1, :]

    r_g_all = recvs.take(n_tiles)
    s_g_all = sends.take(n_tiles)

    def g2_copy(tile):
        t, cols = tile_at(tile)
        return remote(G2.at[t, c, :, cols], G2.at[t, c, :, cols], s_g_all + tile, r_g_all + tile, core)

    def g2_other(tile):
        t, cols = tile_at(tile)
        return remote(G2.at[t, oc, :, cols], G2.at[t, oc, :, cols], s_g_all + tile, r_g_all + tile, core)

    def join(tile, carry):
        t, cols = tile_at(tile)
        part_copy(SZG, RZG, tile, s_g_z, r_g_z, zdev).wait_recv()
        G2[t, c, :, cols] = (SZG[t, :, cols].astype(F32) + RZG[t, :, cols].astype(F32)).astype(BF)
        g2_copy(tile).start()
        return carry

    lax.fori_loop(0, n_tiles, join, 0)

    def norm_back(grads, normals, inv_std, gain_index):
        scaled = [grads[h] * column(h, gain_index) for h in range(2)]
        plain = sum(jnp.sum(scaled[h], axis=0, keepdims=True) for h in range(2)) * inv_d
        cross = sum(jnp.sum(scaled[h] * normals[h], axis=0, keepdims=True) for h in range(2)) * inv_d
        return [inv_std * (scaled[h] - plain - normals[h] * cross) for h in range(2)]

    def second_back(tile, carry):
        t, cols = tile_at(tile)
        g2_other(tile).wait_recv()
        center, inv_std = ST2[t, 0:1, cols], ST2[t, 1:2, cols]
        grads = [G2[t, h, :, cols].astype(F32) for h in range(2)]
        normals = [(HID[t, h, :, cols] - center) * inv_std for h in range(2)]
        back = norm_back(grads, normals, inv_std, VEC_LN2_GAIN)
        for h in range(2):
            grad_hidden = CG[t, h, :, cols].astype(F32) + back[h]
            XG[t, h, :, cols] = grad_hidden.astype(BF)

            @pl.when((t == zz) & (c == h))
            def _():
                GH[:, cols] = grad_hidden
                VGC[:, 2:3] = VGC[:, 2:3] + jnp.sum(grads[h] * normals[h], axis=1, keepdims=True)
                VGC[:, 3:4] = VGC[:, 3:4] + jnp.sum(grads[h], axis=1, keepdims=True)

        return carry

    sent(e_xf)
    lax.fori_loop(0, n_tiles, second_back, 0)
    GB = XG

    r_out_z = recvs.take()

    def wait_out(tile, carry):
        part_copy(OPS, RCO, tile, s_p_core, r_p_core, core).wait_recv()
        return carry

    lax.fori_loop(0, n_tiles, wait_out, 0)
    SZO[...] = (OPO[1 - zz].astype(F32) + RCO[1 - zz].astype(F32)).astype(BF)
    push(SZO, RZO, r_out_z, zdev)
    VGC[:, 4:5] = jnp.sum(GB[zz, c].astype(F32), axis=1, keepdims=True)
    VGC[:, 5:6] = jnp.sum(CG[zz, c].astype(F32), axis=1, keepdims=True)

    window = pl.ds(pl.multiple_of(j * (4 * Q), Q), 5 * Q)
    for t in range(2):
        DATT[:, t * T : (t + 1) * T] = (
            dot_nn(OWB[0, window, :], GB[t, 0]) + dot_nn(OWB[1, window, :], GB[t, 1])
        ).astype(BF)
    r_q1, r_q2 = recvs.take(4), recvs.take(2)
    q1_entries = []

    def q1_push(h, number, place, dev, cond=None):
        q1_entries.append(push(DQ.at[number, h], rq1_hbm.at[place], r_q1 + place, dev, cond))

    for h in range(2):
        total = dot_nt(ATT[block(j), 0:T], GB[0, h]) + dot_nt(ATT[block(j), T:S], GB[1, h])
        DQ[3, h, 0:R, 0:H] = total.astype(BF)
    q1_push(0, 3, 1, xdev, xb == 0)
    q1_push(1, 3, 3, ydev, yb == 0)
    l_x2 = local(x_in, XG.at[zz, c])

    s_f2 = sends.take(2)
    l_f1, l_f2 = locs.take(4), locs.take(2)

    def f2_copy(place):
        if place == 0:
            return remote(ff_part(0, xb + 2 * (1 - yb)), rf2_hbm.at[0], s_f2, r_f2, ydev)
        return remote(ff_part(1, 2 * yb + 1 - xb), rf2_hbm.at[1], s_f2 + 1, r_f2 + 1, xdev)

    spare = ((0, 1 - xb), (0, 3 - xb), (1, 2 * (1 - yb)), (1, 2 * (1 - yb) + 1))
    kept = ((0, xb), (0, 2 + xb), (1, 2 * yb), (1, 2 * yb + 1))

    def first_join():
        for entry in f1_entries:
            when(entry[0], entry[1].wait_send)
        loads = []
        for place in range(4):
            arrived(rf1_hbm.at[place], r_f1 + place)
            load = pltpu.make_async_copy(rf1_hbm.at[place], ff_part(*spare[place]), LS.at[l_f1 + place])
            load.start()
            loads.append(load)
        for load in loads:
            load.wait()

        def add(place):
            h, number = kept[place]
            total = ff_value(h, number) + ff_value(*spare[place])
            FB[number // 2, h, ff_rows(number), :] = total.astype(BF)

        for place in range(4):
            add(place)
        f2_copy(0).start()
        f2_copy(1).start()

    def attend_back(slot, carry):
        rows = slot_rows(slot)
        here = pl.ds(pl.multiple_of(slot * Q, Q), Q)
        queries = QKV[0, rows, :]
        keys_t = QKV[1, rows, :]
        keys = keys_t.T
        values = QKV[2, rows, :].T
        grads_out = DATT[here, :]
        for tile in reversed(range(n_tiles)):
            count = W * (tile + 1)
            first = W * tile * (tile + 1) // 2
            cols = slice(tile * W, (tile + 1) * W)
            scores = dot_nn(keys[:count], queries[:, cols]) + MASK[first : first + count, :]
            probs = jnp.exp(scores - LSE[slot, 0:1, cols])
            grad_probs = dot_nn(values[:count], grads_out[:, cols])
            delta = jnp.sum(probs * grad_probs, axis=0, keepdims=True)
            grad_scores = (probs * (grad_probs - delta)).astype(BF)
            probs_low = probs.astype(BF)
            part_v = dot_nt(grads_out[:, cols], probs_low)
            part_k = dot_nt(queries[:, cols], grad_scores)
            if tile == n_tiles - 1:
                ACCV[...] = part_v
                ACCK[...] = part_k
            else:
                ACCV[:, 0:count] = ACCV[:, 0:count] + part_v
                ACCK[:, 0:count] = ACCK[:, 0:count] + part_k
            GQKV[0, rows, cols] = (dot_nn(keys_t[:, :count], grad_scores) * score_scale).astype(BF)
        GQKV[1, rows, :] = ACCK[...].astype(BF)
        GQKV[2, rows, :] = ACCV[...].astype(BF)

        @pl.when(slot == 3)
        def _():
            first_join()

        return carry

    lax.fori_loop(first_slot, 5, attend_back, 0)

    for m in range(3):
        if m != 1:
            bias_sum = jnp.sum(GQKV[m].astype(F32), axis=1, keepdims=True)
        for h in range(2):
            total = dot_nt(GQKV[m, :, 0:T], N1[0, h]) + dot_nt(GQKV[m, :, T:S], N1[1, h])
            DQ[m, h, :, 0:H] = total.astype(BF)
            if m != 1:
                DQ[m, h, :, H : H + 1] = bias_sum.astype(BF)
        q1_push(0, m, m // 2, xdev, xb != m % 2)
        q1_push(1, m, 2 + m % 2, ydev, yb != m // 2)

    def wait_sends(tile, carry):
        part_copy(PGS, RCG, tile, s_g_core, r_g_core, core).wait_send()
        part_copy(OPS, RCO, tile, s_p_core, r_p_core, core).wait_send()
        part_copy(SZG, RZG, tile, s_g_z, r_g_z, zdev).wait_send()
        g2_copy(tile).wait_send()
        return carry

    lax.fori_loop(0, n_tiles, wait_sends, 0)
    r_n_core, r_n_z = recvs.take(n_tiles), recvs.take()
    s_n_core = sends.take(n_tiles)

    def back_rows(half, tile):
        all_cols = pl.ds(pl.multiple_of(tile * W, W), W)
        total = dot_tn(WB[0, half], GQKV[0, :, all_cols])
        for m in range(1, 3):
            total = total + dot_tn(WB[m, half], GQKV[m, :, all_cols])
        return total

    def first_part(tile, carry):
        t, cols = tile_at(tile)
        PGS[t, :, cols] = back_rows(oc, tile).astype(BF)
        part_copy(PGS, RCG, tile, s_n_core, r_n_core, core).start()
        OPS[t, :, cols] = back_rows(c, tile).astype(BF)
        return carry

    lax.fori_loop(0, n_tiles, first_part, 0)

    def wait_first(tile, carry):
        part_copy(PGS, RCG, tile, s_n_core, r_n_core, core).wait_recv()
        return carry

    lax.fori_loop(0, n_tiles, wait_first, 0)
    SZG[0] = (OPS[1 - zz].astype(F32) + RCG[1 - zz].astype(F32)).astype(BF)
    push(SZG.at[0], RZN, r_n_z, zdev)

    for entry in f1_entries:
        pending[:] = [other for other in pending if other is not entry]
    loads = []
    for h in range(2):
        arrived(rf2_hbm.at[h], r_f2 + h)
        loads.append(local(rf2_hbm.at[h], ff_part(*spare[2 * h])))
    r_zf = recvs.take(4)
    final_cut = (R // 16 + 1) // 2 * 16
    final_chunks = ((0, final_cut), (final_cut, R - final_cut))
    for h in range(2):
        done(loads[h])
        low = (ff_value(h, dp) + ff_value(*spare[2 * h])).astype(BF)
        FB[dp // 2, h, ff_rows(dp), :] = low
        if h == 0:

            @pl.when(first_core)
            def _():
                ZF[0] = low

        for chunk, (start, size) in enumerate(final_chunks):
            part = FB.at[dp // 2, h, pl.ds(pl.multiple_of(lax.rem(dp, 2) * quarter + start, 16), size)]
            rows = pl.ds(start, size)
            push(part, ZF.at[1, rows], r_zf + (2 + chunk), (dp, z2, h), second_core)
            if h == 1:
                push(part, ZF.at[0, rows], r_zf + chunk, (dp, z, 1), first_core)

    arrived(RZO, r_out_z)
    branch_out = OPO[zz].astype(F32) + RCO[zz].astype(F32) + RZO[...].astype(F32)
    OPO[0] = (HID[zz, c] + branch_out + column(c, VEC_PROJ_BIAS)).astype(BF)
    l_out = local(OPO.at[0], out_o)

    for entry in q1_entries:
        sent(entry)
    q_spare = ((1 - xb, 0), (3 - xb, 0), (2 * (1 - yb), 1), (2 * (1 - yb) + 1, 1))
    q_kept = ((xb, 0), (2 + xb, 0), (2 * yb, 1), (2 * yb + 1, 1))
    loads = []
    for place in range(4):
        arrived(rq1_hbm.at[place], r_q1 + place)
        loads.append(local(rq1_hbm.at[place], DQ.at[q_spare[place][0], q_spare[place][1]]))
    for place in range(4):
        done(loads[place])
        (there, h), (here, unused) = q_spare[place], q_kept[place]
        DQ[here, h] = (DQ[here, h].astype(F32) + DQ[there, h].astype(F32)).astype(BF)
    push(DQ.at[xb + 2 * (1 - yb), 0], rq2_hbm.at[0], r_q2, ydev)
    push(DQ.at[2 * yb + 1 - xb, 1], rq2_hbm.at[1], r_q2 + 1, xdev)

    r_gf, r_gq = recvs.take(8), recvs.take(8)

    def gf_at(plane, first, size):
        return gf_o.at[pl.ds(pl.multiple_of(plane * quarter + first, 16), size)]

    def gq_at(plane, first, size):
        return gq_o.at[plane, pl.ds(first, size)]

    def spread(buf, out_at, chunk, r_base):
        first, size = final_chunks[chunk]
        push(buf.at[0, pl.ds(first, size)], out_at(dp, first, size), r_base + 4 * chunk, xdev)
        push(buf.at[0, pl.ds(first, size)], out_at(dp, first, size), r_base + (4 * chunk + 1), ydev)
        return local(buf.at[0, pl.ds(first, size)], out_at(dp, first, size))

    def spread_on(out_at, chunk, r_base):
        first, size = final_chunks[chunk]
        half = size // 32 * 16
        arrived(out_at(xn, first, size), r_base + 4 * chunk)
        part = out_at(xn, first, half)
        push(part, part, r_base + (4 * chunk + 2), ydev)
        arrived(out_at(yn, first, size), r_base + (4 * chunk + 1))
        part = out_at(yn, first + half, size - half)
        push(part, part, r_base + (4 * chunk + 3), xdev)

    def spread_end(out_at, chunk, r_base):
        first, size = final_chunks[chunk]
        half = size // 32 * 16
        arrived(out_at(dg, first, half), r_base + (4 * chunk + 2))
        arrived(out_at(dg, first + half, size - half), r_base + (4 * chunk + 3))

    def ff_final(chunk):
        first, size = final_chunks[chunk]
        rows = pl.ds(first, size)
        arrived(ZF.at[0, rows], r_zf + chunk, second_core)
        arrived(ZF.at[1, rows], r_zf + (2 + chunk))
        here = slice(first, first + size)
        ZF[0, here] = (ZF[0, here].astype(F32) + ZF[1, here].astype(F32)).astype(BF)
        return spread(ZF, gf_at, chunk, r_gf)

    l_gf = [ff_final(0)]

    done(l_x2)
    arrived(RZN, r_n_z)
    r_stat = recvs.take()
    grads = OPS[zz].astype(F32) + RCG[zz].astype(F32) + RZN[...].astype(F32)
    center, inv_std = ST1[zz, 0:1, :], ST1[zz, 1:2, :]
    normals = (XG[zz, c].astype(F32) - center) * inv_std
    scaled = grads * column(c, VEC_LN1_GAIN)
    STX[c, 0:1, :] = jnp.sum(scaled, axis=0, keepdims=True)
    STX[c, 1:2, :] = jnp.sum(scaled * normals, axis=0, keepdims=True)
    push(STX.at[c], STX.at[c], r_stat, core)
    VGC[:, 0:1] = jnp.sum(grads * normals, axis=1, keepdims=True)
    VGC[:, 1:2] = jnp.sum(grads, axis=1, keepdims=True)
    arrived(STX.at[oc], r_stat)
    sums = (STX[0] + STX[1]) * inv_d
    OPO[1] = (GH[...] + inv_std * (scaled - sums[0:1] - normals * sums[1:2])).astype(BF)
    l_ing = local(OPO.at[1], ing_o)

    r_sp, r_spz = recvs.take(4), recvs.take(8)
    turned = VGC[...].T
    SPR[dp, 0:6, 0:H] = turned[0:6, :]
    for peer in peers:
        push(SPR.at[dp], SPR.at[dp], r_sp + dp, (peer, z, c))

    loads = []
    for h in range(2):
        arrived(rq2_hbm.at[h], r_q2 + h)
        loads.append(local(rq2_hbm.at[h], DQ.at[q_spare[2 * h][0], h]))
    r_zq, r_zt = recvs.take(4), recvs.take(2)
    with_tail = (j < 3) & (dp < 3)
    next_block = jnp.minimum(j + 1, 3)
    for h in range(2):
        done(loads[h])
        low = (DQ[dp, h].astype(F32) + DQ[q_spare[2 * h][0], h].astype(F32)).astype(BF)
        DQ[dp, h] = low
        if h == 0:

            @pl.when(first_core)
            def _():
                ZQ[0] = low[0:R]

        push(DQ.at[dp, h, pl.ds(R, TAIL)], ZT.at[c], r_zt + c, (dp, next_block, h), with_tail)
    for chunk, (start, size) in enumerate(final_chunks):
        rows = pl.ds(start, size)
        for h in range(2):
            push(DQ.at[dp, h, rows], ZQ.at[1, rows], r_zq + (2 + chunk), (dp, z2, h), second_core)
        push(DQ.at[dp, 1, rows], ZQ.at[0, rows], r_zq + chunk, (dp, z, 1), first_core)

    l_gf.append(ff_final(1))
    spread_on(gf_at, 0, r_gf)

    for number in range(4):
        arrived(SPR.at[number], r_sp + number, dp != number)
    SPZ[z, c] = SPR[0] + SPR[1] + SPR[2] + SPR[3]
    for step in range(4):
        for side in range(2):
            if step == 0 and side == 0:
                continue
            target = (dp, lax.rem(z + step, 4), c if side == 0 else oc)
            push(SPZ.at[z, c], SPZ.at[z, c], r_spz + (2 * z + c), target)

    gets_tail = (z >= 1) & (dp < 3)

    def qkv_final(chunk):
        first, size = final_chunks[chunk]
        rows = pl.ds(first, size)
        arrived(ZQ.at[0, rows], r_zq + chunk, second_core)
        arrived(ZQ.at[1, rows], r_zq + (2 + chunk))
        here = slice(first, first + size)
        total = ZQ[0, here].astype(F32) + ZQ[1, here].astype(F32)
        ZQ[0, here] = total.astype(BF)
        if chunk == 0:
            for side in range(2):
                arrived(ZT.at[side], r_zt + side, gets_tail)

            @pl.when(gets_tail)
            def _():
                ZQ[0, 0:TAIL] = (total[0:TAIL] + ZT[0].astype(F32) + ZT[1].astype(F32)).astype(BF)

        return spread(ZQ, gq_at, chunk, r_gq)

    l_gq = [qkv_final(0)]
    spread_on(gf_at, 1, r_gf)
    l_gq.append(qkv_final(1))

    for step in range(4):
        for side in range(2):
            if step == 0 and side == 0:
                continue
            zv, cv = lax.rem(z + step, 4), c if side == 0 else oc
            arrived(SPZ.at[zv, cv], r_spz + (2 * zv + cv))
    vectors = SPZ[0, c] + SPZ[1, c] + SPZ[2, c] + SPZ[3, c]
    VOUT[...] = vectors
    VOUT[6:7, :] = SPZ[z, 0, 6:7, :] + SPZ[z2, 1, 6:7, :]
    l_vec_o = local(VOUT, vec_o)

    for chunk in range(2):
        spread_on(gq_at, chunk, r_gq)
    for chunk in range(2):
        spread_end(gf_at, chunk, r_gf)
        spread_end(gq_at, chunk, r_gq)
    for entry in (l_out, l_ing, l_vec_o, *l_gf, *l_gq):
        done(entry)

    def own_sends(slot):
        att_copy(j, slot, s_a_z, r_a_z, zdev).wait_send()
        att_copy(j, slot, s_a_core, r_a_core, core).wait_send()

    slots_of(j, own_sends)
    slots_of(
        owner_of(zp, c),
        lambda slot: att_copy(owner_of(zp, c), slot, s_a_fwd, r_a_fwd, core).wait_send(),
    )

    f2_copy(0).wait_send()
    f2_copy(1).wait_send()
    cot_forward().wait_send()

    for step in (1, 3, 2):
        for number in range(3):
            ow_copy(step, number).wait_send()

    def last_sends(tile, carry):
        part_copy(PGS, RCG, tile, s_n_core, r_n_core, core).wait_send()
        return carry

    lax.fori_loop(0, n_tiles, last_sends, 0)
    for entry in list(pending):
        sent(entry)
    assert sends.used <= SEND_COUNT and recvs.used <= RECV_COUNT and locs.used <= LOCAL_COUNT


def finish_kernel(
    out_in,
    ing_in,
    gf_in,
    gq_in,
    vec_in,
    out_o,
    ing_o,
    qkv_o,
    qvb_o,
    ow_o,
    fc_o,
    proj_o,
    v0,
    v1,
    v2,
    v3,
    v4,
    v5,
    v6,
    GF,
    GQ,
    FST,
    QST,
    OB,
    SEM,
):
    R, H = ow_o.shape
    count = GF.shape[0] // R
    whole = [
        pltpu.make_async_copy(out_in, OB.at[0], SEM.at[0]),
        pltpu.make_async_copy(ing_in, OB.at[1], SEM.at[1]),
    ]
    place = 2
    loads_q, loads_f = [], []
    for m in range(4):
        loads_q.append(pltpu.make_async_copy(gq_in.at[m], GQ.at[m], SEM.at[place + m]))
    place += 4
    for number in range(count):
        rows = pl.ds(number * R, R)
        loads_f.append(pltpu.make_async_copy(gf_in.at[rows], GF.at[rows], SEM.at[place + number]))
    place += count
    for copy in loads_f + loads_q + whole:
        copy.start()
    stores = []
    for number in range(count):
        loads_f[number].wait()
        rows = pl.ds(number * R, R)
        FST[rows, :] = GF[rows, :].astype(F32)
        half = count // 2
        dst = (fc_o if number < half else proj_o).at[pl.ds(number % half * R, R)]
        stores.append(pltpu.make_async_copy(FST.at[rows], dst, SEM.at[place + number]))
        stores[-1].start()
    place += count
    for m in range(4):
        loads_q[m].wait()
        QST[m] = GQ[m, :, 0:H].astype(F32)
        dst = qkv_o.at[m] if m < 3 else ow_o
        stores.append(pltpu.make_async_copy(QST.at[m], dst, SEM.at[place + m]))
        stores[-1].start()
    place += 4
    for number, dst in enumerate((out_o, ing_o)):
        whole[number].wait()
        stores.append(pltpu.make_async_copy(OB.at[number], dst, SEM.at[place + number]))
        stores[-1].start()
    first = H // LANES * LANES
    for number, m in enumerate((0, 2)):
        turned = GQ[m, :, first : first + LANES].astype(F32).T
        qvb_o[number : number + 1, :] = turned[H - first : H - first + 1, :]
    for number, v in enumerate((v0, v1, v2, v3, v4, v5, v6)):
        v[...] = vec_in[number, 0 : v.shape[0]]
    for copy in stores:
        copy.wait()


def fast_body(
    tokens,
    ln1_gain,
    ln1_bias,
    qkv_weight,
    qv_bias,
    out_weight,
    out_bias,
    ln2_gain,
    ln2_bias,
    fc_weight,
    fc_bias,
    proj_weight,
    proj_bias,
    doc_lengths,
    cotangent,
):
    H, T = tokens.shape
    R = out_weight.shape[0]
    FW = fc_weight.shape[1]
    D, S = 2 * H, 2 * T
    HP = (H // LANES + 1) * LANES
    EXT = 5 * HEAD_DIM
    NT = S // KEY_TILE
    wide = (FW // LANES + 1) * LANES
    w3 = jnp.transpose(qkv_weight, (1, 2, 0))
    shape = jax.ShapeDtypeStruct
    anywhere = pl.BlockSpec(memory_space=pl.ANY)
    outs = [
        shape((H, T), BF),
        shape((H, T), BF),
        shape((2 * H, FW), BF),
        shape((4, R, HP), BF),
        shape((8, FW), F32),
        shape((4, D // 4, FW), BF),
        shape((2, D // 4, FW), BF),
        shape((4, EXT, HP), BF),
        shape((2, EXT, HP), BF),
    ]
    vmem = pltpu.VMEM
    mask_rows = KEY_TILE * NT * (NT + 1) // 2
    scratch = [
        vmem((2, 2, H, T), BF),
        vmem((2, 2, H, T), BF),
        vmem((2, 2, H, T), BF),
        vmem((3, 2, EXT, H), BF),
        vmem((EXT, LANES), F32),
        vmem((2, D, H), BF),
        vmem((2, 2, H, FW), BF),
        vmem((FW, LANES), F32),
        vmem((2, 8, wide), F32),
        vmem((8, wide), F32),
        vmem((8, wide), F32),
        vmem((mask_rows, KEY_TILE), F32),
        vmem((3, EXT, S), BF),
        vmem((5, 8, S), F32),
        vmem((D, S), BF),
        vmem((2, 2, H, T), F32),
        vmem((2, 8, T), F32),
        vmem((2, 8, T), F32),
        vmem((2, 2, H, T), BF),
        vmem((FW, S), BF),
        vmem((FW, S), BF),
        vmem((2, H, T), BF),
        vmem((2, H, T), BF),
        vmem((2, H, T), BF),
        vmem((2, H, T), BF),
        vmem((2, H, T), BF),
        vmem((2, H, T), BF),
        vmem((2, H, T), BF),
        vmem((2, 2, H, T), BF),
        vmem((H, T), BF),
        vmem((H, T), BF),
        vmem((H, T), BF),
        vmem((EXT, S), BF),
        vmem((3, EXT, S), BF),
        vmem((HEAD_DIM, S), F32),
        vmem((HEAD_DIM, S), F32),
        vmem((2, 2 * H // 4, FW), BF),
        vmem((4, 2, EXT, HP), BF),
        vmem((2, R, HP), BF),
        vmem((2, EXT - R, HP), BF),
        vmem((H, T), F32),
        vmem((H, LANES), F32),
        vmem((2, 8, T), F32),
        vmem((4, 8, FW), F32),
        vmem((4, 2, 8, FW), F32),
        vmem((8, FW), F32),
        pltpu.SemaphoreType.DMA((SEND_COUNT,)),
        pltpu.SemaphoreType.DMA((RECV_COUNT,)),
        pltpu.SemaphoreType.DMA((LOCAL_COUNT,)),
    ]
    out_rows, in_rows, gf, gq, vectors = pl.pallas_call(
        layer_kernel,
        out_shape=outs,
        in_specs=[anywhere] * 6 + [pl.BlockSpec(memory_space=vmem)] * 9,
        out_specs=[anywhere] * len(outs),
        scratch_shapes=scratch,
        compiler_params=pltpu.CompilerParams(
            collective_id=0, has_side_effects=True, vmem_limit_bytes=VMEM_LIMIT
        ),
    )(
        tokens,
        cotangent,
        w3,
        out_weight,
        fc_weight,
        proj_weight,
        ln1_gain,
        ln1_bias,
        ln2_gain,
        ln2_bias,
        out_bias,
        proj_bias,
        fc_bias,
        qv_bias,
        doc_lengths,
    )[:5]
    in_vmem = pl.BlockSpec(memory_space=vmem)
    finals = pl.pallas_call(
        finish_kernel,
        out_shape=[
            shape((H, T), BF),
            shape((H, T), BF),
            shape((3, R, H), F32),
            shape((2, R), F32),
            shape((R, H), F32),
            shape((H, FW), F32),
            shape((H, FW), F32),
        ]
        + [shape((H,), F32)] * 6
        + [shape((FW,), F32)],
        in_specs=[anywhere] * 4 + [in_vmem],
        out_specs=[anywhere] * 3 + [in_vmem] + [anywhere] * 3 + [in_vmem] * 7,
        scratch_shapes=[
            vmem((D, FW), BF),
            vmem((4, R, HP), BF),
            vmem((D, FW), F32),
            vmem((4, R, H), F32),
            vmem((2, H, T), BF),
            pltpu.SemaphoreType.DMA((32,)),
        ],
        compiler_params=pltpu.CompilerParams(vmem_limit_bytes=VMEM_LIMIT),
    )(out_rows, in_rows, gf, gq, vectors)
    out_final, in_final, qkv_rows, bias_grad, ow_grad, fc_grad, proj_grad = finals[:7]
    ln1_gain_g, ln1_bias_g, ln2_gain_g, ln2_bias_g, out_bias_g, proj_bias_g, fc_bias_g = finals[7:]
    return (
        out_final,
        in_final,
        ln1_gain_g,
        ln1_bias_g,
        jnp.transpose(qkv_rows, (2, 0, 1)),
        bias_grad,
        ow_grad,
        out_bias_g,
        ln2_gain_g,
        ln2_bias_g,
        fc_grad,
        fc_bias_g,
        proj_grad,
        proj_bias_g,
    )


def choose_body(*arrays):
    sizes = {axis: lax.axis_size(axis) for axis in ("dp", "row", "col")}
    H, R = arrays[0].shape[0], arrays[5].shape[0]
    fits = sizes == {"dp": 4, "row": 4, "col": 2} and 4 * R == 2 * H == 17 * HEAD_DIM
    return (fast_body if fits else body)(*arrays)


def solution(mesh):
    return jax.shard_map(
        choose_body,
        mesh=mesh,
        in_specs=(
            P("col", ("dp", "row")),
            P("col"),
            P("col"),
            P("col", None, "row"),
            P(None, "row"),
            P("row", "col"),
            P("col"),
            P("col"),
            P("col"),
            P("col", "row"),
            P("row"),
            P("col", "row"),
            P("col"),
            P(("dp", "col"), None),
            P("col", ("dp", "row")),
        ),
        out_specs=(
            P("col", ("dp", "row")),
            P("col", ("dp", "row")),
            P("col"),
            P("col"),
            P("col", None, "row"),
            P(None, "row"),
            P("row", "col"),
            P("col"),
            P("col"),
            P("col"),
            P("col", "row"),
            P("row"),
            P("col", "row"),
            P("col"),
        ),
        check_vma=False,
    )
```

```python
from functools import partial
import math

import jax
import jax.numpy as jnp
from jax import lax
from jax.experimental import pallas as pl
from jax.experimental.pallas import tpu as pltpu
from jax.sharding import PartitionSpec as P

HEAD_DIM = 64


epsilon = 1e-05
score_scale = 0.125
masked_fill = -1e30
block_limit = 512


def feature_sums(first_sum, second_sum):
    return lax.psum((first_sum, second_sum), "col")


def norm_forward(values, gain_vec, shift_vec):
    feature_count = values.shape[1] * lax.axis_size("col")
    total_sum, square_sum = feature_sums(jnp.sum(values, axis=1), jnp.sum(values * values, axis=1))
    center = total_sum / feature_count
    spread = square_sum / feature_count - center * center
    inv_std = lax.rsqrt(spread + epsilon)
    normal = (values - center[:, None]) * inv_std[:, None]
    return (normal, inv_std, normal * gain_vec + shift_vec)


def norm_backward(upstream, normal, inv_std, gain_vec):
    feature_count = upstream.shape[1] * lax.axis_size("col")
    scaled = upstream * gain_vec
    plain_sum, cross_sum = feature_sums(jnp.sum(scaled, axis=1), jnp.sum(scaled * normal, axis=1))
    return inv_std[:, None] * (
        scaled - plain_sum[:, None] / feature_count - normal * (cross_sum[:, None] / feature_count)
    )


def gather_rows(values):
    return lax.all_gather(values, "row", axis=0, tiled=True)


def gather_cols(values):
    return lax.all_gather(values, "col", axis=0, tiled=True)


def sum_over_rows(row_term, row_total):
    return lax.psum_scatter(
        row_term(jnp.int32(0), row_total * lax.axis_size("row")),
        "row",
        scatter_dimension=0,
        tiled=True,
    )


def sum_over_cols(row_term, row_total):
    return lax.psum_scatter(
        row_term(jnp.int32(0), row_total * lax.axis_size("col")),
        "col",
        scatter_dimension=0,
        tiled=True,
    )


def to_heads(values):
    return lax.all_to_all(values, "row", split_axis=0, concat_axis=2, tiled=True)


def to_tokens(values):
    return lax.all_to_all(values, "row", split_axis=2, concat_axis=0, tiled=True)


def product_term(full_rows, matrix):

    def row_term(first_row, row_count):
        return jnp.dot(full_rows, matrix, preferred_element_type=jnp.float32)

    return row_term


def product_term_back(full_rows, matrix):

    def row_term(first_row, row_count):
        return lax.dot_general(
            full_rows, matrix, (((1,), (1,)), ((), ())), preferred_element_type=jnp.float32
        )

    return row_term


def slice_term(full_rows):

    def row_term(first_row, row_count):
        return full_rows

    return row_term


def inner_rows(left_side, right_side):
    return lax.dot_general(
        left_side, right_side, (((0,), (0,)), ((), ())), preferred_element_type=jnp.float32
    )


def segments_of(lengths, places):
    doc_ends = jnp.cumsum(lengths)
    segment = jnp.sum(
        (doc_ends[None, :] <= places[:, None]).astype(jnp.int32), axis=1, dtype=jnp.int32
    )
    return (segment, places >= doc_ends[-1])


def allowed_pairs(query_place, query_segment, query_padding, key_place, key_segment):
    causal = key_place[None, :] <= query_place[:, None]
    same_doc = key_segment[None, :] == query_segment[:, None]
    itself = key_place[None, :] == query_place[:, None]
    return causal & same_doc & (jnp.logical_not(query_padding)[:, None] | itself)


def attention_parts(queries, keyvals, lengths, query_place):
    seq_total = keyvals.shape[0]
    key_block_size = math.gcd(seq_total, block_limit)
    block_count = seq_total // key_block_size
    key_place = jnp.arange(seq_total, dtype=jnp.int32)
    key_segment = segments_of(lengths, key_place)[0]
    query_segment, query_padding = segments_of(lengths, query_place)
    blocked = (
        keyvals.reshape((block_count, key_block_size) + keyvals.shape[1:]),
        key_place.reshape(block_count, key_block_size),
        key_segment.reshape(block_count, key_block_size),
    )

    def block_scores(key_rows, place_rows, segment_rows):
        raw_scores = (
            jnp.einsum("qhd,khd->hqk", queries, key_rows, preferred_element_type=jnp.float32)
            * score_scale
        )
        allowed = allowed_pairs(
            query_place, query_segment, query_padding, place_rows, segment_rows
        )[None]
        return (raw_scores, allowed)

    return (blocked, block_scores)


def attention_forward(queries, blocked, block_scores):
    query_count, head_count, head_width = queries.shape

    def max_step(running, inputs):
        best_score, mass_sum = running
        kv_block, place_rows, segment_rows = inputs
        raw_scores, allowed = block_scores(kv_block[:, 0], place_rows, segment_rows)
        masked = jnp.where(allowed, raw_scores, masked_fill)
        new_best = jnp.maximum(best_score, jnp.max(masked, axis=2))
        fresh = jnp.sum(jnp.where(allowed, jnp.exp(masked - new_best[:, :, None]), 0.0), axis=2)
        return ((new_best, mass_sum * jnp.exp(best_score - new_best) + fresh), None)

    start_best = jnp.full((head_count, query_count), masked_fill, jnp.float32)
    start_mass = jnp.zeros((head_count, query_count), jnp.float32)
    (best_score, mass_sum), unused = lax.scan(max_step, (start_best, start_mass), blocked)
    log_sum = best_score + jnp.log(mass_sum)

    def out_step(running, inputs):
        kv_block, place_rows, segment_rows = inputs
        raw_scores, allowed = block_scores(kv_block[:, 0], place_rows, segment_rows)
        probs_low = jnp.where(allowed, jnp.exp(raw_scores - log_sum[:, :, None]), 0.0).astype(
            jnp.bfloat16
        )
        return (
            running
            + jnp.einsum(
                "hqk,khd->qhd", probs_low, kv_block[:, 1], preferred_element_type=jnp.float32
            ),
            None,
        )

    attended, unused = lax.scan(
        out_step, jnp.zeros((query_count, head_count, head_width), jnp.float32), blocked
    )
    return (attended, log_sum)


def attention_backward(queries, blocked, block_scores, log_sum, grad_attended):
    query_count, head_count, head_width = queries.shape

    def probs_and_grads(inputs):
        kv_block, place_rows, segment_rows = inputs
        raw_scores, allowed = block_scores(kv_block[:, 0], place_rows, segment_rows)
        probs_f = jnp.where(allowed, jnp.exp(raw_scores - log_sum[:, :, None]), 0.0)
        grad_probs = jnp.einsum(
            "qhd,khd->hqk", grad_attended, kv_block[:, 1], preferred_element_type=jnp.float32
        )
        return (probs_f, grad_probs)

    def delta_step(running, inputs):
        probs_f, grad_probs = probs_and_grads(inputs)
        return (running + jnp.sum(probs_f * grad_probs, axis=2), None)

    delta_sum, unused = lax.scan(
        delta_step, jnp.zeros((head_count, query_count), jnp.float32), blocked
    )

    def grad_step(running, inputs):
        kv_block = inputs[0]
        probs_f, grad_probs = probs_and_grads(inputs)
        grad_scores = (probs_f * (grad_probs - delta_sum[:, :, None])).astype(jnp.bfloat16)
        running = running + jnp.einsum(
            "hqk,khd->qhd", grad_scores, kv_block[:, 0], preferred_element_type=jnp.float32
        )
        grad_keys = (
            jnp.einsum("hqk,qhd->khd", grad_scores, queries, preferred_element_type=jnp.float32)
            * score_scale
        )
        grad_values = jnp.einsum(
            "hqk,qhd->khd",
            probs_f.astype(jnp.bfloat16),
            grad_attended,
            preferred_element_type=jnp.float32,
        )
        return (running, jnp.stack([grad_keys, grad_values], axis=1))

    grad_queries, grad_keyvals = lax.scan(
        grad_step, jnp.zeros((query_count, head_count, head_width), jnp.float32), blocked
    )
    seq_total = grad_keyvals.shape[0] * grad_keyvals.shape[1]
    return (grad_queries * score_scale, grad_keyvals.reshape(seq_total, 2, head_count, head_width))


def body(
    tokens,
    ln1_gain,
    ln1_bias,
    qkv_weight,
    qv_bias,
    out_weight,
    out_bias,
    ln2_gain,
    ln2_bias,
    fc_weight,
    fc_bias,
    proj_weight,
    proj_bias,
    doc_lengths,
    cotangent,
):
    count_rows = lax.axis_size("row")
    count_cols = lax.axis_size("col")
    grid_rows = tokens.shape[1]
    col_width = tokens.shape[0]
    row_width = out_weight.shape[0]
    seq_rows = grid_rows * count_rows // count_cols
    query_rows = seq_rows // count_rows
    full_width = col_width * count_cols
    head_count = full_width // HEAD_DIM
    tokens_f = tokens.astype(jnp.float32).T
    normal1, inv_std1, shaped1 = norm_forward(tokens_f, ln1_gain, ln1_bias)
    qkv_flat = qkv_weight.reshape(col_width, 3 * row_width)
    gathered1 = gather_rows(shaped1.astype(jnp.bfloat16))
    mixed_qkv = sum_over_cols(product_term(gathered1, qkv_flat), seq_rows).reshape(
        seq_rows, 3, row_width
    )
    bias_three = jnp.stack([qv_bias[0], jnp.zeros_like(qv_bias[0]), qv_bias[1]])
    qkv_low = (mixed_qkv + bias_three).astype(jnp.bfloat16)
    local_qkv = to_heads(qkv_low).reshape(query_rows, 3, head_count, HEAD_DIM)
    queries = local_qkv[:, 0]
    keyvals = lax.all_gather(local_qkv[:, 1:], "row", axis=0, tiled=True)
    query_place = lax.axis_index("row") * query_rows + jnp.arange(query_rows, dtype=jnp.int32)
    blocked, block_scores = attention_parts(queries, keyvals, doc_lengths[0], query_place)
    attended_f, log_sum = attention_forward(queries, blocked, block_scores)
    attended_low = attended_f.reshape(query_rows, 1, full_width).astype(jnp.bfloat16)
    attended_grid = to_tokens(attended_low).reshape(seq_rows, row_width)
    gathered_att = gather_cols(attended_grid)
    branch = sum_over_rows(product_term(gathered_att, out_weight), grid_rows)
    hidden = tokens_f + (branch + out_bias)
    normal2, inv_std2, shaped2 = norm_forward(hidden, ln2_gain, ln2_bias)
    normed2 = shaped2.astype(jnp.bfloat16)
    gathered2 = gather_rows(normed2)
    pre_act = sum_over_cols(product_term(gathered2, fc_weight), seq_rows) + fc_bias
    active = jax.nn.gelu(pre_act, approximate=False).astype(jnp.bfloat16)
    gathered_act = gather_cols(active)
    projected = sum_over_rows(product_term_back(gathered_act, proj_weight), grid_rows)
    output = (hidden + projected + proj_bias).astype(jnp.bfloat16).T
    cotangent_rows = cotangent.T
    grad_out = cotangent_rows.astype(jnp.float32)
    unused, gelu_back = jax.vjp(partial(jax.nn.gelu, approximate=False), pre_act)
    grad_gathered = gather_rows(cotangent_rows)
    proj_weight_grad = inner_rows(grad_gathered, gathered_act)
    proj_bias_grad = jnp.sum(grad_gathered, axis=0, dtype=jnp.float32)
    grad_active = sum_over_cols(product_term(grad_gathered, proj_weight), seq_rows)
    grad_pre = gelu_back(grad_active)[0].astype(jnp.bfloat16)
    grad_pre_all = gather_cols(grad_pre)
    fc_weight_grad = inner_rows(gathered2, grad_pre_all)
    fc_bias_grad = jnp.sum(grad_pre_all, axis=0, dtype=jnp.float32)
    grad_normed2 = sum_over_rows(product_term_back(grad_pre_all, fc_weight), grid_rows)
    ln2_gain_part = jnp.sum(grad_normed2 * normal2, axis=0)
    ln2_bias_part = jnp.sum(grad_normed2, axis=0)
    grad_hidden = grad_out + norm_backward(grad_normed2, normal2, inv_std2, ln2_gain)
    branch_gathered = gather_rows(grad_hidden.astype(jnp.bfloat16))
    out_weight_grad = inner_rows(gathered_att, branch_gathered)
    out_bias_grad = jnp.sum(branch_gathered, axis=0, dtype=jnp.float32)
    grad_att_grid = sum_over_cols(product_term_back(branch_gathered, out_weight), seq_rows).astype(
        jnp.bfloat16
    )
    grad_attended = to_heads(grad_att_grid.reshape(seq_rows, 1, row_width)).reshape(
        query_rows, head_count, HEAD_DIM
    )
    grad_queries, grad_keyvals = attention_backward(
        queries, blocked, block_scores, log_sum, grad_attended
    )
    keyval_rows = sum_over_rows(slice_term(grad_keyvals), query_rows)
    grad_qkv_local = (
        jnp.concatenate([grad_queries[:, None], keyval_rows], axis=1)
        .astype(jnp.bfloat16)
        .reshape(query_rows, 3, full_width)
    )
    grad_qkv_grid = to_tokens(grad_qkv_local).reshape(seq_rows, 3 * row_width)
    qkv_gathered = gather_cols(grad_qkv_grid)
    qkv_weight_grad = inner_rows(gathered1, qkv_gathered).reshape(col_width, 3, row_width)
    qkv_bias_sums = jnp.sum(qkv_gathered, axis=0, dtype=jnp.float32).reshape(3, row_width)
    qv_bias_grad = jnp.stack([qkv_bias_sums[0], qkv_bias_sums[2]])
    grad_normed1 = sum_over_rows(product_term_back(qkv_gathered, qkv_flat), grid_rows)
    ln1_gain_part = jnp.sum(grad_normed1 * normal1, axis=0)
    ln1_bias_part = jnp.sum(grad_normed1, axis=0)
    input_grad = (
        (grad_hidden + norm_backward(grad_normed1, normal1, inv_std1, ln1_gain))
        .astype(jnp.bfloat16)
        .T
    )
    summed = lax.psum(
        (
            qkv_weight_grad,
            qv_bias_grad,
            out_weight_grad,
            out_bias_grad,
            fc_weight_grad,
            fc_bias_grad,
            proj_weight_grad,
            proj_bias_grad,
        ),
        "dp",
    )
    gain_sums = lax.psum(
        (ln1_gain_part, ln1_bias_part, ln2_gain_part, ln2_bias_part), ("dp", "row")
    )
    return (
        output,
        input_grad,
        gain_sums[0],
        gain_sums[1],
        summed[0],
        summed[1],
        summed[2],
        summed[3],
        gain_sums[2],
        gain_sums[3],
        summed[4],
        summed[5],
        summed[6],
        summed[7],
    )


BF = jnp.bfloat16
F32 = jnp.float32
MESH = pl.DeviceIdType.MESH
LANES = 128
KEY_TILE = 256
VEC_LN1_GAIN, VEC_LN1_BIAS, VEC_LN2_GAIN, VEC_LN2_BIAS, VEC_OUT_BIAS, VEC_PROJ_BIAS = range(6)


def dot_nn(left, right):
    return lax.dot_general(left, right, (((1,), (0,)), ((), ())), preferred_element_type=F32)


def dot_tn(left, right):
    return lax.dot_general(left, right, (((0,), (0,)), ((), ())), preferred_element_type=F32)


def dot_nt(left, right):
    return lax.dot_general(left, right, (((1,), (1,)), ((), ())), preferred_element_type=F32)


VMEM_LIMIT = 66_000_000


class Slots:
    def __init__(self):
        self.used = 0

    def take(self, count=1):
        first = self.used
        self.used += count
        return first


SEND_COUNT, RECV_COUNT, LOCAL_COUNT = 208, 208, 48


def layer_kernel(
    x_in,
    cot_in,
    w3_in,
    ow_in,
    fc_in,
    proj_in,
    ln1_gain_in,
    ln1_bias_in,
    ln2_gain_in,
    ln2_bias_in,
    out_bias_in,
    proj_bias_in,
    fc_bias_in,
    qv_bias_in,
    doc_in,
    out_o,
    ing_o,
    gf_o,
    gq_o,
    vec_o,
    rf1_hbm,
    rf2_hbm,
    rq1_hbm,
    rq2_hbm,
    XG,
    CG,
    N1,
    WB,
    QB,
    OWB,
    FB,
    COLS,
    PACK,
    PACKF,
    PACKN,
    MASK,
    QKV,
    LSE,
    ATT,
    HID,
    ST1,
    ST2,
    N2,
    ACT,
    GPRE,
    PGS,
    OPS,
    RCG,
    RCO,
    OPO,
    SZG,
    RZG,
    G2,
    SZO,
    RZO,
    RZN,
    DATT,
    GQKV,
    ACCK,
    ACCV,
    ZF,
    DQ,
    ZQ,
    ZT,
    GH,
    VGC,
    STX,
    SPR,
    SPZ,
    VOUT,
    SS,
    RS,
    LS,
):
    H, T = x_in.shape
    R = w3_in.shape[1]
    HP = DQ.shape[3]
    EXT = WB.shape[2]
    TAIL = EXT - R
    D = 2 * H
    S = 2 * T
    W = KEY_TILE
    Q = HEAD_DIM
    FW = fc_in.shape[1]
    per_tok = T // W
    n_tiles = S // W
    inv_d = 1.0 / D

    dp, z, c = lax.axis_index("dp"), lax.axis_index("row"), lax.axis_index("col")
    oc = 1 - c
    zz = lax.rem(z, 2)
    zp = z + 1 - 2 * zz
    z2 = lax.rem(z + 2, 4)
    j = lax.rem(z + 2 * c, 4)
    pair = z // 2
    core = (dp, z, oc)
    zdev = (dp, zp, c)
    xn = dp + 1 - 2 * lax.rem(dp, 2)
    yn = lax.rem(dp + 2, 4)
    dg = 3 - dp
    peers = (xn, yn, dg)
    xb, yb = lax.rem(dp, 2), dp // 2
    xdev, ydev = (xn, z, c), (yn, z, c)
    first_core, second_core = c == 0, c == 1

    sends, recvs, locs = Slots(), Slots(), Slots()
    pending = []

    def remote(src, dst, s_idx, r_idx, dev):
        return pltpu.make_async_remote_copy(
            src_ref=src,
            dst_ref=dst,
            send_sem=SS.at[s_idx],
            recv_sem=RS.at[r_idx],
            device_id=dev,
            device_id_type=MESH,
        )

    def when(cond, fn):
        if cond is None:
            fn()
        else:
            pl.when(cond)(fn)

    def push(src, dst, r_idx, dev, cond=None):
        copy = remote(src, dst, sends.take(), r_idx, dev)
        when(cond, copy.start)
        entry = [cond, copy]
        pending.append(entry)
        return entry

    def sent(entry):
        when(entry[0], entry[1].wait_send)
        pending[:] = [other for other in pending if other is not entry]

    def arrived(dst, r_idx, cond=None):
        when(cond, remote(dst, dst, 0, r_idx, core).wait_recv)

    def local(src, dst, cond=None):
        copy = pltpu.make_async_copy(src, dst, LS.at[locs.take()])
        when(cond, copy.start)
        return (cond, copy)

    def done(entry):
        when(entry[0], entry[1].wait)

    barrier = pltpu.get_barrier_semaphore()
    for step in range(4):
        for side in range(2):
            if step == 0 and side == 0:
                continue
            target = (dp, lax.rem(z + step, 4), c if side == 0 else oc)
            pl.semaphore_signal(barrier, inc=1, device_id=target, device_id_type=MESH)
    for peer in peers:
        pl.semaphore_signal(barrier, inc=1, device_id=(peer, z, c), device_id_type=MESH)
    pl.semaphore_wait(barrier, 10)

    r_x_core, r_x_z, r_x_fwd = recvs.take(), recvs.take(), recvs.take()
    r_w_core, r_w_z, r_w_xy, r_w_tail = recvs.take(), recvs.take(16), recvs.take(8), recvs.take(2)
    r_pack, r_packf, r_packn = recvs.take(), recvs.take(), recvs.take()
    r_f_core, r_f_z, r_f_xy = recvs.take(2), recvs.take(4), recvs.take(8)
    r_o_core, r_o_z, r_o_z0, r_o_xy, r_o_fwd = (
        recvs.take(),
        recvs.take(4),
        recvs.take(4),
        recvs.take(16),
        recvs.take(4),
    )

    def block(number):
        return pl.ds(pl.multiple_of(number * R, 16), R)

    quarter = D // 4
    odd = R - 4 * (R // 64) * 16
    piece = R // 64 * 16

    def quarter_rows(number):
        return pl.ds(pl.multiple_of(number * quarter, 16), quarter)

    def ow_piece(number, plane):
        return pl.ds(pl.multiple_of(number * R + odd + plane * piece, 16), piece)

    def ow_odd(number):
        return pl.ds(pl.multiple_of(number * R, 16), odd)

    my_quarter = quarter_rows(dp)
    more = H // 16 % 4
    share = H // 64 * 16

    def ff_share(plane, large):
        if large:
            return pl.ds(pl.multiple_of(plane * (share + 16), 16), share + 16)
        return pl.ds(pl.multiple_of(more * 16 + plane * share, 16), share)

    ff_kinds = ((True, dp < more), (False, dp >= more))
    w_pieces, row = [], 0
    for plane in range(4):
        left = (3 * R // 16 // 4 + (1 if plane < 3 * R // 16 % 4 else 0)) * 16
        while left:
            rows = min(left, R - row % R)
            w_pieces.append((plane, row // R, row % R, rows))
            row, left = row + rows, left - rows
    has_before = z >= 1
    bias_first = (LANES, LANES + (R // LANES + 1) * LANES)
    doc_count = doc_in.shape[1]
    w_entries = []
    for number, (plane, m, first, size) in enumerate(w_pieces):
        rows = pl.ds(first, size)
        w_entries.append(
            push(
                w3_in.at[m, rows], WB.at[m, c, rows], r_w_z + (2 * number + c), (dp, z2, 1), dp == plane
            )
        )
    pack = PACK.at[c]
    PACK[c] = jnp.zeros(PACK.shape[1:], F32)
    vectors_in = (ln1_gain_in, ln1_bias_in, ln2_gain_in, ln2_bias_in, out_bias_in, proj_bias_in, fc_bias_in)
    for number, vector in enumerate(vectors_in):
        PACK[c, number : number + 1, 0 : vector.shape[0]] = vector[...].astype(F32).reshape(1, -1)
    PACK[c, 7:8, 0:doc_count] = doc_in[...].astype(F32)
    for number in range(2):
        PACK[c, 7:8, bias_first[number] : bias_first[number] + R] = qv_bias_in[number : number + 1, :].astype(F32)
    push(x_in, XG.at[zz, c], r_x_z, zdev)
    push(x_in, XG.at[zz, c], r_x_core, core)
    push(pack, pack, r_pack, core)
    push(w3_in, WB.at[:, 1, pl.ds(0, R)], r_w_core, (dp, z, 0), second_core)
    for place in range(1, 4):
        rows = TAIL - 16 * (place - 1)
        head = w3_in.at[:, pl.ds(0, rows)]
        there = WB.at[:, c, pl.ds(R, rows)]
        push(head, there, r_w_tail + c, (dp, place - 1, 0), z == place)
        push(head, there, r_w_tail + c, (dp, (place + 1) % 4, 1), z == place)
    push(pack, PACKF, r_packf, (dp, z2, 1), first_core)
    push(pack, PACKN, r_packn, (dp, jnp.maximum(z - 1, 0), 0), has_before & first_core)
    push(pack, PACKN, r_packn, (dp, lax.rem(z + 1, 4), 1), has_before & first_core)
    l_x = local(x_in, XG.at[zz, c])
    l_w = local(w3_in, WB.at[:, 0, pl.ds(0, R)], first_core)
    push(fc_in, FB.at[0, 1], r_f_core, (dp, z, 0), second_core)
    push(proj_in, FB.at[1, 1], r_f_core + 1, (dp, z, 0), second_core)
    push(ow_in, OWB.at[c, block(z)], r_o_core, core)
    l_f = local(fc_in, FB.at[0, 0], first_core)
    l_p = local(proj_in, FB.at[1, 0], first_core)
    l_o = local(ow_in, OWB.at[c, block(z)])

    ff_entries = []

    def send_ff(kind):
        source = (fc_in, proj_in)[kind]
        for large, cond in ff_kinds:
            rows = ff_share(dp, large)
            push(source.at[rows], FB.at[kind, c, rows], r_f_z + (2 * kind + c), (dp, z2, 1), cond)

    def pass_ff(kind):
        for large, cond in ff_kinds:
            rows = ff_share(dp, large)
            for h in range(2):
                arrived(FB.at[kind, h, rows], r_f_z + (2 * kind + h), second_core & cond)
            part = FB.at[kind, :, rows]
            for peer in peers:
                ff_entries.append(
                    push(part, part, r_f_xy + (4 * kind + dp), (peer, z, 1), second_core & cond)
                )

    def ff_ready(kind):
        arrived(FB.at[kind, 1], r_f_core + kind, first_core)
        for plane in range(4):
            arrived(
                FB.at[kind, :, ff_share(plane, plane < more)],
                r_f_xy + (4 * kind + plane),
                second_core & (dp != plane),
            )

    for entry in w_entries:
        sent(entry)
    send_ff(0)

    VGC[...] = jnp.zeros_like(VGC)
    GQKV[...] = jnp.zeros_like(GQKV)

    def clear_tail(rows):
        WB[:, :, EXT - rows :, :] = jnp.zeros((3, 2, rows, H), BF)

    for place in range(1, 4):
        pl.when(j == place)(partial(clear_tail, 16 * place))

    arrived(PACK.at[oc], r_pack)
    lengths = PACK[pair, 7:8, 0:LANES]
    place_c = lax.broadcasted_iota(jnp.int32, (S, LANES), 0).astype(F32)
    place_r = lax.broadcasted_iota(jnp.int32, (8, S), 1).astype(F32)
    end = jnp.zeros((1, 1), F32)
    seg_c, seg_r = jnp.zeros_like(place_c), jnp.zeros_like(place_r)
    for number in range(doc_count):
        end = end + lengths[:, number : number + 1]
        seg_c = seg_c + jnp.where(end <= place_c, 1.0, 0.0)
        seg_r = seg_r + jnp.where(end <= place_r, 1.0, 0.0)
    seg_c = jnp.where(end <= place_c, place_c + 2.0 * S, seg_c)
    seg_r = jnp.where(end <= place_r, place_r + 2.0 * S, seg_r)
    for tile in range(n_tiles):
        rows = W * (tile + 1)
        first = W * tile * (tile + 1) // 2
        cols = slice(tile * W, (tile + 1) * W)
        key_seg = jnp.concatenate([seg_c[:rows]] * (W // LANES), axis=1)
        key_place = jnp.concatenate([place_c[:rows]] * (W // LANES), axis=1)
        ok = (key_seg == seg_r[0:1, cols]) & (key_place <= place_r[0:1, cols])
        MASK[first : first + rows, :] = jnp.where(ok, 0.0, masked_fill)

    for h in range(2):
        COLS[h * H : (h + 1) * H, 0:6] = PACK[h].T[0:H, 0:6]

    def column(h, which):
        if isinstance(h, int):
            return COLS[h * H : (h + 1) * H, which : which + 1]
        return COLS[pl.ds(pl.multiple_of(h * H, 16), H), which : which + 1]

    def stats_of(first_half, second_half):
        center = (
            jnp.sum(first_half, axis=0, keepdims=True) + jnp.sum(second_half, axis=0, keepdims=True)
        ) * inv_d
        square = (
            jnp.sum(first_half * first_half, axis=0, keepdims=True)
            + jnp.sum(second_half * second_half, axis=0, keepdims=True)
        ) * inv_d
        return center, lax.rsqrt(square - center * center + epsilon)

    def first_norm(t):
        halves = [XG[t, h].astype(F32) for h in range(2)]
        center, inv_std = stats_of(*halves)
        ST1[t, 0:1, :] = center
        ST1[t, 1:2, :] = inv_std
        for h in range(2):
            shaped = (halves[h] - center) * inv_std * column(h, VEC_LN1_GAIN) + column(
                h, VEC_LN1_BIAS
            )
            N1[t, h, 0:H, :] = shaped.astype(BF)

    done(l_x)
    arrived(XG.at[zz, oc], r_x_core)
    first_norm(zz)

    for number, (plane, m, first, size) in enumerate(w_pieces):
        cond = second_core & (dp == plane)
        rows = pl.ds(first, size)
        for h in range(2):
            arrived(WB.at[m, h, rows], r_w_z + (2 * number + h), cond)
        for peer in peers:
            push(WB.at[m, :, rows], WB.at[m, :, rows], r_w_xy + number, (peer, z, 1), cond)
    arrived(XG.at[1 - zz, c], r_x_z)
    e_xf = push(XG.at[1 - zz, c], XG.at[1 - zz, c], r_x_fwd, core)
    arrived(XG.at[1 - zz, oc], r_x_fwd)
    first_norm(1 - zz)

    done(l_w)
    pass_ff(0)
    for step in (1, 3, 2):
        target = (dp, lax.rem(z + step, 4), c)
        push(ow_in.at[ow_piece(0, dp)], OWB.at[c, ow_piece(z, dp)], r_o_z + z, target)
        push(ow_in.at[ow_odd(0)], OWB.at[c, ow_odd(z)], r_o_z0 + z, target)
    send_ff(1)
    arrived(WB.at[:, 1, pl.ds(0, R)], r_w_core, first_core)
    for number, (plane, m, first, size) in enumerate(w_pieces):
        arrived(WB.at[m, :, pl.ds(first, size)], r_w_xy + number, second_core & (dp != plane))
    for h in range(2):
        for place in range(3):
            arrived(WB.at[:, h, pl.ds(R, TAIL - 16 * place)], r_w_tail + h, j == place)

    arrived(PACKF, r_packf, second_core)
    arrived(PACKN, r_packn, j < 3)

    def bias_columns(source, rows, count):
        turned = source.T
        for m, first in ((0, bias_first[0]), (2, bias_first[1])):
            QB[rows : rows + count, m : m + 1] = turned[first : first + count, 7:8]

    QB[...] = jnp.zeros_like(QB)
    pl.when(first_core)(lambda: bias_columns(PACK[0], 0, R))
    pl.when(second_core)(lambda: bias_columns(PACKF[...], 0, R))
    pl.when(j < 3)(lambda: bias_columns(PACKN[...], R, TAIL))

    for t in range(2):
        for m in range(3):
            mixed = dot_nn(WB[m, 0], N1[t, 0]) + dot_nn(WB[m, 1], N1[t, 1])
            if m != 1:
                mixed = mixed + QB[:, m : m + 1]
            low = mixed.astype(BF)
            if m == 0:
                low = low * jnp.asarray(score_scale, BF)
            QKV[m, :, t * T : (t + 1) * T] = low


    r_a_z, r_a_core, r_a_fwd = recvs.take(5), recvs.take(5), recvs.take(5)
    s_a_z, s_a_core, s_a_fwd = sends.take(5), sends.take(5), sends.take(5)
    first_slot = jnp.where(j == 0, 0, 1)

    def head_rows(owner, slot):
        return pl.ds(pl.multiple_of(owner * (4 * Q) + slot * Q, Q), Q)

    def slot_rows(slot):
        return pl.ds(pl.multiple_of(slot * Q - 16 * j, 16), Q)

    def att_copy(owner, slot, s_base, r_base, dev):
        rows = head_rows(owner, slot)
        return remote(ATT.at[rows], ATT.at[rows], s_base + slot, r_base + slot, dev)

    s_o_xy = sends.take(9)

    def ow_copy(step, number):
        there = lax.rem(z + step, 4)
        rows = OWB.at[c, ow_piece(there, dp)]
        return remote(
            rows, rows, s_o_xy + (3 * (step - 1) + number), r_o_xy + (4 * dp + there), (peers[number], z, c)
        )

    def pass_ow():
        for step in (1, 3, 2):
            there = lax.rem(z + step, 4)
            arrived(OWB.at[c, ow_piece(there, dp)], r_o_z + there)
            for number in range(3):
                ow_copy(step, number).start()

    def attend(slot, carry):
        @pl.when(slot == 2)
        def _():
            pass_ow()

        rows = slot_rows(slot)
        out_rows = head_rows(j, slot)
        queries = QKV[0, rows, :]
        keys = QKV[1, rows, :].T
        values = QKV[2, rows, :]
        for tile in range(n_tiles):
            count = W * (tile + 1)
            first = W * tile * (tile + 1) // 2
            cols = slice(tile * W, (tile + 1) * W)
            scores = dot_nn(keys[:count], queries[:, cols]) + MASK[first : first + count, :]
            best = jnp.max(scores, axis=0, keepdims=True)
            weights = jnp.exp(scores - best)
            mass = jnp.sum(weights, axis=0, keepdims=True)
            probs_low = (weights * (1.0 / mass)).astype(BF)
            ATT[out_rows, cols] = dot_nn(values[:, :count], probs_low).astype(BF)
            LSE[slot, 0:1, cols] = best + jnp.log(mass)
        att_copy(j, slot, s_a_z, r_a_z, zdev).start()
        att_copy(j, slot, s_a_core, r_a_core, core).start()

        return carry

    lax.fori_loop(first_slot, 5, attend, 0)

    r_c_core, r_c_z, r_c_fwd = recvs.take(), recvs.take(), recvs.take()
    push(cot_in, CG.at[zz, c], r_c_z, zdev)
    push(cot_in, CG.at[zz, c], r_c_core, core)
    l_c = local(cot_in, CG.at[zz, c])

    pass_ff(1)

    for step in (1, 3, 2):
        there = lax.rem(z + step, 4)
        arrived(OWB.at[c, ow_odd(there)], r_o_z0 + there)
        for plane in range(4):
            arrived(OWB.at[c, ow_piece(there, plane)], r_o_xy + (4 * plane + there), dp != plane)
        push(OWB.at[c, block(there)], OWB.at[c, block(there)], r_o_fwd + there, core)

    def owner_of(zv, cv):
        return lax.rem(zv + 2 * cv, 4)

    def slots_of(owner, body):
        lax.fori_loop(jnp.where(owner == 0, 0, 1), 5, lambda slot, carry: (body(slot), carry)[1], 0)

    def pass_on(slot):
        att_copy(owner_of(zp, c), slot, s_a_fwd, r_a_z, core).wait_recv()
        att_copy(owner_of(zp, c), slot, s_a_fwd, r_a_fwd, core).start()

    slots_of(owner_of(zp, c), pass_on)
    slots_of(owner_of(z, oc), lambda slot: att_copy(owner_of(z, oc), slot, s_a_core, r_a_core, core).wait_recv())
    slots_of(owner_of(zp, oc), lambda slot: att_copy(owner_of(zp, oc), slot, s_a_fwd, r_a_fwd, core).wait_recv())
    done(l_o)
    arrived(OWB.at[oc, block(z)], r_o_core)
    for step in range(1, 4):
        there = lax.rem(z + step, 4)
        arrived(OWB.at[oc, block(there)], r_o_fwd + there)

    def project(tile, carry):
        t = tile // per_tok
        cols = pl.ds(pl.multiple_of(lax.rem(tile, per_tok) * W, W), W)
        all_cols = pl.ds(pl.multiple_of(tile * W, W), W)
        att = ATT[:, all_cols]
        halves = []
        for h in range(2):
            branch = dot_tn(OWB[h], att)
            halves.append(XG[t, h, :, cols].astype(F32) + (branch + column(h, VEC_OUT_BIAS)))
            HID[t, h, :, cols] = halves[h]
        center, inv_std = stats_of(*halves)
        ST2[t, 0:1, cols] = center
        ST2[t, 1:2, cols] = inv_std
        for h in range(2):
            shaped = (halves[h] - center) * inv_std * column(h, VEC_LN2_GAIN) + column(
                h, VEC_LN2_BIAS
            )
            N2[t, h, :, cols] = shaped.astype(BF)
        return carry

    lax.fori_loop(0, n_tiles, project, 0)

    done(l_f)
    ff_ready(0)

    @pl.when(first_core)
    def _():
        COLS[:, 6:7] = PACK[0].T[0:FW, 6:7]

    @pl.when(second_core)
    def _():
        COLS[:, 6:7] = PACKF[...].T[0:FW, 6:7]

    s_c_fwd = sends.take()

    def cot_forward():
        return remote(CG.at[1 - zz, c], CG.at[1 - zz, c], s_c_fwd, r_c_fwd, core)

    def other_cotangent():
        arrived(CG.at[1 - zz, c], r_c_z)
        cot_forward().start()
        arrived(CG.at[1 - zz, oc], r_c_fwd)


    r_g_core, r_p_core, r_g_z = recvs.take(n_tiles), recvs.take(n_tiles), recvs.take(n_tiles)
    s_g_core, s_p_core, s_g_z = sends.take(n_tiles), sends.take(n_tiles), sends.take(n_tiles)

    def tile_at(tile):
        t = tile // per_tok
        return t, pl.ds(pl.multiple_of(lax.rem(tile, per_tok) * W, W), W)

    def part_copy(buf, dst, tile, s_base, r_base, dev):
        t, cols = tile_at(tile)
        return remote(buf.at[t, :, cols], dst.at[t, :, cols], s_base + tile, r_base + tile, dev)

    def feed(tile, carry):
        t, cols = tile_at(tile)
        all_cols = pl.ds(pl.multiple_of(tile * W, W), W)
        pre = dot_tn(FB[0].reshape(D, FW), N2[t, :, :, cols].reshape(D, W)) + COLS[:, 6:7]
        phi = 0.5 * (1.0 + lax.erf(pre * (2.0**-0.5)))
        ACT[:, all_cols] = (pre * phi).astype(BF)
        slope = phi + pre * jnp.exp(pre * pre * -0.5) * ((2.0 * math.pi) ** -0.5)
        GPRE[:, all_cols] = slope.astype(BF)
        return carry

    lax.fori_loop(0, n_tiles, feed, 0)
    done(l_p)
    ff_ready(1)
    done(l_c)
    arrived(CG.at[zz, oc], r_c_core)

    def feed_back(order, carry):
        t = lax.rem(order + zz, 2)
        pl.when(order == 1)(other_cotangent)
        for number in range(per_tok):
            cols = slice(number * W, (number + 1) * W)
            all_cols = pl.ds(pl.multiple_of(t * T + number * W, W), W)
            grad_act = dot_tn(FB[1].reshape(D, FW), CG[t, :, :, cols].reshape(D, W))
            GPRE[:, all_cols] = (grad_act * GPRE[:, all_cols].astype(F32)).astype(BF)
            PGS[t, :, cols] = dot_nn(FB[0, oc], GPRE[:, all_cols]).astype(BF)
            part_copy(PGS, RCG, t * per_tok + number, s_g_core, r_g_core, core).start()
        for number in range(per_tok):
            cols = slice(number * W, (number + 1) * W)
            all_cols = pl.ds(pl.multiple_of(t * T + number * W, W), W)
            tile = t * per_tok + number
            own = dot_nn(FB[0, c], GPRE[:, all_cols])
            part_copy(PGS, RCG, tile, s_g_core, r_g_core, core).wait_recv()
            SZG[t, :, cols] = (own + RCG[t, :, cols].astype(F32)).astype(BF)
            part_copy(SZG, RZG, tile, s_g_z, r_g_z, zdev).start()
        return carry

    lax.fori_loop(0, 2, feed_back, 0)

    for entry in ff_entries:
        sent(entry)
    r_f1, r_f2 = recvs.take(4), recvs.take(2)
    f1_entries = []

    def ff_grads(number):
        for h in range(2):
            left, right = (N2, GPRE) if number < 2 else (CG, ACT)
            rows = slice(number % 2 * quarter, (number % 2 + 1) * quarter)
            total = dot_nt(left[0, h, rows, :], right[:, 0:T]) + dot_nt(left[1, h, rows, :], right[:, T:S])
            FB[number // 2, h, rows, :] = total.astype(BF)

    def ff_rows(number):
        return quarter_rows(lax.rem(number, 2))

    def ff_part(h, number):
        return FB.at[number // 2, h, ff_rows(number)]

    def ff_value(h, number):
        return FB[number // 2, h, ff_rows(number), :].astype(F32)

    def f1_push(h, number, place, dev, cond=None):
        f1_entries.append(push(ff_part(h, number), rf1_hbm.at[place], r_f1 + place, dev, cond))

    for number in range(2):
        ff_grads(number)
        f1_push(0, number, 0, xdev, xb != number)
        f1_push(1, number, 2 + number, ydev, yb == 1)

    def outward(tile, carry):
        t, cols = tile_at(tile)
        all_cols = pl.ds(pl.multiple_of(tile * W, W), W)
        OPS[t, :, cols] = dot_nn(FB[1, oc], ACT[:, all_cols]).astype(BF)
        part_copy(OPS, RCO, tile, s_p_core, r_p_core, core).start()
        OPO[t, :, cols] = dot_nn(FB[1, c], ACT[:, all_cols]).astype(BF)
        return carry

    lax.fori_loop(0, n_tiles, outward, 0)
    for number in range(2):
        ff_grads(2 + number)
        f1_push(0, 2 + number, 1, xdev, xb != number)
        f1_push(1, 2 + number, 2 + number, ydev, yb == 0)

    SPR[dp] = jnp.zeros(SPR.shape[1:], F32)
    SPR[dp, 6:7, :] = dot_nt(jnp.ones((16, S), BF), GPRE[...])[0:1, :]

    r_g_all = recvs.take(n_tiles)
    s_g_all = sends.take(n_tiles)

    def g2_copy(tile):
        t, cols = tile_at(tile)
        return remote(G2.at[t, c, :, cols], G2.at[t, c, :, cols], s_g_all + tile, r_g_all + tile, core)

    def g2_other(tile):
        t, cols = tile_at(tile)
        return remote(G2.at[t, oc, :, cols], G2.at[t, oc, :, cols], s_g_all + tile, r_g_all + tile, core)

    def join(tile, carry):
        t, cols = tile_at(tile)
        part_copy(SZG, RZG, tile, s_g_z, r_g_z, zdev).wait_recv()
        G2[t, c, :, cols] = (SZG[t, :, cols].astype(F32) + RZG[t, :, cols].astype(F32)).astype(BF)
        g2_copy(tile).start()
        return carry

    lax.fori_loop(0, n_tiles, join, 0)

    def norm_back(grads, normals, inv_std, gain_index):
        scaled = [grads[h] * column(h, gain_index) for h in range(2)]
        plain = sum(jnp.sum(scaled[h], axis=0, keepdims=True) for h in range(2)) * inv_d
        cross = sum(jnp.sum(scaled[h] * normals[h], axis=0, keepdims=True) for h in range(2)) * inv_d
        return [inv_std * (scaled[h] - plain - normals[h] * cross) for h in range(2)]

    def second_back(tile, carry):
        t, cols = tile_at(tile)
        g2_other(tile).wait_recv()
        center, inv_std = ST2[t, 0:1, cols], ST2[t, 1:2, cols]
        grads = [G2[t, h, :, cols].astype(F32) for h in range(2)]
        normals = [(HID[t, h, :, cols] - center) * inv_std for h in range(2)]
        back = norm_back(grads, normals, inv_std, VEC_LN2_GAIN)
        for h in range(2):
            grad_hidden = CG[t, h, :, cols].astype(F32) + back[h]
            XG[t, h, :, cols] = grad_hidden.astype(BF)

            @pl.when((t == zz) & (c == h))
            def _():
                GH[:, cols] = grad_hidden
                VGC[:, 2:3] = VGC[:, 2:3] + jnp.sum(grads[h] * normals[h], axis=1, keepdims=True)
                VGC[:, 3:4] = VGC[:, 3:4] + jnp.sum(grads[h], axis=1, keepdims=True)

        return carry

    sent(e_xf)
    lax.fori_loop(0, n_tiles, second_back, 0)
    GB = XG

    r_out_z = recvs.take()

    def wait_out(tile, carry):
        part_copy(OPS, RCO, tile, s_p_core, r_p_core, core).wait_recv()
        return carry

    lax.fori_loop(0, n_tiles, wait_out, 0)
    SZO[...] = (OPO[1 - zz].astype(F32) + RCO[1 - zz].astype(F32)).astype(BF)
    push(SZO, RZO, r_out_z, zdev)
    VGC[:, 4:5] = jnp.sum(GB[zz, c].astype(F32), axis=1, keepdims=True)
    VGC[:, 5:6] = jnp.sum(CG[zz, c].astype(F32), axis=1, keepdims=True)

    window = pl.ds(pl.multiple_of(j * (4 * Q), Q), 5 * Q)
    for t in range(2):
        DATT[:, t * T : (t + 1) * T] = (
            dot_nn(OWB[0, window, :], GB[t, 0]) + dot_nn(OWB[1, window, :], GB[t, 1])
        ).astype(BF)
    r_q1, r_q2 = recvs.take(4), recvs.take(2)
    q1_entries = []

    def q1_push(h, number, place, dev, cond=None):
        q1_entries.append(push(DQ.at[number, h], rq1_hbm.at[place], r_q1 + place, dev, cond))

    for h in range(2):
        total = dot_nt(ATT[block(j), 0:T], GB[0, h]) + dot_nt(ATT[block(j), T:S], GB[1, h])
        DQ[3, h, 0:R, 0:H] = total.astype(BF)
    q1_push(0, 3, 1, xdev, xb == 0)
    q1_push(1, 3, 3, ydev, yb == 0)
    l_x2 = local(x_in, XG.at[zz, c])

    s_f2 = sends.take(2)
    l_f1, l_f2 = locs.take(4), locs.take(2)

    def f2_copy(place):
        if place == 0:
            return remote(ff_part(0, xb + 2 * (1 - yb)), rf2_hbm.at[0], s_f2, r_f2, ydev)
        return remote(ff_part(1, 2 * yb + 1 - xb), rf2_hbm.at[1], s_f2 + 1, r_f2 + 1, xdev)

    spare = ((0, 1 - xb), (0, 3 - xb), (1, 2 * (1 - yb)), (1, 2 * (1 - yb) + 1))
    kept = ((0, xb), (0, 2 + xb), (1, 2 * yb), (1, 2 * yb + 1))

    def first_join():
        for entry in f1_entries:
            when(entry[0], entry[1].wait_send)
        loads = []
        for place in range(4):
            arrived(rf1_hbm.at[place], r_f1 + place)
            load = pltpu.make_async_copy(rf1_hbm.at[place], ff_part(*spare[place]), LS.at[l_f1 + place])
            load.start()
            loads.append(load)
        for load in loads:
            load.wait()

        def add(place):
            h, number = kept[place]
            total = ff_value(h, number) + ff_value(*spare[place])
            FB[number // 2, h, ff_rows(number), :] = total.astype(BF)

        for place in range(4):
            add(place)
        f2_copy(0).start()
        f2_copy(1).start()

    def attend_back(slot, carry):
        rows = slot_rows(slot)
        here = pl.ds(pl.multiple_of(slot * Q, Q), Q)
        queries = QKV[0, rows, :]
        keys_t = QKV[1, rows, :]
        keys = keys_t.T
        values = QKV[2, rows, :].T
        grads_out = DATT[here, :]
        for tile in reversed(range(n_tiles)):
            count = W * (tile + 1)
            first = W * tile * (tile + 1) // 2
            cols = slice(tile * W, (tile + 1) * W)
            scores = dot_nn(keys[:count], queries[:, cols]) + MASK[first : first + count, :]
            probs = jnp.exp(scores - LSE[slot, 0:1, cols])
            grad_probs = dot_nn(values[:count], grads_out[:, cols])
            delta = jnp.sum(probs * grad_probs, axis=0, keepdims=True)
            grad_scores = (probs * (grad_probs - delta)).astype(BF)
            probs_low = probs.astype(BF)
            part_v = dot_nt(grads_out[:, cols], probs_low)
            part_k = dot_nt(queries[:, cols], grad_scores)
            if tile == n_tiles - 1:
                ACCV[...] = part_v
                ACCK[...] = part_k
            else:
                ACCV[:, 0:count] = ACCV[:, 0:count] + part_v
                ACCK[:, 0:count] = ACCK[:, 0:count] + part_k
            GQKV[0, rows, cols] = (dot_nn(keys_t[:, :count], grad_scores) * score_scale).astype(BF)
        GQKV[1, rows, :] = ACCK[...].astype(BF)
        GQKV[2, rows, :] = ACCV[...].astype(BF)

        @pl.when(slot == 3)
        def _():
            first_join()

        return carry

    lax.fori_loop(first_slot, 5, attend_back, 0)

    for m in range(3):
        if m != 1:
            bias_sum = jnp.sum(GQKV[m].astype(F32), axis=1, keepdims=True)
        for h in range(2):
            total = dot_nt(GQKV[m, :, 0:T], N1[0, h]) + dot_nt(GQKV[m, :, T:S], N1[1, h])
            DQ[m, h, :, 0:H] = total.astype(BF)
            if m != 1:
                DQ[m, h, :, H : H + 1] = bias_sum.astype(BF)
        q1_push(0, m, m // 2, xdev, xb != m % 2)
        q1_push(1, m, 2 + m % 2, ydev, yb != m // 2)

    def wait_sends(tile, carry):
        part_copy(PGS, RCG, tile, s_g_core, r_g_core, core).wait_send()
        part_copy(OPS, RCO, tile, s_p_core, r_p_core, core).wait_send()
        part_copy(SZG, RZG, tile, s_g_z, r_g_z, zdev).wait_send()
        g2_copy(tile).wait_send()
        return carry

    lax.fori_loop(0, n_tiles, wait_sends, 0)
    r_n_core, r_n_z = recvs.take(n_tiles), recvs.take()
    s_n_core = sends.take(n_tiles)

    def back_rows(half, tile):
        all_cols = pl.ds(pl.multiple_of(tile * W, W), W)
        total = dot_tn(WB[0, half], GQKV[0, :, all_cols])
        for m in range(1, 3):
            total = total + dot_tn(WB[m, half], GQKV[m, :, all_cols])
        return total

    def first_part(tile, carry):
        t, cols = tile_at(tile)
        PGS[t, :, cols] = back_rows(oc, tile).astype(BF)
        part_copy(PGS, RCG, tile, s_n_core, r_n_core, core).start()
        OPS[t, :, cols] = back_rows(c, tile).astype(BF)
        return carry

    lax.fori_loop(0, n_tiles, first_part, 0)

    def wait_first(tile, carry):
        part_copy(PGS, RCG, tile, s_n_core, r_n_core, core).wait_recv()
        return carry

    lax.fori_loop(0, n_tiles, wait_first, 0)
    SZG[0] = (OPS[1 - zz].astype(F32) + RCG[1 - zz].astype(F32)).astype(BF)
    push(SZG.at[0], RZN, r_n_z, zdev)

    for entry in f1_entries:
        pending[:] = [other for other in pending if other is not entry]
    loads = []
    for h in range(2):
        arrived(rf2_hbm.at[h], r_f2 + h)
        loads.append(local(rf2_hbm.at[h], ff_part(*spare[2 * h])))
    r_zf = recvs.take(4)
    final_cut = (R // 16 + 1) // 2 * 16
    final_chunks = ((0, final_cut), (final_cut, R - final_cut))
    for h in range(2):
        done(loads[h])
        low = (ff_value(h, dp) + ff_value(*spare[2 * h])).astype(BF)
        FB[dp // 2, h, ff_rows(dp), :] = low
        if h == 0:

            @pl.when(first_core)
            def _():
                ZF[0] = low

        for chunk, (start, size) in enumerate(final_chunks):
            part = FB.at[dp // 2, h, pl.ds(pl.multiple_of(lax.rem(dp, 2) * quarter + start, 16), size)]
            rows = pl.ds(start, size)
            push(part, ZF.at[1, rows], r_zf + (2 + chunk), (dp, z2, h), second_core)
            if h == 1:
                push(part, ZF.at[0, rows], r_zf + chunk, (dp, z, 1), first_core)

    arrived(RZO, r_out_z)
    branch_out = OPO[zz].astype(F32) + RCO[zz].astype(F32) + RZO[...].astype(F32)
    OPO[0] = (HID[zz, c] + branch_out + column(c, VEC_PROJ_BIAS)).astype(BF)
    l_out = local(OPO.at[0], out_o)

    for entry in q1_entries:
        sent(entry)
    q_spare = ((1 - xb, 0), (3 - xb, 0), (2 * (1 - yb), 1), (2 * (1 - yb) + 1, 1))
    q_kept = ((xb, 0), (2 + xb, 0), (2 * yb, 1), (2 * yb + 1, 1))
    loads = []
    for place in range(4):
        arrived(rq1_hbm.at[place], r_q1 + place)
        loads.append(local(rq1_hbm.at[place], DQ.at[q_spare[place][0], q_spare[place][1]]))
    for place in range(4):
        done(loads[place])
        (there, h), (here, unused) = q_spare[place], q_kept[place]
        DQ[here, h] = (DQ[here, h].astype(F32) + DQ[there, h].astype(F32)).astype(BF)
    push(DQ.at[xb + 2 * (1 - yb), 0], rq2_hbm.at[0], r_q2, ydev)
    push(DQ.at[2 * yb + 1 - xb, 1], rq2_hbm.at[1], r_q2 + 1, xdev)

    r_gf, r_gq = recvs.take(8), recvs.take(8)

    def gf_at(plane, first, size):
        return gf_o.at[pl.ds(pl.multiple_of(plane * quarter + first, 16), size)]

    def gq_at(plane, first, size):
        return gq_o.at[plane, pl.ds(first, size)]

    def spread(buf, out_at, chunk, r_base):
        first, size = final_chunks[chunk]
        push(buf.at[0, pl.ds(first, size)], out_at(dp, first, size), r_base + 4 * chunk, xdev)
        push(buf.at[0, pl.ds(first, size)], out_at(dp, first, size), r_base + (4 * chunk + 1), ydev)
        return local(buf.at[0, pl.ds(first, size)], out_at(dp, first, size))

    def spread_on(out_at, chunk, r_base):
        first, size = final_chunks[chunk]
        half = size // 32 * 16
        arrived(out_at(xn, first, size), r_base + 4 * chunk)
        part = out_at(xn, first, half)
        push(part, part, r_base + (4 * chunk + 2), ydev)
        arrived(out_at(yn, first, size), r_base + (4 * chunk + 1))
        part = out_at(yn, first + half, size - half)
        push(part, part, r_base + (4 * chunk + 3), xdev)

    def spread_end(out_at, chunk, r_base):
        first, size = final_chunks[chunk]
        half = size // 32 * 16
        arrived(out_at(dg, first, half), r_base + (4 * chunk + 2))
        arrived(out_at(dg, first + half, size - half), r_base + (4 * chunk + 3))

    def ff_final(chunk):
        first, size = final_chunks[chunk]
        rows = pl.ds(first, size)
        arrived(ZF.at[0, rows], r_zf + chunk, second_core)
        arrived(ZF.at[1, rows], r_zf + (2 + chunk))
        here = slice(first, first + size)
        ZF[0, here] = (ZF[0, here].astype(F32) + ZF[1, here].astype(F32)).astype(BF)
        return spread(ZF, gf_at, chunk, r_gf)

    l_gf = [ff_final(0)]

    done(l_x2)
    arrived(RZN, r_n_z)
    r_stat = recvs.take()
    grads = OPS[zz].astype(F32) + RCG[zz].astype(F32) + RZN[...].astype(F32)
    center, inv_std = ST1[zz, 0:1, :], ST1[zz, 1:2, :]
    normals = (XG[zz, c].astype(F32) - center) * inv_std
    scaled = grads * column(c, VEC_LN1_GAIN)
    STX[c, 0:1, :] = jnp.sum(scaled, axis=0, keepdims=True)
    STX[c, 1:2, :] = jnp.sum(scaled * normals, axis=0, keepdims=True)
    push(STX.at[c], STX.at[c], r_stat, core)
    VGC[:, 0:1] = jnp.sum(grads * normals, axis=1, keepdims=True)
    VGC[:, 1:2] = jnp.sum(grads, axis=1, keepdims=True)
    arrived(STX.at[oc], r_stat)
    sums = (STX[0] + STX[1]) * inv_d
    OPO[1] = (GH[...] + inv_std * (scaled - sums[0:1] - normals * sums[1:2])).astype(BF)
    l_ing = local(OPO.at[1], ing_o)

    r_sp, r_spz = recvs.take(4), recvs.take(8)
    turned = VGC[...].T
    SPR[dp, 0:6, 0:H] = turned[0:6, :]
    for peer in peers:
        push(SPR.at[dp], SPR.at[dp], r_sp + dp, (peer, z, c))

    loads = []
    for h in range(2):
        arrived(rq2_hbm.at[h], r_q2 + h)
        loads.append(local(rq2_hbm.at[h], DQ.at[q_spare[2 * h][0], h]))
    r_zq, r_zt = recvs.take(4), recvs.take(2)
    with_tail = (j < 3) & (dp < 3)
    next_block = jnp.minimum(j + 1, 3)
    for h in range(2):
        done(loads[h])
        low = (DQ[dp, h].astype(F32) + DQ[q_spare[2 * h][0], h].astype(F32)).astype(BF)
        DQ[dp, h] = low
        if h == 0:

            @pl.when(first_core)
            def _():
                ZQ[0] = low[0:R]

        push(DQ.at[dp, h, pl.ds(R, TAIL)], ZT.at[c], r_zt + c, (dp, next_block, h), with_tail)
    for chunk, (start, size) in enumerate(final_chunks):
        rows = pl.ds(start, size)
        for h in range(2):
            push(DQ.at[dp, h, rows], ZQ.at[1, rows], r_zq + (2 + chunk), (dp, z2, h), second_core)
        push(DQ.at[dp, 1, rows], ZQ.at[0, rows], r_zq + chunk, (dp, z, 1), first_core)

    l_gf.append(ff_final(1))
    spread_on(gf_at, 0, r_gf)

    for number in range(4):
        arrived(SPR.at[number], r_sp + number, dp != number)
    SPZ[z, c] = SPR[0] + SPR[1] + SPR[2] + SPR[3]
    for step in range(4):
        for side in range(2):
            if step == 0 and side == 0:
                continue
            target = (dp, lax.rem(z + step, 4), c if side == 0 else oc)
            push(SPZ.at[z, c], SPZ.at[z, c], r_spz + (2 * z + c), target)

    gets_tail = (z >= 1) & (dp < 3)

    def qkv_final(chunk):
        first, size = final_chunks[chunk]
        rows = pl.ds(first, size)
        arrived(ZQ.at[0, rows], r_zq + chunk, second_core)
        arrived(ZQ.at[1, rows], r_zq + (2 + chunk))
        here = slice(first, first + size)
        total = ZQ[0, here].astype(F32) + ZQ[1, here].astype(F32)
        ZQ[0, here] = total.astype(BF)
        if chunk == 0:
            for side in range(2):
                arrived(ZT.at[side], r_zt + side, gets_tail)

            @pl.when(gets_tail)
            def _():
                ZQ[0, 0:TAIL] = (total[0:TAIL] + ZT[0].astype(F32) + ZT[1].astype(F32)).astype(BF)

        return spread(ZQ, gq_at, chunk, r_gq)

    l_gq = [qkv_final(0)]
    spread_on(gf_at, 1, r_gf)
    l_gq.append(qkv_final(1))

    for step in range(4):
        for side in range(2):
            if step == 0 and side == 0:
                continue
            zv, cv = lax.rem(z + step, 4), c if side == 0 else oc
            arrived(SPZ.at[zv, cv], r_spz + (2 * zv + cv))
    vectors = SPZ[0, c] + SPZ[1, c] + SPZ[2, c] + SPZ[3, c]
    VOUT[...] = vectors
    VOUT[6:7, :] = SPZ[z, 0, 6:7, :] + SPZ[z2, 1, 6:7, :]
    l_vec_o = local(VOUT, vec_o)

    for chunk in range(2):
        spread_on(gq_at, chunk, r_gq)
    for chunk in range(2):
        spread_end(gf_at, chunk, r_gf)
        spread_end(gq_at, chunk, r_gq)
    for entry in (l_out, l_ing, l_vec_o, *l_gf, *l_gq):
        done(entry)

    def own_sends(slot):
        att_copy(j, slot, s_a_z, r_a_z, zdev).wait_send()
        att_copy(j, slot, s_a_core, r_a_core, core).wait_send()

    slots_of(j, own_sends)
    slots_of(
        owner_of(zp, c),
        lambda slot: att_copy(owner_of(zp, c), slot, s_a_fwd, r_a_fwd, core).wait_send(),
    )

    f2_copy(0).wait_send()
    f2_copy(1).wait_send()
    cot_forward().wait_send()

    for step in (1, 3, 2):
        for number in range(3):
            ow_copy(step, number).wait_send()

    def last_sends(tile, carry):
        part_copy(PGS, RCG, tile, s_n_core, r_n_core, core).wait_send()
        return carry

    lax.fori_loop(0, n_tiles, last_sends, 0)
    for entry in list(pending):
        sent(entry)
    assert sends.used <= SEND_COUNT and recvs.used <= RECV_COUNT and locs.used <= LOCAL_COUNT


def finish_kernel(
    out_in,
    ing_in,
    gf_in,
    gq_in,
    vec_in,
    out_o,
    ing_o,
    qkv_o,
    qvb_o,
    ow_o,
    fc_o,
    proj_o,
    v0,
    v1,
    v2,
    v3,
    v4,
    v5,
    v6,
    GF,
    GQ,
    FST,
    QST,
    OB,
    SEM,
):
    R, H = ow_o.shape
    count = GF.shape[0] // R
    whole = [
        pltpu.make_async_copy(out_in, OB.at[0], SEM.at[0]),
        pltpu.make_async_copy(ing_in, OB.at[1], SEM.at[1]),
    ]
    place = 2
    loads_q, loads_f = [], []
    for m in range(4):
        loads_q.append(pltpu.make_async_copy(gq_in.at[m], GQ.at[m], SEM.at[place + m]))
    place += 4
    for number in range(count):
        rows = pl.ds(number * R, R)
        loads_f.append(pltpu.make_async_copy(gf_in.at[rows], GF.at[rows], SEM.at[place + number]))
    place += count
    for copy in loads_f + loads_q + whole:
        copy.start()
    stores = []
    for number in range(count):
        loads_f[number].wait()
        rows = pl.ds(number * R, R)
        FST[rows, :] = GF[rows, :].astype(F32)
        half = count // 2
        dst = (fc_o if number < half else proj_o).at[pl.ds(number % half * R, R)]
        stores.append(pltpu.make_async_copy(FST.at[rows], dst, SEM.at[place + number]))
        stores[-1].start()
    place += count
    for m in range(4):
        loads_q[m].wait()
        QST[m] = GQ[m, :, 0:H].astype(F32)
        dst = qkv_o.at[m] if m < 3 else ow_o
        stores.append(pltpu.make_async_copy(QST.at[m], dst, SEM.at[place + m]))
        stores[-1].start()
    place += 4
    for number, dst in enumerate((out_o, ing_o)):
        whole[number].wait()
        stores.append(pltpu.make_async_copy(OB.at[number], dst, SEM.at[place + number]))
        stores[-1].start()
    first = H // LANES * LANES
    for number, m in enumerate((0, 2)):
        turned = GQ[m, :, first : first + LANES].astype(F32).T
        qvb_o[number : number + 1, :] = turned[H - first : H - first + 1, :]
    for number, v in enumerate((v0, v1, v2, v3, v4, v5, v6)):
        v[...] = vec_in[number, 0 : v.shape[0]]
    for copy in stores:
        copy.wait()


def fast_body(
    tokens,
    ln1_gain,
    ln1_bias,
    qkv_weight,
    qv_bias,
    out_weight,
    out_bias,
    ln2_gain,
    ln2_bias,
    fc_weight,
    fc_bias,
    proj_weight,
    proj_bias,
    doc_lengths,
    cotangent,
):
    H, T = tokens.shape
    R = out_weight.shape[0]
    FW = fc_weight.shape[1]
    D, S = 2 * H, 2 * T
    HP = (H // LANES + 1) * LANES
    EXT = 5 * HEAD_DIM
    NT = S // KEY_TILE
    wide = (FW // LANES + 1) * LANES
    w3 = jnp.transpose(qkv_weight, (1, 2, 0))
    shape = jax.ShapeDtypeStruct
    anywhere = pl.BlockSpec(memory_space=pl.ANY)
    outs = [
        shape((H, T), BF),
        shape((H, T), BF),
        shape((2 * H, FW), BF),
        shape((4, R, HP), BF),
        shape((8, FW), F32),
        shape((4, D // 4, FW), BF),
        shape((2, D // 4, FW), BF),
        shape((4, EXT, HP), BF),
        shape((2, EXT, HP), BF),
    ]
    vmem = pltpu.VMEM
    mask_rows = KEY_TILE * NT * (NT + 1) // 2
    scratch = [
        vmem((2, 2, H, T), BF),
        vmem((2, 2, H, T), BF),
        vmem((2, 2, H, T), BF),
        vmem((3, 2, EXT, H), BF),
        vmem((EXT, LANES), F32),
        vmem((2, D, H), BF),
        vmem((2, 2, H, FW), BF),
        vmem((FW, LANES), F32),
        vmem((2, 8, wide), F32),
        vmem((8, wide), F32),
        vmem((8, wide), F32),
        vmem((mask_rows, KEY_TILE), F32),
        vmem((3, EXT, S), BF),
        vmem((5, 8, S), F32),
        vmem((D, S), BF),
        vmem((2, 2, H, T), F32),
        vmem((2, 8, T), F32),
        vmem((2, 8, T), F32),
        vmem((2, 2, H, T), BF),
        vmem((FW, S), BF),
        vmem((FW, S), BF),
        vmem((2, H, T), BF),
        vmem((2, H, T), BF),
        vmem((2, H, T), BF),
        vmem((2, H, T), BF),
        vmem((2, H, T), BF),
        vmem((2, H, T), BF),
        vmem((2, H, T), BF),
        vmem((2, 2, H, T), BF),
        vmem((H, T), BF),
        vmem((H, T), BF),
        vmem((H, T), BF),
        vmem((EXT, S), BF),
        vmem((3, EXT, S), BF),
        vmem((HEAD_DIM, S), F32),
        vmem((HEAD_DIM, S), F32),
        vmem((2, 2 * H // 4, FW), BF),
        vmem((4, 2, EXT, HP), BF),
        vmem((2, R, HP), BF),
        vmem((2, EXT - R, HP), BF),
        vmem((H, T), F32),
        vmem((H, LANES), F32),
        vmem((2, 8, T), F32),
        vmem((4, 8, FW), F32),
        vmem((4, 2, 8, FW), F32),
        vmem((8, FW), F32),
        pltpu.SemaphoreType.DMA((SEND_COUNT,)),
        pltpu.SemaphoreType.DMA((RECV_COUNT,)),
        pltpu.SemaphoreType.DMA((LOCAL_COUNT,)),
    ]
    out_rows, in_rows, gf, gq, vectors = pl.pallas_call(
        layer_kernel,
        out_shape=outs,
        in_specs=[anywhere] * 6 + [pl.BlockSpec(memory_space=vmem)] * 9,
        out_specs=[anywhere] * len(outs),
        scratch_shapes=scratch,
        compiler_params=pltpu.CompilerParams(
            collective_id=0, has_side_effects=True, vmem_limit_bytes=VMEM_LIMIT
        ),
    )(
        tokens,
        cotangent,
        w3,
        out_weight,
        fc_weight,
        proj_weight,
        ln1_gain,
        ln1_bias,
        ln2_gain,
        ln2_bias,
        out_bias,
        proj_bias,
        fc_bias,
        qv_bias,
        doc_lengths,
    )[:5]
    in_vmem = pl.BlockSpec(memory_space=vmem)
    finals = pl.pallas_call(
        finish_kernel,
        out_shape=[
            shape((H, T), BF),
            shape((H, T), BF),
            shape((3, R, H), F32),
            shape((2, R), F32),
            shape((R, H), F32),
            shape((H, FW), F32),
            shape((H, FW), F32),
        ]
        + [shape((H,), F32)] * 6
        + [shape((FW,), F32)],
        in_specs=[anywhere] * 4 + [in_vmem],
        out_specs=[anywhere] * 3 + [in_vmem] + [anywhere] * 3 + [in_vmem] * 7,
        scratch_shapes=[
            vmem((D, FW), BF),
            vmem((4, R, HP), BF),
            vmem((D, FW), F32),
            vmem((4, R, H), F32),
            vmem((2, H, T), BF),
            pltpu.SemaphoreType.DMA((32,)),
        ],
        compiler_params=pltpu.CompilerParams(vmem_limit_bytes=VMEM_LIMIT),
    )(out_rows, in_rows, gf, gq, vectors)
    out_final, in_final, qkv_rows, bias_grad, ow_grad, fc_grad, proj_grad = finals[:7]
    ln1_gain_g, ln1_bias_g, ln2_gain_g, ln2_bias_g, out_bias_g, proj_bias_g, fc_bias_g = finals[7:]
    return (
        out_final,
        in_final,
        ln1_gain_g,
        ln1_bias_g,
        jnp.transpose(qkv_rows, (2, 0, 1)),
        bias_grad,
        ow_grad,
        out_bias_g,
        ln2_gain_g,
        ln2_bias_g,
        fc_grad,
        fc_bias_g,
        proj_grad,
        proj_bias_g,
    )


def choose_body(*arrays):
    sizes = {axis: lax.axis_size(axis) for axis in ("dp", "row", "col")}
    H, R = arrays[0].shape[0], arrays[5].shape[0]
    fits = sizes == {"dp": 4, "row": 4, "col": 2} and 4 * R == 2 * H == 17 * HEAD_DIM
    return (fast_body if fits else body)(*arrays)


def solution(mesh):
    return jax.shard_map(
        choose_body,
        mesh=mesh,
        in_specs=(
            P("col", ("dp", "row")),
            P("col"),
            P("col"),
            P("col", None, "row"),
            P(None, "row"),
            P("row", "col"),
            P("col"),
            P("col"),
            P("col"),
            P("col", "row"),
            P("row"),
            P("col", "row"),
            P("col"),
            P(("dp", "col"), None),
            P("col", ("dp", "row")),
        ),
        out_specs=(
            P("col", ("dp", "row")),
            P("col", ("dp", "row")),
            P("col"),
            P("col"),
            P("col", None, "row"),
            P(None, "row"),
            P("row", "col"),
            P("col"),
            P("col"),
            P("col"),
            P("col", "row"),
            P("row"),
            P("col", "row"),
            P("col"),
        ),
        check_vma=False,
    )
```

```python
from functools import partial
import math

import jax
import jax.numpy as jnp
from jax import lax
from jax.experimental import pallas as pl
from jax.experimental.pallas import tpu as pltpu
from jax.sharding import PartitionSpec as P

HEAD_DIM = 64


epsilon = 1e-05
score_scale = 0.125
masked_fill = -1e30
block_limit = 512


def feature_sums(first_sum, second_sum):
    return lax.psum((first_sum, second_sum), "col")


def norm_forward(values, gain_vec, shift_vec):
    feature_count = values.shape[1] * lax.axis_size("col")
    total_sum, square_sum = feature_sums(jnp.sum(values, axis=1), jnp.sum(values * values, axis=1))
    center = total_sum / feature_count
    spread = square_sum / feature_count - center * center
    inv_std = lax.rsqrt(spread + epsilon)
    normal = (values - center[:, None]) * inv_std[:, None]
    return (normal, inv_std, normal * gain_vec + shift_vec)


def norm_backward(upstream, normal, inv_std, gain_vec):
    feature_count = upstream.shape[1] * lax.axis_size("col")
    scaled = upstream * gain_vec
    plain_sum, cross_sum = feature_sums(jnp.sum(scaled, axis=1), jnp.sum(scaled * normal, axis=1))
    return inv_std[:, None] * (
        scaled - plain_sum[:, None] / feature_count - normal * (cross_sum[:, None] / feature_count)
    )


def gather_rows(values):
    return lax.all_gather(values, "row", axis=0, tiled=True)


def gather_cols(values):
    return lax.all_gather(values, "col", axis=0, tiled=True)


def sum_over_rows(row_term, row_total):
    return lax.psum_scatter(
        row_term(jnp.int32(0), row_total * lax.axis_size("row")),
        "row",
        scatter_dimension=0,
        tiled=True,
    )


def sum_over_cols(row_term, row_total):
    return lax.psum_scatter(
        row_term(jnp.int32(0), row_total * lax.axis_size("col")),
        "col",
        scatter_dimension=0,
        tiled=True,
    )


def to_heads(values):
    return lax.all_to_all(values, "row", split_axis=0, concat_axis=2, tiled=True)


def to_tokens(values):
    return lax.all_to_all(values, "row", split_axis=2, concat_axis=0, tiled=True)


def product_term(full_rows, matrix):

    def row_term(first_row, row_count):
        return jnp.dot(full_rows, matrix, preferred_element_type=jnp.float32)

    return row_term


def product_term_back(full_rows, matrix):

    def row_term(first_row, row_count):
        return lax.dot_general(
            full_rows, matrix, (((1,), (1,)), ((), ())), preferred_element_type=jnp.float32
        )

    return row_term


def slice_term(full_rows):

    def row_term(first_row, row_count):
        return full_rows

    return row_term


def inner_rows(left_side, right_side):
    return lax.dot_general(
        left_side, right_side, (((0,), (0,)), ((), ())), preferred_element_type=jnp.float32
    )


def segments_of(lengths, places):
    doc_ends = jnp.cumsum(lengths)
    segment = jnp.sum(
        (doc_ends[None, :] <= places[:, None]).astype(jnp.int32), axis=1, dtype=jnp.int32
    )
    return (segment, places >= doc_ends[-1])


def allowed_pairs(query_place, query_segment, query_padding, key_place, key_segment):
    causal = key_place[None, :] <= query_place[:, None]
    same_doc = key_segment[None, :] == query_segment[:, None]
    itself = key_place[None, :] == query_place[:, None]
    return causal & same_doc & (jnp.logical_not(query_padding)[:, None] | itself)


def attention_parts(queries, keyvals, lengths, query_place):
    seq_total = keyvals.shape[0]
    key_block_size = math.gcd(seq_total, block_limit)
    block_count = seq_total // key_block_size
    key_place = jnp.arange(seq_total, dtype=jnp.int32)
    key_segment = segments_of(lengths, key_place)[0]
    query_segment, query_padding = segments_of(lengths, query_place)
    blocked = (
        keyvals.reshape((block_count, key_block_size) + keyvals.shape[1:]),
        key_place.reshape(block_count, key_block_size),
        key_segment.reshape(block_count, key_block_size),
    )

    def block_scores(key_rows, place_rows, segment_rows):
        raw_scores = (
            jnp.einsum("qhd,khd->hqk", queries, key_rows, preferred_element_type=jnp.float32)
            * score_scale
        )
        allowed = allowed_pairs(
            query_place, query_segment, query_padding, place_rows, segment_rows
        )[None]
        return (raw_scores, allowed)

    return (blocked, block_scores)


def attention_forward(queries, blocked, block_scores):
    query_count, head_count, head_width = queries.shape

    def max_step(running, inputs):
        best_score, mass_sum = running
        kv_block, place_rows, segment_rows = inputs
        raw_scores, allowed = block_scores(kv_block[:, 0], place_rows, segment_rows)
        masked = jnp.where(allowed, raw_scores, masked_fill)
        new_best = jnp.maximum(best_score, jnp.max(masked, axis=2))
        fresh = jnp.sum(jnp.where(allowed, jnp.exp(masked - new_best[:, :, None]), 0.0), axis=2)
        return ((new_best, mass_sum * jnp.exp(best_score - new_best) + fresh), None)

    start_best = jnp.full((head_count, query_count), masked_fill, jnp.float32)
    start_mass = jnp.zeros((head_count, query_count), jnp.float32)
    (best_score, mass_sum), unused = lax.scan(max_step, (start_best, start_mass), blocked)
    log_sum = best_score + jnp.log(mass_sum)

    def out_step(running, inputs):
        kv_block, place_rows, segment_rows = inputs
        raw_scores, allowed = block_scores(kv_block[:, 0], place_rows, segment_rows)
        probs_low = jnp.where(allowed, jnp.exp(raw_scores - log_sum[:, :, None]), 0.0).astype(
            jnp.bfloat16
        )
        return (
            running
            + jnp.einsum(
                "hqk,khd->qhd", probs_low, kv_block[:, 1], preferred_element_type=jnp.float32
            ),
            None,
        )

    attended, unused = lax.scan(
        out_step, jnp.zeros((query_count, head_count, head_width), jnp.float32), blocked
    )
    return (attended, log_sum)


def attention_backward(queries, blocked, block_scores, log_sum, grad_attended):
    query_count, head_count, head_width = queries.shape

    def probs_and_grads(inputs):
        kv_block, place_rows, segment_rows = inputs
        raw_scores, allowed = block_scores(kv_block[:, 0], place_rows, segment_rows)
        probs_f = jnp.where(allowed, jnp.exp(raw_scores - log_sum[:, :, None]), 0.0)
        grad_probs = jnp.einsum(
            "qhd,khd->hqk", grad_attended, kv_block[:, 1], preferred_element_type=jnp.float32
        )
        return (probs_f, grad_probs)

    def delta_step(running, inputs):
        probs_f, grad_probs = probs_and_grads(inputs)
        return (running + jnp.sum(probs_f * grad_probs, axis=2), None)

    delta_sum, unused = lax.scan(
        delta_step, jnp.zeros((head_count, query_count), jnp.float32), blocked
    )

    def grad_step(running, inputs):
        kv_block = inputs[0]
        probs_f, grad_probs = probs_and_grads(inputs)
        grad_scores = (probs_f * (grad_probs - delta_sum[:, :, None])).astype(jnp.bfloat16)
        running = running + jnp.einsum(
            "hqk,khd->qhd", grad_scores, kv_block[:, 0], preferred_element_type=jnp.float32
        )
        grad_keys = (
            jnp.einsum("hqk,qhd->khd", grad_scores, queries, preferred_element_type=jnp.float32)
            * score_scale
        )
        grad_values = jnp.einsum(
            "hqk,qhd->khd",
            probs_f.astype(jnp.bfloat16),
            grad_attended,
            preferred_element_type=jnp.float32,
        )
        return (running, jnp.stack([grad_keys, grad_values], axis=1))

    grad_queries, grad_keyvals = lax.scan(
        grad_step, jnp.zeros((query_count, head_count, head_width), jnp.float32), blocked
    )
    seq_total = grad_keyvals.shape[0] * grad_keyvals.shape[1]
    return (grad_queries * score_scale, grad_keyvals.reshape(seq_total, 2, head_count, head_width))


def body(
    tokens,
    ln1_gain,
    ln1_bias,
    qkv_weight,
    qv_bias,
    out_weight,
    out_bias,
    ln2_gain,
    ln2_bias,
    fc_weight,
    fc_bias,
    proj_weight,
    proj_bias,
    doc_lengths,
    cotangent,
):
    count_rows = lax.axis_size("row")
    count_cols = lax.axis_size("col")
    grid_rows = tokens.shape[1]
    col_width = tokens.shape[0]
    row_width = out_weight.shape[0]
    seq_rows = grid_rows * count_rows // count_cols
    query_rows = seq_rows // count_rows
    full_width = col_width * count_cols
    head_count = full_width // HEAD_DIM
    tokens_f = tokens.astype(jnp.float32).T
    normal1, inv_std1, shaped1 = norm_forward(tokens_f, ln1_gain, ln1_bias)
    qkv_flat = qkv_weight.reshape(col_width, 3 * row_width)
    gathered1 = gather_rows(shaped1.astype(jnp.bfloat16))
    mixed_qkv = sum_over_cols(product_term(gathered1, qkv_flat), seq_rows).reshape(
        seq_rows, 3, row_width
    )
    bias_three = jnp.stack([qv_bias[0], jnp.zeros_like(qv_bias[0]), qv_bias[1]])
    qkv_low = (mixed_qkv + bias_three).astype(jnp.bfloat16)
    local_qkv = to_heads(qkv_low).reshape(query_rows, 3, head_count, HEAD_DIM)
    queries = local_qkv[:, 0]
    keyvals = lax.all_gather(local_qkv[:, 1:], "row", axis=0, tiled=True)
    query_place = lax.axis_index("row") * query_rows + jnp.arange(query_rows, dtype=jnp.int32)
    blocked, block_scores = attention_parts(queries, keyvals, doc_lengths[0], query_place)
    attended_f, log_sum = attention_forward(queries, blocked, block_scores)
    attended_low = attended_f.reshape(query_rows, 1, full_width).astype(jnp.bfloat16)
    attended_grid = to_tokens(attended_low).reshape(seq_rows, row_width)
    gathered_att = gather_cols(attended_grid)
    branch = sum_over_rows(product_term(gathered_att, out_weight), grid_rows)
    hidden = tokens_f + (branch + out_bias)
    normal2, inv_std2, shaped2 = norm_forward(hidden, ln2_gain, ln2_bias)
    normed2 = shaped2.astype(jnp.bfloat16)
    gathered2 = gather_rows(normed2)
    pre_act = sum_over_cols(product_term(gathered2, fc_weight), seq_rows) + fc_bias
    active = jax.nn.gelu(pre_act, approximate=False).astype(jnp.bfloat16)
    gathered_act = gather_cols(active)
    projected = sum_over_rows(product_term_back(gathered_act, proj_weight), grid_rows)
    output = (hidden + projected + proj_bias).astype(jnp.bfloat16).T
    cotangent_rows = cotangent.T
    grad_out = cotangent_rows.astype(jnp.float32)
    unused, gelu_back = jax.vjp(partial(jax.nn.gelu, approximate=False), pre_act)
    grad_gathered = gather_rows(cotangent_rows)
    proj_weight_grad = inner_rows(grad_gathered, gathered_act)
    proj_bias_grad = jnp.sum(grad_gathered, axis=0, dtype=jnp.float32)
    grad_active = sum_over_cols(product_term(grad_gathered, proj_weight), seq_rows)
    grad_pre = gelu_back(grad_active)[0].astype(jnp.bfloat16)
    grad_pre_all = gather_cols(grad_pre)
    fc_weight_grad = inner_rows(gathered2, grad_pre_all)
    fc_bias_grad = jnp.sum(grad_pre_all, axis=0, dtype=jnp.float32)
    grad_normed2 = sum_over_rows(product_term_back(grad_pre_all, fc_weight), grid_rows)
    ln2_gain_part = jnp.sum(grad_normed2 * normal2, axis=0)
    ln2_bias_part = jnp.sum(grad_normed2, axis=0)
    grad_hidden = grad_out + norm_backward(grad_normed2, normal2, inv_std2, ln2_gain)
    branch_gathered = gather_rows(grad_hidden.astype(jnp.bfloat16))
    out_weight_grad = inner_rows(gathered_att, branch_gathered)
    out_bias_grad = jnp.sum(branch_gathered, axis=0, dtype=jnp.float32)
    grad_att_grid = sum_over_cols(product_term_back(branch_gathered, out_weight), seq_rows).astype(
        jnp.bfloat16
    )
    grad_attended = to_heads(grad_att_grid.reshape(seq_rows, 1, row_width)).reshape(
        query_rows, head_count, HEAD_DIM
    )
    grad_queries, grad_keyvals = attention_backward(
        queries, blocked, block_scores, log_sum, grad_attended
    )
    keyval_rows = sum_over_rows(slice_term(grad_keyvals), query_rows)
    grad_qkv_local = (
        jnp.concatenate([grad_queries[:, None], keyval_rows], axis=1)
        .astype(jnp.bfloat16)
        .reshape(query_rows, 3, full_width)
    )
    grad_qkv_grid = to_tokens(grad_qkv_local).reshape(seq_rows, 3 * row_width)
    qkv_gathered = gather_cols(grad_qkv_grid)
    qkv_weight_grad = inner_rows(gathered1, qkv_gathered).reshape(col_width, 3, row_width)
    qkv_bias_sums = jnp.sum(qkv_gathered, axis=0, dtype=jnp.float32).reshape(3, row_width)
    qv_bias_grad = jnp.stack([qkv_bias_sums[0], qkv_bias_sums[2]])
    grad_normed1 = sum_over_rows(product_term_back(qkv_gathered, qkv_flat), grid_rows)
    ln1_gain_part = jnp.sum(grad_normed1 * normal1, axis=0)
    ln1_bias_part = jnp.sum(grad_normed1, axis=0)
    input_grad = (
        (grad_hidden + norm_backward(grad_normed1, normal1, inv_std1, ln1_gain))
        .astype(jnp.bfloat16)
        .T
    )
    summed = lax.psum(
        (
            qkv_weight_grad,
            qv_bias_grad,
            out_weight_grad,
            out_bias_grad,
            fc_weight_grad,
            fc_bias_grad,
            proj_weight_grad,
            proj_bias_grad,
        ),
        "dp",
    )
    gain_sums = lax.psum(
        (ln1_gain_part, ln1_bias_part, ln2_gain_part, ln2_bias_part), ("dp", "row")
    )
    return (
        output,
        input_grad,
        gain_sums[0],
        gain_sums[1],
        summed[0],
        summed[1],
        summed[2],
        summed[3],
        gain_sums[2],
        gain_sums[3],
        summed[4],
        summed[5],
        summed[6],
        summed[7],
    )


BF = jnp.bfloat16
F32 = jnp.float32
MESH = pl.DeviceIdType.MESH
LANES = 128
KEY_TILE = 256
VEC_LN1_GAIN, VEC_LN1_BIAS, VEC_LN2_GAIN, VEC_LN2_BIAS, VEC_OUT_BIAS, VEC_PROJ_BIAS = range(6)


def dot_nn(left, right):
    return lax.dot_general(left, right, (((1,), (0,)), ((), ())), preferred_element_type=F32)


def dot_tn(left, right):
    return lax.dot_general(left, right, (((0,), (0,)), ((), ())), preferred_element_type=F32)


def dot_nt(left, right):
    return lax.dot_general(left, right, (((1,), (1,)), ((), ())), preferred_element_type=F32)


VMEM_LIMIT = 66_000_000


class Slots:
    def __init__(self):
        self.used = 0

    def take(self, count=1):
        first = self.used
        self.used += count
        return first


SEND_COUNT, RECV_COUNT, LOCAL_COUNT = 208, 208, 48


def layer_kernel(
    x_in,
    cot_in,
    w3_in,
    ow_in,
    fc_in,
    proj_in,
    ln1_gain_in,
    ln1_bias_in,
    ln2_gain_in,
    ln2_bias_in,
    out_bias_in,
    proj_bias_in,
    fc_bias_in,
    qv_bias_in,
    doc_in,
    out_o,
    ing_o,
    gf_o,
    gq_o,
    vec_o,
    rf1_hbm,
    rf2_hbm,
    rq1_hbm,
    rq2_hbm,
    XG,
    CG,
    N1,
    WB,
    QB,
    OWB,
    FB,
    COLS,
    PACK,
    PACKF,
    PACKN,
    MASK,
    QKV,
    LSE,
    ATT,
    HID,
    ST1,
    ST2,
    N2,
    ACT,
    GPRE,
    PGS,
    OPS,
    RCG,
    RCO,
    OPO,
    SZG,
    RZG,
    G2,
    SZO,
    RZO,
    RZN,
    DATT,
    GQKV,
    ACCK,
    ACCV,
    ZF,
    DQ,
    ZQ,
    ZT,
    GH,
    VGC,
    STX,
    SPR,
    SPZ,
    VOUT,
    SS,
    RS,
    LS,
):
    H, T = x_in.shape
    R = w3_in.shape[1]
    HP = DQ.shape[3]
    EXT = WB.shape[2]
    TAIL = EXT - R
    D = 2 * H
    S = 2 * T
    W = KEY_TILE
    Q = HEAD_DIM
    FW = fc_in.shape[1]
    per_tok = T // W
    n_tiles = S // W
    inv_d = 1.0 / D

    dp, z, c = lax.axis_index("dp"), lax.axis_index("row"), lax.axis_index("col")
    oc = 1 - c
    zz = lax.rem(z, 2)
    zp = z + 1 - 2 * zz
    z2 = lax.rem(z + 2, 4)
    j = lax.rem(z + 2 * c, 4)
    pair = z // 2
    core = (dp, z, oc)
    zdev = (dp, zp, c)
    xn = dp + 1 - 2 * lax.rem(dp, 2)
    yn = lax.rem(dp + 2, 4)
    dg = 3 - dp
    peers = (xn, yn, dg)
    xb, yb = lax.rem(dp, 2), dp // 2
    xdev, ydev = (xn, z, c), (yn, z, c)
    first_core, second_core = c == 0, c == 1

    sends, recvs, locs = Slots(), Slots(), Slots()
    pending = []

    def remote(src, dst, s_idx, r_idx, dev):
        return pltpu.make_async_remote_copy(
            src_ref=src,
            dst_ref=dst,
            send_sem=SS.at[s_idx],
            recv_sem=RS.at[r_idx],
            device_id=dev,
            device_id_type=MESH,
        )

    def when(cond, fn):
        if cond is None:
            fn()
        else:
            pl.when(cond)(fn)

    def push(src, dst, r_idx, dev, cond=None):
        copy = remote(src, dst, sends.take(), r_idx, dev)
        when(cond, copy.start)
        entry = [cond, copy]
        pending.append(entry)
        return entry

    def sent(entry):
        when(entry[0], entry[1].wait_send)
        pending[:] = [other for other in pending if other is not entry]

    def arrived(dst, r_idx, cond=None):
        when(cond, remote(dst, dst, 0, r_idx, core).wait_recv)

    def local(src, dst, cond=None):
        copy = pltpu.make_async_copy(src, dst, LS.at[locs.take()])
        when(cond, copy.start)
        return (cond, copy)

    def done(entry):
        when(entry[0], entry[1].wait)

    barrier = pltpu.get_barrier_semaphore()
    for step in range(4):
        for side in range(2):
            if step == 0 and side == 0:
                continue
            target = (dp, lax.rem(z + step, 4), c if side == 0 else oc)
            pl.semaphore_signal(barrier, inc=1, device_id=target, device_id_type=MESH)
    for peer in peers:
        pl.semaphore_signal(barrier, inc=1, device_id=(peer, z, c), device_id_type=MESH)
    pl.semaphore_wait(barrier, 10)

    r_x_core, r_x_z, r_x_fwd = recvs.take(), recvs.take(), recvs.take()
    r_w_core, r_w_z, r_w_xy, r_w_tail = recvs.take(), recvs.take(16), recvs.take(8), recvs.take(2)
    r_pack, r_packf, r_packn = recvs.take(), recvs.take(), recvs.take()
    r_f_core, r_f_z, r_f_xy = recvs.take(2), recvs.take(4), recvs.take(8)
    r_o_core, r_o_z, r_o_z0, r_o_xy, r_o_fwd = (
        recvs.take(),
        recvs.take(4),
        recvs.take(4),
        recvs.take(16),
        recvs.take(4),
    )

    def block(number):
        return pl.ds(pl.multiple_of(number * R, 16), R)

    quarter = D // 4
    odd = R - 4 * (R // 64) * 16
    piece = R // 64 * 16

    def quarter_rows(number):
        return pl.ds(pl.multiple_of(number * quarter, 16), quarter)

    def ow_piece(number, plane):
        return pl.ds(pl.multiple_of(number * R + odd + plane * piece, 16), piece)

    def ow_odd(number):
        return pl.ds(pl.multiple_of(number * R, 16), odd)

    my_quarter = quarter_rows(dp)
    more = H // 16 % 4
    share = H // 64 * 16

    def ff_share(plane, large):
        if large:
            return pl.ds(pl.multiple_of(plane * (share + 16), 16), share + 16)
        return pl.ds(pl.multiple_of(more * 16 + plane * share, 16), share)

    ff_kinds = ((True, dp < more), (False, dp >= more))
    w_pieces, row = [], 0
    for plane in range(4):
        left = (3 * R // 16 // 4 + (1 if plane < 3 * R // 16 % 4 else 0)) * 16
        while left:
            rows = min(left, R - row % R)
            w_pieces.append((plane, row // R, row % R, rows))
            row, left = row + rows, left - rows
    has_before = z >= 1
    bias_first = (LANES, LANES + (R // LANES + 1) * LANES)
    doc_count = doc_in.shape[1]
    w_entries = []
    for number, (plane, m, first, size) in enumerate(w_pieces):
        rows = pl.ds(first, size)
        w_entries.append(
            push(
                w3_in.at[m, rows], WB.at[m, c, rows], r_w_z + (2 * number + c), (dp, z2, 1), dp == plane
            )
        )
    pack = PACK.at[c]
    PACK[c] = jnp.zeros(PACK.shape[1:], F32)
    vectors_in = (ln1_gain_in, ln1_bias_in, ln2_gain_in, ln2_bias_in, out_bias_in, proj_bias_in, fc_bias_in)
    for number, vector in enumerate(vectors_in):
        PACK[c, number : number + 1, 0 : vector.shape[0]] = vector[...].astype(F32).reshape(1, -1)
    PACK[c, 7:8, 0:doc_count] = doc_in[...].astype(F32)
    for number in range(2):
        PACK[c, 7:8, bias_first[number] : bias_first[number] + R] = qv_bias_in[number : number + 1, :].astype(F32)
    push(x_in, XG.at[zz, c], r_x_z, zdev)
    push(x_in, XG.at[zz, c], r_x_core, core)
    push(pack, pack, r_pack, core)
    push(w3_in, WB.at[:, 1, pl.ds(0, R)], r_w_core, (dp, z, 0), second_core)
    for place in range(1, 4):
        rows = TAIL - 16 * (place - 1)
        head = w3_in.at[:, pl.ds(0, rows)]
        there = WB.at[:, c, pl.ds(R, rows)]
        push(head, there, r_w_tail + c, (dp, place - 1, 0), z == place)
        push(head, there, r_w_tail + c, (dp, (place + 1) % 4, 1), z == place)
    push(pack, PACKF, r_packf, (dp, z2, 1), first_core)
    push(pack, PACKN, r_packn, (dp, jnp.maximum(z - 1, 0), 0), has_before & first_core)
    push(pack, PACKN, r_packn, (dp, lax.rem(z + 1, 4), 1), has_before & first_core)
    l_x = local(x_in, XG.at[zz, c])
    l_w = local(w3_in, WB.at[:, 0, pl.ds(0, R)], first_core)
    push(fc_in, FB.at[0, 1], r_f_core, (dp, z, 0), second_core)
    push(proj_in, FB.at[1, 1], r_f_core + 1, (dp, z, 0), second_core)
    push(ow_in, OWB.at[c, block(z)], r_o_core, core)
    l_f = local(fc_in, FB.at[0, 0], first_core)
    l_p = local(proj_in, FB.at[1, 0], first_core)
    l_o = local(ow_in, OWB.at[c, block(z)])

    ff_entries = []

    def send_ff(kind):
        source = (fc_in, proj_in)[kind]
        for large, cond in ff_kinds:
            rows = ff_share(dp, large)
            push(source.at[rows], FB.at[kind, c, rows], r_f_z + (2 * kind + c), (dp, z2, 1), cond)

    def pass_ff(kind):
        for large, cond in ff_kinds:
            rows = ff_share(dp, large)
            for h in range(2):
                arrived(FB.at[kind, h, rows], r_f_z + (2 * kind + h), second_core & cond)
            part = FB.at[kind, :, rows]
            for peer in peers:
                ff_entries.append(
                    push(part, part, r_f_xy + (4 * kind + dp), (peer, z, 1), second_core & cond)
                )

    def ff_ready(kind):
        arrived(FB.at[kind, 1], r_f_core + kind, first_core)
        for plane in range(4):
            arrived(
                FB.at[kind, :, ff_share(plane, plane < more)],
                r_f_xy + (4 * kind + plane),
                second_core & (dp != plane),
            )

    for entry in w_entries:
        sent(entry)
    send_ff(0)

    VGC[...] = jnp.zeros_like(VGC)
    GQKV[...] = jnp.zeros_like(GQKV)

    def clear_tail(rows):
        WB[:, :, EXT - rows :, :] = jnp.zeros((3, 2, rows, H), BF)

    for place in range(1, 4):
        pl.when(j == place)(partial(clear_tail, 16 * place))

    arrived(PACK.at[oc], r_pack)
    lengths = PACK[pair, 7:8, 0:LANES]
    place_c = lax.broadcasted_iota(jnp.int32, (S, LANES), 0).astype(F32)
    place_r = lax.broadcasted_iota(jnp.int32, (8, S), 1).astype(F32)
    end = jnp.zeros((1, 1), F32)
    seg_c, seg_r = jnp.zeros_like(place_c), jnp.zeros_like(place_r)
    for number in range(doc_count):
        end = end + lengths[:, number : number + 1]
        seg_c = seg_c + jnp.where(end <= place_c, 1.0, 0.0)
        seg_r = seg_r + jnp.where(end <= place_r, 1.0, 0.0)
    seg_c = jnp.where(end <= place_c, place_c + 2.0 * S, seg_c)
    seg_r = jnp.where(end <= place_r, place_r + 2.0 * S, seg_r)
    for tile in range(n_tiles):
        rows = W * (tile + 1)
        first = W * tile * (tile + 1) // 2
        cols = slice(tile * W, (tile + 1) * W)
        key_seg = jnp.concatenate([seg_c[:rows]] * (W // LANES), axis=1)
        key_place = jnp.concatenate([place_c[:rows]] * (W // LANES), axis=1)
        ok = (key_seg == seg_r[0:1, cols]) & (key_place <= place_r[0:1, cols])
        MASK[first : first + rows, :] = jnp.where(ok, 0.0, masked_fill)

    for h in range(2):
        COLS[h * H : (h + 1) * H, 0:6] = PACK[h].T[0:H, 0:6]

    def column(h, which):
        if isinstance(h, int):
            return COLS[h * H : (h + 1) * H, which : which + 1]
        return COLS[pl.ds(pl.multiple_of(h * H, 16), H), which : which + 1]

    def stats_of(first_half, second_half):
        center = (
            jnp.sum(first_half, axis=0, keepdims=True) + jnp.sum(second_half, axis=0, keepdims=True)
        ) * inv_d
        square = (
            jnp.sum(first_half * first_half, axis=0, keepdims=True)
            + jnp.sum(second_half * second_half, axis=0, keepdims=True)
        ) * inv_d
        return center, lax.rsqrt(square - center * center + epsilon)

    def first_norm(t):
        halves = [XG[t, h].astype(F32) for h in range(2)]
        center, inv_std = stats_of(*halves)
        ST1[t, 0:1, :] = center
        ST1[t, 1:2, :] = inv_std
        for h in range(2):
            shaped = (halves[h] - center) * inv_std * column(h, VEC_LN1_GAIN) + column(
                h, VEC_LN1_BIAS
            )
            N1[t, h, 0:H, :] = shaped.astype(BF)

    done(l_x)
    arrived(XG.at[zz, oc], r_x_core)
    first_norm(zz)

    for number, (plane, m, first, size) in enumerate(w_pieces):
        cond = second_core & (dp == plane)
        rows = pl.ds(first, size)
        for h in range(2):
            arrived(WB.at[m, h, rows], r_w_z + (2 * number + h), cond)
        for peer in peers:
            push(WB.at[m, :, rows], WB.at[m, :, rows], r_w_xy + number, (peer, z, 1), cond)
    arrived(XG.at[1 - zz, c], r_x_z)
    e_xf = push(XG.at[1 - zz, c], XG.at[1 - zz, c], r_x_fwd, core)
    arrived(XG.at[1 - zz, oc], r_x_fwd)
    first_norm(1 - zz)

    done(l_w)
    pass_ff(0)
    for step in (1, 3, 2):
        target = (dp, lax.rem(z + step, 4), c)
        push(ow_in.at[ow_piece(0, dp)], OWB.at[c, ow_piece(z, dp)], r_o_z + z, target)
        push(ow_in.at[ow_odd(0)], OWB.at[c, ow_odd(z)], r_o_z0 + z, target)
    send_ff(1)
    arrived(WB.at[:, 1, pl.ds(0, R)], r_w_core, first_core)
    for number, (plane, m, first, size) in enumerate(w_pieces):
        arrived(WB.at[m, :, pl.ds(first, size)], r_w_xy + number, second_core & (dp != plane))
    for h in range(2):
        for place in range(3):
            arrived(WB.at[:, h, pl.ds(R, TAIL - 16 * place)], r_w_tail + h, j == place)

    arrived(PACKF, r_packf, second_core)
    arrived(PACKN, r_packn, j < 3)

    def bias_columns(source, rows, count):
        turned = source.T
        for m, first in ((0, bias_first[0]), (2, bias_first[1])):
            QB[rows : rows + count, m : m + 1] = turned[first : first + count, 7:8]

    QB[...] = jnp.zeros_like(QB)
    pl.when(first_core)(lambda: bias_columns(PACK[0], 0, R))
    pl.when(second_core)(lambda: bias_columns(PACKF[...], 0, R))
    pl.when(j < 3)(lambda: bias_columns(PACKN[...], R, TAIL))

    for t in range(2):
        for m in range(3):
            mixed = dot_nn(WB[m, 0], N1[t, 0]) + dot_nn(WB[m, 1], N1[t, 1])
            if m != 1:
                mixed = mixed + QB[:, m : m + 1]
            low = mixed.astype(BF)
            if m == 0:
                low = low * jnp.asarray(score_scale, BF)
            QKV[m, :, t * T : (t + 1) * T] = low


    r_a_z, r_a_core, r_a_fwd = recvs.take(5), recvs.take(5), recvs.take(5)
    s_a_z, s_a_core, s_a_fwd = sends.take(5), sends.take(5), sends.take(5)
    first_slot = jnp.where(j == 0, 0, 1)

    def head_rows(owner, slot):
        return pl.ds(pl.multiple_of(owner * (4 * Q) + slot * Q, Q), Q)

    def slot_rows(slot):
        return pl.ds(pl.multiple_of(slot * Q - 16 * j, 16), Q)

    def att_copy(owner, slot, s_base, r_base, dev):
        rows = head_rows(owner, slot)
        return remote(ATT.at[rows], ATT.at[rows], s_base + slot, r_base + slot, dev)

    s_o_xy = sends.take(9)

    def ow_copy(step, number):
        there = lax.rem(z + step, 4)
        rows = OWB.at[c, ow_piece(there, dp)]
        return remote(
            rows, rows, s_o_xy + (3 * (step - 1) + number), r_o_xy + (4 * dp + there), (peers[number], z, c)
        )

    def pass_ow():
        for step in (1, 3, 2):
            there = lax.rem(z + step, 4)
            arrived(OWB.at[c, ow_piece(there, dp)], r_o_z + there)
            for number in range(3):
                ow_copy(step, number).start()

    def attend(slot, carry):
        @pl.when(slot == 2)
        def _():
            pass_ow()

        rows = slot_rows(slot)
        out_rows = head_rows(j, slot)
        queries = QKV[0, rows, :]
        keys = QKV[1, rows, :].T
        values = QKV[2, rows, :]
        for tile in range(n_tiles):
            count = W * (tile + 1)
            first = W * tile * (tile + 1) // 2
            cols = slice(tile * W, (tile + 1) * W)
            scores = dot_nn(keys[:count], queries[:, cols]) + MASK[first : first + count, :]
            best = jnp.max(scores, axis=0, keepdims=True)
            weights = jnp.exp(scores - best)
            mass = jnp.sum(weights, axis=0, keepdims=True)
            probs_low = (weights * (1.0 / mass)).astype(BF)
            ATT[out_rows, cols] = dot_nn(values[:, :count], probs_low).astype(BF)
            LSE[slot, 0:1, cols] = best + jnp.log(mass)
        att_copy(j, slot, s_a_z, r_a_z, zdev).start()
        att_copy(j, slot, s_a_core, r_a_core, core).start()

        return carry

    lax.fori_loop(first_slot, 5, attend, 0)

    r_c_core, r_c_z, r_c_fwd = recvs.take(), recvs.take(), recvs.take()
    push(cot_in, CG.at[zz, c], r_c_z, zdev)
    push(cot_in, CG.at[zz, c], r_c_core, core)
    l_c = local(cot_in, CG.at[zz, c])

    pass_ff(1)

    for step in (1, 3, 2):
        there = lax.rem(z + step, 4)
        arrived(OWB.at[c, ow_odd(there)], r_o_z0 + there)
        for plane in range(4):
            arrived(OWB.at[c, ow_piece(there, plane)], r_o_xy + (4 * plane + there), dp != plane)
        push(OWB.at[c, block(there)], OWB.at[c, block(there)], r_o_fwd + there, core)

    def owner_of(zv, cv):
        return lax.rem(zv + 2 * cv, 4)

    def slots_of(owner, body):
        lax.fori_loop(jnp.where(owner == 0, 0, 1), 5, lambda slot, carry: (body(slot), carry)[1], 0)

    def pass_on(slot):
        att_copy(owner_of(zp, c), slot, s_a_fwd, r_a_z, core).wait_recv()
        att_copy(owner_of(zp, c), slot, s_a_fwd, r_a_fwd, core).start()

    slots_of(owner_of(zp, c), pass_on)
    slots_of(owner_of(z, oc), lambda slot: att_copy(owner_of(z, oc), slot, s_a_core, r_a_core, core).wait_recv())
    slots_of(owner_of(zp, oc), lambda slot: att_copy(owner_of(zp, oc), slot, s_a_fwd, r_a_fwd, core).wait_recv())
    done(l_o)
    arrived(OWB.at[oc, block(z)], r_o_core)
    for step in range(1, 4):
        there = lax.rem(z + step, 4)
        arrived(OWB.at[oc, block(there)], r_o_fwd + there)

    def project(tile, carry):
        t = tile // per_tok
        cols = pl.ds(pl.multiple_of(lax.rem(tile, per_tok) * W, W), W)
        all_cols = pl.ds(pl.multiple_of(tile * W, W), W)
        att = ATT[:, all_cols]
        halves = []
        for h in range(2):
            branch = dot_tn(OWB[h], att)
            halves.append(XG[t, h, :, cols].astype(F32) + (branch + column(h, VEC_OUT_BIAS)))
            HID[t, h, :, cols] = halves[h]
        center, inv_std = stats_of(*halves)
        ST2[t, 0:1, cols] = center
        ST2[t, 1:2, cols] = inv_std
        for h in range(2):
            shaped = (halves[h] - center) * inv_std * column(h, VEC_LN2_GAIN) + column(
                h, VEC_LN2_BIAS
            )
            N2[t, h, :, cols] = shaped.astype(BF)
        return carry

    lax.fori_loop(0, n_tiles, project, 0)

    done(l_f)
    ff_ready(0)

    @pl.when(first_core)
    def _():
        COLS[:, 6:7] = PACK[0].T[0:FW, 6:7]

    @pl.when(second_core)
    def _():
        COLS[:, 6:7] = PACKF[...].T[0:FW, 6:7]

    s_c_fwd = sends.take()

    def cot_forward():
        return remote(CG.at[1 - zz, c], CG.at[1 - zz, c], s_c_fwd, r_c_fwd, core)

    def other_cotangent():
        arrived(CG.at[1 - zz, c], r_c_z)
        cot_forward().start()
        arrived(CG.at[1 - zz, oc], r_c_fwd)


    r_g_core, r_p_core, r_g_z = recvs.take(n_tiles), recvs.take(n_tiles), recvs.take(n_tiles)
    s_g_core, s_p_core, s_g_z = sends.take(n_tiles), sends.take(n_tiles), sends.take(n_tiles)

    def tile_at(tile):
        t = tile // per_tok
        return t, pl.ds(pl.multiple_of(lax.rem(tile, per_tok) * W, W), W)

    def part_copy(buf, dst, tile, s_base, r_base, dev):
        t, cols = tile_at(tile)
        return remote(buf.at[t, :, cols], dst.at[t, :, cols], s_base + tile, r_base + tile, dev)

    def feed(tile, carry):
        t, cols = tile_at(tile)
        all_cols = pl.ds(pl.multiple_of(tile * W, W), W)
        pre = dot_tn(FB[0].reshape(D, FW), N2[t, :, :, cols].reshape(D, W)) + COLS[:, 6:7]
        phi = 0.5 * (1.0 + lax.erf(pre * (2.0**-0.5)))
        ACT[:, all_cols] = (pre * phi).astype(BF)
        slope = phi + pre * jnp.exp(pre * pre * -0.5) * ((2.0 * math.pi) ** -0.5)
        GPRE[:, all_cols] = slope.astype(BF)
        return carry

    lax.fori_loop(0, n_tiles, feed, 0)
    done(l_p)
    ff_ready(1)
    done(l_c)
    arrived(CG.at[zz, oc], r_c_core)

    def feed_back(order, carry):
        t = lax.rem(order + zz, 2)
        pl.when(order == 1)(other_cotangent)
        for number in range(per_tok):
            cols = slice(number * W, (number + 1) * W)
            all_cols = pl.ds(pl.multiple_of(t * T + number * W, W), W)
            grad_act = dot_tn(FB[1].reshape(D, FW), CG[t, :, :, cols].reshape(D, W))
            GPRE[:, all_cols] = (grad_act * GPRE[:, all_cols].astype(F32)).astype(BF)
            PGS[t, :, cols] = dot_nn(FB[0, oc], GPRE[:, all_cols]).astype(BF)
            part_copy(PGS, RCG, t * per_tok + number, s_g_core, r_g_core, core).start()
        for number in range(per_tok):
            cols = slice(number * W, (number + 1) * W)
            all_cols = pl.ds(pl.multiple_of(t * T + number * W, W), W)
            tile = t * per_tok + number
            own = dot_nn(FB[0, c], GPRE[:, all_cols])
            part_copy(PGS, RCG, tile, s_g_core, r_g_core, core).wait_recv()
            SZG[t, :, cols] = (own + RCG[t, :, cols].astype(F32)).astype(BF)
            part_copy(SZG, RZG, tile, s_g_z, r_g_z, zdev).start()
        return carry

    lax.fori_loop(0, 2, feed_back, 0)

    for entry in ff_entries:
        sent(entry)
    r_f1, r_f2 = recvs.take(4), recvs.take(2)
    f1_entries = []

    def ff_grads(number):
        for h in range(2):
            left, right = (N2, GPRE) if number < 2 else (CG, ACT)
            rows = slice(number % 2 * quarter, (number % 2 + 1) * quarter)
            total = dot_nt(left[0, h, rows, :], right[:, 0:T]) + dot_nt(left[1, h, rows, :], right[:, T:S])
            FB[number // 2, h, rows, :] = total.astype(BF)

    def ff_rows(number):
        return quarter_rows(lax.rem(number, 2))

    def ff_part(h, number):
        return FB.at[number // 2, h, ff_rows(number)]

    def ff_value(h, number):
        return FB[number // 2, h, ff_rows(number), :].astype(F32)

    def f1_push(h, number, place, dev, cond=None):
        f1_entries.append(push(ff_part(h, number), rf1_hbm.at[place], r_f1 + place, dev, cond))

    for number in range(2):
        ff_grads(number)
        f1_push(0, number, 0, xdev, xb != number)
        f1_push(1, number, 2 + number, ydev, yb == 1)

    def outward(tile, carry):
        t, cols = tile_at(tile)
        all_cols = pl.ds(pl.multiple_of(tile * W, W), W)
        OPS[t, :, cols] = dot_nn(FB[1, oc], ACT[:, all_cols]).astype(BF)
        part_copy(OPS, RCO, tile, s_p_core, r_p_core, core).start()
        OPO[t, :, cols] = dot_nn(FB[1, c], ACT[:, all_cols]).astype(BF)
        return carry

    lax.fori_loop(0, n_tiles, outward, 0)
    for number in range(2):
        ff_grads(2 + number)
        f1_push(0, 2 + number, 1, xdev, xb != number)
        f1_push(1, 2 + number, 2 + number, ydev, yb == 0)

    SPR[dp] = jnp.zeros(SPR.shape[1:], F32)
    SPR[dp, 6:7, :] = dot_nt(jnp.ones((16, S), BF), GPRE[...])[0:1, :]

    r_g_all = recvs.take(n_tiles)
    s_g_all = sends.take(n_tiles)

    def g2_copy(tile):
        t, cols = tile_at(tile)
        return remote(G2.at[t, c, :, cols], G2.at[t, c, :, cols], s_g_all + tile, r_g_all + tile, core)

    def g2_other(tile):
        t, cols = tile_at(tile)
        return remote(G2.at[t, oc, :, cols], G2.at[t, oc, :, cols], s_g_all + tile, r_g_all + tile, core)

    def join(tile, carry):
        t, cols = tile_at(tile)
        part_copy(SZG, RZG, tile, s_g_z, r_g_z, zdev).wait_recv()
        G2[t, c, :, cols] = (SZG[t, :, cols].astype(F32) + RZG[t, :, cols].astype(F32)).astype(BF)
        g2_copy(tile).start()
        return carry

    lax.fori_loop(0, n_tiles, join, 0)

    def norm_back(grads, normals, inv_std, gain_index):
        scaled = [grads[h] * column(h, gain_index) for h in range(2)]
        plain = sum(jnp.sum(scaled[h], axis=0, keepdims=True) for h in range(2)) * inv_d
        cross = sum(jnp.sum(scaled[h] * normals[h], axis=0, keepdims=True) for h in range(2)) * inv_d
        return [inv_std * (scaled[h] - plain - normals[h] * cross) for h in range(2)]

    def second_back(tile, carry):
        t, cols = tile_at(tile)
        g2_other(tile).wait_recv()
        center, inv_std = ST2[t, 0:1, cols], ST2[t, 1:2, cols]
        grads = [G2[t, h, :, cols].astype(F32) for h in range(2)]
        normals = [(HID[t, h, :, cols] - center) * inv_std for h in range(2)]
        back = norm_back(grads, normals, inv_std, VEC_LN2_GAIN)
        for h in range(2):
            grad_hidden = CG[t, h, :, cols].astype(F32) + back[h]
            XG[t, h, :, cols] = grad_hidden.astype(BF)

            @pl.when((t == zz) & (c == h))
            def _():
                GH[:, cols] = grad_hidden
                VGC[:, 2:3] = VGC[:, 2:3] + jnp.sum(grads[h] * normals[h], axis=1, keepdims=True)
                VGC[:, 3:4] = VGC[:, 3:4] + jnp.sum(grads[h], axis=1, keepdims=True)

        return carry

    sent(e_xf)
    lax.fori_loop(0, n_tiles, second_back, 0)
    GB = XG

    r_out_z = recvs.take()

    def wait_out(tile, carry):
        part_copy(OPS, RCO, tile, s_p_core, r_p_core, core).wait_recv()
        return carry

    lax.fori_loop(0, n_tiles, wait_out, 0)
    SZO[...] = (OPO[1 - zz].astype(F32) + RCO[1 - zz].astype(F32)).astype(BF)
    push(SZO, RZO, r_out_z, zdev)
    VGC[:, 4:5] = jnp.sum(GB[zz, c].astype(F32), axis=1, keepdims=True)
    VGC[:, 5:6] = jnp.sum(CG[zz, c].astype(F32), axis=1, keepdims=True)

    window = pl.ds(pl.multiple_of(j * (4 * Q), Q), 5 * Q)
    for t in range(2):
        DATT[:, t * T : (t + 1) * T] = (
            dot_nn(OWB[0, window, :], GB[t, 0]) + dot_nn(OWB[1, window, :], GB[t, 1])
        ).astype(BF)
    r_q1, r_q2 = recvs.take(4), recvs.take(2)
    q1_entries = []

    def q1_push(h, number, place, dev, cond=None):
        q1_entries.append(push(DQ.at[number, h], rq1_hbm.at[place], r_q1 + place, dev, cond))

    for h in range(2):
        total = dot_nt(ATT[block(j), 0:T], GB[0, h]) + dot_nt(ATT[block(j), T:S], GB[1, h])
        DQ[3, h, 0:R, 0:H] = total.astype(BF)
    q1_push(0, 3, 1, xdev, xb == 0)
    q1_push(1, 3, 3, ydev, yb == 0)
    l_x2 = local(x_in, XG.at[zz, c])

    s_f2 = sends.take(2)
    l_f1, l_f2 = locs.take(4), locs.take(2)

    def f2_copy(place):
        if place == 0:
            return remote(ff_part(0, xb + 2 * (1 - yb)), rf2_hbm.at[0], s_f2, r_f2, ydev)
        return remote(ff_part(1, 2 * yb + 1 - xb), rf2_hbm.at[1], s_f2 + 1, r_f2 + 1, xdev)

    spare = ((0, 1 - xb), (0, 3 - xb), (1, 2 * (1 - yb)), (1, 2 * (1 - yb) + 1))
    kept = ((0, xb), (0, 2 + xb), (1, 2 * yb), (1, 2 * yb + 1))

    def first_join():
        for entry in f1_entries:
            when(entry[0], entry[1].wait_send)
        def add(place):
            h, number = kept[place]
            total = ff_value(h, number) + ff_value(*spare[place])
            FB[number // 2, h, ff_rows(number), :] = total.astype(BF)

        for half in range(2):
            loads = []
            for place in (2 * half, 2 * half + 1):
                arrived(rf1_hbm.at[place], r_f1 + place)
                load = pltpu.make_async_copy(rf1_hbm.at[place], ff_part(*spare[place]), LS.at[l_f1 + place])
                load.start()
                loads.append(load)
            for side in range(2):
                loads[side].wait()
                add(2 * half + side)
            f2_copy(half).start()

    def attend_back(slot, carry):
        rows = slot_rows(slot)
        here = pl.ds(pl.multiple_of(slot * Q, Q), Q)
        queries = QKV[0, rows, :]
        keys_t = QKV[1, rows, :]
        keys = keys_t.T
        values = QKV[2, rows, :].T
        grads_out = DATT[here, :]
        for tile in reversed(range(n_tiles)):
            count = W * (tile + 1)
            first = W * tile * (tile + 1) // 2
            cols = slice(tile * W, (tile + 1) * W)
            scores = dot_nn(keys[:count], queries[:, cols]) + MASK[first : first + count, :]
            probs = jnp.exp(scores - LSE[slot, 0:1, cols])
            grad_probs = dot_nn(values[:count], grads_out[:, cols])
            delta = jnp.sum(probs * grad_probs, axis=0, keepdims=True)
            grad_scores = (probs * (grad_probs - delta)).astype(BF)
            probs_low = probs.astype(BF)
            part_v = dot_nt(grads_out[:, cols], probs_low)
            part_k = dot_nt(queries[:, cols], grad_scores)
            if tile == n_tiles - 1:
                ACCV[...] = part_v
                ACCK[...] = part_k
            else:
                ACCV[:, 0:count] = ACCV[:, 0:count] + part_v
                ACCK[:, 0:count] = ACCK[:, 0:count] + part_k
            GQKV[0, rows, cols] = (dot_nn(keys_t[:, :count], grad_scores) * score_scale).astype(BF)
        GQKV[1, rows, :] = ACCK[...].astype(BF)
        GQKV[2, rows, :] = ACCV[...].astype(BF)

        @pl.when(slot == 3)
        def _():
            first_join()

        return carry

    lax.fori_loop(first_slot, 5, attend_back, 0)

    for m in range(3):
        if m != 1:
            bias_sum = jnp.sum(GQKV[m].astype(F32), axis=1, keepdims=True)
        for h in range(2):
            total = dot_nt(GQKV[m, :, 0:T], N1[0, h]) + dot_nt(GQKV[m, :, T:S], N1[1, h])
            DQ[m, h, :, 0:H] = total.astype(BF)
            if m != 1:
                DQ[m, h, :, H : H + 1] = bias_sum.astype(BF)
        q1_push(0, m, m // 2, xdev, xb != m % 2)
        q1_push(1, m, 2 + m % 2, ydev, yb != m // 2)

    def wait_sends(tile, carry):
        part_copy(PGS, RCG, tile, s_g_core, r_g_core, core).wait_send()
        part_copy(OPS, RCO, tile, s_p_core, r_p_core, core).wait_send()
        part_copy(SZG, RZG, tile, s_g_z, r_g_z, zdev).wait_send()
        g2_copy(tile).wait_send()
        return carry

    lax.fori_loop(0, n_tiles, wait_sends, 0)
    r_n_core, r_n_z = recvs.take(n_tiles), recvs.take()
    s_n_core = sends.take(n_tiles)

    def back_rows(half, tile):
        all_cols = pl.ds(pl.multiple_of(tile * W, W), W)
        total = dot_tn(WB[0, half], GQKV[0, :, all_cols])
        for m in range(1, 3):
            total = total + dot_tn(WB[m, half], GQKV[m, :, all_cols])
        return total

    def first_part(tile, carry):
        t, cols = tile_at(tile)
        PGS[t, :, cols] = back_rows(oc, tile).astype(BF)
        part_copy(PGS, RCG, tile, s_n_core, r_n_core, core).start()
        OPS[t, :, cols] = back_rows(c, tile).astype(BF)
        return carry

    lax.fori_loop(0, n_tiles, first_part, 0)

    def wait_first(tile, carry):
        part_copy(PGS, RCG, tile, s_n_core, r_n_core, core).wait_recv()
        return carry

    lax.fori_loop(0, n_tiles, wait_first, 0)
    SZG[0] = (OPS[1 - zz].astype(F32) + RCG[1 - zz].astype(F32)).astype(BF)
    push(SZG.at[0], RZN, r_n_z, zdev)

    for entry in f1_entries:
        pending[:] = [other for other in pending if other is not entry]
    loads = []
    for h in range(2):
        arrived(rf2_hbm.at[h], r_f2 + h)
        loads.append(local(rf2_hbm.at[h], ff_part(*spare[2 * h])))
    r_zf = recvs.take(4)
    final_cut = (R // 16 + 1) // 2 * 16
    final_chunks = ((0, final_cut), (final_cut, R - final_cut))
    for h in range(2):
        done(loads[h])
        low = (ff_value(h, dp) + ff_value(*spare[2 * h])).astype(BF)
        FB[dp // 2, h, ff_rows(dp), :] = low
        if h == 0:

            @pl.when(first_core)
            def _():
                ZF[0] = low

        for chunk, (start, size) in enumerate(final_chunks):
            part = FB.at[dp // 2, h, pl.ds(pl.multiple_of(lax.rem(dp, 2) * quarter + start, 16), size)]
            rows = pl.ds(start, size)
            push(part, ZF.at[1, rows], r_zf + (2 + chunk), (dp, z2, h), second_core)
            if h == 1:
                push(part, ZF.at[0, rows], r_zf + chunk, (dp, z, 1), first_core)

    arrived(RZO, r_out_z)
    branch_out = OPO[zz].astype(F32) + RCO[zz].astype(F32) + RZO[...].astype(F32)
    OPO[0] = (HID[zz, c] + branch_out + column(c, VEC_PROJ_BIAS)).astype(BF)
    l_out = local(OPO.at[0], out_o)

    for entry in q1_entries:
        sent(entry)
    q_spare = ((1 - xb, 0), (3 - xb, 0), (2 * (1 - yb), 1), (2 * (1 - yb) + 1, 1))
    q_kept = ((xb, 0), (2 + xb, 0), (2 * yb, 1), (2 * yb + 1, 1))
    for half in range(2):
        loads = []
        for place in (2 * half, 2 * half + 1):
            arrived(rq1_hbm.at[place], r_q1 + place)
            loads.append(local(rq1_hbm.at[place], DQ.at[q_spare[place][0], q_spare[place][1]]))
        for side in range(2):
            done(loads[side])
            (there, h), (here, unused) = q_spare[2 * half + side], q_kept[2 * half + side]
            DQ[here, h] = (DQ[here, h].astype(F32) + DQ[there, h].astype(F32)).astype(BF)
        if half == 0:
            push(DQ.at[xb + 2 * (1 - yb), 0], rq2_hbm.at[0], r_q2, ydev)
        else:
            push(DQ.at[2 * yb + 1 - xb, 1], rq2_hbm.at[1], r_q2 + 1, xdev)

    r_gf, r_gq = recvs.take(8), recvs.take(8)

    def gf_at(plane, first, size):
        return gf_o.at[pl.ds(pl.multiple_of(plane * quarter + first, 16), size)]

    def gq_at(plane, first, size):
        return gq_o.at[plane, pl.ds(first, size)]

    def spread(buf, out_at, chunk, r_base):
        first, size = final_chunks[chunk]
        push(buf.at[0, pl.ds(first, size)], out_at(dp, first, size), r_base + 4 * chunk, xdev)
        push(buf.at[0, pl.ds(first, size)], out_at(dp, first, size), r_base + (4 * chunk + 1), ydev)
        return local(buf.at[0, pl.ds(first, size)], out_at(dp, first, size))

    def spread_on(out_at, chunk, r_base):
        first, size = final_chunks[chunk]
        half = size // 32 * 16
        arrived(out_at(xn, first, size), r_base + 4 * chunk)
        part = out_at(xn, first, half)
        push(part, part, r_base + (4 * chunk + 2), ydev)
        arrived(out_at(yn, first, size), r_base + (4 * chunk + 1))
        part = out_at(yn, first + half, size - half)
        push(part, part, r_base + (4 * chunk + 3), xdev)

    def spread_end(out_at, chunk, r_base):
        first, size = final_chunks[chunk]
        half = size // 32 * 16
        arrived(out_at(dg, first, half), r_base + (4 * chunk + 2))
        arrived(out_at(dg, first + half, size - half), r_base + (4 * chunk + 3))

    def ff_final(chunk):
        first, size = final_chunks[chunk]
        rows = pl.ds(first, size)
        arrived(ZF.at[0, rows], r_zf + chunk, second_core)
        arrived(ZF.at[1, rows], r_zf + (2 + chunk))
        here = slice(first, first + size)
        ZF[0, here] = (ZF[0, here].astype(F32) + ZF[1, here].astype(F32)).astype(BF)
        return spread(ZF, gf_at, chunk, r_gf)

    l_gf = [ff_final(0)]

    done(l_x2)
    arrived(RZN, r_n_z)
    r_stat = recvs.take()
    grads = OPS[zz].astype(F32) + RCG[zz].astype(F32) + RZN[...].astype(F32)
    center, inv_std = ST1[zz, 0:1, :], ST1[zz, 1:2, :]
    normals = (XG[zz, c].astype(F32) - center) * inv_std
    scaled = grads * column(c, VEC_LN1_GAIN)
    STX[c, 0:1, :] = jnp.sum(scaled, axis=0, keepdims=True)
    STX[c, 1:2, :] = jnp.sum(scaled * normals, axis=0, keepdims=True)
    push(STX.at[c], STX.at[c], r_stat, core)
    VGC[:, 0:1] = jnp.sum(grads * normals, axis=1, keepdims=True)
    VGC[:, 1:2] = jnp.sum(grads, axis=1, keepdims=True)
    arrived(STX.at[oc], r_stat)
    sums = (STX[0] + STX[1]) * inv_d
    OPO[1] = (GH[...] + inv_std * (scaled - sums[0:1] - normals * sums[1:2])).astype(BF)
    l_ing = local(OPO.at[1], ing_o)

    r_sp, r_spz = recvs.take(4), recvs.take(8)
    turned = VGC[...].T
    SPR[dp, 0:6, 0:H] = turned[0:6, :]
    for peer in peers:
        push(SPR.at[dp], SPR.at[dp], r_sp + dp, (peer, z, c))

    loads = []
    for h in range(2):
        arrived(rq2_hbm.at[h], r_q2 + h)
        loads.append(local(rq2_hbm.at[h], DQ.at[q_spare[2 * h][0], h]))
    r_zq, r_zt = recvs.take(4), recvs.take(2)
    with_tail = (j < 3) & (dp < 3)
    next_block = jnp.minimum(j + 1, 3)
    for h in range(2):
        done(loads[h])
        low = (DQ[dp, h].astype(F32) + DQ[q_spare[2 * h][0], h].astype(F32)).astype(BF)
        DQ[dp, h] = low
        if h == 0:

            @pl.when(first_core)
            def _():
                ZQ[0] = low[0:R]

        push(DQ.at[dp, h, pl.ds(R, TAIL)], ZT.at[c], r_zt + c, (dp, next_block, h), with_tail)
    for chunk, (start, size) in enumerate(final_chunks):
        rows = pl.ds(start, size)
        for h in range(2):
            push(DQ.at[dp, h, rows], ZQ.at[1, rows], r_zq + (2 + chunk), (dp, z2, h), second_core)
        push(DQ.at[dp, 1, rows], ZQ.at[0, rows], r_zq + chunk, (dp, z, 1), first_core)

    l_gf.append(ff_final(1))
    spread_on(gf_at, 0, r_gf)

    for number in range(4):
        arrived(SPR.at[number], r_sp + number, dp != number)
    SPZ[z, c] = SPR[0] + SPR[1] + SPR[2] + SPR[3]
    for step in range(4):
        for side in range(2):
            if step == 0 and side == 0:
                continue
            target = (dp, lax.rem(z + step, 4), c if side == 0 else oc)
            push(SPZ.at[z, c], SPZ.at[z, c], r_spz + (2 * z + c), target)

    gets_tail = (z >= 1) & (dp < 3)

    def qkv_final(chunk):
        first, size = final_chunks[chunk]
        rows = pl.ds(first, size)
        arrived(ZQ.at[0, rows], r_zq + chunk, second_core)
        arrived(ZQ.at[1, rows], r_zq + (2 + chunk))
        here = slice(first, first + size)
        total = ZQ[0, here].astype(F32) + ZQ[1, here].astype(F32)
        ZQ[0, here] = total.astype(BF)
        if chunk == 0:
            for side in range(2):
                arrived(ZT.at[side], r_zt + side, gets_tail)

            @pl.when(gets_tail)
            def _():
                ZQ[0, 0:TAIL] = (total[0:TAIL] + ZT[0].astype(F32) + ZT[1].astype(F32)).astype(BF)

        return spread(ZQ, gq_at, chunk, r_gq)

    l_gq = [qkv_final(0)]
    spread_on(gf_at, 1, r_gf)
    l_gq.append(qkv_final(1))

    for step in range(4):
        for side in range(2):
            if step == 0 and side == 0:
                continue
            zv, cv = lax.rem(z + step, 4), c if side == 0 else oc
            arrived(SPZ.at[zv, cv], r_spz + (2 * zv + cv))
    vectors = SPZ[0, c] + SPZ[1, c] + SPZ[2, c] + SPZ[3, c]
    VOUT[...] = vectors
    VOUT[6:7, :] = SPZ[z, 0, 6:7, :] + SPZ[z2, 1, 6:7, :]
    l_vec_o = local(VOUT, vec_o)

    for chunk in range(2):
        spread_on(gq_at, chunk, r_gq)
    for chunk in range(2):
        spread_end(gf_at, chunk, r_gf)
        spread_end(gq_at, chunk, r_gq)
    for entry in (l_out, l_ing, l_vec_o, *l_gf, *l_gq):
        done(entry)

    def own_sends(slot):
        att_copy(j, slot, s_a_z, r_a_z, zdev).wait_send()
        att_copy(j, slot, s_a_core, r_a_core, core).wait_send()

    slots_of(j, own_sends)
    slots_of(
        owner_of(zp, c),
        lambda slot: att_copy(owner_of(zp, c), slot, s_a_fwd, r_a_fwd, core).wait_send(),
    )

    f2_copy(0).wait_send()
    f2_copy(1).wait_send()
    cot_forward().wait_send()

    for step in (1, 3, 2):
        for number in range(3):
            ow_copy(step, number).wait_send()

    def last_sends(tile, carry):
        part_copy(PGS, RCG, tile, s_n_core, r_n_core, core).wait_send()
        return carry

    lax.fori_loop(0, n_tiles, last_sends, 0)
    for entry in list(pending):
        sent(entry)
    assert sends.used <= SEND_COUNT and recvs.used <= RECV_COUNT and locs.used <= LOCAL_COUNT


def finish_kernel(
    out_in,
    ing_in,
    gf_in,
    gq_in,
    vec_in,
    out_o,
    ing_o,
    qkv_o,
    qvb_o,
    ow_o,
    fc_o,
    proj_o,
    v0,
    v1,
    v2,
    v3,
    v4,
    v5,
    v6,
    GF,
    GQ,
    FST,
    QST,
    OB,
    SEM,
):
    R, H = ow_o.shape
    count = GF.shape[0] // R
    whole = [
        pltpu.make_async_copy(out_in, OB.at[0], SEM.at[0]),
        pltpu.make_async_copy(ing_in, OB.at[1], SEM.at[1]),
    ]
    place = 2
    loads_q, loads_f = [], []
    for m in range(4):
        loads_q.append(pltpu.make_async_copy(gq_in.at[m], GQ.at[m], SEM.at[place + m]))
    place += 4
    for number in range(count):
        rows = pl.ds(number * R, R)
        loads_f.append(pltpu.make_async_copy(gf_in.at[rows], GF.at[rows], SEM.at[place + number]))
    place += count
    for copy in loads_f + loads_q + whole:
        copy.start()
    stores = []
    for number in range(count):
        loads_f[number].wait()
        rows = pl.ds(number * R, R)
        FST[rows, :] = GF[rows, :].astype(F32)
        half = count // 2
        dst = (fc_o if number < half else proj_o).at[pl.ds(number % half * R, R)]
        stores.append(pltpu.make_async_copy(FST.at[rows], dst, SEM.at[place + number]))
        stores[-1].start()
    place += count
    for m in range(4):
        loads_q[m].wait()
        QST[m] = GQ[m, :, 0:H].astype(F32)
        dst = qkv_o.at[m] if m < 3 else ow_o
        stores.append(pltpu.make_async_copy(QST.at[m], dst, SEM.at[place + m]))
        stores[-1].start()
    place += 4
    for number, dst in enumerate((out_o, ing_o)):
        whole[number].wait()
        stores.append(pltpu.make_async_copy(OB.at[number], dst, SEM.at[place + number]))
        stores[-1].start()
    first = H // LANES * LANES
    for number, m in enumerate((0, 2)):
        turned = GQ[m, :, first : first + LANES].astype(F32).T
        qvb_o[number : number + 1, :] = turned[H - first : H - first + 1, :]
    for number, v in enumerate((v0, v1, v2, v3, v4, v5, v6)):
        v[...] = vec_in[number, 0 : v.shape[0]]
    for copy in stores:
        copy.wait()


def fast_body(
    tokens,
    ln1_gain,
    ln1_bias,
    qkv_weight,
    qv_bias,
    out_weight,
    out_bias,
    ln2_gain,
    ln2_bias,
    fc_weight,
    fc_bias,
    proj_weight,
    proj_bias,
    doc_lengths,
    cotangent,
):
    H, T = tokens.shape
    R = out_weight.shape[0]
    FW = fc_weight.shape[1]
    D, S = 2 * H, 2 * T
    HP = (H // LANES + 1) * LANES
    EXT = 5 * HEAD_DIM
    NT = S // KEY_TILE
    wide = (FW // LANES + 1) * LANES
    w3 = jnp.transpose(qkv_weight, (1, 2, 0))
    shape = jax.ShapeDtypeStruct
    anywhere = pl.BlockSpec(memory_space=pl.ANY)
    outs = [
        shape((H, T), BF),
        shape((H, T), BF),
        shape((2 * H, FW), BF),
        shape((4, R, HP), BF),
        shape((8, FW), F32),
        shape((4, D // 4, FW), BF),
        shape((2, D // 4, FW), BF),
        shape((4, EXT, HP), BF),
        shape((2, EXT, HP), BF),
    ]
    vmem = pltpu.VMEM
    mask_rows = KEY_TILE * NT * (NT + 1) // 2
    scratch = [
        vmem((2, 2, H, T), BF),
        vmem((2, 2, H, T), BF),
        vmem((2, 2, H, T), BF),
        vmem((3, 2, EXT, H), BF),
        vmem((EXT, LANES), F32),
        vmem((2, D, H), BF),
        vmem((2, 2, H, FW), BF),
        vmem((FW, LANES), F32),
        vmem((2, 8, wide), F32),
        vmem((8, wide), F32),
        vmem((8, wide), F32),
        vmem((mask_rows, KEY_TILE), F32),
        vmem((3, EXT, S), BF),
        vmem((5, 8, S), F32),
        vmem((D, S), BF),
        vmem((2, 2, H, T), F32),
        vmem((2, 8, T), F32),
        vmem((2, 8, T), F32),
        vmem((2, 2, H, T), BF),
        vmem((FW, S), BF),
        vmem((FW, S), BF),
        vmem((2, H, T), BF),
        vmem((2, H, T), BF),
        vmem((2, H, T), BF),
        vmem((2, H, T), BF),
        vmem((2, H, T), BF),
        vmem((2, H, T), BF),
        vmem((2, H, T), BF),
        vmem((2, 2, H, T), BF),
        vmem((H, T), BF),
        vmem((H, T), BF),
        vmem((H, T), BF),
        vmem((EXT, S), BF),
        vmem((3, EXT, S), BF),
        vmem((HEAD_DIM, S), F32),
        vmem((HEAD_DIM, S), F32),
        vmem((2, 2 * H // 4, FW), BF),
        vmem((4, 2, EXT, HP), BF),
        vmem((2, R, HP), BF),
        vmem((2, EXT - R, HP), BF),
        vmem((H, T), F32),
        vmem((H, LANES), F32),
        vmem((2, 8, T), F32),
        vmem((4, 8, FW), F32),
        vmem((4, 2, 8, FW), F32),
        vmem((8, FW), F32),
        pltpu.SemaphoreType.DMA((SEND_COUNT,)),
        pltpu.SemaphoreType.DMA((RECV_COUNT,)),
        pltpu.SemaphoreType.DMA((LOCAL_COUNT,)),
    ]
    out_rows, in_rows, gf, gq, vectors = pl.pallas_call(
        layer_kernel,
        out_shape=outs,
        in_specs=[anywhere] * 6 + [pl.BlockSpec(memory_space=vmem)] * 9,
        out_specs=[anywhere] * len(outs),
        scratch_shapes=scratch,
        compiler_params=pltpu.CompilerParams(
            collective_id=0, has_side_effects=True, vmem_limit_bytes=VMEM_LIMIT
        ),
    )(
        tokens,
        cotangent,
        w3,
        out_weight,
        fc_weight,
        proj_weight,
        ln1_gain,
        ln1_bias,
        ln2_gain,
        ln2_bias,
        out_bias,
        proj_bias,
        fc_bias,
        qv_bias,
        doc_lengths,
    )[:5]
    in_vmem = pl.BlockSpec(memory_space=vmem)
    finals = pl.pallas_call(
        finish_kernel,
        out_shape=[
            shape((H, T), BF),
            shape((H, T), BF),
            shape((3, R, H), F32),
            shape((2, R), F32),
            shape((R, H), F32),
            shape((H, FW), F32),
            shape((H, FW), F32),
        ]
        + [shape((H,), F32)] * 6
        + [shape((FW,), F32)],
        in_specs=[anywhere] * 4 + [in_vmem],
        out_specs=[anywhere] * 3 + [in_vmem] + [anywhere] * 3 + [in_vmem] * 7,
        scratch_shapes=[
            vmem((D, FW), BF),
            vmem((4, R, HP), BF),
            vmem((D, FW), F32),
            vmem((4, R, H), F32),
            vmem((2, H, T), BF),
            pltpu.SemaphoreType.DMA((32,)),
        ],
        compiler_params=pltpu.CompilerParams(vmem_limit_bytes=VMEM_LIMIT),
    )(out_rows, in_rows, gf, gq, vectors)
    out_final, in_final, qkv_rows, bias_grad, ow_grad, fc_grad, proj_grad = finals[:7]
    ln1_gain_g, ln1_bias_g, ln2_gain_g, ln2_bias_g, out_bias_g, proj_bias_g, fc_bias_g = finals[7:]
    return (
        out_final,
        in_final,
        ln1_gain_g,
        ln1_bias_g,
        jnp.transpose(qkv_rows, (2, 0, 1)),
        bias_grad,
        ow_grad,
        out_bias_g,
        ln2_gain_g,
        ln2_bias_g,
        fc_grad,
        fc_bias_g,
        proj_grad,
        proj_bias_g,
    )


def choose_body(*arrays):
    sizes = {axis: lax.axis_size(axis) for axis in ("dp", "row", "col")}
    H, R = arrays[0].shape[0], arrays[5].shape[0]
    fits = sizes == {"dp": 4, "row": 4, "col": 2} and 4 * R == 2 * H == 17 * HEAD_DIM
    return (fast_body if fits else body)(*arrays)


def solution(mesh):
    return jax.shard_map(
        choose_body,
        mesh=mesh,
        in_specs=(
            P("col", ("dp", "row")),
            P("col"),
            P("col"),
            P("col", None, "row"),
            P(None, "row"),
            P("row", "col"),
            P("col"),
            P("col"),
            P("col"),
            P("col", "row"),
            P("row"),
            P("col", "row"),
            P("col"),
            P(("dp", "col"), None),
            P("col", ("dp", "row")),
        ),
        out_specs=(
            P("col", ("dp", "row")),
            P("col", ("dp", "row")),
            P("col"),
            P("col"),
            P("col", None, "row"),
            P(None, "row"),
            P("row", "col"),
            P("col"),
            P("col"),
            P("col"),
            P("col", "row"),
            P("row"),
            P("col", "row"),
            P("col"),
        ),
        check_vma=False,
    )
```
